32 devices in a mesh: groups: 2 (over x), dap: 16 (over z, y, core).
Axes of the slice: x: 2, y: 2, z: 4, core: 2. Of those that a mesh axis runs over, the one named last changes fastest.
Arguments:
- pair_map: bfloat16 [64, 32, 128], P(('groups', 'dap')), parts along dimension 0, may hold values from -30 to 30
- cotangent: bfloat16 [64, 32, 128], P(('groups', 'dap')), parts along dimension 0, may hold values from -6 to 6
- lengths: int32 [2], P('groups'), parts along dimension 0, may hold values from 16 to 32
- norm_gains: float32 [3, 128], replicated, may hold values from 0.25 to 1.75
- edge_weight: bfloat16 [128, 512], replicated, may hold values from -0.5 to 0.5
- mult_gate_weight: bfloat16 [128, 128], replicated, may hold values from -0.5 to 0.5
- mult_out_weight: bfloat16 [128, 128], replicated, may hold values from -0.5 to 0.5
- attention_weight: bfloat16 [128, 512], replicated, may hold values from -0.5 to 0.5
- bias_weight: bfloat16 [128, 4], replicated, may hold values from -0.5 to 0.5
- attention_out_weight: bfloat16 [128, 128], replicated, may hold values from -0.5 to 0.5
Outputs:
- grad_pair: bfloat16 [64, 32, 128], P(('groups', 'dap')), parts along dimension 0
- grad_gains: float32 [6, 128], P('groups'), parts along dimension 0
- grad_edge: float32 [256, 512], P('groups'), parts along dimension 0
- grad_mult_gate: float32 [256, 128], P('groups'), parts along dimension 0
- grad_mult_out: float32 [256, 128], P('groups'), parts along dimension 0
- grad_attention: float32 [256, 512], P('groups'), parts along dimension 0
- grad_bias: float32 [256, 4], P('groups'), parts along dimension 0
- grad_attention_out: float32 [256, 128], P('groups'), parts along dimension 0
The draws below stay inside these ranges and needn't reach their ends.
There are 2 independent parts, one for each index of `groups`. The reference program is written for one: setup_inputs(seed, part) draws one part's arguments, and reference() takes and returns one part's arrays. A program takes and returns all parts, laid end to end along the dimension named above; an argument that names none is the same for every part. Nothing has to cross between parts.
Inputs may be any that keep to these rules, and one draw needn't show every extreme that they name: Residues from index lengths[0] on are padding.
All inputs are finite; a program needn't handle non-finite values.
Results may differ from the reference program's by a relative error of at most 0.013.
Values may be sent and summed in bfloat16 or wider, within the bound.
No kernel may reach another device: no remote copies, remote signals or barrier semaphores. Data moves between devices by JAX's collectives and lax.ppermute only.
A program may use at most 64 MiB of HBM per device.

```python
import math
import jax
import jax.numpy as jnp
from jax import lax

C = 128
HEADS = 4
HEAD_DIM = 32
N_RES = 32


def draw_pair_map(key, part):
    key = jax.random.fold_in(key, 11)
    base_key, rank_key = jax.random.split(key, 2)
    channel_rank = jax.random.permutation(rank_key, C).astype(jnp.float32)
    channel_scale = jnp.power(10.0, channel_rank / (C - 1))
    base_values = jnp.clip(jax.random.normal(base_key, (N_RES, N_RES, C)), -3.0, 3.0)
    return (base_values * channel_scale).astype(jnp.bfloat16)


def steps_of(rng, dims, shards, low, largest):
    def one(position, parts):
        heights = jax.random.uniform(jax.random.fold_in(jax.random.fold_in(rng, 6), position), (parts,), jnp.float32, low / len(shards), largest / len(shards))
        return jnp.repeat(jnp.exp(heights), dims[position] // parts).reshape((-1,) + (1,) * (len(dims) - position - 1))

    factor_of = one(*shards[0])
    for cut in shards[1:]:
        factor_of = factor_of * one(*cut)
    return factor_of


def centred(rng, shape, width, bound, pieces=(), held_as=jnp.bfloat16):
    gain = steps_of(rng, shape, pieces, -0.22, 0.18) if pieces else 1.0
    values = jax.random.normal(rng, shape, jnp.float32) * width * gain
    return jnp.minimum(jnp.maximum(values, -bound), bound).astype(held_as)


def setup_inputs(seed: int = 0, part: int = 0) -> dict:
    key_of = jax.random.split(jax.random.key(seed), 11)
    part_splits = jax.random.split(jax.random.fold_in(key_of[10], part), 11)
    return {
        "pair_map": draw_pair_map(jax.random.fold_in(jax.random.fold_in(key_of[10], part), 71), part),
        "cotangent": centred(part_splits[1], (N_RES, N_RES, C), 1.0, 6.0, ((0, 16),)),
        "lengths": jax.random.randint(part_splits[2], (1,), N_RES // 2, N_RES + 1).astype(jnp.int32),
        "norm_gains": jnp.clip(1.0 + 0.15 * jax.random.normal(key_of[3], (3, C), jnp.float32), 0.25, 1.75),
        "edge_weight": centred(key_of[4], (C, 4 * C), C ** -0.5, 0.5),
        "mult_gate_weight": centred(key_of[5], (C, C), C ** -0.5, 0.5),
        "mult_out_weight": centred(key_of[6], (C, C), C ** -0.5, 0.5),
        "attention_weight": centred(key_of[7], (C, 4 * HEADS * HEAD_DIM), C ** -0.5, 0.5),
        "bias_weight": centred(key_of[8], (C, HEADS), C ** -0.5, 0.5),
        "attention_out_weight": centred(key_of[9], (HEADS * HEAD_DIM, C), (HEADS * HEAD_DIM) ** -0.5, 0.5),
    }


epsilon = 1e-05

def norm_forward(values, gain_row):
    center = values - lax.optimization_barrier(jnp.mean(values, axis=-1, keepdims=True))
    inv_std = lax.rsqrt(lax.optimization_barrier(jnp.mean(center * center, axis=-1, keepdims=True)) + epsilon)
    normed = center * inv_std
    return (normed * gain_row, normed, inv_std)

def norm_backward(grad_out, normed, inv_std, gain_row):
    scaled = grad_out * gain_row
    first_mean = lax.optimization_barrier(jnp.mean(scaled, axis=-1, keepdims=True))
    second_mean = lax.optimization_barrier(jnp.mean(scaled * normed, axis=-1, keepdims=True))
    return inv_std * (scaled - first_mean - normed * second_mean)

def round_trip(values):
    return lax.optimization_barrier(values.astype(jnp.bfloat16)).astype(jnp.float32)

def exact_einsum(formula, first_op, second_op):
    return jnp.einsum(formula, first_op, second_op, precision=lax.Precision.HIGHEST)

def flat_product(left_side, right_side):
    result = jnp.dot(left_side.reshape(-1, left_side.shape[-1]), right_side, preferred_element_type=jnp.float32)
    return result.reshape(left_side.shape[:-1] + (right_side.shape[-1],))

def cell_sum(left_side, right_side):
    return jnp.dot(left_side.reshape(-1, left_side.shape[-1]).T, right_side.reshape(-1, right_side.shape[-1]), preferred_element_type=jnp.float32)

def reference(pair_map, cotangent, lengths, norm_gains, edge_weight, mult_gate_weight, mult_out_weight, attention_weight, bias_weight, attention_out_weight):
    full_size = pair_map.shape[0]
    channels = pair_map.shape[2]
    inner_width = HEADS * HEAD_DIM
    head_scale = 1.0 / math.sqrt(HEAD_DIM)
    valid_all = (jnp.arange(full_size) < lengths[0]).astype(jnp.float32)
    mask_pair = (valid_all[:, None] * valid_all[None, :])[:, :, None]
    pair_f32 = pair_map.astype(jnp.float32)
    normed_full, hat_in, scale_in = norm_forward(pair_f32, norm_gains[0])
    normed_x = normed_full.astype(jnp.bfloat16)
    projected = flat_product(normed_x, edge_weight)
    left_gate = projected[..., :channels]
    left_value = projected[..., channels:2 * channels]
    right_gate = projected[..., 2 * channels:3 * channels]
    right_value = projected[..., 3 * channels:]
    left_sig = jax.nn.sigmoid(left_gate)
    right_sig = jax.nn.sigmoid(right_gate)
    left_edges = round_trip(mask_pair * left_sig * left_value)
    right_edges = round_trip(mask_pair * right_sig * right_value)
    product = exact_einsum('ikc,jkc->ijc', left_edges, right_edges)
    update_full, hat_mid, scale_mid = norm_forward(product, norm_gains[1])
    update = update_full.astype(jnp.bfloat16)
    edge_out = flat_product(update, mult_out_weight)
    gate_sig = jax.nn.sigmoid(flat_product(normed_x, mult_gate_weight))
    middle = pair_f32 + gate_sig * edge_out
    normed_mid, hat_attn, scale_attn = norm_forward(middle, norm_gains[2])
    normed_y = normed_mid.astype(jnp.bfloat16)
    bias_cells = flat_product(normed_y, bias_weight).astype(jnp.bfloat16)
    packed = flat_product(normed_y, attention_weight).reshape(full_size, full_size, 4, HEADS, HEAD_DIM)
    query_vectors = round_trip(packed[:, :, 0] * head_scale)
    key_vectors = round_trip(packed[:, :, 1])
    value_vectors = round_trip(packed[:, :, 2])
    att_gate = jax.nn.sigmoid(packed[:, :, 3])
    grad_gated = flat_product(cotangent, attention_out_weight.T).reshape(full_size, full_size, HEADS, HEAD_DIM)
    grad_att = round_trip(grad_gated * att_gate)

    def attend_head(operands):
        query_head, key_head, value_head, bias_head, grad_head = operands
        scores = exact_einsum('ijd,kjd->jik', query_head, key_head) + bias_head.astype(jnp.float32).T[None]
        exp_scores = valid_all * jnp.exp(scores)
        attention = exp_scores / lax.optimization_barrier(jnp.sum(exp_scores, axis=-1, keepdims=True))
        attention_half = round_trip(attention)
        attended_head = exact_einsum('jik,kjd->ijd', attention_half, value_head)
        grad_attention = exact_einsum('ijd,kjd->jik', grad_head, value_head)
        row_dots = lax.optimization_barrier(jnp.sum(grad_head * attended_head, axis=-1)).T
        grad_scores = attention * (grad_attention - row_dots[:, :, None])
        scores_half = round_trip(grad_scores)
        grad_query_head = exact_einsum('jik,kjd->ijd', scores_half, key_head)
        grad_key_head = exact_einsum('jik,ijd->kjd', scores_half, query_head)
        grad_value_head = exact_einsum('jik,ijd->kjd', attention_half, grad_head)
        bias_grads = lax.optimization_barrier(jnp.sum(grad_scores, axis=0)).T
        return (attended_head, grad_query_head, grad_key_head, grad_value_head, bias_grads)
    head_first = (jnp.moveaxis(query_vectors, 2, 0), jnp.moveaxis(key_vectors, 2, 0), jnp.moveaxis(value_vectors, 2, 0), jnp.moveaxis(bias_cells, 2, 0), jnp.moveaxis(grad_att, 2, 0))
    attended, grad_query, grad_key, grad_value, bias_grads = lax.map(attend_head, head_first)
    attended = jnp.moveaxis(attended, 0, 2)
    grad_query = jnp.moveaxis(grad_query, 0, 2)
    grad_key = jnp.moveaxis(grad_key, 0, 2)
    grad_value = jnp.moveaxis(grad_value, 0, 2)
    gated = (att_gate * attended).astype(jnp.bfloat16).reshape(full_size, full_size, inner_width)
    attn_out_sum = cell_sum(gated, cotangent)
    grad_gate_pre = grad_gated * attended * att_gate * (1.0 - att_gate)
    grad_packed = jnp.stack([grad_query * head_scale, grad_key, grad_value, grad_gate_pre], axis=2)
    grad_packed = grad_packed.reshape(full_size, full_size, 4 * inner_width).astype(jnp.bfloat16)
    attention_sum = cell_sum(normed_y, grad_packed)
    bias_half = jnp.moveaxis(bias_grads, 0, 2).astype(jnp.bfloat16)
    bias_sum = cell_sum(normed_y, bias_half)
    grad_normed_y = round_trip(flat_product(grad_packed, attention_weight.T)) + flat_product(bias_half, bias_weight.T)
    gain_attn_sum = lax.optimization_barrier(jnp.sum(grad_normed_y * hat_attn, axis=(0, 1)))
    grad_middle = cotangent.astype(jnp.float32) + norm_backward(grad_normed_y, hat_attn, scale_attn, norm_gains[2])
    grad_edge_out = (grad_middle * gate_sig).astype(jnp.bfloat16)
    grad_gate = (grad_middle * edge_out * gate_sig * (1.0 - gate_sig)).astype(jnp.bfloat16)
    mult_out_sum = cell_sum(update, grad_edge_out)
    mult_gate_sum = cell_sum(normed_x, grad_gate)
    grad_update = flat_product(grad_edge_out, mult_out_weight.T)
    gain_mid_sum = lax.optimization_barrier(jnp.sum(grad_update * hat_mid, axis=(0, 1)))
    grad_product = round_trip(norm_backward(grad_update, hat_mid, scale_mid, norm_gains[1]))
    grad_left = exact_einsum('ijc,jkc->ikc', grad_product, right_edges)
    grad_right = exact_einsum('ijc,ikc->jkc', grad_product, left_edges)
    grad_proj = jnp.concatenate([grad_left * mask_pair * left_value * left_sig * (1.0 - left_sig), grad_left * mask_pair * left_sig, grad_right * mask_pair * right_value * right_sig * (1.0 - right_sig), grad_right * mask_pair * right_sig], axis=-1).astype(jnp.bfloat16)
    edge_sum = cell_sum(normed_x, grad_proj)
    grad_normed_x = flat_product(grad_proj, edge_weight.T) + flat_product(grad_gate, mult_gate_weight.T)
    gain_in_sum = lax.optimization_barrier(jnp.sum(grad_normed_x * hat_in, axis=(0, 1)))
    grad_pair = (grad_middle + norm_backward(grad_normed_x, hat_in, scale_in, norm_gains[0])).astype(jnp.bfloat16)
    inverse = 1.0 / full_size
    grad_gains = jnp.stack([gain_in_sum, gain_mid_sum, gain_attn_sum]) * inverse
    return (grad_pair, grad_gains, edge_sum * inverse, mult_gate_sum * inverse, mult_out_sum * inverse, attention_sum * inverse, bias_sum * inverse, attn_out_sum * inverse)
```

```python
import functools
import math

import jax
import jax.numpy as jnp
from jax import lax
from jax.experimental import pallas as pl
from jax.experimental.pallas import tpu as pltpu
from jax.sharding import PartitionSpec as P

HEADS = 4
HEAD_DIM = 32


epsilon = 1e-05


def norm_forward(values, gain_row):
    center = values - jnp.mean(values, axis=-1, keepdims=True)
    inv_std = lax.rsqrt(jnp.mean(center * center, axis=-1, keepdims=True) + epsilon)
    normed = center * inv_std
    return (normed * gain_row, normed, inv_std)


def norm_backward(grad_out, normed, inv_std, gain_row):
    scaled = grad_out * gain_row
    first_mean = jnp.mean(scaled, axis=-1, keepdims=True)
    second_mean = jnp.mean(scaled * normed, axis=-1, keepdims=True)
    return inv_std * (scaled - first_mean - normed * second_mean)


def distributed_plan(
    pair_map,
    cotangent,
    lengths,
    norm_gains,
    edge_weight,
    mult_gate_weight,
    mult_out_weight,
    attention_weight,
    bias_weight,
    attention_out_weight,
):
    row_count, full_size, channels = pair_map.shape
    inner_width = HEADS * HEAD_DIM
    head_scale = 1.0 / math.sqrt(HEAD_DIM)
    first_row = lax.axis_index("dap") * row_count
    real_count = lengths[0]
    valid_all = (jnp.arange(full_size) < real_count).astype(jnp.float32)
    valid_rows = (first_row + jnp.arange(row_count) < real_count).astype(jnp.float32)
    mask_pair = (valid_rows[:, None] * valid_all[None, :])[:, :, None]
    pair_f32 = pair_map.astype(jnp.float32)
    normed_full, hat_in, scale_in = norm_forward(pair_f32, norm_gains[0])
    normed_x = normed_full.astype(jnp.bfloat16)
    projected = jnp.einsum("rnc,cf->rnf", normed_x, edge_weight, preferred_element_type=jnp.float32)
    left_gate = projected[..., :channels]
    left_value = projected[..., channels : 2 * channels]
    right_gate = projected[..., 2 * channels : 3 * channels]
    right_value = projected[..., 3 * channels :]
    left_sig = jax.nn.sigmoid(left_gate)
    right_sig = jax.nn.sigmoid(right_gate)
    left_edges = (mask_pair * left_sig * left_value).astype(jnp.bfloat16)
    right_edges = (mask_pair * right_sig * right_value).astype(jnp.bfloat16)
    product = jnp.einsum(
        "ikc,jkc->ijc",
        left_edges,
        lax.all_gather(right_edges, "dap", axis=0, tiled=True),
        preferred_element_type=jnp.float32,
    )
    update_full, hat_mid, scale_mid = norm_forward(product, norm_gains[1])
    update = update_full.astype(jnp.bfloat16)
    edge_out = jnp.einsum(
        "rnc,cf->rnf", update, mult_out_weight, preferred_element_type=jnp.float32
    )
    gate_sig = jax.nn.sigmoid(
        jnp.einsum("rnc,cf->rnf", normed_x, mult_gate_weight, preferred_element_type=jnp.float32)
    )
    middle = pair_f32 + gate_sig * edge_out
    normed_mid, hat_attn, scale_attn = norm_forward(middle, norm_gains[2])
    normed_y = normed_mid.astype(jnp.bfloat16)
    bias_local = jnp.einsum(
        "kic,ch->hki", normed_y, bias_weight, preferred_element_type=jnp.float32
    ).astype(jnp.bfloat16)
    bias_whole = lax.all_gather(bias_local, "dap", axis=1, tiled=True)
    bias_query = jnp.swapaxes(bias_whole, 1, 2).astype(jnp.float32)
    column_y, column_cot = (
        lax.all_to_all(normed_y, "dap", split_axis=1, concat_axis=0, tiled=True),
        lax.all_to_all(cotangent, "dap", split_axis=1, concat_axis=0, tiled=True),
    )
    packed = jnp.einsum(
        "ijc,cf->ijf", column_y, attention_weight, preferred_element_type=jnp.float32
    )
    packed = packed.reshape(full_size, row_count, 4, HEADS, HEAD_DIM)
    query_vectors = (packed[:, :, 0] * head_scale).astype(jnp.bfloat16)
    key_vectors = packed[:, :, 1].astype(jnp.bfloat16)
    value_vectors = packed[:, :, 2].astype(jnp.bfloat16)
    att_gate = jax.nn.sigmoid(packed[:, :, 3])
    scores = (
        jnp.einsum(
            "ijhd,kjhd->jhik", query_vectors, key_vectors, preferred_element_type=jnp.float32
        )
        + bias_query[None]
    )
    exp_scores = valid_all * jnp.exp(scores)
    attention = exp_scores / jnp.sum(exp_scores, axis=-1, keepdims=True)
    attention_half = attention.astype(jnp.bfloat16)
    attended = jnp.einsum(
        "jhik,kjhd->ijhd", attention_half, value_vectors, preferred_element_type=jnp.float32
    )
    gated = (att_gate * attended).astype(jnp.bfloat16).reshape(full_size, row_count, inner_width)
    part_attn_out = jnp.einsum("ijf,ijc->fc", gated, column_cot, preferred_element_type=jnp.float32)
    grad_gated = jnp.einsum(
        "ijc,fc->ijf", column_cot, attention_out_weight, preferred_element_type=jnp.float32
    )
    grad_gated = grad_gated.reshape(full_size, row_count, HEADS, HEAD_DIM)
    grad_att = (grad_gated * att_gate).astype(jnp.bfloat16)
    grad_gate_pre = grad_gated * attended * att_gate * (1.0 - att_gate)
    grad_attention = jnp.einsum(
        "ijhd,kjhd->jhik", grad_att, value_vectors, preferred_element_type=jnp.float32
    )
    row_dots = jnp.transpose(jnp.sum(grad_att.astype(jnp.float32) * attended, axis=-1), (1, 2, 0))
    grad_scores = attention * (grad_attention - row_dots[..., None])
    scores_half = grad_scores.astype(jnp.bfloat16)
    grad_query = jnp.einsum(
        "jhik,kjhd->ijhd", scores_half, key_vectors, preferred_element_type=jnp.float32
    )
    grad_key = jnp.einsum(
        "jhik,ijhd->kjhd", scores_half, query_vectors, preferred_element_type=jnp.float32
    )
    grad_value = jnp.einsum(
        "jhik,ijhd->kjhd", attention_half, grad_att, preferred_element_type=jnp.float32
    )
    grad_packed = jnp.stack([grad_query * head_scale, grad_key, grad_value, grad_gate_pre], axis=2)
    grad_packed = grad_packed.reshape(full_size, row_count, 4 * inner_width).astype(jnp.bfloat16)
    part_attention = jnp.einsum(
        "ijc,ijf->cf", column_y, grad_packed, preferred_element_type=jnp.float32
    )
    column_grad = jnp.einsum(
        "ijf,cf->ijc", grad_packed, attention_weight, preferred_element_type=jnp.float32
    ).astype(jnp.bfloat16)
    row_grad = lax.all_to_all(column_grad, "dap", split_axis=0, concat_axis=1, tiled=True)
    score_sums = jnp.sum(grad_scores, axis=0)
    taken = score_sums
    bias_half = lax.psum_scatter(
        jnp.transpose(taken, (2, 0, 1)), "dap", scatter_dimension=0, tiled=True
    ).astype(jnp.bfloat16)
    part_bias = jnp.einsum("kic,khi->ch", normed_y, bias_half, preferred_element_type=jnp.float32)
    grad_normed_y = row_grad.astype(jnp.float32) + jnp.einsum(
        "khi,ch->kic", bias_half, bias_weight, preferred_element_type=jnp.float32
    )
    part_gain_attn = jnp.sum(grad_normed_y * hat_attn, axis=(0, 1))
    grad_middle = cotangent.astype(jnp.float32) + norm_backward(
        grad_normed_y, hat_attn, scale_attn, norm_gains[2]
    )
    grad_edge_out = (grad_middle * gate_sig).astype(jnp.bfloat16)
    grad_gate = (grad_middle * edge_out * gate_sig * (1.0 - gate_sig)).astype(jnp.bfloat16)
    part_mult_out = jnp.einsum(
        "rnc,rnf->cf", update, grad_edge_out, preferred_element_type=jnp.float32
    )
    part_mult_gate = jnp.einsum(
        "rnc,rnf->cf", normed_x, grad_gate, preferred_element_type=jnp.float32
    )
    grad_update = jnp.einsum(
        "rnf,cf->rnc", grad_edge_out, mult_out_weight, preferred_element_type=jnp.float32
    )
    part_gain_mid = jnp.sum(grad_update * hat_mid, axis=(0, 1))
    grad_product = norm_backward(grad_update, hat_mid, scale_mid, norm_gains[1]).astype(
        jnp.bfloat16
    )
    taken = grad_product
    grad_left = jnp.einsum(
        "ijc,jkc->ikc",
        taken,
        lax.all_gather(right_edges, "dap", axis=0, tiled=True),
        preferred_element_type=jnp.float32,
    )
    grad_cols = lax.all_to_all(grad_product, "dap", split_axis=1, concat_axis=0, tiled=True)
    taken = grad_cols
    grad_right = jnp.einsum(
        "ijc,ikc->jkc",
        taken,
        lax.all_gather(left_edges, "dap", axis=0, tiled=True),
        preferred_element_type=jnp.float32,
    )
    grad_proj = jnp.concatenate(
        [
            grad_left * mask_pair * left_value * left_sig * (1.0 - left_sig),
            grad_left * mask_pair * left_sig,
            grad_right * mask_pair * right_value * right_sig * (1.0 - right_sig),
            grad_right * mask_pair * right_sig,
        ],
        axis=-1,
    ).astype(jnp.bfloat16)
    part_edge = jnp.einsum("rnc,rnf->cf", normed_x, grad_proj, preferred_element_type=jnp.float32)
    grad_normed_x = jnp.einsum(
        "rnf,cf->rnc", grad_proj, edge_weight, preferred_element_type=jnp.float32
    )
    grad_normed_x = grad_normed_x + jnp.einsum(
        "rnf,cf->rnc", grad_gate, mult_gate_weight, preferred_element_type=jnp.float32
    )
    part_gain_in = jnp.sum(grad_normed_x * hat_in, axis=(0, 1))
    grad_pair = (
        grad_middle + norm_backward(grad_normed_x, hat_in, scale_in, norm_gains[0])
    ).astype(jnp.bfloat16)
    totals = lax.psum(
        (
            part_gain_in,
            part_gain_mid,
            part_edge,
            part_mult_gate,
            part_mult_out,
            part_gain_attn,
            part_attention,
            part_bias,
            part_attn_out,
        ),
        "dap",
    )
    (
        gain_in_sum,
        gain_mid_sum,
        edge_sum,
        mult_gate_sum,
        mult_out_sum,
        gain_attn_sum,
        attention_sum,
        bias_sum,
        attn_out_sum,
    ) = totals
    inverse = 1.0 / full_size
    grad_gains = jnp.stack([gain_in_sum, gain_mid_sum, gain_attn_sum]) * inverse
    return (
        grad_pair,
        grad_gains,
        edge_sum * inverse,
        mult_gate_sum * inverse,
        mult_out_sum * inverse,
        attention_sum * inverse,
        bias_sum * inverse,
        attn_out_sum * inverse,
    )


ROW_BLOCK = 8
VMEM_LIMIT = 56 * 2**20
HALF = jnp.bfloat16
FULL = jnp.float32


def dot_nn(left, right):
    return lax.dot_general(left, right, (((1,), (0,)), ((), ())), preferred_element_type=FULL)


def dot_nt(left, right):
    return lax.dot_general(left, right, (((1,), (1,)), ((), ())), preferred_element_type=FULL)


def dot_tn(left, right):
    return lax.dot_general(left, right, (((0,), (0,)), ((), ())), preferred_element_type=FULL)


def dot_wide(values, ones):
    high = values.astype(HALF)
    low = (values - high.astype(FULL)).astype(HALF)
    return dot_nn(high, ones) + dot_nn(low, ones)


def head_blocks(row_width, col_width, dtype):
    shape = (HEADS * row_width, HEADS * col_width)
    row = lax.broadcasted_iota(jnp.int32, shape, 0)
    col = lax.broadcasted_iota(jnp.int32, shape, 1)
    same = None
    for h in range(HEADS):
        here = (row >= h * row_width) & (row < (h + 1) * row_width)
        here = here & (col >= h * col_width) & (col < (h + 1) * col_width)
        same = here if same is None else same | here
    return jnp.where(same, 1.0, 0.0).astype(dtype)


def replicated_kernel(
    size,
    own_rows,
    pair_ref,
    cot_ref,
    lengths_ref,
    gains_ref,
    edge_w_ref,
    gate_w_ref,
    out_w_ref,
    att_w_ref,
    bias_w_ref,
    att_out_w_ref,
    grad_pair_ref,
    grad_gains_ref,
    grad_edge_ref,
    grad_gate_w_ref,
    grad_out_w_ref,
    grad_att_w_ref,
    grad_bias_ref,
    grad_att_out_ref,
    wide,
    half,
    grad_packed_ref,
    grad_proj_ref,
    bias_ref,
    bias_rep_ref,
):
    channels = pair_ref.shape[1]
    block = ROW_BLOCK * size
    blocks = size // ROW_BLOCK
    lanes = HEADS * size
    head_scale = 1.0 / math.sqrt(HEAD_DIM)
    (
        left_ref,
        right_ref,
        right_t_ref,
        left_a_ref,
        left_b_ref,
        right_a_ref,
        right_b_ref,
        gate_ref,
        cot_full_ref,
        hat_mid_ref,
        scale_mid_ref,
        edge_out_ref,
        hat_y_ref,
        scale_y_ref,
        y_ref,
        att_gate_ref,
        grad_gated_ref,
        grad_y_ref,
        grad_middle_ref,
        grad_product_ref,
    ) = (wide.at[at] for at in range(WIDE_ARRAYS))
    (
        x_half_ref,
        update_ref,
        y_t_ref,
        cot_t_ref,
        query_ref,
        key_ref,
        value_ref,
        grad_att_ref,
        gated_ref,
        grad_edge_out_ref,
    ) = (half.at[at] for at in range(HALF_ARRAYS))
    real = lengths_ref[0]
    gain_x = gains_ref[0:1, :]
    gain_mid = gains_ref[1:2, :]
    gain_y = gains_ref[2:3, :]

    def rows_of(at):
        return pl.ds(pl.multiple_of(at * block, block), block)

    def columns_of(ref, at):
        return jnp.concatenate(
            [ref[pl.ds(at * ROW_BLOCK + a, size, stride=size), :] for a in range(ROW_BLOCK)], axis=0
        )

    def project(at, carry):
        rows = rows_of(at)
        hat, _ = norm_of(pair_ref[rows, :].astype(FULL))
        normed = (hat * gain_x).astype(HALF)
        x_half_ref[rows, :] = normed
        projected = dot_nn(normed, edge_w_ref[...])
        gate_ref[rows, :] = jax.nn.sigmoid(dot_nn(normed, gate_w_ref[...]))
        shape = (ROW_BLOCK, size, channels)
        row = lax.broadcasted_iota(jnp.int32, shape, 0) + at * ROW_BLOCK
        col = lax.broadcasted_iota(jnp.int32, shape, 1)
        mask = jnp.where((row < real) & (col < real), 1.0, 0.0).reshape(block, channels)
        for side, (edge, first, second) in enumerate(
            ((left_ref, left_a_ref, left_b_ref), (right_ref, right_a_ref, right_b_ref))
        ):
            base = 2 * side * channels
            sig = jax.nn.sigmoid(projected[:, base : base + channels])
            value = projected[:, base + channels : base + 2 * channels]
            masked = mask * sig
            product = masked * value
            edge[rows, :] = product.astype(HALF).astype(FULL)
            first[rows, :] = product * (1.0 - sig)
            second[rows, :] = masked
        cot_full_ref[rows, :] = cot_ref[rows, :].astype(FULL)
        return carry

    lax.fori_loop(0, blocks, project, 0)

    def turn(at, carry):
        right_t_ref[rows_of(at), :] = columns_of(right_ref, at)
        return carry

    lax.fori_loop(0, blocks, turn, 0)

    def outer_sum(at, row_ref, row_stride, block_stride, block_ref):
        sums = [jnp.zeros((size, channels), FULL)] * ROW_BLOCK
        for k in range(size):
            whole = block_ref[k * size : (k + 1) * size, :]
            for a in range(ROW_BLOCK):
                row = (at * ROW_BLOCK + a) * block_stride + k * row_stride
                sums[a] = sums[a] + row_ref[pl.ds(row, 1), :] * whole
        return jnp.concatenate(sums, axis=0)

    def multiply(at, carry):
        rows = rows_of(at)
        product = outer_sum(at, left_ref, 1, size, right_t_ref)
        hat, scale = norm_of(product)
        hat_mid_ref[rows, :] = hat
        scale_mid_ref[rows, :] = jnp.broadcast_to(scale, hat.shape)
        update = (hat * gain_mid).astype(HALF)
        update_ref[rows, :] = update
        edge_out = dot_nn(update, out_w_ref[...])
        edge_out_ref[rows, :] = edge_out
        middle = pair_ref[rows, :].astype(FULL) + gate_ref[rows, :] * edge_out
        hat, scale = norm_of(middle)
        hat_y_ref[rows, :] = hat
        scale_y_ref[rows, :] = jnp.broadcast_to(scale, hat.shape)
        y_ref[rows, :] = hat * gain_y
        return carry

    lax.fori_loop(0, blocks, multiply, 0)

    lane = lax.broadcasted_iota(jnp.int32, (1, lanes), 1)
    eye_row = lax.broadcasted_iota(jnp.int32, (size, lanes), 0)
    eye_lane = lax.broadcasted_iota(jnp.int32, (size, lanes), 1)
    same_cell = eye_lane == eye_row
    real_lane = lane < real
    bias_rep = jnp.where(lane < size, bias_w_ref[:, 0:1].astype(FULL), 0.0)
    for h in range(1, HEADS):
        same_cell = same_cell | (eye_lane == eye_row + h * size)
        inside = (lane >= h * size) & (lane < (h + 1) * size)
        real_lane = real_lane & (lane < size) if h == 1 else real_lane
        real_lane = real_lane | (inside & (lane < h * size + real))
        bias_rep = jnp.where(inside, bias_w_ref[:, h : h + 1].astype(FULL), bias_rep)
    same_cell = jnp.where(same_cell, 1.0, 0.0)
    valid = jnp.where(real_lane, 1.0, 0.0)
    bias_rep_ref[...] = bias_rep.astype(HALF)

    def prepare(at, carry):
        rows = rows_of(at)
        y = columns_of(y_ref, at).astype(HALF)
        cot = columns_of(cot_full_ref, at).astype(HALF)
        y_t_ref[rows, :] = y
        cot_t_ref[rows, :] = cot
        packed = dot_nn(y, att_w_ref[...])
        query_ref[rows, :] = (packed[:, :channels] * head_scale).astype(HALF)
        key_ref[rows, :] = packed[:, channels : 2 * channels].astype(HALF)
        value_ref[rows, :] = packed[:, 2 * channels : 3 * channels].astype(HALF)
        gate = jax.nn.sigmoid(packed[:, 3 * channels :])
        att_gate_ref[rows, :] = gate
        grad_gated = dot_nt(cot, att_out_w_ref[...])
        grad_gated_ref[rows, :] = grad_gated
        grad_att_ref[rows, :] = (grad_gated * gate).astype(HALF)
        spread = dot_nn(y, bias_rep_ref[...]).astype(HALF).astype(FULL)
        spread = spread.reshape(ROW_BLOCK, size, lanes) * same_cell[None]
        bias_ref[pl.ds(at * ROW_BLOCK, ROW_BLOCK), :] = jnp.sum(spread, axis=1)
        return carry

    lax.fori_loop(0, blocks, prepare, 0)

    head_mask = head_blocks(size, HEAD_DIM, HALF)
    head_mask_full = head_blocks(size, HEAD_DIM, FULL)
    key_ones = head_blocks(size, size, HALF)
    dim_ones = head_blocks(HEAD_DIM, size, HALF)

    def attend(at, score_sum):
        rows = rows_of(at)
        parts = [slice(a * size, (a + 1) * size) for a in range(ROW_BLOCK)]
        query, key, value, grad_att = (
            ref[rows, :] for ref in (query_ref, key_ref, value_ref, grad_att_ref)
        )
        keys = [jnp.concatenate([key[p]] * HEADS, axis=0) * head_mask for p in parts]
        values = [jnp.concatenate([value[p]] * HEADS, axis=0) * head_mask for p in parts]
        bias = bias_ref[...]
        scores = jnp.concatenate(
            [dot_nt(query[p], keys[a]) + bias for a, p in enumerate(parts)], axis=0
        )
        exp_scores = valid * jnp.exp(scores)
        attention = exp_scores / dot_wide(exp_scores, key_ones)
        attention_half = attention.astype(HALF)
        attended = jnp.concatenate(
            [dot_nn(attention_half[p], values[a]) for a, p in enumerate(parts)], axis=0
        )
        grad_attention = jnp.concatenate(
            [dot_nt(grad_att[p], values[a]) for a, p in enumerate(parts)], axis=0
        )
        row_dots = dot_wide(grad_att.astype(FULL) * attended, dim_ones)
        grad_scores = attention * (grad_attention - row_dots)
        scores_half = grad_scores.astype(HALF)
        for p in parts:
            score_sum = score_sum + grad_scores[p]
        grad_query = jnp.concatenate(
            [dot_nn(scores_half[p], keys[a]) for a, p in enumerate(parts)], axis=0
        )

        def per_key(weights, vectors):
            folded = []
            for p in parts:
                whole = dot_tn(weights[p], vectors[p]) * head_mask_full
                folded.append(sum(whole[h * size : (h + 1) * size] for h in range(HEADS)))
            return jnp.concatenate(folded, axis=0)

        grad_key = per_key(scores_half, query)
        grad_value = per_key(attention_half, grad_att)
        gate = att_gate_ref[rows, :]
        gated = gate * attended
        gated_ref[rows, :] = gated.astype(HALF)
        grad_gate_pre = grad_gated_ref[rows, :] * gated * (1.0 - gate)
        grad_packed = jnp.concatenate(
            [
                (grad_query * head_scale).astype(HALF),
                grad_key.astype(HALF),
                grad_value.astype(HALF),
                grad_gate_pre.astype(HALF),
            ],
            axis=1,
        )
        grad_packed_ref[rows, : 4 * channels] = grad_packed
        grad_y_ref[rows, :] = dot_nt(grad_packed, att_w_ref[...])
        return score_sum

    score_sum = lax.fori_loop(0, blocks, attend, jnp.zeros((size, lanes), FULL))
    bias_ref[...] = score_sum.astype(HALF).astype(FULL)

    def spread_bias(at, carry):
        rows = rows_of(at)
        part = bias_ref[pl.ds(at * ROW_BLOCK, ROW_BLOCK), :]
        spread = (part[:, None, :] * same_cell[None]).reshape(block, lanes).astype(HALF)
        grad_packed_ref[rows, 4 * channels :] = spread
        grad_y_ref[rows, :] += dot_nt(spread, bias_rep_ref[...])
        return carry

    lax.fori_loop(0, blocks, spread_bias, 0)

    def middle_back(at, carry):
        rows = rows_of(at)
        grad_y = columns_of(grad_y_ref, at)
        grad_middle = cot_full_ref[rows, :] + norm_back(
            grad_y, hat_y_ref[rows, :], scale_y_ref[rows, :], gain_y
        )
        grad_middle_ref[rows, :] = grad_middle
        gate = gate_ref[rows, :]
        gated = grad_middle * gate
        grad_edge_out = gated.astype(HALF)
        grad_edge_out_ref[rows, :] = grad_edge_out
        grad_gate = gated * edge_out_ref[rows, :] * (1.0 - gate)
        grad_proj_ref[rows, 4 * channels :] = grad_gate.astype(HALF)
        grad_update = dot_nt(grad_edge_out, out_w_ref[...])
        grad_product = norm_back(grad_update, hat_mid_ref[rows, :], scale_mid_ref[rows, :], gain_mid)
        grad_product_ref[rows, :] = grad_product.astype(HALF).astype(FULL)
        return carry

    lax.fori_loop(0, blocks, middle_back, 0)

    def edges_back(at, carry):
        rows = rows_of(at)
        grad_left = outer_sum(at, grad_product_ref, 1, size, right_ref)
        grad_proj_ref[rows, :channels] = (grad_left * left_a_ref[rows, :]).astype(HALF)
        grad_proj_ref[rows, channels : 2 * channels] = (grad_left * left_b_ref[rows, :]).astype(HALF)
        grad_right = outer_sum(at, grad_product_ref, size, 1, left_ref)
        grad_proj_ref[rows, 2 * channels : 3 * channels] = (grad_right * right_a_ref[rows, :]).astype(HALF)
        grad_proj_ref[rows, 3 * channels : 4 * channels] = (grad_right * right_b_ref[rows, :]).astype(HALF)
        return carry

    lax.fori_loop(0, blocks, edges_back, 0)

    inverse = 1.0 / size
    x_half = x_half_ref[...]
    edge_sum = dot_tn(x_half, grad_proj_ref[:, : 4 * channels]) * inverse
    gate_sum = dot_tn(x_half, grad_proj_ref[:, 4 * channels :]) * inverse
    grad_edge_ref[...] = edge_sum
    grad_gate_w_ref[...] = gate_sum
    out_sum = dot_tn(update_ref[...], grad_edge_out_ref[...]) * inverse
    grad_out_w_ref[...] = out_sum
    y_t = y_t_ref[...]
    att_sum = dot_tn(y_t, grad_packed_ref[:, : 4 * channels]) * inverse
    grad_att_w_ref[...] = att_sum
    bias_sum = dot_tn(y_t, grad_packed_ref[:, 4 * channels :]) * inverse
    grad_att_out_ref[...] = dot_tn(gated_ref[...], cot_t_ref[...]) * inverse
    for h in range(HEADS):
        grad_bias_ref[:, h : h + 1] = jnp.sum(
            bias_sum[:, h * size : (h + 1) * size], axis=1, keepdims=True
        )

    def gain_sum(pairs):
        total = sum(
            jnp.sum(weight.astype(FULL) * grad, axis=1, keepdims=True) for weight, grad in pairs
        )
        return jnp.transpose(jnp.broadcast_to(total, (channels, channels)))[0:1, :]

    grad_gains_ref[0:1, :] = gain_sum(((edge_w_ref[...], edge_sum), (gate_w_ref[...], gate_sum))) / gain_x
    grad_gains_ref[1:2, :] = gain_sum(((out_w_ref[...], out_sum),)) / gain_mid
    grad_gains_ref[2:3, :] = gain_sum(((att_w_ref[...], att_sum), (bias_rep_ref[...], bias_sum))) / gain_y

    first, count = own_rows()
    own = pl.ds(pl.multiple_of(first * size, count * size), count * size)
    hat, scale = norm_of(pair_ref[own, :].astype(FULL))
    grad_x = dot_nt(grad_proj_ref[own, : 4 * channels], edge_w_ref[...])
    grad_x = grad_x + dot_nt(grad_proj_ref[own, 4 * channels :], gate_w_ref[...])
    grad_pair = grad_middle_ref[own, :] + norm_back(grad_x, hat, scale, gain_x)
    grad_pair_ref[...] = grad_pair.astype(grad_pair_ref.dtype)


WIDE_ARRAYS = 20
HALF_ARRAYS = 10


def norm_of(values):
    center = values - jnp.mean(values, axis=-1, keepdims=True)
    scale = lax.rsqrt(jnp.mean(center * center, axis=-1, keepdims=True) + epsilon)
    return center * scale, scale


def norm_back(grad_out, hat, scale, gain):
    scaled = grad_out * gain
    first_mean = jnp.mean(scaled, axis=-1, keepdims=True)
    second_mean = jnp.mean(scaled * hat, axis=-1, keepdims=True)
    return scale * (scaled - first_mean - hat * second_mean)


def scratch_of(size, channels):
    cells = size * size
    lanes = HEADS * size
    return [
        pltpu.VMEM((WIDE_ARRAYS, cells, channels), FULL),
        pltpu.VMEM((HALF_ARRAYS, cells, channels), HALF),
        pltpu.VMEM((cells, 4 * channels + lanes), HALF),
        pltpu.VMEM((cells, 5 * channels), HALF),
        pltpu.VMEM((size, lanes), FULL),
        pltpu.VMEM((channels, lanes), HALF),
    ]


def scratch_bytes(size, channels):
    return sum(math.prod(s.shape) * jnp.dtype(s.dtype).itemsize for s in scratch_of(size, channels))


def whole_crop(size, own_rows, row_count, *operands):
    channels = operands[0].shape[-1]
    out_shape = (
        jax.ShapeDtypeStruct((row_count * size, channels), HALF),
        jax.ShapeDtypeStruct((3, channels), FULL),
        jax.ShapeDtypeStruct((channels, 4 * channels), FULL),
        jax.ShapeDtypeStruct((channels, channels), FULL),
        jax.ShapeDtypeStruct((channels, channels), FULL),
        jax.ShapeDtypeStruct((channels, 4 * channels), FULL),
        jax.ShapeDtypeStruct((channels, HEADS), FULL),
        jax.ShapeDtypeStruct((channels, channels), FULL),
    )
    vmem = pl.BlockSpec(memory_space=pltpu.VMEM)
    in_specs = [vmem] * len(operands)
    in_specs[2] = pl.BlockSpec(memory_space=pltpu.SMEM)
    return pl.pallas_call(
        functools.partial(replicated_kernel, size, own_rows),
        out_shape=out_shape,
        in_specs=in_specs,
        out_specs=[vmem] * len(out_shape),
        scratch_shapes=scratch_of(size, channels),
        compiler_params=pltpu.CompilerParams(vmem_limit_bytes=VMEM_LIMIT),
    )(*operands)


def gather_rows(rows, axis_size):
    return lax.all_to_all(
        jnp.broadcast_to(rows[None], (axis_size,) + rows.shape), "dap", split_axis=0, concat_axis=0
    )


def replicated_plan(axis_size, pair_map, cotangent, *rest):
    row_count, size, channels = pair_map.shape
    both = gather_rows(jnp.stack([pair_map, cotangent]), axis_size)
    pair_whole = both[:, 0].reshape(size * size, channels)
    cot_whole = both[:, 1].reshape(size * size, channels)

    def own_rows():
        return lax.axis_index("dap") * row_count, row_count

    outs = whole_crop(size, own_rows, row_count, pair_whole, cot_whole, *rest)
    return (outs[0].reshape(pair_map.shape),) + tuple(outs[1:])


def per_device(axis_size, pair_map, *rest):
    _, size, channels = pair_map.shape
    if size % ROW_BLOCK == 0 and scratch_bytes(size, channels) <= VMEM_LIMIT // 2:
        return replicated_plan(axis_size, pair_map, *rest)
    return distributed_plan(pair_map, *rest)


def solution(mesh):
    return jax.shard_map(
        functools.partial(per_device, mesh.shape["dap"]),
        mesh=mesh,
        in_specs=(
            P(("groups", "dap"), None, None),
            P(("groups", "dap"), None, None),
            P("groups"),
            P(),
            P(),
            P(),
            P(),
            P(),
            P(),
            P(),
        ),
        out_specs=(
            P(("groups", "dap"), None, None),
            P("groups", None),
            P("groups", None),
            P("groups", None),
            P("groups", None),
            P("groups", None),
            P("groups", None),
            P("groups", None),
        ),
        check_vma=False,
    )
```

```python
import functools
import math

import jax
import jax.numpy as jnp
from jax import lax
from jax.experimental import pallas as pl
from jax.experimental.pallas import tpu as pltpu
from jax.sharding import PartitionSpec as P

HEADS = 4
HEAD_DIM = 32


epsilon = 1e-05


def norm_forward(values, gain_row):
    center = values - jnp.mean(values, axis=-1, keepdims=True)
    inv_std = lax.rsqrt(jnp.mean(center * center, axis=-1, keepdims=True) + epsilon)
    normed = center * inv_std
    return (normed * gain_row, normed, inv_std)


def norm_backward(grad_out, normed, inv_std, gain_row):
    scaled = grad_out * gain_row
    first_mean = jnp.mean(scaled, axis=-1, keepdims=True)
    second_mean = jnp.mean(scaled * normed, axis=-1, keepdims=True)
    return inv_std * (scaled - first_mean - normed * second_mean)


def distributed_plan(
    pair_map,
    cotangent,
    lengths,
    norm_gains,
    edge_weight,
    mult_gate_weight,
    mult_out_weight,
    attention_weight,
    bias_weight,
    attention_out_weight,
):
    row_count, full_size, channels = pair_map.shape
    inner_width = HEADS * HEAD_DIM
    head_scale = 1.0 / math.sqrt(HEAD_DIM)
    first_row = lax.axis_index("dap") * row_count
    real_count = lengths[0]
    valid_all = (jnp.arange(full_size) < real_count).astype(jnp.float32)
    valid_rows = (first_row + jnp.arange(row_count) < real_count).astype(jnp.float32)
    mask_pair = (valid_rows[:, None] * valid_all[None, :])[:, :, None]
    pair_f32 = pair_map.astype(jnp.float32)
    normed_full, hat_in, scale_in = norm_forward(pair_f32, norm_gains[0])
    normed_x = normed_full.astype(jnp.bfloat16)
    projected = jnp.einsum("rnc,cf->rnf", normed_x, edge_weight, preferred_element_type=jnp.float32)
    left_gate = projected[..., :channels]
    left_value = projected[..., channels : 2 * channels]
    right_gate = projected[..., 2 * channels : 3 * channels]
    right_value = projected[..., 3 * channels :]
    left_sig = jax.nn.sigmoid(left_gate)
    right_sig = jax.nn.sigmoid(right_gate)
    left_edges = (mask_pair * left_sig * left_value).astype(jnp.bfloat16)
    right_edges = (mask_pair * right_sig * right_value).astype(jnp.bfloat16)
    product = jnp.einsum(
        "ikc,jkc->ijc",
        left_edges,
        lax.all_gather(right_edges, "dap", axis=0, tiled=True),
        preferred_element_type=jnp.float32,
    )
    update_full, hat_mid, scale_mid = norm_forward(product, norm_gains[1])
    update = update_full.astype(jnp.bfloat16)
    edge_out = jnp.einsum(
        "rnc,cf->rnf", update, mult_out_weight, preferred_element_type=jnp.float32
    )
    gate_sig = jax.nn.sigmoid(
        jnp.einsum("rnc,cf->rnf", normed_x, mult_gate_weight, preferred_element_type=jnp.float32)
    )
    middle = pair_f32 + gate_sig * edge_out
    normed_mid, hat_attn, scale_attn = norm_forward(middle, norm_gains[2])
    normed_y = normed_mid.astype(jnp.bfloat16)
    bias_local = jnp.einsum(
        "kic,ch->hki", normed_y, bias_weight, preferred_element_type=jnp.float32
    ).astype(jnp.bfloat16)
    bias_whole = lax.all_gather(bias_local, "dap", axis=1, tiled=True)
    bias_query = jnp.swapaxes(bias_whole, 1, 2).astype(jnp.float32)
    column_y, column_cot = (
        lax.all_to_all(normed_y, "dap", split_axis=1, concat_axis=0, tiled=True),
        lax.all_to_all(cotangent, "dap", split_axis=1, concat_axis=0, tiled=True),
    )
    packed = jnp.einsum(
        "ijc,cf->ijf", column_y, attention_weight, preferred_element_type=jnp.float32
    )
    packed = packed.reshape(full_size, row_count, 4, HEADS, HEAD_DIM)
    query_vectors = (packed[:, :, 0] * head_scale).astype(jnp.bfloat16)
    key_vectors = packed[:, :, 1].astype(jnp.bfloat16)
    value_vectors = packed[:, :, 2].astype(jnp.bfloat16)
    att_gate = jax.nn.sigmoid(packed[:, :, 3])
    scores = (
        jnp.einsum(
            "ijhd,kjhd->jhik", query_vectors, key_vectors, preferred_element_type=jnp.float32
        )
        + bias_query[None]
    )
    exp_scores = valid_all * jnp.exp(scores)
    attention = exp_scores / jnp.sum(exp_scores, axis=-1, keepdims=True)
    attention_half = attention.astype(jnp.bfloat16)
    attended = jnp.einsum(
        "jhik,kjhd->ijhd", attention_half, value_vectors, preferred_element_type=jnp.float32
    )
    gated = (att_gate * attended).astype(jnp.bfloat16).reshape(full_size, row_count, inner_width)
    part_attn_out = jnp.einsum("ijf,ijc->fc", gated, column_cot, preferred_element_type=jnp.float32)
    grad_gated = jnp.einsum(
        "ijc,fc->ijf", column_cot, attention_out_weight, preferred_element_type=jnp.float32
    )
    grad_gated = grad_gated.reshape(full_size, row_count, HEADS, HEAD_DIM)
    grad_att = (grad_gated * att_gate).astype(jnp.bfloat16)
    grad_gate_pre = grad_gated * attended * att_gate * (1.0 - att_gate)
    grad_attention = jnp.einsum(
        "ijhd,kjhd->jhik", grad_att, value_vectors, preferred_element_type=jnp.float32
    )
    row_dots = jnp.transpose(jnp.sum(grad_att.astype(jnp.float32) * attended, axis=-1), (1, 2, 0))
    grad_scores = attention * (grad_attention - row_dots[..., None])
    scores_half = grad_scores.astype(jnp.bfloat16)
    grad_query = jnp.einsum(
        "jhik,kjhd->ijhd", scores_half, key_vectors, preferred_element_type=jnp.float32
    )
    grad_key = jnp.einsum(
        "jhik,ijhd->kjhd", scores_half, query_vectors, preferred_element_type=jnp.float32
    )
    grad_value = jnp.einsum(
        "jhik,ijhd->kjhd", attention_half, grad_att, preferred_element_type=jnp.float32
    )
    grad_packed = jnp.stack([grad_query * head_scale, grad_key, grad_value, grad_gate_pre], axis=2)
    grad_packed = grad_packed.reshape(full_size, row_count, 4 * inner_width).astype(jnp.bfloat16)
    part_attention = jnp.einsum(
        "ijc,ijf->cf", column_y, grad_packed, preferred_element_type=jnp.float32
    )
    column_grad = jnp.einsum(
        "ijf,cf->ijc", grad_packed, attention_weight, preferred_element_type=jnp.float32
    ).astype(jnp.bfloat16)
    row_grad = lax.all_to_all(column_grad, "dap", split_axis=0, concat_axis=1, tiled=True)
    score_sums = jnp.sum(grad_scores, axis=0)
    taken = score_sums
    bias_half = lax.psum_scatter(
        jnp.transpose(taken, (2, 0, 1)), "dap", scatter_dimension=0, tiled=True
    ).astype(jnp.bfloat16)
    part_bias = jnp.einsum("kic,khi->ch", normed_y, bias_half, preferred_element_type=jnp.float32)
    grad_normed_y = row_grad.astype(jnp.float32) + jnp.einsum(
        "khi,ch->kic", bias_half, bias_weight, preferred_element_type=jnp.float32
    )
    part_gain_attn = jnp.sum(grad_normed_y * hat_attn, axis=(0, 1))
    grad_middle = cotangent.astype(jnp.float32) + norm_backward(
        grad_normed_y, hat_attn, scale_attn, norm_gains[2]
    )
    grad_edge_out = (grad_middle * gate_sig).astype(jnp.bfloat16)
    grad_gate = (grad_middle * edge_out * gate_sig * (1.0 - gate_sig)).astype(jnp.bfloat16)
    part_mult_out = jnp.einsum(
        "rnc,rnf->cf", update, grad_edge_out, preferred_element_type=jnp.float32
    )
    part_mult_gate = jnp.einsum(
        "rnc,rnf->cf", normed_x, grad_gate, preferred_element_type=jnp.float32
    )
    grad_update = jnp.einsum(
        "rnf,cf->rnc", grad_edge_out, mult_out_weight, preferred_element_type=jnp.float32
    )
    part_gain_mid = jnp.sum(grad_update * hat_mid, axis=(0, 1))
    grad_product = norm_backward(grad_update, hat_mid, scale_mid, norm_gains[1]).astype(
        jnp.bfloat16
    )
    taken = grad_product
    grad_left = jnp.einsum(
        "ijc,jkc->ikc",
        taken,
        lax.all_gather(right_edges, "dap", axis=0, tiled=True),
        preferred_element_type=jnp.float32,
    )
    grad_cols = lax.all_to_all(grad_product, "dap", split_axis=1, concat_axis=0, tiled=True)
    taken = grad_cols
    grad_right = jnp.einsum(
        "ijc,ikc->jkc",
        taken,
        lax.all_gather(left_edges, "dap", axis=0, tiled=True),
        preferred_element_type=jnp.float32,
    )
    grad_proj = jnp.concatenate(
        [
            grad_left * mask_pair * left_value * left_sig * (1.0 - left_sig),
            grad_left * mask_pair * left_sig,
            grad_right * mask_pair * right_value * right_sig * (1.0 - right_sig),
            grad_right * mask_pair * right_sig,
        ],
        axis=-1,
    ).astype(jnp.bfloat16)
    part_edge = jnp.einsum("rnc,rnf->cf", normed_x, grad_proj, preferred_element_type=jnp.float32)
    grad_normed_x = jnp.einsum(
        "rnf,cf->rnc", grad_proj, edge_weight, preferred_element_type=jnp.float32
    )
    grad_normed_x = grad_normed_x + jnp.einsum(
        "rnf,cf->rnc", grad_gate, mult_gate_weight, preferred_element_type=jnp.float32
    )
    part_gain_in = jnp.sum(grad_normed_x * hat_in, axis=(0, 1))
    grad_pair = (
        grad_middle + norm_backward(grad_normed_x, hat_in, scale_in, norm_gains[0])
    ).astype(jnp.bfloat16)
    totals = lax.psum(
        (
            part_gain_in,
            part_gain_mid,
            part_edge,
            part_mult_gate,
            part_mult_out,
            part_gain_attn,
            part_attention,
            part_bias,
            part_attn_out,
        ),
        "dap",
    )
    (
        gain_in_sum,
        gain_mid_sum,
        edge_sum,
        mult_gate_sum,
        mult_out_sum,
        gain_attn_sum,
        attention_sum,
        bias_sum,
        attn_out_sum,
    ) = totals
    inverse = 1.0 / full_size
    grad_gains = jnp.stack([gain_in_sum, gain_mid_sum, gain_attn_sum]) * inverse
    return (
        grad_pair,
        grad_gains,
        edge_sum * inverse,
        mult_gate_sum * inverse,
        mult_out_sum * inverse,
        attention_sum * inverse,
        bias_sum * inverse,
        attn_out_sum * inverse,
    )


ROW_BLOCK = 8
VMEM_LIMIT = 24 * 2**20
HALF = jnp.bfloat16
FULL = jnp.float32


def dot_nn(left, right):
    return lax.dot_general(left, right, (((1,), (0,)), ((), ())), preferred_element_type=FULL)


def dot_nt(left, right):
    return lax.dot_general(left, right, (((1,), (1,)), ((), ())), preferred_element_type=FULL)


def dot_tn(left, right):
    return lax.dot_general(left, right, (((0,), (0,)), ((), ())), preferred_element_type=FULL)


def dot_wide(values, ones):
    high = values.astype(HALF)
    low = (values - high.astype(FULL)).astype(HALF)
    return dot_nn(high, ones) + dot_nn(low, ones)


def head_blocks(row_width, col_width, dtype):
    shape = (HEADS * row_width, HEADS * col_width)
    row = lax.broadcasted_iota(jnp.int32, shape, 0)
    col = lax.broadcasted_iota(jnp.int32, shape, 1)
    same = None
    for h in range(HEADS):
        here = (row >= h * row_width) & (row < (h + 1) * row_width)
        here = here & (col >= h * col_width) & (col < (h + 1) * col_width)
        same = here if same is None else same | here
    return jnp.where(same, 1.0, 0.0).astype(dtype)


def replicated_kernel(
    size,
    own_rows,
    same_ref,
    other_ref,
    lengths_ref,
    gains_ref,
    edge_w_ref,
    gate_w_ref,
    out_w_ref,
    att_w_ref,
    bias_w_ref,
    att_out_w_ref,
    grad_pair_ref,
    grad_gains_ref,
    grad_edge_ref,
    grad_gate_w_ref,
    grad_out_w_ref,
    grad_att_w_ref,
    grad_bias_ref,
    grad_att_out_ref,
    wide,
    half,
    grad_packed_ref,
    grad_proj_ref,
    bias_ref,
    bias_rep_ref,
):
    channels = gains_ref.shape[1]
    block = ROW_BLOCK * size
    blocks = size // ROW_BLOCK
    lanes = HEADS * size
    head_scale = 1.0 / math.sqrt(HEAD_DIM)
    (
        left_ref,
        right_ref,
        right_t_ref,
        left_a_ref,
        left_b_ref,
        right_a_ref,
        right_b_ref,
        gate_ref,
        cot_full_ref,
        hat_mid_ref,
        scale_mid_ref,
        edge_out_ref,
        hat_y_ref,
        scale_y_ref,
        y_ref,
        att_gate_ref,
        grad_gated_ref,
        grad_y_ref,
        grad_middle_ref,
        grad_product_ref,
        pair_ref,
    ) = (wide.at[at] for at in range(WIDE_ARRAYS))
    (
        x_half_ref,
        update_ref,
        y_t_ref,
        cot_t_ref,
        query_ref,
        key_ref,
        value_ref,
        grad_att_ref,
        gated_ref,
        grad_edge_out_ref,
    ) = (half.at[at] for at in range(HALF_ARRAYS))
    real = lengths_ref[0]
    gain_x = gains_ref[0:1, :]
    gain_mid = gains_ref[1:2, :]
    gain_y = gains_ref[2:3, :]

    def rows_of(at):
        return pl.ds(pl.multiple_of(at * block, block), block)

    def columns_of(ref, at):
        return jnp.concatenate(
            [ref[pl.ds(at * ROW_BLOCK + a, size, stride=size), :] for a in range(ROW_BLOCK)], axis=0
        )

    first, count = own_rows()
    parity = lax.rem(first // count, 2)
    for source, turn_of in ((same_ref, parity), (other_ref, 1 - parity)):
        for pair_of_devices in range(source.shape[0]):
            start = (2 * pair_of_devices + turn_of) * (count * size)
            place = pl.ds(pl.multiple_of(start, count * size), count * size)
            pair_ref[place, :] = source[pair_of_devices, 0].reshape(count * size, channels).astype(FULL)
            cot_full_ref[place, :] = source[pair_of_devices, 1].reshape(count * size, channels).astype(FULL)

    def project(at, carry):
        rows = rows_of(at)
        hat, _ = norm_of(pair_ref[rows, :])
        normed = (hat * gain_x).astype(HALF)
        x_half_ref[rows, :] = normed
        projected = dot_nn(normed, edge_w_ref[...])
        gate_ref[rows, :] = jax.nn.sigmoid(dot_nn(normed, gate_w_ref[...]))
        shape = (ROW_BLOCK, size, channels)
        row = lax.broadcasted_iota(jnp.int32, shape, 0) + at * ROW_BLOCK
        col = lax.broadcasted_iota(jnp.int32, shape, 1)
        mask = jnp.where((row < real) & (col < real), 1.0, 0.0).reshape(block, channels)
        for side, (edge, first, second) in enumerate(
            ((left_ref, left_a_ref, left_b_ref), (right_ref, right_a_ref, right_b_ref))
        ):
            base = 2 * side * channels
            sig = jax.nn.sigmoid(projected[:, base : base + channels])
            value = projected[:, base + channels : base + 2 * channels]
            masked = mask * sig
            product = masked * value
            edge[rows, :] = product.astype(HALF).astype(FULL)
            first[rows, :] = product * (1.0 - sig)
            second[rows, :] = masked
        return carry

    lax.fori_loop(0, blocks, project, 0)

    def turn(at, carry):
        right_t_ref[rows_of(at), :] = columns_of(right_ref, at)
        return carry

    lax.fori_loop(0, blocks, turn, 0)

    def outer_sum(at, row_ref, row_stride, block_stride, block_ref):
        sums = [jnp.zeros((size, channels), FULL)] * ROW_BLOCK
        for k in range(size):
            whole = block_ref[k * size : (k + 1) * size, :]
            for a in range(ROW_BLOCK):
                row = (at * ROW_BLOCK + a) * block_stride + k * row_stride
                sums[a] = sums[a] + row_ref[pl.ds(row, 1), :] * whole
        return jnp.concatenate(sums, axis=0)

    def multiply(at, carry):
        rows = rows_of(at)
        product = outer_sum(at, left_ref, 1, size, right_t_ref)
        hat, scale = norm_of(product)
        hat_mid_ref[rows, :] = hat
        scale_mid_ref[rows, :] = jnp.broadcast_to(scale, hat.shape)
        update = (hat * gain_mid).astype(HALF)
        update_ref[rows, :] = update
        edge_out = dot_nn(update, out_w_ref[...])
        edge_out_ref[rows, :] = edge_out
        middle = pair_ref[rows, :] + gate_ref[rows, :] * edge_out
        hat, scale = norm_of(middle)
        hat_y_ref[rows, :] = hat
        scale_y_ref[rows, :] = jnp.broadcast_to(scale, hat.shape)
        y_ref[rows, :] = hat * gain_y
        return carry

    lax.fori_loop(0, blocks, multiply, 0)

    lane = lax.broadcasted_iota(jnp.int32, (1, lanes), 1)
    eye_row = lax.broadcasted_iota(jnp.int32, (size, lanes), 0)
    eye_lane = lax.broadcasted_iota(jnp.int32, (size, lanes), 1)
    same_cell = eye_lane == eye_row
    real_lane = lane < real
    for h in range(1, HEADS):
        same_cell = same_cell | (eye_lane == eye_row + h * size)
        inside = (lane >= h * size) & (lane < (h + 1) * size)
        real_lane = real_lane & (lane < size) if h == 1 else real_lane
        real_lane = real_lane | (inside & (lane < h * size + real))
    same_cell = jnp.where(same_cell, 1.0, 0.0)
    valid = jnp.where(real_lane, 1.0, 0.0)
    bias_rows = bias_w_ref[...].astype(FULL)
    for h in range(HEADS):
        bias_rep_ref[h * size : (h + 1) * size, :] = jnp.broadcast_to(
            bias_rows[h : h + 1], (size, channels)
        ).astype(HALF)

    def prepare(at, carry):
        rows = rows_of(at)
        y = columns_of(y_ref, at).astype(HALF)
        cot = columns_of(cot_full_ref, at).astype(HALF)
        y_t_ref[rows, :] = y
        cot_t_ref[rows, :] = cot
        packed = dot_nn(y, att_w_ref[...])
        query_ref[rows, :] = (packed[:, :channels] * head_scale).astype(HALF)
        key_ref[rows, :] = packed[:, channels : 2 * channels].astype(HALF)
        value_ref[rows, :] = packed[:, 2 * channels : 3 * channels].astype(HALF)
        gate = jax.nn.sigmoid(packed[:, 3 * channels :])
        att_gate_ref[rows, :] = gate
        grad_gated = dot_nt(cot, att_out_w_ref[...])
        grad_gated_ref[rows, :] = grad_gated
        grad_att_ref[rows, :] = (grad_gated * gate).astype(HALF)
        spread = dot_nt(y, bias_rep_ref[...]).astype(HALF).astype(FULL)
        spread = spread.reshape(ROW_BLOCK, size, lanes) * same_cell[None]
        bias_ref[pl.ds(at * ROW_BLOCK, ROW_BLOCK), :] = jnp.sum(spread, axis=1)
        return carry

    lax.fori_loop(0, blocks, prepare, 0)

    head_mask = head_blocks(size, HEAD_DIM, HALF)
    head_mask_full = head_blocks(size, HEAD_DIM, FULL)
    key_ones = head_blocks(size, size, HALF)
    dim_ones = head_blocks(HEAD_DIM, size, HALF)

    def attend(at, score_sum):
        rows = rows_of(at)
        parts = [slice(a * size, (a + 1) * size) for a in range(ROW_BLOCK)]
        query, key, value, grad_att = (
            ref[rows, :] for ref in (query_ref, key_ref, value_ref, grad_att_ref)
        )
        keys = [jnp.concatenate([key[p]] * HEADS, axis=0) * head_mask for p in parts]
        values = [jnp.concatenate([value[p]] * HEADS, axis=0) * head_mask for p in parts]
        bias = bias_ref[...]
        scores = jnp.concatenate(
            [dot_nt(query[p], keys[a]) + bias for a, p in enumerate(parts)], axis=0
        )
        exp_scores = valid * jnp.exp(scores)
        attention = exp_scores / dot_wide(exp_scores, key_ones)
        attention_half = attention.astype(HALF)
        attended = jnp.concatenate(
            [dot_nn(attention_half[p], values[a]) for a, p in enumerate(parts)], axis=0
        )
        grad_attention = jnp.concatenate(
            [dot_nt(grad_att[p], values[a]) for a, p in enumerate(parts)], axis=0
        )
        row_dots = dot_wide(grad_att.astype(FULL) * attended, dim_ones)
        grad_scores = attention * (grad_attention - row_dots)
        scores_half = grad_scores.astype(HALF)
        for p in parts:
            score_sum = score_sum + grad_scores[p]
        grad_query = jnp.concatenate(
            [dot_nn(scores_half[p], keys[a]) for a, p in enumerate(parts)], axis=0
        )

        def per_key(weights, vectors):
            folded = []
            for p in parts:
                whole = dot_tn(weights[p], vectors[p]) * head_mask_full
                folded.append(sum(whole[h * size : (h + 1) * size] for h in range(HEADS)))
            return jnp.concatenate(folded, axis=0)

        grad_key = per_key(scores_half, query)
        grad_value = per_key(attention_half, grad_att)
        gate = att_gate_ref[rows, :]
        gated = gate * attended
        gated_ref[rows, :] = gated.astype(HALF)
        grad_gate_pre = grad_gated_ref[rows, :] * gated * (1.0 - gate)
        grad_packed = jnp.concatenate(
            [
                (grad_query * head_scale).astype(HALF),
                grad_key.astype(HALF),
                grad_value.astype(HALF),
                grad_gate_pre.astype(HALF),
            ],
            axis=1,
        )
        grad_packed_ref[rows, : 4 * channels] = grad_packed
        grad_y_ref[rows, :] = dot_nt(grad_packed, att_w_ref[...])
        return score_sum

    score_sum = lax.fori_loop(0, blocks, attend, jnp.zeros((size, lanes), FULL))
    bias_ref[...] = score_sum.astype(HALF).astype(FULL)

    def spread_bias(at, carry):
        rows = rows_of(at)
        part = bias_ref[pl.ds(at * ROW_BLOCK, ROW_BLOCK), :]
        spread = (part[:, None, :] * same_cell[None]).reshape(block, lanes).astype(HALF)
        grad_packed_ref[rows, 4 * channels :] = spread
        grad_y_ref[rows, :] += dot_nn(spread, bias_rep_ref[...])
        return carry

    lax.fori_loop(0, blocks, spread_bias, 0)

    def middle_back(at, carry):
        rows = rows_of(at)
        grad_y = columns_of(grad_y_ref, at)
        grad_middle = cot_full_ref[rows, :] + norm_back(
            grad_y, hat_y_ref[rows, :], scale_y_ref[rows, :], gain_y
        )
        grad_middle_ref[rows, :] = grad_middle
        gate = gate_ref[rows, :]
        gated = grad_middle * gate
        grad_edge_out = gated.astype(HALF)
        grad_edge_out_ref[rows, :] = grad_edge_out
        grad_gate = gated * edge_out_ref[rows, :] * (1.0 - gate)
        grad_proj_ref[rows, 4 * channels :] = grad_gate.astype(HALF)
        grad_update = dot_nt(grad_edge_out, out_w_ref[...])
        grad_product = norm_back(grad_update, hat_mid_ref[rows, :], scale_mid_ref[rows, :], gain_mid)
        grad_product_ref[rows, :] = grad_product.astype(HALF).astype(FULL)
        return carry

    lax.fori_loop(0, blocks, middle_back, 0)

    def edges_back(at, carry):
        rows = rows_of(at)
        grad_left = outer_sum(at, grad_product_ref, 1, size, right_ref)
        grad_proj_ref[rows, :channels] = (grad_left * left_a_ref[rows, :]).astype(HALF)
        grad_proj_ref[rows, channels : 2 * channels] = (grad_left * left_b_ref[rows, :]).astype(HALF)
        grad_right = outer_sum(at, grad_product_ref, size, 1, left_ref)
        grad_proj_ref[rows, 2 * channels : 3 * channels] = (grad_right * right_a_ref[rows, :]).astype(HALF)
        grad_proj_ref[rows, 3 * channels : 4 * channels] = (grad_right * right_b_ref[rows, :]).astype(HALF)
        return carry

    lax.fori_loop(0, blocks, edges_back, 0)

    inverse = 1.0 / size
    x_half = x_half_ref[...]
    edge_sum = dot_tn(x_half, grad_proj_ref[:, : 4 * channels]) * inverse
    gate_sum = dot_tn(x_half, grad_proj_ref[:, 4 * channels :]) * inverse
    grad_edge_ref[...] = edge_sum
    grad_gate_w_ref[...] = gate_sum
    out_sum = dot_tn(update_ref[...], grad_edge_out_ref[...]) * inverse
    grad_out_w_ref[...] = out_sum
    y_t = y_t_ref[...]
    att_sum = dot_tn(y_t, grad_packed_ref[:, : 4 * channels]) * inverse
    grad_att_w_ref[...] = att_sum
    bias_sum = dot_tn(grad_packed_ref[:, 4 * channels :], y_t) * inverse
    grad_att_out_ref[...] = dot_tn(gated_ref[...], cot_t_ref[...]) * inverse
    for h in range(HEADS):
        grad_bias_ref[h : h + 1, :] = jnp.sum(
            bias_sum[h * size : (h + 1) * size], axis=0, keepdims=True
        )

    def gain_sum(pairs):
        total = sum(
            jnp.sum(weight.astype(FULL) * grad, axis=1, keepdims=True) for weight, grad in pairs
        )
        return jnp.transpose(jnp.broadcast_to(total, (channels, channels)))[0:1, :]

    grad_gains_ref[0:1, :] = gain_sum(((edge_w_ref[...], edge_sum), (gate_w_ref[...], gate_sum))) / gain_x
    grad_gains_ref[1:2, :] = gain_sum(((out_w_ref[...], out_sum),)) / gain_mid
    bias_part = jnp.sum(bias_rep_ref[...].astype(FULL) * bias_sum, axis=0, keepdims=True)
    grad_gains_ref[2:3, :] = (gain_sum(((att_w_ref[...], att_sum),)) + bias_part) / gain_y

    own = pl.ds(pl.multiple_of(first * size, count * size), count * size)
    hat, scale = norm_of(pair_ref[own, :])
    grad_x = dot_nt(grad_proj_ref[own, : 4 * channels], edge_w_ref[...])
    grad_x = grad_x + dot_nt(grad_proj_ref[own, 4 * channels :], gate_w_ref[...])
    grad_pair = grad_middle_ref[own, :] + norm_back(grad_x, hat, scale, gain_x)
    grad_pair_ref[...] = grad_pair.astype(grad_pair_ref.dtype)


WIDE_ARRAYS = 21
HALF_ARRAYS = 10


def norm_of(values):
    center = values - jnp.mean(values, axis=-1, keepdims=True)
    scale = lax.rsqrt(jnp.mean(center * center, axis=-1, keepdims=True) + epsilon)
    return center * scale, scale


def norm_back(grad_out, hat, scale, gain):
    scaled = grad_out * gain
    first_mean = jnp.mean(scaled, axis=-1, keepdims=True)
    second_mean = jnp.mean(scaled * hat, axis=-1, keepdims=True)
    return scale * (scaled - first_mean - hat * second_mean)


def scratch_of(size, channels):
    cells = size * size
    lanes = HEADS * size
    return [
        pltpu.VMEM((WIDE_ARRAYS, cells, channels), FULL),
        pltpu.VMEM((HALF_ARRAYS, cells, channels), HALF),
        pltpu.VMEM((cells, 4 * channels + lanes), HALF),
        pltpu.VMEM((cells, 5 * channels), HALF),
        pltpu.VMEM((size, lanes), FULL),
        pltpu.VMEM((lanes, channels), HALF),
    ]


def scratch_bytes(size, channels):
    return sum(math.prod(s.shape) * jnp.dtype(s.dtype).itemsize for s in scratch_of(size, channels))


def whole_crop(size, own_rows, row_count, *operands):
    channels = operands[0].shape[-1]
    out_shape = (
        jax.ShapeDtypeStruct((row_count * size, channels), HALF),
        jax.ShapeDtypeStruct((3, channels), FULL),
        jax.ShapeDtypeStruct((channels, 4 * channels), FULL),
        jax.ShapeDtypeStruct((channels, channels), FULL),
        jax.ShapeDtypeStruct((channels, channels), FULL),
        jax.ShapeDtypeStruct((channels, 4 * channels), FULL),
        jax.ShapeDtypeStruct((HEADS, channels), FULL),
        jax.ShapeDtypeStruct((channels, channels), FULL),
    )
    vmem = pl.BlockSpec(memory_space=pltpu.VMEM)
    in_specs = [vmem] * len(operands)
    in_specs[2] = pl.BlockSpec(memory_space=pltpu.SMEM)
    return pl.pallas_call(
        functools.partial(replicated_kernel, size, own_rows),
        out_shape=out_shape,
        in_specs=in_specs,
        out_specs=[vmem] * len(out_shape),
        scratch_shapes=scratch_of(size, channels),
        compiler_params=pltpu.CompilerParams(vmem_limit_bytes=VMEM_LIMIT),
    )(*operands)


def gather_rows(rows, axis_size):
    pairs = axis_size // 2
    same_parity = [list(range(parity, axis_size, 2)) for parity in range(2)]
    same = lax.all_to_all(
        jnp.broadcast_to(rows[None], (pairs,) + rows.shape),
        "dap",
        split_axis=0,
        concat_axis=0,
        axis_index_groups=same_parity,
    )
    other = lax.ppermute(same, "dap", [(d, d ^ 1) for d in range(axis_size)])
    return same, other


def replicated_plan(axis_size, pair_map, cotangent, lengths, norm_gains, *weights):
    row_count, size, channels = pair_map.shape
    same, other = gather_rows(jnp.stack([pair_map, cotangent]), axis_size)
    edge_w, gate_w, out_w, att_w, bias_w, att_out_w = weights

    def own_rows():
        return lax.axis_index("dap") * row_count, row_count

    outs = list(
        whole_crop(
            size, own_rows, row_count, same, other, lengths, norm_gains, edge_w, gate_w, out_w, att_w, bias_w.T, att_out_w
        )
    )
    outs[0] = outs[0].reshape(pair_map.shape)
    outs[6] = outs[6].T
    return tuple(outs)


def per_device(axis_size, pair_map, *rest):
    _, size, channels = pair_map.shape
    fits = size % ROW_BLOCK == 0 and scratch_bytes(size, channels) <= VMEM_LIMIT * 3 // 4
    if fits and axis_size % 2 == 0:
        return replicated_plan(axis_size, pair_map, *rest)
    return distributed_plan(pair_map, *rest)


def solution(mesh):
    return jax.shard_map(
        functools.partial(per_device, mesh.shape["dap"]),
        mesh=mesh,
        in_specs=(
            P(("groups", "dap"), None, None),
            P(("groups", "dap"), None, None),
            P("groups"),
            P(),
            P(),
            P(),
            P(),
            P(),
            P(),
            P(),
        ),
        out_specs=(
            P(("groups", "dap"), None, None),
            P("groups", None),
            P("groups", None),
            P("groups", None),
            P("groups", None),
            P("groups", None),
            P("groups", None),
            P("groups", None),
        ),
        check_vma=False,
    )
```

```python
import functools
import math

import jax
import jax.numpy as jnp
from jax import lax
from jax.experimental import pallas as pl
from jax.experimental.pallas import tpu as pltpu
from jax.sharding import PartitionSpec as P

HEADS = 4
HEAD_DIM = 32


epsilon = 1e-05


def norm_forward(values, gain_row):
    center = values - jnp.mean(values, axis=-1, keepdims=True)
    inv_std = lax.rsqrt(jnp.mean(center * center, axis=-1, keepdims=True) + epsilon)
    normed = center * inv_std
    return (normed * gain_row, normed, inv_std)


def norm_backward(grad_out, normed, inv_std, gain_row):
    scaled = grad_out * gain_row
    first_mean = jnp.mean(scaled, axis=-1, keepdims=True)
    second_mean = jnp.mean(scaled * normed, axis=-1, keepdims=True)
    return inv_std * (scaled - first_mean - normed * second_mean)


def distributed_plan(
    pair_map,
    cotangent,
    lengths,
    norm_gains,
    edge_weight,
    mult_gate_weight,
    mult_out_weight,
    attention_weight,
    bias_weight,
    attention_out_weight,
):
    row_count, full_size, channels = pair_map.shape
    inner_width = HEADS * HEAD_DIM
    head_scale = 1.0 / math.sqrt(HEAD_DIM)
    first_row = lax.axis_index("dap") * row_count
    real_count = lengths[0]
    valid_all = (jnp.arange(full_size) < real_count).astype(jnp.float32)
    valid_rows = (first_row + jnp.arange(row_count) < real_count).astype(jnp.float32)
    mask_pair = (valid_rows[:, None] * valid_all[None, :])[:, :, None]
    pair_f32 = pair_map.astype(jnp.float32)
    normed_full, hat_in, scale_in = norm_forward(pair_f32, norm_gains[0])
    normed_x = normed_full.astype(jnp.bfloat16)
    projected = jnp.einsum("rnc,cf->rnf", normed_x, edge_weight, preferred_element_type=jnp.float32)
    left_gate = projected[..., :channels]
    left_value = projected[..., channels : 2 * channels]
    right_gate = projected[..., 2 * channels : 3 * channels]
    right_value = projected[..., 3 * channels :]
    left_sig = jax.nn.sigmoid(left_gate)
    right_sig = jax.nn.sigmoid(right_gate)
    left_edges = (mask_pair * left_sig * left_value).astype(jnp.bfloat16)
    right_edges = (mask_pair * right_sig * right_value).astype(jnp.bfloat16)
    product = jnp.einsum(
        "ikc,jkc->ijc",
        left_edges,
        lax.all_gather(right_edges, "dap", axis=0, tiled=True),
        preferred_element_type=jnp.float32,
    )
    update_full, hat_mid, scale_mid = norm_forward(product, norm_gains[1])
    update = update_full.astype(jnp.bfloat16)
    edge_out = jnp.einsum(
        "rnc,cf->rnf", update, mult_out_weight, preferred_element_type=jnp.float32
    )
    gate_sig = jax.nn.sigmoid(
        jnp.einsum("rnc,cf->rnf", normed_x, mult_gate_weight, preferred_element_type=jnp.float32)
    )
    middle = pair_f32 + gate_sig * edge_out
    normed_mid, hat_attn, scale_attn = norm_forward(middle, norm_gains[2])
    normed_y = normed_mid.astype(jnp.bfloat16)
    bias_local = jnp.einsum(
        "kic,ch->hki", normed_y, bias_weight, preferred_element_type=jnp.float32
    ).astype(jnp.bfloat16)
    bias_whole = lax.all_gather(bias_local, "dap", axis=1, tiled=True)
    bias_query = jnp.swapaxes(bias_whole, 1, 2).astype(jnp.float32)
    column_y, column_cot = (
        lax.all_to_all(normed_y, "dap", split_axis=1, concat_axis=0, tiled=True),
        lax.all_to_all(cotangent, "dap", split_axis=1, concat_axis=0, tiled=True),
    )
    packed = jnp.einsum(
        "ijc,cf->ijf", column_y, attention_weight, preferred_element_type=jnp.float32
    )
    packed = packed.reshape(full_size, row_count, 4, HEADS, HEAD_DIM)
    query_vectors = (packed[:, :, 0] * head_scale).astype(jnp.bfloat16)
    key_vectors = packed[:, :, 1].astype(jnp.bfloat16)
    value_vectors = packed[:, :, 2].astype(jnp.bfloat16)
    att_gate = jax.nn.sigmoid(packed[:, :, 3])
    scores = (
        jnp.einsum(
            "ijhd,kjhd->jhik", query_vectors, key_vectors, preferred_element_type=jnp.float32
        )
        + bias_query[None]
    )
    exp_scores = valid_all * jnp.exp(scores)
    attention = exp_scores / jnp.sum(exp_scores, axis=-1, keepdims=True)
    attention_half = attention.astype(jnp.bfloat16)
    attended = jnp.einsum(
        "jhik,kjhd->ijhd", attention_half, value_vectors, preferred_element_type=jnp.float32
    )
    gated = (att_gate * attended).astype(jnp.bfloat16).reshape(full_size, row_count, inner_width)
    part_attn_out = jnp.einsum("ijf,ijc->fc", gated, column_cot, preferred_element_type=jnp.float32)
    grad_gated = jnp.einsum(
        "ijc,fc->ijf", column_cot, attention_out_weight, preferred_element_type=jnp.float32
    )
    grad_gated = grad_gated.reshape(full_size, row_count, HEADS, HEAD_DIM)
    grad_att = (grad_gated * att_gate).astype(jnp.bfloat16)
    grad_gate_pre = grad_gated * attended * att_gate * (1.0 - att_gate)
    grad_attention = jnp.einsum(
        "ijhd,kjhd->jhik", grad_att, value_vectors, preferred_element_type=jnp.float32
    )
    row_dots = jnp.transpose(jnp.sum(grad_att.astype(jnp.float32) * attended, axis=-1), (1, 2, 0))
    grad_scores = attention * (grad_attention - row_dots[..., None])
    scores_half = grad_scores.astype(jnp.bfloat16)
    grad_query = jnp.einsum(
        "jhik,kjhd->ijhd", scores_half, key_vectors, preferred_element_type=jnp.float32
    )
    grad_key = jnp.einsum(
        "jhik,ijhd->kjhd", scores_half, query_vectors, preferred_element_type=jnp.float32
    )
    grad_value = jnp.einsum(
        "jhik,ijhd->kjhd", attention_half, grad_att, preferred_element_type=jnp.float32
    )
    grad_packed = jnp.stack([grad_query * head_scale, grad_key, grad_value, grad_gate_pre], axis=2)
    grad_packed = grad_packed.reshape(full_size, row_count, 4 * inner_width).astype(jnp.bfloat16)
    part_attention = jnp.einsum(
        "ijc,ijf->cf", column_y, grad_packed, preferred_element_type=jnp.float32
    )
    column_grad = jnp.einsum(
        "ijf,cf->ijc", grad_packed, attention_weight, preferred_element_type=jnp.float32
    ).astype(jnp.bfloat16)
    row_grad = lax.all_to_all(column_grad, "dap", split_axis=0, concat_axis=1, tiled=True)
    score_sums = jnp.sum(grad_scores, axis=0)
    taken = score_sums
    bias_half = lax.psum_scatter(
        jnp.transpose(taken, (2, 0, 1)), "dap", scatter_dimension=0, tiled=True
    ).astype(jnp.bfloat16)
    part_bias = jnp.einsum("kic,khi->ch", normed_y, bias_half, preferred_element_type=jnp.float32)
    grad_normed_y = row_grad.astype(jnp.float32) + jnp.einsum(
        "khi,ch->kic", bias_half, bias_weight, preferred_element_type=jnp.float32
    )
    part_gain_attn = jnp.sum(grad_normed_y * hat_attn, axis=(0, 1))
    grad_middle = cotangent.astype(jnp.float32) + norm_backward(
        grad_normed_y, hat_attn, scale_attn, norm_gains[2]
    )
    grad_edge_out = (grad_middle * gate_sig).astype(jnp.bfloat16)
    grad_gate = (grad_middle * edge_out * gate_sig * (1.0 - gate_sig)).astype(jnp.bfloat16)
    part_mult_out = jnp.einsum(
        "rnc,rnf->cf", update, grad_edge_out, preferred_element_type=jnp.float32
    )
    part_mult_gate = jnp.einsum(
        "rnc,rnf->cf", normed_x, grad_gate, preferred_element_type=jnp.float32
    )
    grad_update = jnp.einsum(
        "rnf,cf->rnc", grad_edge_out, mult_out_weight, preferred_element_type=jnp.float32
    )
    part_gain_mid = jnp.sum(grad_update * hat_mid, axis=(0, 1))
    grad_product = norm_backward(grad_update, hat_mid, scale_mid, norm_gains[1]).astype(
        jnp.bfloat16
    )
    taken = grad_product
    grad_left = jnp.einsum(
        "ijc,jkc->ikc",
        taken,
        lax.all_gather(right_edges, "dap", axis=0, tiled=True),
        preferred_element_type=jnp.float32,
    )
    grad_cols = lax.all_to_all(grad_product, "dap", split_axis=1, concat_axis=0, tiled=True)
    taken = grad_cols
    grad_right = jnp.einsum(
        "ijc,ikc->jkc",
        taken,
        lax.all_gather(left_edges, "dap", axis=0, tiled=True),
        preferred_element_type=jnp.float32,
    )
    grad_proj = jnp.concatenate(
        [
            grad_left * mask_pair * left_value * left_sig * (1.0 - left_sig),
            grad_left * mask_pair * left_sig,
            grad_right * mask_pair * right_value * right_sig * (1.0 - right_sig),
            grad_right * mask_pair * right_sig,
        ],
        axis=-1,
    ).astype(jnp.bfloat16)
    part_edge = jnp.einsum("rnc,rnf->cf", normed_x, grad_proj, preferred_element_type=jnp.float32)
    grad_normed_x = jnp.einsum(
        "rnf,cf->rnc", grad_proj, edge_weight, preferred_element_type=jnp.float32
    )
    grad_normed_x = grad_normed_x + jnp.einsum(
        "rnf,cf->rnc", grad_gate, mult_gate_weight, preferred_element_type=jnp.float32
    )
    part_gain_in = jnp.sum(grad_normed_x * hat_in, axis=(0, 1))
    grad_pair = (
        grad_middle + norm_backward(grad_normed_x, hat_in, scale_in, norm_gains[0])
    ).astype(jnp.bfloat16)
    totals = lax.psum(
        (
            part_gain_in,
            part_gain_mid,
            part_edge,
            part_mult_gate,
            part_mult_out,
            part_gain_attn,
            part_attention,
            part_bias,
            part_attn_out,
        ),
        "dap",
    )
    (
        gain_in_sum,
        gain_mid_sum,
        edge_sum,
        mult_gate_sum,
        mult_out_sum,
        gain_attn_sum,
        attention_sum,
        bias_sum,
        attn_out_sum,
    ) = totals
    inverse = 1.0 / full_size
    grad_gains = jnp.stack([gain_in_sum, gain_mid_sum, gain_attn_sum]) * inverse
    return (
        grad_pair,
        grad_gains,
        edge_sum * inverse,
        mult_gate_sum * inverse,
        mult_out_sum * inverse,
        attention_sum * inverse,
        bias_sum * inverse,
        attn_out_sum * inverse,
    )


ROW_BLOCK = 8
VMEM_LIMIT = 24 * 2**20
HALF = jnp.bfloat16
FULL = jnp.float32


def dot_nn(left, right):
    return lax.dot_general(left, right, (((1,), (0,)), ((), ())), preferred_element_type=FULL)


def dot_nt(left, right):
    return lax.dot_general(left, right, (((1,), (1,)), ((), ())), preferred_element_type=FULL)


def dot_tn(left, right):
    return lax.dot_general(left, right, (((0,), (0,)), ((), ())), preferred_element_type=FULL)


def dot_wide(values, ones):
    high = values.astype(HALF)
    low = (values - high.astype(FULL)).astype(HALF)
    return dot_nn(high, ones) + dot_nn(low, ones)


def head_blocks(row_width, col_width, dtype):
    shape = (HEADS * row_width, HEADS * col_width)
    row = lax.broadcasted_iota(jnp.int32, shape, 0)
    col = lax.broadcasted_iota(jnp.int32, shape, 1)
    same = None
    for h in range(HEADS):
        here = (row >= h * row_width) & (row < (h + 1) * row_width)
        here = here & (col >= h * col_width) & (col < (h + 1) * col_width)
        same = here if same is None else same | here
    return jnp.where(same, 1.0, 0.0).astype(dtype)


def replicated_kernel(
    size,
    devices,
    *refs,
):
    pair_blocks, cot_blocks, refs = refs[:devices], refs[devices : 2 * devices], refs[2 * devices :]
    lengths_ref, gains_ref, edge_w_ref, gate_w_ref, out_w_ref, att_w_ref, bias_w_ref, att_out_w_ref = refs[:8]
    grad_pair_ref, grad_gains_ref, grad_edge_ref, grad_gate_w_ref, grad_out_w_ref = refs[8:13]
    grad_att_w_ref, grad_bias_ref, grad_att_out_ref = refs[13:16]
    wide, half, grad_packed_ref, grad_proj_ref, bias_ref, bias_rep_ref = refs[16:]
    channels = gains_ref.shape[1]
    block = ROW_BLOCK * size
    blocks = size // ROW_BLOCK
    lanes = HEADS * size
    head_scale = 1.0 / math.sqrt(HEAD_DIM)
    (
        left_ref,
        right_ref,
        right_t_ref,
        left_a_ref,
        left_b_ref,
        right_a_ref,
        right_b_ref,
        gate_ref,
        cot_full_ref,
        hat_mid_ref,
        scale_mid_ref,
        edge_out_ref,
        hat_y_ref,
        scale_y_ref,
        y_ref,
        att_gate_ref,
        grad_gated_ref,
        grad_y_ref,
        grad_middle_ref,
        grad_product_ref,
        pair_ref,
    ) = (wide.at[at] for at in range(WIDE_ARRAYS))
    (
        x_half_ref,
        update_ref,
        y_t_ref,
        cot_t_ref,
        query_ref,
        key_ref,
        value_ref,
        grad_att_ref,
        gated_ref,
        grad_edge_out_ref,
    ) = (half.at[at] for at in range(HALF_ARRAYS))
    real = lengths_ref[0]
    gain_x = gains_ref[0:1, :]
    gain_mid = gains_ref[1:2, :]
    gain_y = gains_ref[2:3, :]

    def rows_of(at):
        return pl.ds(pl.multiple_of(at * block, block), block)

    def columns_of(ref, at):
        return jnp.concatenate(
            [ref[pl.ds(at * ROW_BLOCK + a, size, stride=size), :] for a in range(ROW_BLOCK)], axis=0
        )

    me = lax.axis_index("dap")
    own_cells = size * size // devices
    for mask, (pair_block, cot_block) in enumerate(zip(pair_blocks, cot_blocks)):
        place = pl.ds(pl.multiple_of((me ^ mask) * own_cells, own_cells), own_cells)
        pair_ref[place, :] = pair_block[...].reshape(own_cells, channels).astype(FULL)
        cot_full_ref[place, :] = cot_block[...].reshape(own_cells, channels).astype(FULL)

    def project(at, carry):
        rows = rows_of(at)
        hat, _ = norm_of(pair_ref[rows, :])
        normed = (hat * gain_x).astype(HALF)
        x_half_ref[rows, :] = normed
        projected = dot_nn(normed, edge_w_ref[...])
        gate_ref[rows, :] = jax.nn.sigmoid(dot_nn(normed, gate_w_ref[...]))
        shape = (ROW_BLOCK, size, channels)
        row = lax.broadcasted_iota(jnp.int32, shape, 0) + at * ROW_BLOCK
        col = lax.broadcasted_iota(jnp.int32, shape, 1)
        mask = jnp.where((row < real) & (col < real), 1.0, 0.0).reshape(block, channels)
        for side, (edge, first, second) in enumerate(
            ((left_ref, left_a_ref, left_b_ref), (right_ref, right_a_ref, right_b_ref))
        ):
            base = 2 * side * channels
            sig = jax.nn.sigmoid(projected[:, base : base + channels])
            value = projected[:, base + channels : base + 2 * channels]
            masked = mask * sig
            product = masked * value
            edge[rows, :] = product.astype(HALF).astype(FULL)
            first[rows, :] = product * (1.0 - sig)
            second[rows, :] = masked
        return carry

    lax.fori_loop(0, blocks, project, 0)

    def turn(at, carry):
        right_t_ref[rows_of(at), :] = columns_of(right_ref, at)
        return carry

    lax.fori_loop(0, blocks, turn, 0)

    def outer_sum(at, row_ref, row_stride, block_stride, block_ref):
        sums = [jnp.zeros((size, channels), FULL)] * ROW_BLOCK
        for k in range(size):
            whole = block_ref[k * size : (k + 1) * size, :]
            for a in range(ROW_BLOCK):
                row = (at * ROW_BLOCK + a) * block_stride + k * row_stride
                sums[a] = sums[a] + row_ref[pl.ds(row, 1), :] * whole
        return jnp.concatenate(sums, axis=0)

    def multiply(at, carry):
        rows = rows_of(at)
        product = outer_sum(at, left_ref, 1, size, right_t_ref)
        hat, scale = norm_of(product)
        hat_mid_ref[rows, :] = hat
        scale_mid_ref[rows, :] = jnp.broadcast_to(scale, hat.shape)
        update = (hat * gain_mid).astype(HALF)
        update_ref[rows, :] = update
        edge_out = dot_nn(update, out_w_ref[...])
        edge_out_ref[rows, :] = edge_out
        middle = pair_ref[rows, :] + gate_ref[rows, :] * edge_out
        hat, scale = norm_of(middle)
        hat_y_ref[rows, :] = hat
        scale_y_ref[rows, :] = jnp.broadcast_to(scale, hat.shape)
        y_ref[rows, :] = hat * gain_y
        return carry

    lax.fori_loop(0, blocks, multiply, 0)

    lane = lax.broadcasted_iota(jnp.int32, (1, lanes), 1)
    eye_row = lax.broadcasted_iota(jnp.int32, (size, lanes), 0)
    eye_lane = lax.broadcasted_iota(jnp.int32, (size, lanes), 1)
    same_cell = eye_lane == eye_row
    real_lane = lane < real
    for h in range(1, HEADS):
        same_cell = same_cell | (eye_lane == eye_row + h * size)
        inside = (lane >= h * size) & (lane < (h + 1) * size)
        real_lane = real_lane & (lane < size) if h == 1 else real_lane
        real_lane = real_lane | (inside & (lane < h * size + real))
    same_cell = jnp.where(same_cell, 1.0, 0.0)
    valid = jnp.where(real_lane, 1.0, 0.0)
    bias_rows = bias_w_ref[...].astype(FULL)
    for h in range(HEADS):
        bias_rep_ref[h * size : (h + 1) * size, :] = jnp.broadcast_to(
            bias_rows[h : h + 1], (size, channels)
        ).astype(HALF)

    def prepare(at, carry):
        rows = rows_of(at)
        y = columns_of(y_ref, at).astype(HALF)
        cot = columns_of(cot_full_ref, at).astype(HALF)
        y_t_ref[rows, :] = y
        cot_t_ref[rows, :] = cot
        packed = dot_nn(y, att_w_ref[...])
        query_ref[rows, :] = (packed[:, :channels] * head_scale).astype(HALF)
        key_ref[rows, :] = packed[:, channels : 2 * channels].astype(HALF)
        value_ref[rows, :] = packed[:, 2 * channels : 3 * channels].astype(HALF)
        gate = jax.nn.sigmoid(packed[:, 3 * channels :])
        att_gate_ref[rows, :] = gate
        grad_gated = dot_nt(cot, att_out_w_ref[...])
        grad_gated_ref[rows, :] = grad_gated
        grad_att_ref[rows, :] = (grad_gated * gate).astype(HALF)
        spread = dot_nt(y, bias_rep_ref[...]).astype(HALF).astype(FULL)
        spread = spread.reshape(ROW_BLOCK, size, lanes) * same_cell[None]
        bias_ref[pl.ds(at * ROW_BLOCK, ROW_BLOCK), :] = jnp.sum(spread, axis=1)
        return carry

    lax.fori_loop(0, blocks, prepare, 0)

    head_mask = head_blocks(size, HEAD_DIM, HALF)
    head_mask_full = head_blocks(size, HEAD_DIM, FULL)
    key_ones = head_blocks(size, size, HALF)
    dim_ones = head_blocks(HEAD_DIM, size, HALF)

    def attend(at, score_sum):
        rows = rows_of(at)
        parts = [slice(a * size, (a + 1) * size) for a in range(ROW_BLOCK)]
        query, key, value, grad_att = (
            ref[rows, :] for ref in (query_ref, key_ref, value_ref, grad_att_ref)
        )
        keys = [jnp.concatenate([key[p]] * HEADS, axis=0) * head_mask for p in parts]
        values = [jnp.concatenate([value[p]] * HEADS, axis=0) * head_mask for p in parts]
        bias = bias_ref[...]
        scores = jnp.concatenate(
            [dot_nt(query[p], keys[a]) + bias for a, p in enumerate(parts)], axis=0
        )
        exp_scores = valid * jnp.exp(scores)
        attention = exp_scores / dot_wide(exp_scores, key_ones)
        attention_half = attention.astype(HALF)
        attended = jnp.concatenate(
            [dot_nn(attention_half[p], values[a]) for a, p in enumerate(parts)], axis=0
        )
        grad_attention = jnp.concatenate(
            [dot_nt(grad_att[p], values[a]) for a, p in enumerate(parts)], axis=0
        )
        row_dots = dot_wide(grad_att.astype(FULL) * attended, dim_ones)
        grad_scores = attention * (grad_attention - row_dots)
        scores_half = grad_scores.astype(HALF)
        for p in parts:
            score_sum = score_sum + grad_scores[p]
        grad_query = jnp.concatenate(
            [dot_nn(scores_half[p], keys[a]) for a, p in enumerate(parts)], axis=0
        )

        def per_key(weights, vectors):
            folded = []
            for p in parts:
                whole = dot_tn(weights[p], vectors[p]) * head_mask_full
                folded.append(sum(whole[h * size : (h + 1) * size] for h in range(HEADS)))
            return jnp.concatenate(folded, axis=0)

        grad_key = per_key(scores_half, query)
        grad_value = per_key(attention_half, grad_att)
        gate = att_gate_ref[rows, :]
        gated = gate * attended
        gated_ref[rows, :] = gated.astype(HALF)
        grad_gate_pre = grad_gated_ref[rows, :] * gated * (1.0 - gate)
        grad_packed = jnp.concatenate(
            [
                (grad_query * head_scale).astype(HALF),
                grad_key.astype(HALF),
                grad_value.astype(HALF),
                grad_gate_pre.astype(HALF),
            ],
            axis=1,
        )
        grad_packed_ref[rows, : 4 * channels] = grad_packed
        grad_y_ref[rows, :] = dot_nt(grad_packed, att_w_ref[...])
        return score_sum

    score_sum = lax.fori_loop(0, blocks, attend, jnp.zeros((size, lanes), FULL))
    bias_ref[...] = score_sum.astype(HALF).astype(FULL)

    def spread_bias(at, carry):
        rows = rows_of(at)
        part = bias_ref[pl.ds(at * ROW_BLOCK, ROW_BLOCK), :]
        spread = (part[:, None, :] * same_cell[None]).reshape(block, lanes).astype(HALF)
        grad_packed_ref[rows, 4 * channels :] = spread
        grad_y_ref[rows, :] += dot_nn(spread, bias_rep_ref[...])
        return carry

    lax.fori_loop(0, blocks, spread_bias, 0)

    def middle_back(at, carry):
        rows = rows_of(at)
        grad_y = columns_of(grad_y_ref, at)
        grad_middle = cot_full_ref[rows, :] + norm_back(
            grad_y, hat_y_ref[rows, :], scale_y_ref[rows, :], gain_y
        )
        grad_middle_ref[rows, :] = grad_middle
        gate = gate_ref[rows, :]
        gated = grad_middle * gate
        grad_edge_out = gated.astype(HALF)
        grad_edge_out_ref[rows, :] = grad_edge_out
        grad_gate = gated * edge_out_ref[rows, :] * (1.0 - gate)
        grad_proj_ref[rows, 4 * channels :] = grad_gate.astype(HALF)
        grad_update = dot_nt(grad_edge_out, out_w_ref[...])
        grad_product = norm_back(grad_update, hat_mid_ref[rows, :], scale_mid_ref[rows, :], gain_mid)
        grad_product_ref[rows, :] = grad_product.astype(HALF).astype(FULL)
        return carry

    lax.fori_loop(0, blocks, middle_back, 0)

    def edges_back(at, carry):
        rows = rows_of(at)
        grad_left = outer_sum(at, grad_product_ref, 1, size, right_ref)
        grad_proj_ref[rows, :channels] = (grad_left * left_a_ref[rows, :]).astype(HALF)
        grad_proj_ref[rows, channels : 2 * channels] = (grad_left * left_b_ref[rows, :]).astype(HALF)
        grad_right = outer_sum(at, grad_product_ref, size, 1, left_ref)
        grad_proj_ref[rows, 2 * channels : 3 * channels] = (grad_right * right_a_ref[rows, :]).astype(HALF)
        grad_proj_ref[rows, 3 * channels : 4 * channels] = (grad_right * right_b_ref[rows, :]).astype(HALF)
        return carry

    lax.fori_loop(0, blocks, edges_back, 0)

    inverse = 1.0 / size
    x_half = x_half_ref[...]
    edge_sum = dot_tn(x_half, grad_proj_ref[:, : 4 * channels]) * inverse
    gate_sum = dot_tn(x_half, grad_proj_ref[:, 4 * channels :]) * inverse
    grad_edge_ref[...] = edge_sum
    grad_gate_w_ref[...] = gate_sum
    out_sum = dot_tn(update_ref[...], grad_edge_out_ref[...]) * inverse
    grad_out_w_ref[...] = out_sum
    y_t = y_t_ref[...]
    att_sum = dot_tn(y_t, grad_packed_ref[:, : 4 * channels]) * inverse
    grad_att_w_ref[...] = att_sum
    bias_sum = dot_tn(grad_packed_ref[:, 4 * channels :], y_t) * inverse
    grad_att_out_ref[...] = dot_tn(gated_ref[...], cot_t_ref[...]) * inverse
    for h in range(HEADS):
        grad_bias_ref[h : h + 1, :] = jnp.sum(
            bias_sum[h * size : (h + 1) * size], axis=0, keepdims=True
        )

    def gain_sum(pairs):
        total = sum(
            jnp.sum(weight.astype(FULL) * grad, axis=1, keepdims=True) for weight, grad in pairs
        )
        return jnp.transpose(jnp.broadcast_to(total, (channels, channels)))[0:1, :]

    grad_gains_ref[0:1, :] = gain_sum(((edge_w_ref[...], edge_sum), (gate_w_ref[...], gate_sum))) / gain_x
    grad_gains_ref[1:2, :] = gain_sum(((out_w_ref[...], out_sum),)) / gain_mid
    bias_part = jnp.sum(bias_rep_ref[...].astype(FULL) * bias_sum, axis=0, keepdims=True)
    grad_gains_ref[2:3, :] = (gain_sum(((att_w_ref[...], att_sum),)) + bias_part) / gain_y

    own = pl.ds(pl.multiple_of(me * own_cells, own_cells), own_cells)
    hat, scale = norm_of(pair_ref[own, :])
    grad_x = dot_nt(grad_proj_ref[own, : 4 * channels], edge_w_ref[...])
    grad_x = grad_x + dot_nt(grad_proj_ref[own, 4 * channels :], gate_w_ref[...])
    grad_pair = grad_middle_ref[own, :] + norm_back(grad_x, hat, scale, gain_x)
    grad_pair_ref[...] = grad_pair.astype(grad_pair_ref.dtype)


WIDE_ARRAYS = 21
HALF_ARRAYS = 10


def norm_of(values):
    center = values - jnp.mean(values, axis=-1, keepdims=True)
    scale = lax.rsqrt(jnp.mean(center * center, axis=-1, keepdims=True) + epsilon)
    return center * scale, scale


def norm_back(grad_out, hat, scale, gain):
    scaled = grad_out * gain
    first_mean = jnp.mean(scaled, axis=-1, keepdims=True)
    second_mean = jnp.mean(scaled * hat, axis=-1, keepdims=True)
    return scale * (scaled - first_mean - hat * second_mean)


def scratch_of(size, channels):
    cells = size * size
    lanes = HEADS * size
    return [
        pltpu.VMEM((WIDE_ARRAYS, cells, channels), FULL),
        pltpu.VMEM((HALF_ARRAYS, cells, channels), HALF),
        pltpu.VMEM((cells, 4 * channels + lanes), HALF),
        pltpu.VMEM((cells, 5 * channels), HALF),
        pltpu.VMEM((size, lanes), FULL),
        pltpu.VMEM((lanes, channels), HALF),
    ]


def scratch_bytes(size, channels):
    return sum(math.prod(s.shape) * jnp.dtype(s.dtype).itemsize for s in scratch_of(size, channels))


def whole_crop(size, pair_blocks, cot_blocks, lengths, *rest):
    devices = len(pair_blocks)
    channels = pair_blocks[0].shape[-1]
    out_shape = (
        jax.ShapeDtypeStruct((size * size // devices, channels), HALF),
        jax.ShapeDtypeStruct((3, channels), FULL),
        jax.ShapeDtypeStruct((channels, 4 * channels), FULL),
        jax.ShapeDtypeStruct((channels, channels), FULL),
        jax.ShapeDtypeStruct((channels, channels), FULL),
        jax.ShapeDtypeStruct((channels, 4 * channels), FULL),
        jax.ShapeDtypeStruct((HEADS, channels), FULL),
        jax.ShapeDtypeStruct((channels, channels), FULL),
    )
    vmem = pl.BlockSpec(memory_space=pltpu.VMEM)
    smem = pl.BlockSpec(memory_space=pltpu.SMEM)
    return pl.pallas_call(
        functools.partial(replicated_kernel, size, devices),
        out_shape=out_shape,
        in_specs=[vmem] * (2 * devices) + [smem] + [vmem] * len(rest),
        out_specs=[vmem] * len(out_shape),
        scratch_shapes=scratch_of(size, channels),
        compiler_params=pltpu.CompilerParams(vmem_limit_bytes=VMEM_LIMIT),
    )(*pair_blocks, *cot_blocks, lengths, *rest)


def gather_blocks(own, axis_size):
    bits = axis_size.bit_length() - 1
    blocks = {0: own}
    for low, high in ((bits - 1, bits), (1, bits - 1), (0, min(1, bits - 1))):
        held = list(blocks.items())
        for mask in range(1 << low, 1 << high, 1 << low):
            swap = [(d, d ^ mask) for d in range(axis_size)]
            for at, block in held:
                blocks[at | mask] = lax.ppermute(block, "dap", swap)
    return [blocks[at] for at in range(axis_size)]


def replicated_plan(axis_size, pair_map, cotangent, lengths, norm_gains, *weights):
    edge_w, gate_w, out_w, att_w, bias_w, att_out_w = weights
    outs = list(
        whole_crop(
            pair_map.shape[1],
            gather_blocks(pair_map, axis_size),
            gather_blocks(cotangent, axis_size),
            lengths,
            norm_gains,
            edge_w,
            gate_w,
            out_w,
            att_w,
            bias_w.T,
            att_out_w,
        )
    )
    outs[0] = outs[0].reshape(pair_map.shape)
    outs[6] = outs[6].T
    return tuple(outs)


def per_device(axis_size, pair_map, *rest):
    _, size, channels = pair_map.shape
    fits = size % ROW_BLOCK == 0 and scratch_bytes(size, channels) <= VMEM_LIMIT * 3 // 4
    if fits and axis_size >= 4 and axis_size & (axis_size - 1) == 0:
        return replicated_plan(axis_size, pair_map, *rest)
    return distributed_plan(pair_map, *rest)


def solution(mesh):
    return jax.shard_map(
        functools.partial(per_device, mesh.shape["dap"]),
        mesh=mesh,
        in_specs=(
            P(("groups", "dap"), None, None),
            P(("groups", "dap"), None, None),
            P("groups"),
            P(),
            P(),
            P(),
            P(),
            P(),
            P(),
            P(),
        ),
        out_specs=(
            P(("groups", "dap"), None, None),
            P("groups", None),
            P("groups", None),
            P("groups", None),
            P("groups", None),
            P("groups", None),
            P("groups", None),
            P("groups", None),
        ),
        check_vma=False,
    )
```

```python
import functools
import math

import jax
import jax.numpy as jnp
from jax import lax
from jax.experimental import pallas as pl
from jax.experimental.pallas import tpu as pltpu
from jax.sharding import PartitionSpec as P

HEADS = 4
HEAD_DIM = 32


epsilon = 1e-05


def norm_forward(values, gain_row):
    center = values - jnp.mean(values, axis=-1, keepdims=True)
    inv_std = lax.rsqrt(jnp.mean(center * center, axis=-1, keepdims=True) + epsilon)
    normed = center * inv_std
    return (normed * gain_row, normed, inv_std)


def norm_backward(grad_out, normed, inv_std, gain_row):
    scaled = grad_out * gain_row
    first_mean = jnp.mean(scaled, axis=-1, keepdims=True)
    second_mean = jnp.mean(scaled * normed, axis=-1, keepdims=True)
    return inv_std * (scaled - first_mean - normed * second_mean)


def distributed_plan(
    pair_map,
    cotangent,
    lengths,
    norm_gains,
    edge_weight,
    mult_gate_weight,
    mult_out_weight,
    attention_weight,
    bias_weight,
    attention_out_weight,
):
    row_count, full_size, channels = pair_map.shape
    inner_width = HEADS * HEAD_DIM
    head_scale = 1.0 / math.sqrt(HEAD_DIM)
    first_row = lax.axis_index("dap") * row_count
    real_count = lengths[0]
    valid_all = (jnp.arange(full_size) < real_count).astype(jnp.float32)
    valid_rows = (first_row + jnp.arange(row_count) < real_count).astype(jnp.float32)
    mask_pair = (valid_rows[:, None] * valid_all[None, :])[:, :, None]
    pair_f32 = pair_map.astype(jnp.float32)
    normed_full, hat_in, scale_in = norm_forward(pair_f32, norm_gains[0])
    normed_x = normed_full.astype(jnp.bfloat16)
    projected = jnp.einsum("rnc,cf->rnf", normed_x, edge_weight, preferred_element_type=jnp.float32)
    left_gate = projected[..., :channels]
    left_value = projected[..., channels : 2 * channels]
    right_gate = projected[..., 2 * channels : 3 * channels]
    right_value = projected[..., 3 * channels :]
    left_sig = jax.nn.sigmoid(left_gate)
    right_sig = jax.nn.sigmoid(right_gate)
    left_edges = (mask_pair * left_sig * left_value).astype(jnp.bfloat16)
    right_edges = (mask_pair * right_sig * right_value).astype(jnp.bfloat16)
    product = jnp.einsum(
        "ikc,jkc->ijc",
        left_edges,
        lax.all_gather(right_edges, "dap", axis=0, tiled=True),
        preferred_element_type=jnp.float32,
    )
    update_full, hat_mid, scale_mid = norm_forward(product, norm_gains[1])
    update = update_full.astype(jnp.bfloat16)
    edge_out = jnp.einsum(
        "rnc,cf->rnf", update, mult_out_weight, preferred_element_type=jnp.float32
    )
    gate_sig = jax.nn.sigmoid(
        jnp.einsum("rnc,cf->rnf", normed_x, mult_gate_weight, preferred_element_type=jnp.float32)
    )
    middle = pair_f32 + gate_sig * edge_out
    normed_mid, hat_attn, scale_attn = norm_forward(middle, norm_gains[2])
    normed_y = normed_mid.astype(jnp.bfloat16)
    bias_local = jnp.einsum(
        "kic,ch->hki", normed_y, bias_weight, preferred_element_type=jnp.float32
    ).astype(jnp.bfloat16)
    bias_whole = lax.all_gather(bias_local, "dap", axis=1, tiled=True)
    bias_query = jnp.swapaxes(bias_whole, 1, 2).astype(jnp.float32)
    column_y, column_cot = (
        lax.all_to_all(normed_y, "dap", split_axis=1, concat_axis=0, tiled=True),
        lax.all_to_all(cotangent, "dap", split_axis=1, concat_axis=0, tiled=True),
    )
    packed = jnp.einsum(
        "ijc,cf->ijf", column_y, attention_weight, preferred_element_type=jnp.float32
    )
    packed = packed.reshape(full_size, row_count, 4, HEADS, HEAD_DIM)
    query_vectors = (packed[:, :, 0] * head_scale).astype(jnp.bfloat16)
    key_vectors = packed[:, :, 1].astype(jnp.bfloat16)
    value_vectors = packed[:, :, 2].astype(jnp.bfloat16)
    att_gate = jax.nn.sigmoid(packed[:, :, 3])
    scores = (
        jnp.einsum(
            "ijhd,kjhd->jhik", query_vectors, key_vectors, preferred_element_type=jnp.float32
        )
        + bias_query[None]
    )
    exp_scores = valid_all * jnp.exp(scores)
    attention = exp_scores / jnp.sum(exp_scores, axis=-1, keepdims=True)
    attention_half = attention.astype(jnp.bfloat16)
    attended = jnp.einsum(
        "jhik,kjhd->ijhd", attention_half, value_vectors, preferred_element_type=jnp.float32
    )
    gated = (att_gate * attended).astype(jnp.bfloat16).reshape(full_size, row_count, inner_width)
    part_attn_out = jnp.einsum("ijf,ijc->fc", gated, column_cot, preferred_element_type=jnp.float32)
    grad_gated = jnp.einsum(
        "ijc,fc->ijf", column_cot, attention_out_weight, preferred_element_type=jnp.float32
    )
    grad_gated = grad_gated.reshape(full_size, row_count, HEADS, HEAD_DIM)
    grad_att = (grad_gated * att_gate).astype(jnp.bfloat16)
    grad_gate_pre = grad_gated * attended * att_gate * (1.0 - att_gate)
    grad_attention = jnp.einsum(
        "ijhd,kjhd->jhik", grad_att, value_vectors, preferred_element_type=jnp.float32
    )
    row_dots = jnp.transpose(jnp.sum(grad_att.astype(jnp.float32) * attended, axis=-1), (1, 2, 0))
    grad_scores = attention * (grad_attention - row_dots[..., None])
    scores_half = grad_scores.astype(jnp.bfloat16)
    grad_query = jnp.einsum(
        "jhik,kjhd->ijhd", scores_half, key_vectors, preferred_element_type=jnp.float32
    )
    grad_key = jnp.einsum(
        "jhik,ijhd->kjhd", scores_half, query_vectors, preferred_element_type=jnp.float32
    )
    grad_value = jnp.einsum(
        "jhik,ijhd->kjhd", attention_half, grad_att, preferred_element_type=jnp.float32
    )
    grad_packed = jnp.stack([grad_query * head_scale, grad_key, grad_value, grad_gate_pre], axis=2)
    grad_packed = grad_packed.reshape(full_size, row_count, 4 * inner_width).astype(jnp.bfloat16)
    part_attention = jnp.einsum(
        "ijc,ijf->cf", column_y, grad_packed, preferred_element_type=jnp.float32
    )
    column_grad = jnp.einsum(
        "ijf,cf->ijc", grad_packed, attention_weight, preferred_element_type=jnp.float32
    ).astype(jnp.bfloat16)
    row_grad = lax.all_to_all(column_grad, "dap", split_axis=0, concat_axis=1, tiled=True)
    score_sums = jnp.sum(grad_scores, axis=0)
    taken = score_sums
    bias_half = lax.psum_scatter(
        jnp.transpose(taken, (2, 0, 1)), "dap", scatter_dimension=0, tiled=True
    ).astype(jnp.bfloat16)
    part_bias = jnp.einsum("kic,khi->ch", normed_y, bias_half, preferred_element_type=jnp.float32)
    grad_normed_y = row_grad.astype(jnp.float32) + jnp.einsum(
        "khi,ch->kic", bias_half, bias_weight, preferred_element_type=jnp.float32
    )
    part_gain_attn = jnp.sum(grad_normed_y * hat_attn, axis=(0, 1))
    grad_middle = cotangent.astype(jnp.float32) + norm_backward(
        grad_normed_y, hat_attn, scale_attn, norm_gains[2]
    )
    grad_edge_out = (grad_middle * gate_sig).astype(jnp.bfloat16)
    grad_gate = (grad_middle * edge_out * gate_sig * (1.0 - gate_sig)).astype(jnp.bfloat16)
    part_mult_out = jnp.einsum(
        "rnc,rnf->cf", update, grad_edge_out, preferred_element_type=jnp.float32
    )
    part_mult_gate = jnp.einsum(
        "rnc,rnf->cf", normed_x, grad_gate, preferred_element_type=jnp.float32
    )
    grad_update = jnp.einsum(
        "rnf,cf->rnc", grad_edge_out, mult_out_weight, preferred_element_type=jnp.float32
    )
    part_gain_mid = jnp.sum(grad_update * hat_mid, axis=(0, 1))
    grad_product = norm_backward(grad_update, hat_mid, scale_mid, norm_gains[1]).astype(
        jnp.bfloat16
    )
    taken = grad_product
    grad_left = jnp.einsum(
        "ijc,jkc->ikc",
        taken,
        lax.all_gather(right_edges, "dap", axis=0, tiled=True),
        preferred_element_type=jnp.float32,
    )
    grad_cols = lax.all_to_all(grad_product, "dap", split_axis=1, concat_axis=0, tiled=True)
    taken = grad_cols
    grad_right = jnp.einsum(
        "ijc,ikc->jkc",
        taken,
        lax.all_gather(left_edges, "dap", axis=0, tiled=True),
        preferred_element_type=jnp.float32,
    )
    grad_proj = jnp.concatenate(
        [
            grad_left * mask_pair * left_value * left_sig * (1.0 - left_sig),
            grad_left * mask_pair * left_sig,
            grad_right * mask_pair * right_value * right_sig * (1.0 - right_sig),
            grad_right * mask_pair * right_sig,
        ],
        axis=-1,
    ).astype(jnp.bfloat16)
    part_edge = jnp.einsum("rnc,rnf->cf", normed_x, grad_proj, preferred_element_type=jnp.float32)
    grad_normed_x = jnp.einsum(
        "rnf,cf->rnc", grad_proj, edge_weight, preferred_element_type=jnp.float32
    )
    grad_normed_x = grad_normed_x + jnp.einsum(
        "rnf,cf->rnc", grad_gate, mult_gate_weight, preferred_element_type=jnp.float32
    )
    part_gain_in = jnp.sum(grad_normed_x * hat_in, axis=(0, 1))
    grad_pair = (
        grad_middle + norm_backward(grad_normed_x, hat_in, scale_in, norm_gains[0])
    ).astype(jnp.bfloat16)
    totals = lax.psum(
        (
            part_gain_in,
            part_gain_mid,
            part_edge,
            part_mult_gate,
            part_mult_out,
            part_gain_attn,
            part_attention,
            part_bias,
            part_attn_out,
        ),
        "dap",
    )
    (
        gain_in_sum,
        gain_mid_sum,
        edge_sum,
        mult_gate_sum,
        mult_out_sum,
        gain_attn_sum,
        attention_sum,
        bias_sum,
        attn_out_sum,
    ) = totals
    inverse = 1.0 / full_size
    grad_gains = jnp.stack([gain_in_sum, gain_mid_sum, gain_attn_sum]) * inverse
    return (
        grad_pair,
        grad_gains,
        edge_sum * inverse,
        mult_gate_sum * inverse,
        mult_out_sum * inverse,
        attention_sum * inverse,
        bias_sum * inverse,
        attn_out_sum * inverse,
    )


ROW_BLOCK = 8
VMEM_SLACK = 8 * 2**20
VMEM_SHARE = 32 * 2**20
HALF = jnp.bfloat16
FULL = jnp.float32


def dot_nn(left, right):
    return lax.dot_general(left, right, (((1,), (0,)), ((), ())), preferred_element_type=FULL)


def dot_nt(left, right):
    return lax.dot_general(left, right, (((1,), (1,)), ((), ())), preferred_element_type=FULL)


def dot_tn(left, right):
    return lax.dot_general(left, right, (((0,), (0,)), ((), ())), preferred_element_type=FULL)


def dot_wide(values, ones):
    high = values.astype(HALF)
    low = (values - high.astype(FULL)).astype(HALF)
    return dot_nn(high, ones) + dot_nn(low, ones)


def head_blocks(row_width, col_width, dtype):
    shape = (HEADS * row_width, HEADS * col_width)
    row = lax.broadcasted_iota(jnp.int32, shape, 0)
    col = lax.broadcasted_iota(jnp.int32, shape, 1)
    same = None
    for h in range(HEADS):
        here = (row >= h * row_width) & (row < (h + 1) * row_width)
        here = here & (col >= h * col_width) & (col < (h + 1) * col_width)
        same = here if same is None else same | here
    return jnp.where(same, 1.0, 0.0).astype(dtype)


def spread_rows(target, blocks, devices):
    me = lax.axis_index("dap")
    cells = target.shape[0] // devices
    for other, source in enumerate(blocks):
        parity = lax.rem(me + other, 2)
        for pair in range(source.shape[0]):
            place = pl.ds(pl.multiple_of((2 * pair + parity) * cells, cells), cells)
            target[place, :] = source[pair].reshape(cells, target.shape[1]).astype(FULL)


def block_tools(size):
    block = ROW_BLOCK * size

    def rows_of(at):
        return pl.ds(pl.multiple_of(at * block, block), block)

    def columns_of(ref, at):
        return jnp.concatenate(
            [ref[pl.ds(at * ROW_BLOCK + a, size, stride=size), :] for a in range(ROW_BLOCK)], axis=0
        )

    return rows_of, columns_of


def outer_sum(size, at, row_ref, row_stride, block_stride, block_ref):
    sums = [jnp.zeros((size, block_ref.shape[1]), FULL)] * ROW_BLOCK
    for k in range(size):
        whole = block_ref[k * size : (k + 1) * size, :]
        for a in range(ROW_BLOCK):
            row = (at * ROW_BLOCK + a) * block_stride + k * row_stride
            sums[a] = sums[a] + row_ref[pl.ds(row, 1), :] * whole
    return jnp.concatenate(sums, axis=0)


def same_cell_of(size):
    row = lax.broadcasted_iota(jnp.int32, (size, HEADS * size), 0)
    lane = lax.broadcasted_iota(jnp.int32, (size, HEADS * size), 1)
    same = lane == row
    for h in range(1, HEADS):
        same = same | (lane == row + h * size)
    return jnp.where(same, 1.0, 0.0)


def real_lanes(size, real):
    lane = lax.broadcasted_iota(jnp.int32, (1, HEADS * size), 1)
    inside = lane < real
    for h in range(1, HEADS):
        inside = inside | ((lane >= h * size) & (lane < h * size + real))
    return jnp.where(inside, 1.0, 0.0)


def spread_bias_weight(target, bias_w_ref, size):
    bias_rows = bias_w_ref[...].astype(FULL)
    for h in range(HEADS):
        target[h * size : (h + 1) * size, :] = jnp.broadcast_to(
            bias_rows[h : h + 1], (size, bias_rows.shape[1])
        ).astype(HALF)


def forward_kernel(
    size,
    devices,
    same_ref,
    other_ref,
    lengths_ref,
    gains_ref,
    edge_w_ref,
    gate_w_ref,
    out_w_ref,
    att_w_ref,
    bias_w_ref,
    left_ref,
    right_ref,
    left_a_ref,
    left_b_ref,
    right_a_ref,
    right_b_ref,
    gate_ref,
    hat_mid_ref,
    scale_mid_ref,
    edge_out_ref,
    hat_y_ref,
    scale_y_ref,
    att_gate_ref,
    x_half_ref,
    update_ref,
    y_t_ref,
    query_ref,
    key_ref,
    value_ref,
    bias_ref,
    pair_ref,
    right_t_ref,
    y_ref,
    bias_rep_ref,
):
    channels = gains_ref.shape[1]
    block = ROW_BLOCK * size
    blocks = size // ROW_BLOCK
    lanes = HEADS * size
    head_scale = 1.0 / math.sqrt(HEAD_DIM)
    rows_of, columns_of = block_tools(size)
    real = lengths_ref[0]
    gain_x = gains_ref[0:1, :]
    gain_mid = gains_ref[1:2, :]
    gain_y = gains_ref[2:3, :]
    spread_rows(pair_ref, (same_ref, other_ref), devices)

    def project(at, carry):
        rows = rows_of(at)
        hat, _ = norm_of(pair_ref[rows, :])
        normed = (hat * gain_x).astype(HALF)
        x_half_ref[rows, :] = normed
        projected = dot_nn(normed, edge_w_ref[...])
        gate_ref[rows, :] = jax.nn.sigmoid(dot_nn(normed, gate_w_ref[...]))
        shape = (ROW_BLOCK, size, channels)
        row = lax.broadcasted_iota(jnp.int32, shape, 0) + at * ROW_BLOCK
        col = lax.broadcasted_iota(jnp.int32, shape, 1)
        mask = jnp.where((row < real) & (col < real), 1.0, 0.0).reshape(block, channels)
        for side, (edge, first, second) in enumerate(
            ((left_ref, left_a_ref, left_b_ref), (right_ref, right_a_ref, right_b_ref))
        ):
            base = 2 * side * channels
            sig = jax.nn.sigmoid(projected[:, base : base + channels])
            value = projected[:, base + channels : base + 2 * channels]
            masked = mask * sig
            product = masked * value
            edge[rows, :] = product.astype(HALF).astype(FULL)
            first[rows, :] = product * (1.0 - sig)
            second[rows, :] = masked
        return carry

    lax.fori_loop(0, blocks, project, 0)

    def turn(at, carry):
        right_t_ref[rows_of(at), :] = columns_of(right_ref, at)
        return carry

    lax.fori_loop(0, blocks, turn, 0)

    def multiply(at, carry):
        rows = rows_of(at)
        product = outer_sum(size, at, left_ref, 1, size, right_t_ref)
        hat, scale = norm_of(product)
        hat_mid_ref[rows, :] = hat
        scale_mid_ref[rows, :] = jnp.broadcast_to(scale, hat.shape)
        update = (hat * gain_mid).astype(HALF)
        update_ref[rows, :] = update
        edge_out = dot_nn(update, out_w_ref[...])
        edge_out_ref[rows, :] = edge_out
        middle = pair_ref[rows, :] + gate_ref[rows, :] * edge_out
        hat, scale = norm_of(middle)
        hat_y_ref[rows, :] = hat
        scale_y_ref[rows, :] = jnp.broadcast_to(scale, hat.shape)
        y_ref[rows, :] = hat * gain_y
        return carry

    lax.fori_loop(0, blocks, multiply, 0)

    same_cell = same_cell_of(size)
    spread_bias_weight(bias_rep_ref, bias_w_ref, size)

    def prepare(at, carry):
        rows = rows_of(at)
        y = columns_of(y_ref, at).astype(HALF)
        y_t_ref[rows, :] = y
        packed = dot_nn(y, att_w_ref[...])
        query_ref[rows, :] = (packed[:, :channels] * head_scale).astype(HALF)
        key_ref[rows, :] = packed[:, channels : 2 * channels].astype(HALF)
        value_ref[rows, :] = packed[:, 2 * channels : 3 * channels].astype(HALF)
        att_gate_ref[rows, :] = jax.nn.sigmoid(packed[:, 3 * channels :])
        spread = dot_nt(y, bias_rep_ref[...]).astype(HALF).astype(FULL)
        spread = spread.reshape(ROW_BLOCK, size, lanes) * same_cell[None]
        bias_ref[pl.ds(at * ROW_BLOCK, ROW_BLOCK), :] = jnp.sum(spread, axis=1)
        return carry

    lax.fori_loop(0, blocks, prepare, 0)


def backward_kernel(
    size,
    devices,
    pair_ref,
    cot_blocks_ref,
    lengths_ref,
    gains_ref,
    edge_w_ref,
    gate_w_ref,
    out_w_ref,
    att_w_ref,
    bias_w_ref,
    att_out_w_ref,
    left_ref,
    right_ref,
    left_a_ref,
    left_b_ref,
    right_a_ref,
    right_b_ref,
    gate_ref,
    hat_mid_ref,
    scale_mid_ref,
    edge_out_ref,
    hat_y_ref,
    scale_y_ref,
    att_gate_ref,
    x_half_ref,
    update_ref,
    y_t_ref,
    query_ref,
    key_ref,
    value_ref,
    bias_ref,
    grad_pair_ref,
    grad_gains_ref,
    grad_edge_ref,
    grad_gate_w_ref,
    grad_out_w_ref,
    grad_att_w_ref,
    grad_bias_ref,
    grad_att_out_ref,
    cot_ref,
    grad_gated_ref,
    grad_y_ref,
    grad_middle_ref,
    grad_product_ref,
    cot_t_ref,
    grad_att_ref,
    gated_ref,
    grad_edge_out_ref,
    grad_packed_ref,
    grad_proj_ref,
    bias_grad_ref,
    bias_rep_ref,
):
    channels = gains_ref.shape[1]
    block = ROW_BLOCK * size
    blocks = size // ROW_BLOCK
    lanes = HEADS * size
    head_scale = 1.0 / math.sqrt(HEAD_DIM)
    rows_of, columns_of = block_tools(size)
    gain_x = gains_ref[0:1, :]
    gain_mid = gains_ref[1:2, :]
    gain_y = gains_ref[2:3, :]
    same_cell = same_cell_of(size)
    valid = real_lanes(size, lengths_ref[0])
    spread_bias_weight(bias_rep_ref, bias_w_ref, size)
    cot_ref[...] = cot_blocks_ref[...].reshape(size * size, channels).astype(FULL)

    def prepare(at, carry):
        rows = rows_of(at)
        cot = columns_of(cot_ref, at).astype(HALF)
        cot_t_ref[rows, :] = cot
        grad_gated = dot_nt(cot, att_out_w_ref[...])
        grad_gated_ref[rows, :] = grad_gated
        grad_att_ref[rows, :] = (grad_gated * att_gate_ref[rows, :]).astype(HALF)
        return carry

    lax.fori_loop(0, blocks, prepare, 0)

    head_mask = head_blocks(size, HEAD_DIM, HALF)
    head_mask_full = head_blocks(size, HEAD_DIM, FULL)
    key_ones = head_blocks(size, size, HALF)
    dim_ones = head_blocks(HEAD_DIM, size, HALF)

    def attend(at, score_sum):
        rows = rows_of(at)
        parts = [slice(a * size, (a + 1) * size) for a in range(ROW_BLOCK)]
        query, key, value, grad_att = (
            ref[rows, :] for ref in (query_ref, key_ref, value_ref, grad_att_ref)
        )
        keys = [jnp.concatenate([key[p]] * HEADS, axis=0) * head_mask for p in parts]
        values = [jnp.concatenate([value[p]] * HEADS, axis=0) * head_mask for p in parts]
        bias = bias_ref[...]
        scores = jnp.concatenate(
            [dot_nt(query[p], keys[a]) + bias for a, p in enumerate(parts)], axis=0
        )
        exp_scores = valid * jnp.exp(scores)
        attention = exp_scores / dot_wide(exp_scores, key_ones)
        attention_half = attention.astype(HALF)
        attended = jnp.concatenate(
            [dot_nn(attention_half[p], values[a]) for a, p in enumerate(parts)], axis=0
        )
        grad_attention = jnp.concatenate(
            [dot_nt(grad_att[p], values[a]) for a, p in enumerate(parts)], axis=0
        )
        row_dots = dot_wide(grad_att.astype(FULL) * attended, dim_ones)
        grad_scores = attention * (grad_attention - row_dots)
        scores_half = grad_scores.astype(HALF)
        for p in parts:
            score_sum = score_sum + grad_scores[p]
        grad_query = jnp.concatenate(
            [dot_nn(scores_half[p], keys[a]) for a, p in enumerate(parts)], axis=0
        )

        def per_key(weights, vectors):
            folded = []
            for p in parts:
                whole = dot_tn(weights[p], vectors[p]) * head_mask_full
                folded.append(sum(whole[h * size : (h + 1) * size] for h in range(HEADS)))
            return jnp.concatenate(folded, axis=0)

        grad_key = per_key(scores_half, query)
        grad_value = per_key(attention_half, grad_att)
        gate = att_gate_ref[rows, :]
        gated = gate * attended
        gated_ref[rows, :] = gated.astype(HALF)
        grad_gate_pre = grad_gated_ref[rows, :] * gated * (1.0 - gate)
        grad_packed = jnp.concatenate(
            [
                (grad_query * head_scale).astype(HALF),
                grad_key.astype(HALF),
                grad_value.astype(HALF),
                grad_gate_pre.astype(HALF),
            ],
            axis=1,
        )
        grad_packed_ref[rows, : 4 * channels] = grad_packed
        grad_y_ref[rows, :] = dot_nt(grad_packed, att_w_ref[...])
        return score_sum

    score_sum = lax.fori_loop(0, blocks, attend, jnp.zeros((size, lanes), FULL))
    bias_grad_ref[...] = score_sum.astype(HALF).astype(FULL)

    def spread_bias(at, carry):
        rows = rows_of(at)
        part = bias_grad_ref[pl.ds(at * ROW_BLOCK, ROW_BLOCK), :]
        spread = (part[:, None, :] * same_cell[None]).reshape(block, lanes).astype(HALF)
        grad_packed_ref[rows, 4 * channels :] = spread
        grad_y_ref[rows, :] += dot_nn(spread, bias_rep_ref[...])
        return carry

    lax.fori_loop(0, blocks, spread_bias, 0)

    def middle_back(at, carry):
        rows = rows_of(at)
        grad_y = columns_of(grad_y_ref, at)
        grad_middle = cot_ref[rows, :] + norm_back(
            grad_y, hat_y_ref[rows, :], scale_y_ref[rows, :], gain_y
        )
        grad_middle_ref[rows, :] = grad_middle
        gate = gate_ref[rows, :]
        gated = grad_middle * gate
        grad_edge_out = gated.astype(HALF)
        grad_edge_out_ref[rows, :] = grad_edge_out
        grad_gate = gated * edge_out_ref[rows, :] * (1.0 - gate)
        grad_proj_ref[rows, 4 * channels :] = grad_gate.astype(HALF)
        grad_update = dot_nt(grad_edge_out, out_w_ref[...])
        grad_product = norm_back(grad_update, hat_mid_ref[rows, :], scale_mid_ref[rows, :], gain_mid)
        grad_product_ref[rows, :] = grad_product.astype(HALF).astype(FULL)
        return carry

    lax.fori_loop(0, blocks, middle_back, 0)

    def edges_back(at, carry):
        rows = rows_of(at)
        grad_left = outer_sum(size, at, grad_product_ref, 1, size, right_ref)
        grad_proj_ref[rows, :channels] = (grad_left * left_a_ref[rows, :]).astype(HALF)
        grad_proj_ref[rows, channels : 2 * channels] = (grad_left * left_b_ref[rows, :]).astype(HALF)
        grad_right = outer_sum(size, at, grad_product_ref, size, 1, left_ref)
        grad_proj_ref[rows, 2 * channels : 3 * channels] = (grad_right * right_a_ref[rows, :]).astype(HALF)
        grad_proj_ref[rows, 3 * channels : 4 * channels] = (grad_right * right_b_ref[rows, :]).astype(HALF)
        return carry

    lax.fori_loop(0, blocks, edges_back, 0)

    inverse = 1.0 / size
    x_sum = dot_tn(x_half_ref[...], grad_proj_ref[...]) * inverse
    edge_sum, gate_sum = x_sum[:, : 4 * channels], x_sum[:, 4 * channels :]
    grad_edge_ref[...] = edge_sum
    grad_gate_w_ref[...] = gate_sum
    out_sum = dot_tn(update_ref[...], grad_edge_out_ref[...]) * inverse
    grad_out_w_ref[...] = out_sum
    y_sum = dot_tn(y_t_ref[...], grad_packed_ref[...]) * inverse
    att_sum, bias_sum = y_sum[:, : 4 * channels], jnp.transpose(y_sum[:, 4 * channels :])
    grad_att_w_ref[...] = att_sum
    grad_att_out_ref[...] = dot_tn(gated_ref[...], cot_t_ref[...]) * inverse
    for h in range(HEADS):
        grad_bias_ref[h : h + 1, :] = jnp.sum(
            bias_sum[h * size : (h + 1) * size], axis=0, keepdims=True
        )

    def gain_sum(pairs):
        total = sum(
            jnp.sum(weight.astype(FULL) * grad, axis=1, keepdims=True) for weight, grad in pairs
        )
        return jnp.transpose(jnp.broadcast_to(total, (channels, channels)))[0:1, :]

    grad_gains_ref[0:1, :] = gain_sum(((edge_w_ref[...], edge_sum), (gate_w_ref[...], gate_sum))) / gain_x
    grad_gains_ref[1:2, :] = gain_sum(((out_w_ref[...], out_sum),)) / gain_mid
    bias_part = jnp.sum(bias_rep_ref[...].astype(FULL) * bias_sum, axis=0, keepdims=True)
    grad_gains_ref[2:3, :] = (gain_sum(((att_w_ref[...], att_sum),)) + bias_part) / gain_y

    own_cells = size * size // devices
    own = pl.ds(pl.multiple_of(lax.axis_index("dap") * own_cells, own_cells), own_cells)
    hat, scale = norm_of(pair_ref[...].reshape(own_cells, channels).astype(FULL))
    grad_x = dot_nt(grad_proj_ref[own, : 4 * channels], edge_w_ref[...])
    grad_x = grad_x + dot_nt(grad_proj_ref[own, 4 * channels :], gate_w_ref[...])
    grad_pair = grad_middle_ref[own, :] + norm_back(grad_x, hat, scale, gain_x)
    grad_pair_ref[...] = grad_pair.astype(grad_pair_ref.dtype)


def norm_of(values):
    center = values - jnp.mean(values, axis=-1, keepdims=True)
    scale = lax.rsqrt(jnp.mean(center * center, axis=-1, keepdims=True) + epsilon)
    return center * scale, scale


def norm_back(grad_out, hat, scale, gain):
    scaled = grad_out * gain
    first_mean = jnp.mean(scaled, axis=-1, keepdims=True)
    second_mean = jnp.mean(scaled * hat, axis=-1, keepdims=True)
    return scale * (scaled - first_mean - hat * second_mean)


def cell_arrays(size, channels, full_count, half_count):
    shape = (size * size, channels)
    return [(shape, FULL)] * full_count + [(shape, HALF)] * half_count


def saved_arrays(size, channels):
    return cell_arrays(size, channels, 13, 6) + [((size, HEADS * size), FULL)]


def forward_scratch(size, channels):
    return cell_arrays(size, channels, 3, 0) + [((HEADS * size, channels), HALF)]


def backward_scratch(size, channels):
    cells, lanes = size * size, HEADS * size
    return cell_arrays(size, channels, 5, 4) + [
        ((cells, 4 * channels + lanes), HALF),
        ((cells, 5 * channels), HALF),
        ((size, lanes), FULL),
        ((lanes, channels), HALF),
    ]


def bytes_of(arrays):
    return sum(math.prod(shape) * jnp.dtype(dtype).itemsize for shape, dtype in arrays)


def run_kernel(kernel, operands, outs, scratch, lengths_at):
    vmem = pl.BlockSpec(memory_space=pltpu.VMEM)
    in_specs = [vmem] * len(operands)
    in_specs[lengths_at] = pl.BlockSpec(memory_space=pltpu.SMEM)
    return pl.pallas_call(
        kernel,
        out_shape=[jax.ShapeDtypeStruct(*out) for out in outs],
        in_specs=in_specs,
        out_specs=[vmem] * len(outs),
        scratch_shapes=[pltpu.VMEM(*part) for part in scratch],
        compiler_params=pltpu.CompilerParams(vmem_limit_bytes=bytes_of(scratch) + VMEM_SLACK),
    )(*operands)


def gather_pairs(rows, axis_size):
    pairs = axis_size // 2
    same_parity = [list(range(parity, axis_size, 2)) for parity in range(2)]
    same = lax.all_to_all(
        jnp.broadcast_to(rows[None], (pairs,) + rows.shape),
        "dap",
        split_axis=0,
        concat_axis=0,
        axis_index_groups=same_parity,
    )
    return same, lax.ppermute(same, "dap", [(d, d ^ 1) for d in range(axis_size)])


def gather_all(rows, axis_size):
    return lax.all_to_all(
        jnp.broadcast_to(rows[None], (axis_size,) + rows.shape), "dap", split_axis=0, concat_axis=0
    )


def replicated_plan(
    axis_size,
    pair_map,
    cotangent,
    lengths,
    norm_gains,
    edge_weight,
    mult_gate_weight,
    mult_out_weight,
    attention_weight,
    bias_weight,
    attention_out_weight,
):
    _, size, channels = pair_map.shape
    bias_w = bias_weight.T
    same, other = gather_pairs(pair_map, axis_size)
    same, other, cotangent = lax.optimization_barrier((same, other, cotangent))
    cot_blocks = gather_all(cotangent, axis_size)
    shared = (lengths, norm_gains, edge_weight, mult_gate_weight, mult_out_weight, attention_weight, bias_w)
    saved = run_kernel(
        functools.partial(forward_kernel, size, axis_size),
        (same, other) + shared,
        saved_arrays(size, channels),
        forward_scratch(size, channels),
        2,
    )
    square, wide = ((channels, channels), FULL), ((channels, 4 * channels), FULL)
    outs = run_kernel(
        functools.partial(backward_kernel, size, axis_size),
        (pair_map, cot_blocks) + shared + (attention_out_weight,) + tuple(saved),
        [
            ((size * size // axis_size, channels), HALF),
            ((3, channels), FULL),
            wide,
            square,
            square,
            wide,
            ((HEADS, channels), FULL),
            square,
        ],
        backward_scratch(size, channels),
        2,
    )
    return (outs[0].reshape(pair_map.shape), *outs[1:6], outs[6].T, outs[7])


def per_device(axis_size, pair_map, *rest):
    _, size, channels = pair_map.shape
    arrays = saved_arrays(size, channels) + backward_scratch(size, channels)
    fits = size % ROW_BLOCK == 0 and bytes_of(arrays) <= VMEM_SHARE
    if fits and axis_size % 2 == 0:
        return replicated_plan(axis_size, pair_map, *rest)
    return distributed_plan(pair_map, *rest)


def solution(mesh):
    return jax.shard_map(
        functools.partial(per_device, mesh.shape["dap"]),
        mesh=mesh,
        in_specs=(
            P(("groups", "dap"), None, None),
            P(("groups", "dap"), None, None),
            P("groups"),
            P(),
            P(),
            P(),
            P(),
            P(),
            P(),
            P(),
        ),
        out_specs=(
            P(("groups", "dap"), None, None),
            P("groups", None),
            P("groups", None),
            P("groups", None),
            P("groups", None),
            P("groups", None),
            P("groups", None),
            P("groups", None),
        ),
        check_vma=False,
    )
```

```python
import functools
import math

import jax
import jax.numpy as jnp
from jax import lax
from jax.experimental import pallas as pl
from jax.experimental.pallas import tpu as pltpu
from jax.sharding import PartitionSpec as P

HEADS = 4
HEAD_DIM = 32


epsilon = 1e-05


def norm_forward(values, gain_row):
    center = values - jnp.mean(values, axis=-1, keepdims=True)
    inv_std = lax.rsqrt(jnp.mean(center * center, axis=-1, keepdims=True) + epsilon)
    normed = center * inv_std
    return (normed * gain_row, normed, inv_std)


def norm_backward(grad_out, normed, inv_std, gain_row):
    scaled = grad_out * gain_row
    first_mean = jnp.mean(scaled, axis=-1, keepdims=True)
    second_mean = jnp.mean(scaled * normed, axis=-1, keepdims=True)
    return inv_std * (scaled - first_mean - normed * second_mean)


def distributed_plan(
    pair_map,
    cotangent,
    lengths,
    norm_gains,
    edge_weight,
    mult_gate_weight,
    mult_out_weight,
    attention_weight,
    bias_weight,
    attention_out_weight,
):
    row_count, full_size, channels = pair_map.shape
    inner_width = HEADS * HEAD_DIM
    head_scale = 1.0 / math.sqrt(HEAD_DIM)
    first_row = lax.axis_index("dap") * row_count
    real_count = lengths[0]
    valid_all = (jnp.arange(full_size) < real_count).astype(jnp.float32)
    valid_rows = (first_row + jnp.arange(row_count) < real_count).astype(jnp.float32)
    mask_pair = (valid_rows[:, None] * valid_all[None, :])[:, :, None]
    pair_f32 = pair_map.astype(jnp.float32)
    normed_full, hat_in, scale_in = norm_forward(pair_f32, norm_gains[0])
    normed_x = normed_full.astype(jnp.bfloat16)
    projected = jnp.einsum("rnc,cf->rnf", normed_x, edge_weight, preferred_element_type=jnp.float32)
    left_gate = projected[..., :channels]
    left_value = projected[..., channels : 2 * channels]
    right_gate = projected[..., 2 * channels : 3 * channels]
    right_value = projected[..., 3 * channels :]
    left_sig = jax.nn.sigmoid(left_gate)
    right_sig = jax.nn.sigmoid(right_gate)
    left_edges = (mask_pair * left_sig * left_value).astype(jnp.bfloat16)
    right_edges = (mask_pair * right_sig * right_value).astype(jnp.bfloat16)
    product = jnp.einsum(
        "ikc,jkc->ijc",
        left_edges,
        lax.all_gather(right_edges, "dap", axis=0, tiled=True),
        preferred_element_type=jnp.float32,
    )
    update_full, hat_mid, scale_mid = norm_forward(product, norm_gains[1])
    update = update_full.astype(jnp.bfloat16)
    edge_out = jnp.einsum(
        "rnc,cf->rnf", update, mult_out_weight, preferred_element_type=jnp.float32
    )
    gate_sig = jax.nn.sigmoid(
        jnp.einsum("rnc,cf->rnf", normed_x, mult_gate_weight, preferred_element_type=jnp.float32)
    )
    middle = pair_f32 + gate_sig * edge_out
    normed_mid, hat_attn, scale_attn = norm_forward(middle, norm_gains[2])
    normed_y = normed_mid.astype(jnp.bfloat16)
    bias_local = jnp.einsum(
        "kic,ch->hki", normed_y, bias_weight, preferred_element_type=jnp.float32
    ).astype(jnp.bfloat16)
    bias_whole = lax.all_gather(bias_local, "dap", axis=1, tiled=True)
    bias_query = jnp.swapaxes(bias_whole, 1, 2).astype(jnp.float32)
    column_y, column_cot = (
        lax.all_to_all(normed_y, "dap", split_axis=1, concat_axis=0, tiled=True),
        lax.all_to_all(cotangent, "dap", split_axis=1, concat_axis=0, tiled=True),
    )
    packed = jnp.einsum(
        "ijc,cf->ijf", column_y, attention_weight, preferred_element_type=jnp.float32
    )
    packed = packed.reshape(full_size, row_count, 4, HEADS, HEAD_DIM)
    query_vectors = (packed[:, :, 0] * head_scale).astype(jnp.bfloat16)
    key_vectors = packed[:, :, 1].astype(jnp.bfloat16)
    value_vectors = packed[:, :, 2].astype(jnp.bfloat16)
    att_gate = jax.nn.sigmoid(packed[:, :, 3])
    scores = (
        jnp.einsum(
            "ijhd,kjhd->jhik", query_vectors, key_vectors, preferred_element_type=jnp.float32
        )
        + bias_query[None]
    )
    exp_scores = valid_all * jnp.exp(scores)
    attention = exp_scores / jnp.sum(exp_scores, axis=-1, keepdims=True)
    attention_half = attention.astype(jnp.bfloat16)
    attended = jnp.einsum(
        "jhik,kjhd->ijhd", attention_half, value_vectors, preferred_element_type=jnp.float32
    )
    gated = (att_gate * attended).astype(jnp.bfloat16).reshape(full_size, row_count, inner_width)
    part_attn_out = jnp.einsum("ijf,ijc->fc", gated, column_cot, preferred_element_type=jnp.float32)
    grad_gated = jnp.einsum(
        "ijc,fc->ijf", column_cot, attention_out_weight, preferred_element_type=jnp.float32
    )
    grad_gated = grad_gated.reshape(full_size, row_count, HEADS, HEAD_DIM)
    grad_att = (grad_gated * att_gate).astype(jnp.bfloat16)
    grad_gate_pre = grad_gated * attended * att_gate * (1.0 - att_gate)
    grad_attention = jnp.einsum(
        "ijhd,kjhd->jhik", grad_att, value_vectors, preferred_element_type=jnp.float32
    )
    row_dots = jnp.transpose(jnp.sum(grad_att.astype(jnp.float32) * attended, axis=-1), (1, 2, 0))
    grad_scores = attention * (grad_attention - row_dots[..., None])
    scores_half = grad_scores.astype(jnp.bfloat16)
    grad_query = jnp.einsum(
        "jhik,kjhd->ijhd", scores_half, key_vectors, preferred_element_type=jnp.float32
    )
    grad_key = jnp.einsum(
        "jhik,ijhd->kjhd", scores_half, query_vectors, preferred_element_type=jnp.float32
    )
    grad_value = jnp.einsum(
        "jhik,ijhd->kjhd", attention_half, grad_att, preferred_element_type=jnp.float32
    )
    grad_packed = jnp.stack([grad_query * head_scale, grad_key, grad_value, grad_gate_pre], axis=2)
    grad_packed = grad_packed.reshape(full_size, row_count, 4 * inner_width).astype(jnp.bfloat16)
    part_attention = jnp.einsum(
        "ijc,ijf->cf", column_y, grad_packed, preferred_element_type=jnp.float32
    )
    column_grad = jnp.einsum(
        "ijf,cf->ijc", grad_packed, attention_weight, preferred_element_type=jnp.float32
    ).astype(jnp.bfloat16)
    row_grad = lax.all_to_all(column_grad, "dap", split_axis=0, concat_axis=1, tiled=True)
    score_sums = jnp.sum(grad_scores, axis=0)
    taken = score_sums
    bias_half = lax.psum_scatter(
        jnp.transpose(taken, (2, 0, 1)), "dap", scatter_dimension=0, tiled=True
    ).astype(jnp.bfloat16)
    part_bias = jnp.einsum("kic,khi->ch", normed_y, bias_half, preferred_element_type=jnp.float32)
    grad_normed_y = row_grad.astype(jnp.float32) + jnp.einsum(
        "khi,ch->kic", bias_half, bias_weight, preferred_element_type=jnp.float32
    )
    part_gain_attn = jnp.sum(grad_normed_y * hat_attn, axis=(0, 1))
    grad_middle = cotangent.astype(jnp.float32) + norm_backward(
        grad_normed_y, hat_attn, scale_attn, norm_gains[2]
    )
    grad_edge_out = (grad_middle * gate_sig).astype(jnp.bfloat16)
    grad_gate = (grad_middle * edge_out * gate_sig * (1.0 - gate_sig)).astype(jnp.bfloat16)
    part_mult_out = jnp.einsum(
        "rnc,rnf->cf", update, grad_edge_out, preferred_element_type=jnp.float32
    )
    part_mult_gate = jnp.einsum(
        "rnc,rnf->cf", normed_x, grad_gate, preferred_element_type=jnp.float32
    )
    grad_update = jnp.einsum(
        "rnf,cf->rnc", grad_edge_out, mult_out_weight, preferred_element_type=jnp.float32
    )
    part_gain_mid = jnp.sum(grad_update * hat_mid, axis=(0, 1))
    grad_product = norm_backward(grad_update, hat_mid, scale_mid, norm_gains[1]).astype(
        jnp.bfloat16
    )
    taken = grad_product
    grad_left = jnp.einsum(
        "ijc,jkc->ikc",
        taken,
        lax.all_gather(right_edges, "dap", axis=0, tiled=True),
        preferred_element_type=jnp.float32,
    )
    grad_cols = lax.all_to_all(grad_product, "dap", split_axis=1, concat_axis=0, tiled=True)
    taken = grad_cols
    grad_right = jnp.einsum(
        "ijc,ikc->jkc",
        taken,
        lax.all_gather(left_edges, "dap", axis=0, tiled=True),
        preferred_element_type=jnp.float32,
    )
    grad_proj = jnp.concatenate(
        [
            grad_left * mask_pair * left_value * left_sig * (1.0 - left_sig),
            grad_left * mask_pair * left_sig,
            grad_right * mask_pair * right_value * right_sig * (1.0 - right_sig),
            grad_right * mask_pair * right_sig,
        ],
        axis=-1,
    ).astype(jnp.bfloat16)
    part_edge = jnp.einsum("rnc,rnf->cf", normed_x, grad_proj, preferred_element_type=jnp.float32)
    grad_normed_x = jnp.einsum(
        "rnf,cf->rnc", grad_proj, edge_weight, preferred_element_type=jnp.float32
    )
    grad_normed_x = grad_normed_x + jnp.einsum(
        "rnf,cf->rnc", grad_gate, mult_gate_weight, preferred_element_type=jnp.float32
    )
    part_gain_in = jnp.sum(grad_normed_x * hat_in, axis=(0, 1))
    grad_pair = (
        grad_middle + norm_backward(grad_normed_x, hat_in, scale_in, norm_gains[0])
    ).astype(jnp.bfloat16)
    totals = lax.psum(
        (
            part_gain_in,
            part_gain_mid,
            part_edge,
            part_mult_gate,
            part_mult_out,
            part_gain_attn,
            part_attention,
            part_bias,
            part_attn_out,
        ),
        "dap",
    )
    (
        gain_in_sum,
        gain_mid_sum,
        edge_sum,
        mult_gate_sum,
        mult_out_sum,
        gain_attn_sum,
        attention_sum,
        bias_sum,
        attn_out_sum,
    ) = totals
    inverse = 1.0 / full_size
    grad_gains = jnp.stack([gain_in_sum, gain_mid_sum, gain_attn_sum]) * inverse
    return (
        grad_pair,
        grad_gains,
        edge_sum * inverse,
        mult_gate_sum * inverse,
        mult_out_sum * inverse,
        attention_sum * inverse,
        bias_sum * inverse,
        attn_out_sum * inverse,
    )


ROW_BLOCK = 8
VMEM_SLACK = 8 * 2**20
VMEM_SHARE = 32 * 2**20
HALF = jnp.bfloat16
FULL = jnp.float32


def dot_nn(left, right):
    return lax.dot_general(left, right, (((1,), (0,)), ((), ())), preferred_element_type=FULL)


def dot_nt(left, right):
    return lax.dot_general(left, right, (((1,), (1,)), ((), ())), preferred_element_type=FULL)


def dot_tn(left, right):
    return lax.dot_general(left, right, (((0,), (0,)), ((), ())), preferred_element_type=FULL)


def dot_wide(values, ones):
    high = values.astype(HALF)
    low = (values - high.astype(FULL)).astype(HALF)
    return dot_nn(high, ones) + dot_nn(low, ones)


def head_blocks(row_width, col_width, dtype):
    shape = (HEADS * row_width, HEADS * col_width)
    row = lax.broadcasted_iota(jnp.int32, shape, 0)
    col = lax.broadcasted_iota(jnp.int32, shape, 1)
    same = None
    for h in range(HEADS):
        here = (row >= h * row_width) & (row < (h + 1) * row_width)
        here = here & (col >= h * col_width) & (col < (h + 1) * col_width)
        same = here if same is None else same | here
    return jnp.where(same, 1.0, 0.0).astype(dtype)


def place_rows(targets, blocks, masks):
    me = lax.axis_index("dap")
    for at, mask in enumerate(masks):
        for part, target in enumerate(targets):
            cells = target.shape[0] // (2 * len(masks))
            place = pl.ds(pl.multiple_of((me ^ mask) * cells, cells), cells)
            target[place, :] = blocks[at, part].reshape(cells, target.shape[1]).astype(FULL)


def block_tools(size):
    block = ROW_BLOCK * size

    def rows_of(at):
        return pl.ds(pl.multiple_of(at * block, block), block)

    def columns_of(ref, at):
        return jnp.concatenate(
            [ref[pl.ds(at * ROW_BLOCK + a, size, stride=size), :] for a in range(ROW_BLOCK)], axis=0
        )

    return rows_of, columns_of


def outer_sum(size, at, row_ref, row_stride, block_stride, block_ref):
    sums = [jnp.zeros((size, block_ref.shape[1]), FULL)] * ROW_BLOCK
    for k in range(size):
        whole = block_ref[k * size : (k + 1) * size, :]
        for a in range(ROW_BLOCK):
            row = (at * ROW_BLOCK + a) * block_stride + k * row_stride
            sums[a] = sums[a] + row_ref[pl.ds(row, 1), :] * whole
    return jnp.concatenate(sums, axis=0)


def same_cell_of(size):
    row = lax.broadcasted_iota(jnp.int32, (size, HEADS * size), 0)
    lane = lax.broadcasted_iota(jnp.int32, (size, HEADS * size), 1)
    same = lane == row
    for h in range(1, HEADS):
        same = same | (lane == row + h * size)
    return jnp.where(same, 1.0, 0.0)


def real_lanes(size, real):
    lane = lax.broadcasted_iota(jnp.int32, (1, HEADS * size), 1)
    inside = lane < real
    for h in range(1, HEADS):
        inside = inside | ((lane >= h * size) & (lane < h * size + real))
    return jnp.where(inside, 1.0, 0.0)


def spread_bias_weight(target, bias_w_ref, size):
    bias_rows = bias_w_ref[...].astype(FULL)
    for h in range(HEADS):
        target[h * size : (h + 1) * size, :] = jnp.broadcast_to(
            bias_rows[h : h + 1], (size, bias_rows.shape[1])
        ).astype(HALF)


def forward(
    size,
    pair_ref,
    real,
    gains_ref,
    weights,
    saved,
    scratch,
):
    channels = gains_ref.shape[1]
    block = ROW_BLOCK * size
    blocks = size // ROW_BLOCK
    lanes = HEADS * size
    head_scale = 1.0 / math.sqrt(HEAD_DIM)
    rows_of, columns_of = block_tools(size)
    edge_w_ref, gate_w_ref, out_w_ref, att_w_ref, _, _ = weights
    (
        left_ref,
        right_ref,
        left_a_ref,
        left_b_ref,
        right_a_ref,
        right_b_ref,
        gate_ref,
        hat_mid_ref,
        scale_mid_ref,
        edge_out_ref,
        hat_y_ref,
        scale_y_ref,
        att_gate_ref,
        x_half_ref,
        update_ref,
        y_t_ref,
        query_ref,
        key_ref,
        value_ref,
        bias_ref,
        bias_rep_ref,
    ) = saved
    right_t_ref, y_ref = scratch
    gain_x = gains_ref[0:1, :]
    gain_mid = gains_ref[1:2, :]
    gain_y = gains_ref[2:3, :]

    def project(at, carry):
        rows = rows_of(at)
        hat, _ = norm_of(pair_ref[rows, :])
        normed = (hat * gain_x).astype(HALF)
        x_half_ref[rows, :] = normed
        projected = dot_nn(normed, edge_w_ref[...])
        gate_ref[rows, :] = jax.nn.sigmoid(dot_nn(normed, gate_w_ref[...]))
        shape = (ROW_BLOCK, size, channels)
        row = lax.broadcasted_iota(jnp.int32, shape, 0) + at * ROW_BLOCK
        col = lax.broadcasted_iota(jnp.int32, shape, 1)
        mask = jnp.where((row < real) & (col < real), 1.0, 0.0).reshape(block, channels)
        for side, (edge, first, second) in enumerate(
            ((left_ref, left_a_ref, left_b_ref), (right_ref, right_a_ref, right_b_ref))
        ):
            base = 2 * side * channels
            sig = jax.nn.sigmoid(projected[:, base : base + channels])
            value = projected[:, base + channels : base + 2 * channels]
            masked = mask * sig
            product = masked * value
            edge[rows, :] = product.astype(HALF).astype(FULL)
            first[rows, :] = product * (1.0 - sig)
            second[rows, :] = masked
        return carry

    lax.fori_loop(0, blocks, project, 0)

    def turn(at, carry):
        right_t_ref[rows_of(at), :] = columns_of(right_ref, at)
        return carry

    lax.fori_loop(0, blocks, turn, 0)

    def multiply(at, carry):
        rows = rows_of(at)
        product = outer_sum(size, at, left_ref, 1, size, right_t_ref)
        hat, scale = norm_of(product)
        hat_mid_ref[rows, :] = hat
        scale_mid_ref[rows, :] = jnp.broadcast_to(scale, hat.shape)
        update = (hat * gain_mid).astype(HALF)
        update_ref[rows, :] = update
        edge_out = dot_nn(update, out_w_ref[...])
        edge_out_ref[rows, :] = edge_out
        middle = pair_ref[rows, :] + gate_ref[rows, :] * edge_out
        hat, scale = norm_of(middle)
        hat_y_ref[rows, :] = hat
        scale_y_ref[rows, :] = jnp.broadcast_to(scale, hat.shape)
        y_ref[rows, :] = hat * gain_y
        return carry

    lax.fori_loop(0, blocks, multiply, 0)

    same_cell = same_cell_of(size)

    def prepare(at, carry):
        rows = rows_of(at)
        y = columns_of(y_ref, at).astype(HALF)
        y_t_ref[rows, :] = y
        packed = dot_nn(y, att_w_ref[...])
        query_ref[rows, :] = (packed[:, :channels] * head_scale).astype(HALF)
        key_ref[rows, :] = packed[:, channels : 2 * channels].astype(HALF)
        value_ref[rows, :] = packed[:, 2 * channels : 3 * channels].astype(HALF)
        att_gate_ref[rows, :] = jax.nn.sigmoid(packed[:, 3 * channels :])
        spread = dot_nt(y, bias_rep_ref[...]).astype(HALF).astype(FULL)
        spread = spread.reshape(ROW_BLOCK, size, lanes) * same_cell[None]
        bias_ref[pl.ds(at * ROW_BLOCK, ROW_BLOCK), :] = jnp.sum(spread, axis=1)
        return carry

    lax.fori_loop(0, blocks, prepare, 0)


def backward(
    size,
    devices,
    pair_ref,
    cot_ref,
    real,
    gains_ref,
    weights,
    saved,
    outs,
    scratch,
):
    channels = gains_ref.shape[1]
    block = ROW_BLOCK * size
    blocks = size // ROW_BLOCK
    lanes = HEADS * size
    head_scale = 1.0 / math.sqrt(HEAD_DIM)
    rows_of, columns_of = block_tools(size)
    edge_w_ref, gate_w_ref, out_w_ref, att_w_ref, _, att_out_w_ref = weights
    (
        left_ref,
        right_ref,
        left_a_ref,
        left_b_ref,
        right_a_ref,
        right_b_ref,
        gate_ref,
        hat_mid_ref,
        scale_mid_ref,
        edge_out_ref,
        hat_y_ref,
        scale_y_ref,
        att_gate_ref,
        x_half_ref,
        update_ref,
        y_t_ref,
        query_ref,
        key_ref,
        value_ref,
        bias_ref,
        bias_rep_ref,
    ) = saved
    (
        grad_pair_ref,
        grad_gains_ref,
        grad_edge_ref,
        grad_gate_w_ref,
        grad_out_w_ref,
        grad_att_w_ref,
        grad_bias_ref,
        grad_att_out_ref,
    ) = outs
    (
        grad_gated_ref,
        grad_y_ref,
        grad_middle_ref,
        grad_product_ref,
        cot_t_ref,
        grad_att_ref,
        gated_ref,
        grad_edge_out_ref,
        grad_packed_ref,
        grad_proj_ref,
        bias_grad_ref,
    ) = scratch
    gain_x = gains_ref[0:1, :]
    gain_mid = gains_ref[1:2, :]
    gain_y = gains_ref[2:3, :]
    same_cell = same_cell_of(size)
    valid = real_lanes(size, real)

    def prepare(at, carry):
        rows = rows_of(at)
        cot = columns_of(cot_ref, at).astype(HALF)
        cot_t_ref[rows, :] = cot
        grad_gated = dot_nt(cot, att_out_w_ref[...])
        grad_gated_ref[rows, :] = grad_gated
        grad_att_ref[rows, :] = (grad_gated * att_gate_ref[rows, :]).astype(HALF)
        return carry

    lax.fori_loop(0, blocks, prepare, 0)

    head_mask = head_blocks(size, HEAD_DIM, HALF)
    head_mask_full = head_blocks(size, HEAD_DIM, FULL)
    key_ones = head_blocks(size, size, HALF)
    dim_ones = head_blocks(HEAD_DIM, size, HALF)

    def attend(at, score_sum):
        rows = rows_of(at)
        parts = [slice(a * size, (a + 1) * size) for a in range(ROW_BLOCK)]
        query, key, value, grad_att = (
            ref[rows, :] for ref in (query_ref, key_ref, value_ref, grad_att_ref)
        )
        keys = [jnp.concatenate([key[p]] * HEADS, axis=0) * head_mask for p in parts]
        values = [jnp.concatenate([value[p]] * HEADS, axis=0) * head_mask for p in parts]
        bias = bias_ref[...]
        scores = jnp.concatenate(
            [dot_nt(query[p], keys[a]) + bias for a, p in enumerate(parts)], axis=0
        )
        exp_scores = valid * jnp.exp(scores)
        attention = exp_scores / dot_wide(exp_scores, key_ones)
        attention_half = attention.astype(HALF)
        attended = jnp.concatenate(
            [dot_nn(attention_half[p], values[a]) for a, p in enumerate(parts)], axis=0
        )
        grad_attention = jnp.concatenate(
            [dot_nt(grad_att[p], values[a]) for a, p in enumerate(parts)], axis=0
        )
        row_dots = dot_wide(grad_att.astype(FULL) * attended, dim_ones)
        grad_scores = attention * (grad_attention - row_dots)
        scores_half = grad_scores.astype(HALF)
        for p in parts:
            score_sum = score_sum + grad_scores[p]
        grad_query = jnp.concatenate(
            [dot_nn(scores_half[p], keys[a]) for a, p in enumerate(parts)], axis=0
        )

        def per_key(weights, vectors):
            folded = []
            for p in parts:
                whole = dot_tn(weights[p], vectors[p]) * head_mask_full
                folded.append(sum(whole[h * size : (h + 1) * size] for h in range(HEADS)))
            return jnp.concatenate(folded, axis=0)

        grad_key = per_key(scores_half, query)
        grad_value = per_key(attention_half, grad_att)
        gate = att_gate_ref[rows, :]
        gated = gate * attended
        gated_ref[rows, :] = gated.astype(HALF)
        grad_gate_pre = grad_gated_ref[rows, :] * gated * (1.0 - gate)
        grad_packed = jnp.concatenate(
            [
                (grad_query * head_scale).astype(HALF),
                grad_key.astype(HALF),
                grad_value.astype(HALF),
                grad_gate_pre.astype(HALF),
            ],
            axis=1,
        )
        grad_packed_ref[rows, : 4 * channels] = grad_packed
        grad_y_ref[rows, :] = dot_nt(grad_packed, att_w_ref[...])
        return score_sum

    score_sum = lax.fori_loop(0, blocks, attend, jnp.zeros((size, lanes), FULL))
    bias_grad_ref[...] = score_sum.astype(HALF).astype(FULL)

    def spread_bias(at, carry):
        rows = rows_of(at)
        part = bias_grad_ref[pl.ds(at * ROW_BLOCK, ROW_BLOCK), :]
        spread = (part[:, None, :] * same_cell[None]).reshape(block, lanes).astype(HALF)
        grad_packed_ref[rows, 4 * channels :] = spread
        grad_y_ref[rows, :] += dot_nn(spread, bias_rep_ref[...])
        return carry

    lax.fori_loop(0, blocks, spread_bias, 0)

    def middle_back(at, carry):
        rows = rows_of(at)
        grad_y = columns_of(grad_y_ref, at)
        grad_middle = cot_ref[rows, :] + norm_back(
            grad_y, hat_y_ref[rows, :], scale_y_ref[rows, :], gain_y
        )
        grad_middle_ref[rows, :] = grad_middle
        gate = gate_ref[rows, :]
        gated = grad_middle * gate
        grad_edge_out = gated.astype(HALF)
        grad_edge_out_ref[rows, :] = grad_edge_out
        grad_gate = gated * edge_out_ref[rows, :] * (1.0 - gate)
        grad_proj_ref[rows, 4 * channels :] = grad_gate.astype(HALF)
        grad_update = dot_nt(grad_edge_out, out_w_ref[...])
        grad_product = norm_back(grad_update, hat_mid_ref[rows, :], scale_mid_ref[rows, :], gain_mid)
        grad_product_ref[rows, :] = grad_product.astype(HALF).astype(FULL)
        return carry

    lax.fori_loop(0, blocks, middle_back, 0)

    def edges_back(at, carry):
        rows = rows_of(at)
        grad_left = outer_sum(size, at, grad_product_ref, 1, size, right_ref)
        grad_proj_ref[rows, :channels] = (grad_left * left_a_ref[rows, :]).astype(HALF)
        grad_proj_ref[rows, channels : 2 * channels] = (grad_left * left_b_ref[rows, :]).astype(HALF)
        grad_right = outer_sum(size, at, grad_product_ref, size, 1, left_ref)
        grad_proj_ref[rows, 2 * channels : 3 * channels] = (grad_right * right_a_ref[rows, :]).astype(HALF)
        grad_proj_ref[rows, 3 * channels : 4 * channels] = (grad_right * right_b_ref[rows, :]).astype(HALF)
        return carry

    lax.fori_loop(0, blocks, edges_back, 0)

    inverse = 1.0 / size
    x_sum = dot_tn(x_half_ref[...], grad_proj_ref[...]) * inverse
    edge_sum, gate_sum = x_sum[:, : 4 * channels], x_sum[:, 4 * channels :]
    grad_edge_ref[...] = edge_sum
    grad_gate_w_ref[...] = gate_sum
    out_sum = dot_tn(update_ref[...], grad_edge_out_ref[...]) * inverse
    grad_out_w_ref[...] = out_sum
    y_sum = dot_tn(y_t_ref[...], grad_packed_ref[...]) * inverse
    att_sum, bias_sum = y_sum[:, : 4 * channels], jnp.transpose(y_sum[:, 4 * channels :])
    grad_att_w_ref[...] = att_sum
    grad_att_out_ref[...] = dot_tn(gated_ref[...], cot_t_ref[...]) * inverse
    for h in range(HEADS):
        grad_bias_ref[h : h + 1, :] = jnp.sum(
            bias_sum[h * size : (h + 1) * size], axis=0, keepdims=True
        )

    def gain_sum(pairs):
        total = sum(
            jnp.sum(weight.astype(FULL) * grad, axis=1, keepdims=True) for weight, grad in pairs
        )
        return jnp.transpose(jnp.broadcast_to(total, (channels, channels)))[0:1, :]

    grad_gains_ref[0:1, :] = gain_sum(((edge_w_ref[...], edge_sum), (gate_w_ref[...], gate_sum))) / gain_x
    grad_gains_ref[1:2, :] = gain_sum(((out_w_ref[...], out_sum),)) / gain_mid
    bias_part = jnp.sum(bias_rep_ref[...].astype(FULL) * bias_sum, axis=0, keepdims=True)
    grad_gains_ref[2:3, :] = (gain_sum(((att_w_ref[...], att_sum),)) + bias_part) / gain_y

    own_cells = size * size // devices
    own = pl.ds(pl.multiple_of(lax.axis_index("dap") * own_cells, own_cells), own_cells)
    hat, scale = norm_of(pair_ref[own, :])
    grad_x = dot_nt(grad_proj_ref[own, : 4 * channels], edge_w_ref[...])
    grad_x = grad_x + dot_nt(grad_proj_ref[own, 4 * channels :], gate_w_ref[...])
    grad_pair = grad_middle_ref[own, :] + norm_back(grad_x, hat, scale, gain_x)
    grad_pair_ref[...] = grad_pair.astype(grad_pair_ref.dtype)


def whole_kernel(size, masks, near_ref, far_ref, lengths_ref, gains_ref, *refs):
    counts = [len(part) for part in kernel_arrays(size, 1)]
    weights, outs, refs = refs[:6], refs[6:14], refs[14:]
    pair_ref, cot_ref = refs[:2]
    parts, at = [], 2
    for count in counts:
        parts.append(refs[at : at + count])
        at += count
    saved, forward_scratch, backward_scratch = parts
    place_rows((pair_ref, cot_ref), near_ref, masks)
    place_rows((pair_ref, cot_ref), far_ref, [mask ^ 1 for mask in masks])
    spread_bias_weight(saved[-1], weights[4], size)
    real = lengths_ref[0]
    forward(size, pair_ref, real, gains_ref, weights, saved, forward_scratch)
    backward(size, 2 * len(masks), pair_ref, cot_ref, real, gains_ref, weights, saved, outs, backward_scratch)


def norm_of(values):
    center = values - jnp.mean(values, axis=-1, keepdims=True)
    scale = lax.rsqrt(jnp.mean(center * center, axis=-1, keepdims=True) + epsilon)
    return center * scale, scale


def norm_back(grad_out, hat, scale, gain):
    scaled = grad_out * gain
    first_mean = jnp.mean(scaled, axis=-1, keepdims=True)
    second_mean = jnp.mean(scaled * hat, axis=-1, keepdims=True)
    return scale * (scaled - first_mean - hat * second_mean)


def cell_arrays(size, channels, full_count, half_count):
    shape = (size * size, channels)
    return [(shape, FULL)] * full_count + [(shape, HALF)] * half_count


def kernel_arrays(size, channels):
    cells, lanes = size * size, HEADS * size
    saved = cell_arrays(size, channels, 13, 6) + [((size, lanes), FULL), ((lanes, channels), HALF)]
    forward_scratch = cell_arrays(size, channels, 2, 0)
    backward_scratch = cell_arrays(size, channels, 4, 4) + [
        ((cells, 4 * channels + lanes), HALF),
        ((cells, 5 * channels), HALF),
        ((size, lanes), FULL),
    ]
    return saved, forward_scratch, backward_scratch


def scratch_arrays(size, channels):
    return cell_arrays(size, channels, 2, 0) + sum(kernel_arrays(size, channels), [])


def bytes_of(arrays):
    return sum(math.prod(shape) * jnp.dtype(dtype).itemsize for shape, dtype in arrays)


def gather_blocks(own, axis_size):
    bits = axis_size.bit_length() - 1

    def swapped(held, mask):
        return lax.ppermute(held, "dap", [(d, d ^ mask) for d in range(axis_size)])

    held, masks = own[None], [0]
    for low, high in ((bits - 1, bits), (1, bits - 1)):
        steps = range(1 << low, 1 << high, 1 << low)
        if low > 0 and len(steps) > 0:
            held = jnp.concatenate([held] + [swapped(held, step) for step in steps], axis=0)
            masks = masks + [mask ^ step for step in steps for mask in masks]
    return held, swapped(held, 1), masks


def replicated_plan(
    axis_size,
    pair_map,
    cotangent,
    lengths,
    norm_gains,
    edge_weight,
    mult_gate_weight,
    mult_out_weight,
    attention_weight,
    bias_weight,
    attention_out_weight,
):
    _, size, channels = pair_map.shape
    near, far, masks = gather_blocks(jnp.stack([pair_map, cotangent]), axis_size)
    square, wide = ((channels, channels), FULL), ((channels, 4 * channels), FULL)
    out_shapes = [
        ((size * size // axis_size, channels), HALF),
        ((3, channels), FULL),
        wide,
        square,
        square,
        wide,
        ((HEADS, channels), FULL),
        square,
    ]
    scratch = scratch_arrays(size, channels)
    vmem = pl.BlockSpec(memory_space=pltpu.VMEM)
    smem = pl.BlockSpec(memory_space=pltpu.SMEM)
    outs = pl.pallas_call(
        functools.partial(whole_kernel, size, masks),
        out_shape=[jax.ShapeDtypeStruct(*out) for out in out_shapes],
        in_specs=[vmem, vmem, smem] + [vmem] * 7,
        out_specs=[vmem] * len(out_shapes),
        scratch_shapes=[pltpu.VMEM(*part) for part in scratch],
        compiler_params=pltpu.CompilerParams(vmem_limit_bytes=bytes_of(scratch) + VMEM_SLACK),
    )(
        near,
        far,
        lengths,
        norm_gains,
        edge_weight,
        mult_gate_weight,
        mult_out_weight,
        attention_weight,
        bias_weight.T,
        attention_out_weight,
    )
    return (outs[0].reshape(pair_map.shape), *outs[1:6], outs[6].T, outs[7])


def per_device(axis_size, pair_map, *rest):
    _, size, channels = pair_map.shape
    fits = size % ROW_BLOCK == 0 and bytes_of(scratch_arrays(size, channels)) <= VMEM_SHARE
    if fits and axis_size >= 4 and axis_size & (axis_size - 1) == 0:
        return replicated_plan(axis_size, pair_map, *rest)
    return distributed_plan(pair_map, *rest)


def solution(mesh):
    return jax.shard_map(
        functools.partial(per_device, mesh.shape["dap"]),
        mesh=mesh,
        in_specs=(
            P(("groups", "dap"), None, None),
            P(("groups", "dap"), None, None),
            P("groups"),
            P(),
            P(),
            P(),
            P(),
            P(),
            P(),
            P(),
        ),
        out_specs=(
            P(("groups", "dap"), None, None),
            P("groups", None),
            P("groups", None),
            P("groups", None),
            P("groups", None),
            P("groups", None),
            P("groups", None),
            P("groups", None),
        ),
        check_vma=False,
    )
```

```python
import functools
import math

import jax
import jax.numpy as jnp
from jax import lax
from jax.experimental import pallas as pl
from jax.experimental.pallas import tpu as pltpu
from jax.sharding import PartitionSpec as P

HEADS = 4
HEAD_DIM = 32


epsilon = 1e-05


def norm_forward(values, gain_row):
    center = values - jnp.mean(values, axis=-1, keepdims=True)
    inv_std = lax.rsqrt(jnp.mean(center * center, axis=-1, keepdims=True) + epsilon)
    normed = center * inv_std
    return (normed * gain_row, normed, inv_std)


def norm_backward(grad_out, normed, inv_std, gain_row):
    scaled = grad_out * gain_row
    first_mean = jnp.mean(scaled, axis=-1, keepdims=True)
    second_mean = jnp.mean(scaled * normed, axis=-1, keepdims=True)
    return inv_std * (scaled - first_mean - normed * second_mean)


def distributed_plan(
    pair_map,
    cotangent,
    lengths,
    norm_gains,
    edge_weight,
    mult_gate_weight,
    mult_out_weight,
    attention_weight,
    bias_weight,
    attention_out_weight,
):
    row_count, full_size, channels = pair_map.shape
    inner_width = HEADS * HEAD_DIM
    head_scale = 1.0 / math.sqrt(HEAD_DIM)
    first_row = lax.axis_index("dap") * row_count
    real_count = lengths[0]
    valid_all = (jnp.arange(full_size) < real_count).astype(jnp.float32)
    valid_rows = (first_row + jnp.arange(row_count) < real_count).astype(jnp.float32)
    mask_pair = (valid_rows[:, None] * valid_all[None, :])[:, :, None]
    pair_f32 = pair_map.astype(jnp.float32)
    normed_full, hat_in, scale_in = norm_forward(pair_f32, norm_gains[0])
    normed_x = normed_full.astype(jnp.bfloat16)
    projected = jnp.einsum("rnc,cf->rnf", normed_x, edge_weight, preferred_element_type=jnp.float32)
    left_gate = projected[..., :channels]
    left_value = projected[..., channels : 2 * channels]
    right_gate = projected[..., 2 * channels : 3 * channels]
    right_value = projected[..., 3 * channels :]
    left_sig = jax.nn.sigmoid(left_gate)
    right_sig = jax.nn.sigmoid(right_gate)
    left_edges = (mask_pair * left_sig * left_value).astype(jnp.bfloat16)
    right_edges = (mask_pair * right_sig * right_value).astype(jnp.bfloat16)
    product = jnp.einsum(
        "ikc,jkc->ijc",
        left_edges,
        lax.all_gather(right_edges, "dap", axis=0, tiled=True),
        preferred_element_type=jnp.float32,
    )
    update_full, hat_mid, scale_mid = norm_forward(product, norm_gains[1])
    update = update_full.astype(jnp.bfloat16)
    edge_out = jnp.einsum(
        "rnc,cf->rnf", update, mult_out_weight, preferred_element_type=jnp.float32
    )
    gate_sig = jax.nn.sigmoid(
        jnp.einsum("rnc,cf->rnf", normed_x, mult_gate_weight, preferred_element_type=jnp.float32)
    )
    middle = pair_f32 + gate_sig * edge_out
    normed_mid, hat_attn, scale_attn = norm_forward(middle, norm_gains[2])
    normed_y = normed_mid.astype(jnp.bfloat16)
    bias_local = jnp.einsum(
        "kic,ch->hki", normed_y, bias_weight, preferred_element_type=jnp.float32
    ).astype(jnp.bfloat16)
    bias_whole = lax.all_gather(bias_local, "dap", axis=1, tiled=True)
    bias_query = jnp.swapaxes(bias_whole, 1, 2).astype(jnp.float32)
    column_y, column_cot = (
        lax.all_to_all(normed_y, "dap", split_axis=1, concat_axis=0, tiled=True),
        lax.all_to_all(cotangent, "dap", split_axis=1, concat_axis=0, tiled=True),
    )
    packed = jnp.einsum(
        "ijc,cf->ijf", column_y, attention_weight, preferred_element_type=jnp.float32
    )
    packed = packed.reshape(full_size, row_count, 4, HEADS, HEAD_DIM)
    query_vectors = (packed[:, :, 0] * head_scale).astype(jnp.bfloat16)
    key_vectors = packed[:, :, 1].astype(jnp.bfloat16)
    value_vectors = packed[:, :, 2].astype(jnp.bfloat16)
    att_gate = jax.nn.sigmoid(packed[:, :, 3])
    scores = (
        jnp.einsum(
            "ijhd,kjhd->jhik", query_vectors, key_vectors, preferred_element_type=jnp.float32
        )
        + bias_query[None]
    )
    exp_scores = valid_all * jnp.exp(scores)
    attention = exp_scores / jnp.sum(exp_scores, axis=-1, keepdims=True)
    attention_half = attention.astype(jnp.bfloat16)
    attended = jnp.einsum(
        "jhik,kjhd->ijhd", attention_half, value_vectors, preferred_element_type=jnp.float32
    )
    gated = (att_gate * attended).astype(jnp.bfloat16).reshape(full_size, row_count, inner_width)
    part_attn_out = jnp.einsum("ijf,ijc->fc", gated, column_cot, preferred_element_type=jnp.float32)
    grad_gated = jnp.einsum(
        "ijc,fc->ijf", column_cot, attention_out_weight, preferred_element_type=jnp.float32
    )
    grad_gated = grad_gated.reshape(full_size, row_count, HEADS, HEAD_DIM)
    grad_att = (grad_gated * att_gate).astype(jnp.bfloat16)
    grad_gate_pre = grad_gated * attended * att_gate * (1.0 - att_gate)
    grad_attention = jnp.einsum(
        "ijhd,kjhd->jhik", grad_att, value_vectors, preferred_element_type=jnp.float32
    )
    row_dots = jnp.transpose(jnp.sum(grad_att.astype(jnp.float32) * attended, axis=-1), (1, 2, 0))
    grad_scores = attention * (grad_attention - row_dots[..., None])
    scores_half = grad_scores.astype(jnp.bfloat16)
    grad_query = jnp.einsum(
        "jhik,kjhd->ijhd", scores_half, key_vectors, preferred_element_type=jnp.float32
    )
    grad_key = jnp.einsum(
        "jhik,ijhd->kjhd", scores_half, query_vectors, preferred_element_type=jnp.float32
    )
    grad_value = jnp.einsum(
        "jhik,ijhd->kjhd", attention_half, grad_att, preferred_element_type=jnp.float32
    )
    grad_packed = jnp.stack([grad_query * head_scale, grad_key, grad_value, grad_gate_pre], axis=2)
    grad_packed = grad_packed.reshape(full_size, row_count, 4 * inner_width).astype(jnp.bfloat16)
    part_attention = jnp.einsum(
        "ijc,ijf->cf", column_y, grad_packed, preferred_element_type=jnp.float32
    )
    column_grad = jnp.einsum(
        "ijf,cf->ijc", grad_packed, attention_weight, preferred_element_type=jnp.float32
    ).astype(jnp.bfloat16)
    row_grad = lax.all_to_all(column_grad, "dap", split_axis=0, concat_axis=1, tiled=True)
    score_sums = jnp.sum(grad_scores, axis=0)
    taken = score_sums
    bias_half = lax.psum_scatter(
        jnp.transpose(taken, (2, 0, 1)), "dap", scatter_dimension=0, tiled=True
    ).astype(jnp.bfloat16)
    part_bias = jnp.einsum("kic,khi->ch", normed_y, bias_half, preferred_element_type=jnp.float32)
    grad_normed_y = row_grad.astype(jnp.float32) + jnp.einsum(
        "khi,ch->kic", bias_half, bias_weight, preferred_element_type=jnp.float32
    )
    part_gain_attn = jnp.sum(grad_normed_y * hat_attn, axis=(0, 1))
    grad_middle = cotangent.astype(jnp.float32) + norm_backward(
        grad_normed_y, hat_attn, scale_attn, norm_gains[2]
    )
    grad_edge_out = (grad_middle * gate_sig).astype(jnp.bfloat16)
    grad_gate = (grad_middle * edge_out * gate_sig * (1.0 - gate_sig)).astype(jnp.bfloat16)
    part_mult_out = jnp.einsum(
        "rnc,rnf->cf", update, grad_edge_out, preferred_element_type=jnp.float32
    )
    part_mult_gate = jnp.einsum(
        "rnc,rnf->cf", normed_x, grad_gate, preferred_element_type=jnp.float32
    )
    grad_update = jnp.einsum(
        "rnf,cf->rnc", grad_edge_out, mult_out_weight, preferred_element_type=jnp.float32
    )
    part_gain_mid = jnp.sum(grad_update * hat_mid, axis=(0, 1))
    grad_product = norm_backward(grad_update, hat_mid, scale_mid, norm_gains[1]).astype(
        jnp.bfloat16
    )
    taken = grad_product
    grad_left = jnp.einsum(
        "ijc,jkc->ikc",
        taken,
        lax.all_gather(right_edges, "dap", axis=0, tiled=True),
        preferred_element_type=jnp.float32,
    )
    grad_cols = lax.all_to_all(grad_product, "dap", split_axis=1, concat_axis=0, tiled=True)
    taken = grad_cols
    grad_right = jnp.einsum(
        "ijc,ikc->jkc",
        taken,
        lax.all_gather(left_edges, "dap", axis=0, tiled=True),
        preferred_element_type=jnp.float32,
    )
    grad_proj = jnp.concatenate(
        [
            grad_left * mask_pair * left_value * left_sig * (1.0 - left_sig),
            grad_left * mask_pair * left_sig,
            grad_right * mask_pair * right_value * right_sig * (1.0 - right_sig),
            grad_right * mask_pair * right_sig,
        ],
        axis=-1,
    ).astype(jnp.bfloat16)
    part_edge = jnp.einsum("rnc,rnf->cf", normed_x, grad_proj, preferred_element_type=jnp.float32)
    grad_normed_x = jnp.einsum(
        "rnf,cf->rnc", grad_proj, edge_weight, preferred_element_type=jnp.float32
    )
    grad_normed_x = grad_normed_x + jnp.einsum(
        "rnf,cf->rnc", grad_gate, mult_gate_weight, preferred_element_type=jnp.float32
    )
    part_gain_in = jnp.sum(grad_normed_x * hat_in, axis=(0, 1))
    grad_pair = (
        grad_middle + norm_backward(grad_normed_x, hat_in, scale_in, norm_gains[0])
    ).astype(jnp.bfloat16)
    totals = lax.psum(
        (
            part_gain_in,
            part_gain_mid,
            part_edge,
            part_mult_gate,
            part_mult_out,
            part_gain_attn,
            part_attention,
            part_bias,
            part_attn_out,
        ),
        "dap",
    )
    (
        gain_in_sum,
        gain_mid_sum,
        edge_sum,
        mult_gate_sum,
        mult_out_sum,
        gain_attn_sum,
        attention_sum,
        bias_sum,
        attn_out_sum,
    ) = totals
    inverse = 1.0 / full_size
    grad_gains = jnp.stack([gain_in_sum, gain_mid_sum, gain_attn_sum]) * inverse
    return (
        grad_pair,
        grad_gains,
        edge_sum * inverse,
        mult_gate_sum * inverse,
        mult_out_sum * inverse,
        attention_sum * inverse,
        bias_sum * inverse,
        attn_out_sum * inverse,
    )


ROW_BLOCK = 8
VMEM_SLACK = 8 * 2**20
VMEM_SHARE = 32 * 2**20
HALF = jnp.bfloat16
FULL = jnp.float32


def dot_nn(left, right):
    return lax.dot_general(left, right, (((1,), (0,)), ((), ())), preferred_element_type=FULL)


def dot_nt(left, right):
    return lax.dot_general(left, right, (((1,), (1,)), ((), ())), preferred_element_type=FULL)


def dot_tn(left, right):
    return lax.dot_general(left, right, (((0,), (0,)), ((), ())), preferred_element_type=FULL)


def dot_wide(values, ones):
    high = values.astype(HALF)
    low = (values - high.astype(FULL)).astype(HALF)
    return dot_nn(high, ones) + dot_nn(low, ones)


def head_blocks(row_width, col_width, dtype):
    shape = (HEADS * row_width, HEADS * col_width)
    row = lax.broadcasted_iota(jnp.int32, shape, 0)
    col = lax.broadcasted_iota(jnp.int32, shape, 1)
    same = None
    for h in range(HEADS):
        here = (row >= h * row_width) & (row < (h + 1) * row_width)
        here = here & (col >= h * col_width) & (col < (h + 1) * col_width)
        same = here if same is None else same | here
    return jnp.where(same, 1.0, 0.0).astype(dtype)


def place_rows(target, near_ref, far_ref, masks):
    me = lax.axis_index("dap")
    cells = target.shape[0] // (2 * len(masks))
    for other, blocks in enumerate((near_ref, far_ref)):
        for at, mask in enumerate(masks):
            place = pl.ds(pl.multiple_of((me ^ mask ^ other) * cells, cells), cells)
            target[place, :] = blocks[at].reshape(cells, target.shape[1]).astype(FULL)


def block_tools(size):
    block = ROW_BLOCK * size

    def rows_of(at):
        return pl.ds(pl.multiple_of(at * block, block), block)

    def columns_of(ref, at):
        return jnp.concatenate(
            [ref[pl.ds(at * ROW_BLOCK + a, size, stride=size), :] for a in range(ROW_BLOCK)], axis=0
        )

    return rows_of, columns_of


def outer_sum(size, at, row_ref, row_stride, block_stride, block_ref):
    sums = [jnp.zeros((size, block_ref.shape[1]), FULL)] * ROW_BLOCK
    for k in range(size):
        whole = block_ref[k * size : (k + 1) * size, :]
        for a in range(ROW_BLOCK):
            row = (at * ROW_BLOCK + a) * block_stride + k * row_stride
            sums[a] = sums[a] + row_ref[pl.ds(row, 1), :] * whole
    return jnp.concatenate(sums, axis=0)


def same_cell_of(size):
    row = lax.broadcasted_iota(jnp.int32, (size, HEADS * size), 0)
    lane = lax.broadcasted_iota(jnp.int32, (size, HEADS * size), 1)
    same = lane == row
    for h in range(1, HEADS):
        same = same | (lane == row + h * size)
    return jnp.where(same, 1.0, 0.0)


def real_lanes(size, real):
    lane = lax.broadcasted_iota(jnp.int32, (1, HEADS * size), 1)
    inside = lane < real
    for h in range(1, HEADS):
        inside = inside | ((lane >= h * size) & (lane < h * size + real))
    return jnp.where(inside, 1.0, 0.0)


def spread_bias_weight(target, bias_w_ref, size):
    bias_rows = bias_w_ref[...].astype(FULL)
    for h in range(HEADS):
        target[h * size : (h + 1) * size, :] = jnp.broadcast_to(
            bias_rows[h : h + 1], (size, bias_rows.shape[1])
        ).astype(HALF)


def multiply_kernel(
    size,
    masks,
    near_ref,
    far_ref,
    lengths_ref,
    gains_ref,
    edge_w_ref,
    gate_w_ref,
    out_w_ref,
    left_ref,
    right_ref,
    left_a_ref,
    left_b_ref,
    right_a_ref,
    right_b_ref,
    gate_ref,
    hat_mid_ref,
    scale_mid_ref,
    edge_out_ref,
    hat_y_ref,
    scale_y_ref,
    y_ref,
    x_half_ref,
    update_ref,
    pair_ref,
    right_t_ref,
):
    channels = gains_ref.shape[1]
    block = ROW_BLOCK * size
    blocks = size // ROW_BLOCK
    rows_of, columns_of = block_tools(size)
    real = lengths_ref[0]
    gain_x = gains_ref[0:1, :]
    gain_mid = gains_ref[1:2, :]
    gain_y = gains_ref[2:3, :]
    place_rows(pair_ref, near_ref, far_ref, masks)

    def project(at, carry):
        rows = rows_of(at)
        hat, _ = norm_of(pair_ref[rows, :])
        normed = (hat * gain_x).astype(HALF)
        x_half_ref[rows, :] = normed
        projected = dot_nn(normed, edge_w_ref[...])
        gate_ref[rows, :] = jax.nn.sigmoid(dot_nn(normed, gate_w_ref[...]))
        shape = (ROW_BLOCK, size, channels)
        row = lax.broadcasted_iota(jnp.int32, shape, 0) + at * ROW_BLOCK
        col = lax.broadcasted_iota(jnp.int32, shape, 1)
        mask = jnp.where((row < real) & (col < real), 1.0, 0.0).reshape(block, channels)
        for side, (edge, first, second) in enumerate(
            ((left_ref, left_a_ref, left_b_ref), (right_ref, right_a_ref, right_b_ref))
        ):
            base = 2 * side * channels
            sig = jax.nn.sigmoid(projected[:, base : base + channels])
            value = projected[:, base + channels : base + 2 * channels]
            masked = mask * sig
            product = masked * value
            edge[rows, :] = product.astype(HALF).astype(FULL)
            first[rows, :] = product * (1.0 - sig)
            second[rows, :] = masked
        return carry

    lax.fori_loop(0, blocks, project, 0)

    def turn(at, carry):
        right_t_ref[rows_of(at), :] = columns_of(right_ref, at)
        return carry

    lax.fori_loop(0, blocks, turn, 0)

    def multiply(at, carry):
        rows = rows_of(at)
        product = outer_sum(size, at, left_ref, 1, size, right_t_ref)
        hat, scale = norm_of(product)
        hat_mid_ref[rows, :] = hat
        scale_mid_ref[rows, :] = jnp.broadcast_to(scale, hat.shape)
        update = (hat * gain_mid).astype(HALF)
        update_ref[rows, :] = update
        edge_out = dot_nn(update, out_w_ref[...])
        edge_out_ref[rows, :] = edge_out
        middle = pair_ref[rows, :] + gate_ref[rows, :] * edge_out
        hat, scale = norm_of(middle)
        hat_y_ref[rows, :] = hat
        scale_y_ref[rows, :] = jnp.broadcast_to(scale, hat.shape)
        y_ref[rows, :] = hat * gain_y
        return carry

    lax.fori_loop(0, blocks, multiply, 0)


def project_kernel(
    size,
    y_ref,
    att_w_ref,
    bias_w_ref,
    att_gate_ref,
    bias_ref,
    y_t_ref,
    query_ref,
    key_ref,
    value_ref,
    bias_rep_ref,
):
    channels = y_ref.shape[1]
    lanes = HEADS * size
    head_scale = 1.0 / math.sqrt(HEAD_DIM)
    rows_of, columns_of = block_tools(size)
    same_cell = same_cell_of(size)
    spread_bias_weight(bias_rep_ref, bias_w_ref, size)

    def prepare(at, carry):
        rows = rows_of(at)
        y = columns_of(y_ref, at).astype(HALF)
        y_t_ref[rows, :] = y
        packed = dot_nn(y, att_w_ref[...])
        query_ref[rows, :] = (packed[:, :channels] * head_scale).astype(HALF)
        key_ref[rows, :] = packed[:, channels : 2 * channels].astype(HALF)
        value_ref[rows, :] = packed[:, 2 * channels : 3 * channels].astype(HALF)
        att_gate_ref[rows, :] = jax.nn.sigmoid(packed[:, 3 * channels :])
        spread = dot_nt(y, bias_rep_ref[...]).astype(HALF).astype(FULL)
        spread = spread.reshape(ROW_BLOCK, size, lanes) * same_cell[None]
        bias_ref[pl.ds(at * ROW_BLOCK, ROW_BLOCK), :] = jnp.sum(spread, axis=1)
        return carry

    lax.fori_loop(0, size // ROW_BLOCK, prepare, 0)


def attend_kernel(
    size,
    masks,
    near_ref,
    far_ref,
    lengths_ref,
    att_w_ref,
    att_out_w_ref,
    att_gate_ref,
    bias_ref,
    y_t_ref,
    query_ref,
    key_ref,
    value_ref,
    bias_rep_ref,
    cot_ref,
    grad_y_ref,
    grad_att_w_ref,
    grad_bias_ref,
    grad_att_out_ref,
    gain_part_ref,
    grad_gated_ref,
    cot_t_ref,
    grad_att_ref,
    gated_ref,
    grad_packed_ref,
    bias_grad_ref,
):
    channels = cot_ref.shape[1]
    block = ROW_BLOCK * size
    blocks = size // ROW_BLOCK
    lanes = HEADS * size
    head_scale = 1.0 / math.sqrt(HEAD_DIM)
    rows_of, columns_of = block_tools(size)
    same_cell = same_cell_of(size)
    valid = real_lanes(size, lengths_ref[0])
    place_rows(cot_ref, near_ref, far_ref, masks)

    def prepare(at, carry):
        rows = rows_of(at)
        cot = columns_of(cot_ref, at).astype(HALF)
        cot_t_ref[rows, :] = cot
        grad_gated = dot_nt(cot, att_out_w_ref[...])
        grad_gated_ref[rows, :] = grad_gated
        grad_att_ref[rows, :] = (grad_gated * att_gate_ref[rows, :]).astype(HALF)
        return carry

    lax.fori_loop(0, blocks, prepare, 0)

    head_mask = head_blocks(size, HEAD_DIM, HALF)
    head_mask_full = head_blocks(size, HEAD_DIM, FULL)
    key_ones = head_blocks(size, size, HALF)
    dim_ones = head_blocks(HEAD_DIM, size, HALF)

    def attend(at, score_sum):
        rows = rows_of(at)
        parts = [slice(a * size, (a + 1) * size) for a in range(ROW_BLOCK)]
        query, key, value, grad_att = (
            ref[rows, :] for ref in (query_ref, key_ref, value_ref, grad_att_ref)
        )
        keys = [jnp.concatenate([key[p]] * HEADS, axis=0) * head_mask for p in parts]
        values = [jnp.concatenate([value[p]] * HEADS, axis=0) * head_mask for p in parts]
        bias = bias_ref[...]
        scores = jnp.concatenate(
            [dot_nt(query[p], keys[a]) + bias for a, p in enumerate(parts)], axis=0
        )
        exp_scores = valid * jnp.exp(scores)
        attention = exp_scores / dot_wide(exp_scores, key_ones)
        attention_half = attention.astype(HALF)
        attended = jnp.concatenate(
            [dot_nn(attention_half[p], values[a]) for a, p in enumerate(parts)], axis=0
        )
        grad_attention = jnp.concatenate(
            [dot_nt(grad_att[p], values[a]) for a, p in enumerate(parts)], axis=0
        )
        row_dots = dot_wide(grad_att.astype(FULL) * attended, dim_ones)
        grad_scores = attention * (grad_attention - row_dots)
        scores_half = grad_scores.astype(HALF)
        for p in parts:
            score_sum = score_sum + grad_scores[p]
        grad_query = jnp.concatenate(
            [dot_nn(scores_half[p], keys[a]) for a, p in enumerate(parts)], axis=0
        )

        def per_key(weights, vectors):
            folded = []
            for p in parts:
                whole = dot_tn(weights[p], vectors[p]) * head_mask_full
                folded.append(sum(whole[h * size : (h + 1) * size] for h in range(HEADS)))
            return jnp.concatenate(folded, axis=0)

        grad_key = per_key(scores_half, query)
        grad_value = per_key(attention_half, grad_att)
        gate = att_gate_ref[rows, :]
        gated = gate * attended
        gated_ref[rows, :] = gated.astype(HALF)
        grad_gate_pre = grad_gated_ref[rows, :] * gated * (1.0 - gate)
        grad_packed = jnp.concatenate(
            [
                (grad_query * head_scale).astype(HALF),
                grad_key.astype(HALF),
                grad_value.astype(HALF),
                grad_gate_pre.astype(HALF),
            ],
            axis=1,
        )
        grad_packed_ref[rows, : 4 * channels] = grad_packed
        grad_y_ref[rows, :] = dot_nt(grad_packed, att_w_ref[...])
        return score_sum

    score_sum = lax.fori_loop(0, blocks, attend, jnp.zeros((size, lanes), FULL))
    bias_grad_ref[...] = score_sum.astype(HALF).astype(FULL)

    def spread_bias(at, carry):
        rows = rows_of(at)
        part = bias_grad_ref[pl.ds(at * ROW_BLOCK, ROW_BLOCK), :]
        spread = (part[:, None, :] * same_cell[None]).reshape(block, lanes).astype(HALF)
        grad_packed_ref[rows, 4 * channels :] = spread
        grad_y_ref[rows, :] += dot_nn(spread, bias_rep_ref[...])
        return carry

    lax.fori_loop(0, blocks, spread_bias, 0)

    inverse = 1.0 / size
    y_sum = dot_tn(y_t_ref[...], grad_packed_ref[...]) * inverse
    att_sum, bias_sum = y_sum[:, : 4 * channels], jnp.transpose(y_sum[:, 4 * channels :])
    grad_att_w_ref[...] = att_sum
    grad_att_out_ref[...] = dot_tn(gated_ref[...], cot_t_ref[...]) * inverse
    for h in range(HEADS):
        grad_bias_ref[h : h + 1, :] = jnp.sum(
            bias_sum[h * size : (h + 1) * size], axis=0, keepdims=True
        )
    bias_part = jnp.sum(bias_rep_ref[...].astype(FULL) * bias_sum, axis=0, keepdims=True)
    gain_part_ref[...] = gain_sum(((att_w_ref[...], att_sum),)) + bias_part


def gain_sum(pairs):
    total = sum(jnp.sum(weight.astype(FULL) * grad, axis=1, keepdims=True) for weight, grad in pairs)
    channels = total.shape[0]
    return jnp.transpose(jnp.broadcast_to(total, (channels, channels)))[0:1, :]


def edges_kernel(
    size,
    devices,
    pair_ref,
    gains_ref,
    edge_w_ref,
    gate_w_ref,
    out_w_ref,
    left_ref,
    right_ref,
    left_a_ref,
    left_b_ref,
    right_a_ref,
    right_b_ref,
    gate_ref,
    hat_mid_ref,
    scale_mid_ref,
    edge_out_ref,
    hat_y_ref,
    scale_y_ref,
    x_half_ref,
    update_ref,
    cot_ref,
    grad_y_ref,
    gain_part_ref,
    grad_pair_ref,
    grad_gains_ref,
    grad_edge_ref,
    grad_gate_w_ref,
    grad_out_w_ref,
    grad_middle_ref,
    grad_product_ref,
    grad_edge_out_ref,
    grad_proj_ref,
):
    channels = gains_ref.shape[1]
    blocks = size // ROW_BLOCK
    rows_of, columns_of = block_tools(size)
    gain_x = gains_ref[0:1, :]
    gain_mid = gains_ref[1:2, :]
    gain_y = gains_ref[2:3, :]

    def middle_back(at, carry):
        rows = rows_of(at)
        grad_y = columns_of(grad_y_ref, at)
        grad_middle = cot_ref[rows, :] + norm_back(
            grad_y, hat_y_ref[rows, :], scale_y_ref[rows, :], gain_y
        )
        grad_middle_ref[rows, :] = grad_middle
        gate = gate_ref[rows, :]
        gated = grad_middle * gate
        grad_edge_out = gated.astype(HALF)
        grad_edge_out_ref[rows, :] = grad_edge_out
        grad_gate = gated * edge_out_ref[rows, :] * (1.0 - gate)
        grad_proj_ref[rows, 4 * channels :] = grad_gate.astype(HALF)
        grad_update = dot_nt(grad_edge_out, out_w_ref[...])
        grad_product = norm_back(grad_update, hat_mid_ref[rows, :], scale_mid_ref[rows, :], gain_mid)
        grad_product_ref[rows, :] = grad_product.astype(HALF).astype(FULL)
        return carry

    lax.fori_loop(0, blocks, middle_back, 0)

    def edges_back(at, carry):
        rows = rows_of(at)
        grad_left = outer_sum(size, at, grad_product_ref, 1, size, right_ref)
        grad_proj_ref[rows, :channels] = (grad_left * left_a_ref[rows, :]).astype(HALF)
        grad_proj_ref[rows, channels : 2 * channels] = (grad_left * left_b_ref[rows, :]).astype(HALF)
        grad_right = outer_sum(size, at, grad_product_ref, size, 1, left_ref)
        grad_proj_ref[rows, 2 * channels : 3 * channels] = (grad_right * right_a_ref[rows, :]).astype(HALF)
        grad_proj_ref[rows, 3 * channels : 4 * channels] = (grad_right * right_b_ref[rows, :]).astype(HALF)
        return carry

    lax.fori_loop(0, blocks, edges_back, 0)

    inverse = 1.0 / size
    x_sum = dot_tn(x_half_ref[...], grad_proj_ref[...]) * inverse
    edge_sum, gate_sum = x_sum[:, : 4 * channels], x_sum[:, 4 * channels :]
    grad_edge_ref[...] = edge_sum
    grad_gate_w_ref[...] = gate_sum
    out_sum = dot_tn(update_ref[...], grad_edge_out_ref[...]) * inverse
    grad_out_w_ref[...] = out_sum
    grad_gains_ref[0:1, :] = gain_sum(((edge_w_ref[...], edge_sum), (gate_w_ref[...], gate_sum))) / gain_x
    grad_gains_ref[1:2, :] = gain_sum(((out_w_ref[...], out_sum),)) / gain_mid
    grad_gains_ref[2:3, :] = gain_part_ref[...] / gain_y

    own_cells = size * size // devices
    own = pl.ds(pl.multiple_of(lax.axis_index("dap") * own_cells, own_cells), own_cells)
    hat, scale = norm_of(pair_ref[...].reshape(own_cells, channels).astype(FULL))
    grad_x = dot_nt(grad_proj_ref[own, : 4 * channels], edge_w_ref[...])
    grad_x = grad_x + dot_nt(grad_proj_ref[own, 4 * channels :], gate_w_ref[...])
    grad_pair = grad_middle_ref[own, :] + norm_back(grad_x, hat, scale, gain_x)
    grad_pair_ref[...] = grad_pair.astype(grad_pair_ref.dtype)


def norm_of(values):
    center = values - jnp.mean(values, axis=-1, keepdims=True)
    scale = lax.rsqrt(jnp.mean(center * center, axis=-1, keepdims=True) + epsilon)
    return center * scale, scale


def norm_back(grad_out, hat, scale, gain):
    scaled = grad_out * gain
    first_mean = jnp.mean(scaled, axis=-1, keepdims=True)
    second_mean = jnp.mean(scaled * hat, axis=-1, keepdims=True)
    return scale * (scaled - first_mean - hat * second_mean)


def bytes_of(arrays):
    return sum(math.prod(shape) * jnp.dtype(dtype).itemsize for shape, dtype in arrays)


def run_kernel(kernel, operands, outs, scratch, seconds, lengths_at=None):
    vmem = pl.BlockSpec(memory_space=pltpu.VMEM)
    in_specs = [vmem] * len(operands)
    if lengths_at is not None:
        in_specs[lengths_at] = pl.BlockSpec(memory_space=pltpu.SMEM)
    return pl.pallas_call(
        kernel,
        out_shape=[jax.ShapeDtypeStruct(*out) for out in outs],
        in_specs=in_specs,
        out_specs=[vmem] * len(outs),
        scratch_shapes=[pltpu.VMEM(*part) for part in scratch],
        compiler_params=pltpu.CompilerParams(vmem_limit_bytes=bytes_of(scratch) + VMEM_SLACK),
        cost_estimate=pl.CostEstimate(flops=0, bytes_accessed=int(seconds * 3.6e12), transcendentals=0),
    )(*operands)


def replicated_plan(
    axis_size,
    pair_map,
    cotangent,
    lengths,
    norm_gains,
    edge_weight,
    mult_gate_weight,
    mult_out_weight,
    attention_weight,
    bias_weight,
    attention_out_weight,
):
    _, size, channels = pair_map.shape
    cells, lanes = size * size, HEADS * size
    bits = axis_size.bit_length() - 1
    far_step = 1 << (bits - 1)
    near_steps = range(2, far_step, 2)

    def swapped(held, mask):
        return lax.ppermute(held, "dap", [(d, d ^ mask) for d in range(axis_size)])

    def joined(held, steps):
        return jnp.concatenate([held] + [swapped(held, step) for step in steps], axis=0)

    masks = [0, far_step]
    masks = masks + [mask ^ step for step in near_steps for mask in masks]
    pair_near = joined(pair_map[None], (far_step,))
    cot_near = joined(cotangent[None], (far_step,))
    pair_near = joined(pair_near, near_steps)
    pair_near, cot_near = lax.optimization_barrier((pair_near, cot_near))
    pair_far = swapped(pair_near, 1)
    cot_parts = [cot_near] + [swapped(cot_near, step) for step in near_steps]

    full, half = ((cells, channels), FULL), ((cells, channels), HALF)
    square, wide = ((channels, channels), FULL), ((channels, 4 * channels), FULL)
    *kept, y, x_half, update = run_kernel(
        functools.partial(multiply_kernel, size, masks),
        (pair_near, pair_far, lengths, norm_gains, edge_weight, mult_gate_weight, mult_out_weight),
        [full] * 13 + [half] * 2,
        [full] * 2,
        5e-6,
        2,
    )
    y, *cot_parts = lax.optimization_barrier((y, *cot_parts))
    cot_near = jnp.concatenate(cot_parts, axis=0)
    cot_far = swapped(cot_near, 1)
    projections = run_kernel(
        functools.partial(project_kernel, size),
        (y, attention_weight, bias_weight.T),
        [full, ((size, lanes), FULL)] + [half] * 4 + [((lanes, channels), HALF)],
        [],
        2e-6,
    )
    cot, grad_y, grad_att_w, grad_bias, grad_att_out, gain_part = run_kernel(
        functools.partial(attend_kernel, size, masks),
        (cot_near, cot_far, lengths, attention_weight, attention_out_weight, *projections),
        [full, full, wide, ((HEADS, channels), FULL), square, ((1, channels), FULL)],
        [full] + [half] * 3 + [((cells, 4 * channels + lanes), HALF), ((size, lanes), FULL)],
        7e-6,
        2,
    )
    grad_pair, grad_gains, grad_edge, grad_gate_w, grad_out_w = run_kernel(
        functools.partial(edges_kernel, size, axis_size),
        (pair_map, norm_gains, edge_weight, mult_gate_weight, mult_out_weight, *kept, x_half, update, cot, grad_y, gain_part),
        [((cells // axis_size, channels), HALF), ((3, channels), FULL), wide, square, square],
        [full] * 2 + [half] + [((cells, 5 * channels), HALF)],
        6e-6,
    )
    return (
        grad_pair.reshape(pair_map.shape),
        grad_gains,
        grad_edge,
        grad_gate_w,
        grad_out_w,
        grad_att_w,
        grad_bias.T,
        grad_att_out,
    )


def per_device(axis_size, pair_map, *rest):
    _, size, channels = pair_map.shape
    fits = size % ROW_BLOCK == 0 and 25 * bytes_of([((size, size, channels), FULL)]) <= VMEM_SHARE
    if fits and axis_size >= 8 and axis_size & (axis_size - 1) == 0:
        return replicated_plan(axis_size, pair_map, *rest)
    return distributed_plan(pair_map, *rest)


def solution(mesh):
    return jax.shard_map(
        functools.partial(per_device, mesh.shape["dap"]),
        mesh=mesh,
        in_specs=(
            P(("groups", "dap"), None, None),
            P(("groups", "dap"), None, None),
            P("groups"),
            P(),
            P(),
            P(),
            P(),
            P(),
            P(),
            P(),
        ),
        out_specs=(
            P(("groups", "dap"), None, None),
            P("groups", None),
            P("groups", None),
            P("groups", None),
            P("groups", None),
            P("groups", None),
            P("groups", None),
            P("groups", None),
        ),
        check_vma=False,
    )
```

```python
import functools
import math

import jax
import jax.numpy as jnp
from jax import lax
from jax.experimental import pallas as pl
from jax.experimental.pallas import tpu as pltpu
from jax.sharding import PartitionSpec as P

HEADS = 4
HEAD_DIM = 32


epsilon = 1e-05


def norm_forward(values, gain_row):
    center = values - jnp.mean(values, axis=-1, keepdims=True)
    inv_std = lax.rsqrt(jnp.mean(center * center, axis=-1, keepdims=True) + epsilon)
    normed = center * inv_std
    return (normed * gain_row, normed, inv_std)


def norm_backward(grad_out, normed, inv_std, gain_row):
    scaled = grad_out * gain_row
    first_mean = jnp.mean(scaled, axis=-1, keepdims=True)
    second_mean = jnp.mean(scaled * normed, axis=-1, keepdims=True)
    return inv_std * (scaled - first_mean - normed * second_mean)


def distributed_plan(
    pair_map,
    cotangent,
    lengths,
    norm_gains,
    edge_weight,
    mult_gate_weight,
    mult_out_weight,
    attention_weight,
    bias_weight,
    attention_out_weight,
):
    row_count, full_size, channels = pair_map.shape
    inner_width = HEADS * HEAD_DIM
    head_scale = 1.0 / math.sqrt(HEAD_DIM)
    first_row = lax.axis_index("dap") * row_count
    real_count = lengths[0]
    valid_all = (jnp.arange(full_size) < real_count).astype(jnp.float32)
    valid_rows = (first_row + jnp.arange(row_count) < real_count).astype(jnp.float32)
    mask_pair = (valid_rows[:, None] * valid_all[None, :])[:, :, None]
    pair_f32 = pair_map.astype(jnp.float32)
    normed_full, hat_in, scale_in = norm_forward(pair_f32, norm_gains[0])
    normed_x = normed_full.astype(jnp.bfloat16)
    projected = jnp.einsum("rnc,cf->rnf", normed_x, edge_weight, preferred_element_type=jnp.float32)
    left_gate = projected[..., :channels]
    left_value = projected[..., channels : 2 * channels]
    right_gate = projected[..., 2 * channels : 3 * channels]
    right_value = projected[..., 3 * channels :]
    left_sig = jax.nn.sigmoid(left_gate)
    right_sig = jax.nn.sigmoid(right_gate)
    left_edges = (mask_pair * left_sig * left_value).astype(jnp.bfloat16)
    right_edges = (mask_pair * right_sig * right_value).astype(jnp.bfloat16)
    product = jnp.einsum(
        "ikc,jkc->ijc",
        left_edges,
        lax.all_gather(right_edges, "dap", axis=0, tiled=True),
        preferred_element_type=jnp.float32,
    )
    update_full, hat_mid, scale_mid = norm_forward(product, norm_gains[1])
    update = update_full.astype(jnp.bfloat16)
    edge_out = jnp.einsum(
        "rnc,cf->rnf", update, mult_out_weight, preferred_element_type=jnp.float32
    )
    gate_sig = jax.nn.sigmoid(
        jnp.einsum("rnc,cf->rnf", normed_x, mult_gate_weight, preferred_element_type=jnp.float32)
    )
    middle = pair_f32 + gate_sig * edge_out
    normed_mid, hat_attn, scale_attn = norm_forward(middle, norm_gains[2])
    normed_y = normed_mid.astype(jnp.bfloat16)
    bias_local = jnp.einsum(
        "kic,ch->hki", normed_y, bias_weight, preferred_element_type=jnp.float32
    ).astype(jnp.bfloat16)
    bias_whole = lax.all_gather(bias_local, "dap", axis=1, tiled=True)
    bias_query = jnp.swapaxes(bias_whole, 1, 2).astype(jnp.float32)
    column_y, column_cot = (
        lax.all_to_all(normed_y, "dap", split_axis=1, concat_axis=0, tiled=True),
        lax.all_to_all(cotangent, "dap", split_axis=1, concat_axis=0, tiled=True),
    )
    packed = jnp.einsum(
        "ijc,cf->ijf", column_y, attention_weight, preferred_element_type=jnp.float32
    )
    packed = packed.reshape(full_size, row_count, 4, HEADS, HEAD_DIM)
    query_vectors = (packed[:, :, 0] * head_scale).astype(jnp.bfloat16)
    key_vectors = packed[:, :, 1].astype(jnp.bfloat16)
    value_vectors = packed[:, :, 2].astype(jnp.bfloat16)
    att_gate = jax.nn.sigmoid(packed[:, :, 3])
    scores = (
        jnp.einsum(
            "ijhd,kjhd->jhik", query_vectors, key_vectors, preferred_element_type=jnp.float32
        )
        + bias_query[None]
    )
    exp_scores = valid_all * jnp.exp(scores)
    attention = exp_scores / jnp.sum(exp_scores, axis=-1, keepdims=True)
    attention_half = attention.astype(jnp.bfloat16)
    attended = jnp.einsum(
        "jhik,kjhd->ijhd", attention_half, value_vectors, preferred_element_type=jnp.float32
    )
    gated = (att_gate * attended).astype(jnp.bfloat16).reshape(full_size, row_count, inner_width)
    part_attn_out = jnp.einsum("ijf,ijc->fc", gated, column_cot, preferred_element_type=jnp.float32)
    grad_gated = jnp.einsum(
        "ijc,fc->ijf", column_cot, attention_out_weight, preferred_element_type=jnp.float32
    )
    grad_gated = grad_gated.reshape(full_size, row_count, HEADS, HEAD_DIM)
    grad_att = (grad_gated * att_gate).astype(jnp.bfloat16)
    grad_gate_pre = grad_gated * attended * att_gate * (1.0 - att_gate)
    grad_attention = jnp.einsum(
        "ijhd,kjhd->jhik", grad_att, value_vectors, preferred_element_type=jnp.float32
    )
    row_dots = jnp.transpose(jnp.sum(grad_att.astype(jnp.float32) * attended, axis=-1), (1, 2, 0))
    grad_scores = attention * (grad_attention - row_dots[..., None])
    scores_half = grad_scores.astype(jnp.bfloat16)
    grad_query = jnp.einsum(
        "jhik,kjhd->ijhd", scores_half, key_vectors, preferred_element_type=jnp.float32
    )
    grad_key = jnp.einsum(
        "jhik,ijhd->kjhd", scores_half, query_vectors, preferred_element_type=jnp.float32
    )
    grad_value = jnp.einsum(
        "jhik,ijhd->kjhd", attention_half, grad_att, preferred_element_type=jnp.float32
    )
    grad_packed = jnp.stack([grad_query * head_scale, grad_key, grad_value, grad_gate_pre], axis=2)
    grad_packed = grad_packed.reshape(full_size, row_count, 4 * inner_width).astype(jnp.bfloat16)
    part_attention = jnp.einsum(
        "ijc,ijf->cf", column_y, grad_packed, preferred_element_type=jnp.float32
    )
    column_grad = jnp.einsum(
        "ijf,cf->ijc", grad_packed, attention_weight, preferred_element_type=jnp.float32
    ).astype(jnp.bfloat16)
    row_grad = lax.all_to_all(column_grad, "dap", split_axis=0, concat_axis=1, tiled=True)
    score_sums = jnp.sum(grad_scores, axis=0)
    taken = score_sums
    bias_half = lax.psum_scatter(
        jnp.transpose(taken, (2, 0, 1)), "dap", scatter_dimension=0, tiled=True
    ).astype(jnp.bfloat16)
    part_bias = jnp.einsum("kic,khi->ch", normed_y, bias_half, preferred_element_type=jnp.float32)
    grad_normed_y = row_grad.astype(jnp.float32) + jnp.einsum(
        "khi,ch->kic", bias_half, bias_weight, preferred_element_type=jnp.float32
    )
    part_gain_attn = jnp.sum(grad_normed_y * hat_attn, axis=(0, 1))
    grad_middle = cotangent.astype(jnp.float32) + norm_backward(
        grad_normed_y, hat_attn, scale_attn, norm_gains[2]
    )
    grad_edge_out = (grad_middle * gate_sig).astype(jnp.bfloat16)
    grad_gate = (grad_middle * edge_out * gate_sig * (1.0 - gate_sig)).astype(jnp.bfloat16)
    part_mult_out = jnp.einsum(
        "rnc,rnf->cf", update, grad_edge_out, preferred_element_type=jnp.float32
    )
    part_mult_gate = jnp.einsum(
        "rnc,rnf->cf", normed_x, grad_gate, preferred_element_type=jnp.float32
    )
    grad_update = jnp.einsum(
        "rnf,cf->rnc", grad_edge_out, mult_out_weight, preferred_element_type=jnp.float32
    )
    part_gain_mid = jnp.sum(grad_update * hat_mid, axis=(0, 1))
    grad_product = norm_backward(grad_update, hat_mid, scale_mid, norm_gains[1]).astype(
        jnp.bfloat16
    )
    taken = grad_product
    grad_left = jnp.einsum(
        "ijc,jkc->ikc",
        taken,
        lax.all_gather(right_edges, "dap", axis=0, tiled=True),
        preferred_element_type=jnp.float32,
    )
    grad_cols = lax.all_to_all(grad_product, "dap", split_axis=1, concat_axis=0, tiled=True)
    taken = grad_cols
    grad_right = jnp.einsum(
        "ijc,ikc->jkc",
        taken,
        lax.all_gather(left_edges, "dap", axis=0, tiled=True),
        preferred_element_type=jnp.float32,
    )
    grad_proj = jnp.concatenate(
        [
            grad_left * mask_pair * left_value * left_sig * (1.0 - left_sig),
            grad_left * mask_pair * left_sig,
            grad_right * mask_pair * right_value * right_sig * (1.0 - right_sig),
            grad_right * mask_pair * right_sig,
        ],
        axis=-1,
    ).astype(jnp.bfloat16)
    part_edge = jnp.einsum("rnc,rnf->cf", normed_x, grad_proj, preferred_element_type=jnp.float32)
    grad_normed_x = jnp.einsum(
        "rnf,cf->rnc", grad_proj, edge_weight, preferred_element_type=jnp.float32
    )
    grad_normed_x = grad_normed_x + jnp.einsum(
        "rnf,cf->rnc", grad_gate, mult_gate_weight, preferred_element_type=jnp.float32
    )
    part_gain_in = jnp.sum(grad_normed_x * hat_in, axis=(0, 1))
    grad_pair = (
        grad_middle + norm_backward(grad_normed_x, hat_in, scale_in, norm_gains[0])
    ).astype(jnp.bfloat16)
    totals = lax.psum(
        (
            part_gain_in,
            part_gain_mid,
            part_edge,
            part_mult_gate,
            part_mult_out,
            part_gain_attn,
            part_attention,
            part_bias,
            part_attn_out,
        ),
        "dap",
    )
    (
        gain_in_sum,
        gain_mid_sum,
        edge_sum,
        mult_gate_sum,
        mult_out_sum,
        gain_attn_sum,
        attention_sum,
        bias_sum,
        attn_out_sum,
    ) = totals
    inverse = 1.0 / full_size
    grad_gains = jnp.stack([gain_in_sum, gain_mid_sum, gain_attn_sum]) * inverse
    return (
        grad_pair,
        grad_gains,
        edge_sum * inverse,
        mult_gate_sum * inverse,
        mult_out_sum * inverse,
        attention_sum * inverse,
        bias_sum * inverse,
        attn_out_sum * inverse,
    )


ROW_BLOCK = 8
VMEM_SLACK = 8 * 2**20
VMEM_SHARE = 32 * 2**20
HALF = jnp.bfloat16
FULL = jnp.float32


def dot_nn(left, right):
    return lax.dot_general(left, right, (((1,), (0,)), ((), ())), preferred_element_type=FULL)


def dot_nt(left, right):
    return lax.dot_general(left, right, (((1,), (1,)), ((), ())), preferred_element_type=FULL)


def dot_tn(left, right):
    return lax.dot_general(left, right, (((0,), (0,)), ((), ())), preferred_element_type=FULL)


def dot_wide(values, ones):
    high = values.astype(HALF)
    low = (values - high.astype(FULL)).astype(HALF)
    return dot_nn(jnp.concatenate([high, low], axis=1), jnp.concatenate([ones, ones], axis=0))


def lane_mean(values):
    channels = values.shape[1]
    return dot_wide(values, jnp.ones((channels, channels), HALF)) * (1.0 / channels)


def sigmoid(values):
    return pltpu.reciprocal(1.0 + jnp.exp(-values), approx=True)


def head_blocks(row_width, col_width, dtype):
    shape = (HEADS * row_width, HEADS * col_width)
    row = lax.broadcasted_iota(jnp.int32, shape, 0)
    col = lax.broadcasted_iota(jnp.int32, shape, 1)
    same = None
    for h in range(HEADS):
        here = (row >= h * row_width) & (row < (h + 1) * row_width)
        here = here & (col >= h * col_width) & (col < (h + 1) * col_width)
        same = here if same is None else same | here
    return jnp.where(same, 1.0, 0.0).astype(dtype)


def place_rows(target, part, near_ref, far_ref, masks):
    me = lax.axis_index("dap")
    cells = target.shape[0] // (2 * len(masks))
    for other, blocks in enumerate((near_ref, far_ref)):
        for at, mask in enumerate(masks):
            place = pl.ds(pl.multiple_of((me ^ mask ^ other) * cells, cells), cells)
            target[place, :] = blocks[at, part].reshape(cells, target.shape[1]).astype(FULL)


def block_tools(size):
    block = ROW_BLOCK * size

    def rows_of(at):
        return pl.ds(pl.multiple_of(at * block, block), block)

    def columns_of(ref, at):
        return jnp.concatenate(
            [ref[pl.ds(at * ROW_BLOCK + a, size, stride=size), :] for a in range(ROW_BLOCK)], axis=0
        )

    return rows_of, columns_of


def outer_sum(size, at, row_ref, row_stride, block_stride, block_ref):
    sums = [jnp.zeros((size, block_ref.shape[1]), FULL)] * ROW_BLOCK
    for k in range(size):
        whole = block_ref[k * size : (k + 1) * size, :]
        for a in range(ROW_BLOCK):
            row = (at * ROW_BLOCK + a) * block_stride + k * row_stride
            sums[a] = sums[a] + row_ref[pl.ds(row, 1), :] * whole
    return jnp.concatenate(sums, axis=0)


def same_cell_of(size):
    row = lax.broadcasted_iota(jnp.int32, (size, HEADS * size), 0)
    lane = lax.broadcasted_iota(jnp.int32, (size, HEADS * size), 1)
    same = lane == row
    for h in range(1, HEADS):
        same = same | (lane == row + h * size)
    return jnp.where(same, 1.0, 0.0)


def real_lanes(size, real):
    lane = lax.broadcasted_iota(jnp.int32, (1, HEADS * size), 1)
    inside = lane < real
    for h in range(1, HEADS):
        inside = inside | ((lane >= h * size) & (lane < h * size + real))
    return jnp.where(inside, 1.0, 0.0)


def spread_bias_weight(target, bias_w_ref, size):
    bias_rows = bias_w_ref[...].astype(FULL)
    for h in range(HEADS):
        target[h * size : (h + 1) * size, :] = jnp.broadcast_to(
            bias_rows[h : h + 1], (size, bias_rows.shape[1])
        ).astype(HALF)


def multiply_kernel(
    size,
    masks,
    near_ref,
    far_ref,
    lengths_ref,
    gains_ref,
    edge_w_ref,
    gate_w_ref,
    out_w_ref,
    left_ref,
    right_ref,
    left_a_ref,
    left_b_ref,
    right_a_ref,
    right_b_ref,
    gate_ref,
    hat_mid_ref,
    scale_mid_ref,
    edge_out_ref,
    hat_y_ref,
    scale_y_ref,
    y_ref,
    x_half_ref,
    update_ref,
    pair_ref,
    right_t_ref,
):
    channels = gains_ref.shape[1]
    block = ROW_BLOCK * size
    blocks = size // ROW_BLOCK
    rows_of, columns_of = block_tools(size)
    real = lengths_ref[0]
    gain_x = gains_ref[0:1, :]
    gain_mid = gains_ref[1:2, :]
    gain_y = gains_ref[2:3, :]
    place_rows(pair_ref, 0, near_ref, far_ref, masks)

    def project(at, carry):
        rows = rows_of(at)
        hat, _ = kernel_norm(pair_ref[rows, :])
        normed = (hat * gain_x).astype(HALF)
        x_half_ref[rows, :] = normed
        projected = dot_nn(normed, edge_w_ref[...])
        gate_ref[rows, :] = sigmoid(dot_nn(normed, gate_w_ref[...]))
        shape = (ROW_BLOCK, size, channels)
        row = lax.broadcasted_iota(jnp.int32, shape, 0) + at * ROW_BLOCK
        col = lax.broadcasted_iota(jnp.int32, shape, 1)
        mask = jnp.where((row < real) & (col < real), 1.0, 0.0).reshape(block, channels)
        for side, (edge, first, second) in enumerate(
            ((left_ref, left_a_ref, left_b_ref), (right_ref, right_a_ref, right_b_ref))
        ):
            base = 2 * side * channels
            sig = sigmoid(projected[:, base : base + channels])
            value = projected[:, base + channels : base + 2 * channels]
            masked = mask * sig
            product = masked * value
            edge[rows, :] = product.astype(HALF).astype(FULL)
            first[rows, :] = product * (1.0 - sig)
            second[rows, :] = masked
        return carry

    lax.fori_loop(0, blocks, project, 0)

    def turn(at, carry):
        right_t_ref[rows_of(at), :] = columns_of(right_ref, at)
        return carry

    lax.fori_loop(0, blocks, turn, 0)

    def multiply(at, carry):
        rows = rows_of(at)
        product = outer_sum(size, at, left_ref, 1, size, right_t_ref)
        hat, scale = kernel_norm(product)
        hat_mid_ref[rows, :] = hat
        scale_mid_ref[rows, :] = scale
        update = (hat * gain_mid).astype(HALF)
        update_ref[rows, :] = update
        edge_out = dot_nn(update, out_w_ref[...])
        edge_out_ref[rows, :] = edge_out
        middle = pair_ref[rows, :] + gate_ref[rows, :] * edge_out
        hat, scale = kernel_norm(middle)
        hat_y_ref[rows, :] = hat
        scale_y_ref[rows, :] = scale
        y_ref[rows, :] = hat * gain_y
        return carry

    lax.fori_loop(0, blocks, multiply, 0)


def project_kernel(
    size,
    y_ref,
    att_w_ref,
    bias_w_ref,
    att_gate_ref,
    bias_ref,
    y_t_ref,
    query_ref,
    key_ref,
    value_ref,
    bias_rep_ref,
):
    channels = y_ref.shape[1]
    lanes = HEADS * size
    head_scale = 1.0 / math.sqrt(HEAD_DIM)
    rows_of, columns_of = block_tools(size)
    same_cell = same_cell_of(size)
    spread_bias_weight(bias_rep_ref, bias_w_ref, size)

    def prepare(at, carry):
        rows = rows_of(at)
        y = columns_of(y_ref, at).astype(HALF)
        y_t_ref[rows, :] = y
        packed = dot_nn(y, att_w_ref[...])
        query_ref[rows, :] = (packed[:, :channels] * head_scale).astype(HALF)
        key_ref[rows, :] = packed[:, channels : 2 * channels].astype(HALF)
        value_ref[rows, :] = packed[:, 2 * channels : 3 * channels].astype(HALF)
        att_gate_ref[rows, :] = sigmoid(packed[:, 3 * channels :])
        spread = dot_nt(y, bias_rep_ref[...]).astype(HALF).astype(FULL)
        spread = spread.reshape(ROW_BLOCK, size, lanes) * same_cell[None]
        bias_ref[pl.ds(at * ROW_BLOCK, ROW_BLOCK), :] = jnp.sum(spread, axis=1)
        return carry

    lax.fori_loop(0, size // ROW_BLOCK, prepare, 0)


def attend_kernel(
    size,
    masks,
    near_ref,
    far_ref,
    lengths_ref,
    att_w_ref,
    att_out_w_ref,
    att_gate_ref,
    bias_ref,
    y_t_ref,
    query_ref,
    key_ref,
    value_ref,
    bias_rep_ref,
    cot_ref,
    grad_y_ref,
    grad_att_w_ref,
    grad_bias_ref,
    grad_att_out_ref,
    gain_part_ref,
    grad_gated_ref,
    cot_t_ref,
    grad_att_ref,
    gated_ref,
    grad_packed_ref,
    bias_grad_ref,
):
    channels = cot_ref.shape[1]
    block = ROW_BLOCK * size
    blocks = size // ROW_BLOCK
    lanes = HEADS * size
    head_scale = 1.0 / math.sqrt(HEAD_DIM)
    rows_of, columns_of = block_tools(size)
    same_cell = same_cell_of(size)
    valid = real_lanes(size, lengths_ref[0])
    place_rows(cot_ref, 1, near_ref, far_ref, masks)

    def prepare(at, carry):
        rows = rows_of(at)
        cot = columns_of(cot_ref, at).astype(HALF)
        cot_t_ref[rows, :] = cot
        grad_gated = dot_nt(cot, att_out_w_ref[...])
        grad_gated_ref[rows, :] = grad_gated
        grad_att_ref[rows, :] = (grad_gated * att_gate_ref[rows, :]).astype(HALF)
        return carry

    lax.fori_loop(0, blocks, prepare, 0)

    head_mask = head_blocks(size, HEAD_DIM, HALF)
    head_mask_full = head_blocks(size, HEAD_DIM, FULL)
    key_ones = head_blocks(size, size, HALF)
    dim_ones = head_blocks(HEAD_DIM, size, HALF)

    def attend(at, score_sum):
        rows = rows_of(at)
        parts = [slice(a * size, (a + 1) * size) for a in range(ROW_BLOCK)]
        query, key, value, grad_att = (
            ref[rows, :] for ref in (query_ref, key_ref, value_ref, grad_att_ref)
        )
        keys = [jnp.concatenate([key[p]] * HEADS, axis=0) * head_mask for p in parts]
        values = [jnp.concatenate([value[p]] * HEADS, axis=0) * head_mask for p in parts]
        bias = bias_ref[...]
        scores = jnp.concatenate(
            [dot_nt(query[p], keys[a]) + bias for a, p in enumerate(parts)], axis=0
        )
        exp_scores = valid * jnp.exp(scores)
        attention = exp_scores / dot_wide(exp_scores, key_ones)
        attention_half = attention.astype(HALF)
        attended = jnp.concatenate(
            [dot_nn(attention_half[p], values[a]) for a, p in enumerate(parts)], axis=0
        )
        grad_attention = jnp.concatenate(
            [dot_nt(grad_att[p], values[a]) for a, p in enumerate(parts)], axis=0
        )
        row_dots = dot_wide(grad_att.astype(FULL) * attended, dim_ones)
        grad_scores = attention * (grad_attention - row_dots)
        scores_half = grad_scores.astype(HALF)
        for p in parts:
            score_sum = score_sum + grad_scores[p]
        grad_query = jnp.concatenate(
            [dot_nn(scores_half[p], keys[a]) for a, p in enumerate(parts)], axis=0
        )

        def per_key(weights, vectors):
            folded = []
            for p in parts:
                whole = dot_tn(weights[p], vectors[p]) * head_mask_full
                folded.append(sum(whole[h * size : (h + 1) * size] for h in range(HEADS)))
            return jnp.concatenate(folded, axis=0)

        grad_key = per_key(scores_half, query)
        grad_value = per_key(attention_half, grad_att)
        gate = att_gate_ref[rows, :]
        gated = gate * attended
        gated_ref[rows, :] = gated.astype(HALF)
        grad_gate_pre = grad_gated_ref[rows, :] * gated * (1.0 - gate)
        grad_packed = jnp.concatenate(
            [
                (grad_query * head_scale).astype(HALF),
                grad_key.astype(HALF),
                grad_value.astype(HALF),
                grad_gate_pre.astype(HALF),
            ],
            axis=1,
        )
        grad_packed_ref[rows, : 4 * channels] = grad_packed
        grad_y_ref[rows, :] = dot_nt(grad_packed, att_w_ref[...])
        return score_sum

    score_sum = lax.fori_loop(0, blocks, attend, jnp.zeros((size, lanes), FULL), unroll=2)
    bias_grad_ref[...] = score_sum.astype(HALF).astype(FULL)

    def spread_bias(at, carry):
        rows = rows_of(at)
        part = bias_grad_ref[pl.ds(at * ROW_BLOCK, ROW_BLOCK), :]
        spread = (part[:, None, :] * same_cell[None]).reshape(block, lanes).astype(HALF)
        grad_packed_ref[rows, 4 * channels :] = spread
        grad_y_ref[rows, :] += dot_nn(spread, bias_rep_ref[...])
        return carry

    lax.fori_loop(0, blocks, spread_bias, 0)

    inverse = 1.0 / size
    y_sum = dot_tn(y_t_ref[...], grad_packed_ref[...]) * inverse
    att_sum, bias_sum = y_sum[:, : 4 * channels], jnp.transpose(y_sum[:, 4 * channels :])
    grad_att_w_ref[...] = att_sum
    grad_att_out_ref[...] = dot_tn(gated_ref[...], cot_t_ref[...]) * inverse
    for h in range(HEADS):
        grad_bias_ref[h : h + 1, :] = jnp.sum(
            bias_sum[h * size : (h + 1) * size], axis=0, keepdims=True
        )
    bias_part = jnp.sum(bias_rep_ref[...].astype(FULL) * bias_sum, axis=0, keepdims=True)
    gain_part_ref[...] = gain_sum(((att_w_ref[...], att_sum),)) + bias_part


def gain_sum(pairs):
    total = sum(jnp.sum(weight.astype(FULL) * grad, axis=1, keepdims=True) for weight, grad in pairs)
    channels = total.shape[0]
    return jnp.transpose(jnp.broadcast_to(total, (channels, channels)))[0:1, :]


def edges_kernel(
    size,
    devices,
    pair_ref,
    gains_ref,
    edge_w_ref,
    gate_w_ref,
    out_w_ref,
    left_ref,
    right_ref,
    left_a_ref,
    left_b_ref,
    right_a_ref,
    right_b_ref,
    gate_ref,
    hat_mid_ref,
    scale_mid_ref,
    edge_out_ref,
    hat_y_ref,
    scale_y_ref,
    x_half_ref,
    update_ref,
    cot_ref,
    grad_y_ref,
    gain_part_ref,
    grad_pair_ref,
    grad_gains_ref,
    grad_edge_ref,
    grad_gate_w_ref,
    grad_out_w_ref,
    grad_middle_ref,
    grad_product_ref,
    grad_proj_ref,
    x_sum_ref,
    out_sum_ref,
):
    channels = gains_ref.shape[1]
    blocks = size // ROW_BLOCK
    rows_of, columns_of = block_tools(size)
    gain_x = gains_ref[0:1, :]
    gain_mid = gains_ref[1:2, :]
    gain_y = gains_ref[2:3, :]

    x_sum_ref[...] = jnp.zeros(x_sum_ref.shape, FULL)
    out_sum_ref[...] = jnp.zeros(out_sum_ref.shape, FULL)

    def middle_back(at, carry):
        rows = rows_of(at)
        grad_y = columns_of(grad_y_ref, at)
        grad_middle = cot_ref[rows, :] + kernel_norm_back(
            grad_y, hat_y_ref[rows, :], scale_y_ref[rows, :], gain_y
        )
        grad_middle_ref[rows, :] = grad_middle
        gate = gate_ref[rows, :]
        gated = grad_middle * gate
        grad_edge_out = gated.astype(HALF)
        grad_gate = (gated * edge_out_ref[rows, :] * (1.0 - gate)).astype(HALF)
        grad_proj_ref[rows, 4 * channels :] = grad_gate
        x_sum_ref[:, 4 * channels :] += dot_tn(x_half_ref[rows, :], grad_gate)
        out_sum_ref[...] += dot_tn(update_ref[rows, :], grad_edge_out)
        grad_update = dot_nt(grad_edge_out, out_w_ref[...])
        grad_product = kernel_norm_back(grad_update, hat_mid_ref[rows, :], scale_mid_ref[rows, :], gain_mid)
        grad_product_ref[rows, :] = grad_product.astype(HALF).astype(FULL)
        return carry

    lax.fori_loop(0, blocks, middle_back, 0)

    def edges_back(at, carry):
        rows = rows_of(at)
        x_half = x_half_ref[rows, :]
        for side, (first_ref, second_ref, strides, other_ref) in enumerate(
            (
                (left_a_ref, left_b_ref, (1, size), right_ref),
                (right_a_ref, right_b_ref, (size, 1), left_ref),
            )
        ):
            grad = outer_sum(size, at, grad_product_ref, *strides, other_ref)
            both = jnp.concatenate(
                [(grad * first_ref[rows, :]).astype(HALF), (grad * second_ref[rows, :]).astype(HALF)], axis=1
            )
            place = slice(2 * side * channels, 2 * (side + 1) * channels)
            grad_proj_ref[rows, place] = both
            x_sum_ref[:, place] += dot_tn(x_half, both)
        return carry

    lax.fori_loop(0, blocks, edges_back, 0)

    inverse = 1.0 / size
    x_sum = x_sum_ref[...] * inverse
    edge_sum, gate_sum = x_sum[:, : 4 * channels], x_sum[:, 4 * channels :]
    grad_edge_ref[...] = edge_sum
    grad_gate_w_ref[...] = gate_sum
    out_sum = out_sum_ref[...] * inverse
    grad_out_w_ref[...] = out_sum
    grad_gains_ref[0:1, :] = gain_sum(((edge_w_ref[...], edge_sum), (gate_w_ref[...], gate_sum))) / gain_x
    grad_gains_ref[1:2, :] = gain_sum(((out_w_ref[...], out_sum),)) / gain_mid
    grad_gains_ref[2:3, :] = gain_part_ref[...] / gain_y

    own_cells = size * size // devices
    own = pl.ds(pl.multiple_of(lax.axis_index("dap") * own_cells, own_cells), own_cells)
    hat, scale = kernel_norm(pair_ref[...].reshape(own_cells, channels).astype(FULL))
    grad_x = dot_nt(grad_proj_ref[own, : 4 * channels], edge_w_ref[...])
    grad_x = grad_x + dot_nt(grad_proj_ref[own, 4 * channels :], gate_w_ref[...])
    grad_pair = grad_middle_ref[own, :] + kernel_norm_back(grad_x, hat, scale, gain_x)
    grad_pair_ref[...] = grad_pair.astype(grad_pair_ref.dtype)


def kernel_norm(values):
    center = values - lane_mean(values)
    scale = lax.rsqrt(lane_mean(center * center) + epsilon)
    return center * scale, scale


def kernel_norm_back(grad_out, hat, scale, gain):
    scaled = grad_out * gain
    return scale * (scaled - lane_mean(scaled) - hat * lane_mean(scaled * hat))


def bytes_of(arrays):
    return sum(math.prod(shape) * jnp.dtype(dtype).itemsize for shape, dtype in arrays)


def run_kernel(kernel, operands, outs, scratch, seconds, lengths_at=None):
    vmem = pl.BlockSpec(memory_space=pltpu.VMEM)
    in_specs = [vmem] * len(operands)
    if lengths_at is not None:
        in_specs[lengths_at] = pl.BlockSpec(memory_space=pltpu.SMEM)
    return pl.pallas_call(
        kernel,
        out_shape=[jax.ShapeDtypeStruct(*out) for out in outs],
        in_specs=in_specs,
        out_specs=[vmem] * len(outs),
        scratch_shapes=[pltpu.VMEM(*part) for part in scratch],
        compiler_params=pltpu.CompilerParams(vmem_limit_bytes=bytes_of(scratch) + VMEM_SLACK),
        cost_estimate=pl.CostEstimate(flops=0, bytes_accessed=int(seconds * 3.6e12), transcendentals=0),
    )(*operands)


def replicated_plan(
    axis_size,
    pair_map,
    cotangent,
    lengths,
    norm_gains,
    edge_weight,
    mult_gate_weight,
    mult_out_weight,
    attention_weight,
    bias_weight,
    attention_out_weight,
):
    _, size, channels = pair_map.shape
    cells, lanes = size * size, HEADS * size
    bits = axis_size.bit_length() - 1
    far_step = 1 << (bits - 1)
    near_steps = range(2, far_step, 2)

    def swapped(held, mask):
        return lax.ppermute(held, "dap", [(d, d ^ mask) for d in range(axis_size)])

    held = jnp.stack(
        [jnp.stack([pair_map, cotangent]), jnp.stack([swapped(pair_map, far_step), swapped(cotangent, far_step)])]
    )
    masks = [0, far_step]
    near = jnp.concatenate([held] + [swapped(held, step) for step in near_steps], axis=0)
    masks = masks + [mask ^ step for step in near_steps for mask in masks]
    far = swapped(near, 1)

    full, half = ((cells, channels), FULL), ((cells, channels), HALF)
    square, wide = ((channels, channels), FULL), ((channels, 4 * channels), FULL)
    *kept, y, x_half, update = run_kernel(
        functools.partial(multiply_kernel, size, masks),
        (near, far, lengths, norm_gains, edge_weight, mult_gate_weight, mult_out_weight),
        [full] * 13 + [half] * 2,
        [full] * 2,
        5e-6,
        2,
    )
    projections = run_kernel(
        functools.partial(project_kernel, size),
        (y, attention_weight, bias_weight.T),
        [full, ((size, lanes), FULL)] + [half] * 4 + [((lanes, channels), HALF)],
        [],
        2e-6,
    )
    cot, grad_y, grad_att_w, grad_bias, grad_att_out, gain_part = run_kernel(
        functools.partial(attend_kernel, size, masks),
        (near, far, lengths, attention_weight, attention_out_weight, *projections),
        [full, full, wide, ((HEADS, channels), FULL), square, ((1, channels), FULL)],
        [full] + [half] * 3 + [((cells, 4 * channels + lanes), HALF), ((size, lanes), FULL)],
        7e-6,
        2,
    )
    grad_pair, grad_gains, grad_edge, grad_gate_w, grad_out_w = run_kernel(
        functools.partial(edges_kernel, size, axis_size),
        (pair_map, norm_gains, edge_weight, mult_gate_weight, mult_out_weight, *kept, x_half, update, cot, grad_y, gain_part),
        [((cells // axis_size, channels), HALF), ((3, channels), FULL), wide, square, square],
        [full] * 2 + [((cells, 5 * channels), HALF), ((channels, 5 * channels), FULL), square],
        6e-6,
    )
    return (
        grad_pair.reshape(pair_map.shape),
        grad_gains,
        grad_edge,
        grad_gate_w,
        grad_out_w,
        grad_att_w,
        grad_bias.T,
        grad_att_out,
    )


def per_device(axis_size, pair_map, *rest):
    _, size, channels = pair_map.shape
    fits = size % ROW_BLOCK == 0 and 25 * bytes_of([((size, size, channels), FULL)]) <= VMEM_SHARE
    if fits and axis_size >= 8 and axis_size & (axis_size - 1) == 0:
        return replicated_plan(axis_size, pair_map, *rest)
    return distributed_plan(pair_map, *rest)


def solution(mesh):
    return jax.shard_map(
        functools.partial(per_device, mesh.shape["dap"]),
        mesh=mesh,
        in_specs=(
            P(("groups", "dap"), None, None),
            P(("groups", "dap"), None, None),
            P("groups"),
            P(),
            P(),
            P(),
            P(),
            P(),
            P(),
            P(),
        ),
        out_specs=(
            P(("groups", "dap"), None, None),
            P("groups", None),
            P("groups", None),
            P("groups", None),
            P("groups", None),
            P("groups", None),
            P("groups", None),
            P("groups", None),
        ),
        check_vma=False,
    )
```

```python
import functools
import math

import jax
import jax.numpy as jnp
from jax import lax
from jax.experimental import pallas as pl
from jax.experimental.pallas import tpu as pltpu
from jax.sharding import PartitionSpec as P

HEADS = 4
HEAD_DIM = 32


epsilon = 1e-05


def norm_forward(values, gain_row):
    center = values - jnp.mean(values, axis=-1, keepdims=True)
    inv_std = lax.rsqrt(jnp.mean(center * center, axis=-1, keepdims=True) + epsilon)
    normed = center * inv_std
    return (normed * gain_row, normed, inv_std)


def norm_backward(grad_out, normed, inv_std, gain_row):
    scaled = grad_out * gain_row
    first_mean = jnp.mean(scaled, axis=-1, keepdims=True)
    second_mean = jnp.mean(scaled * normed, axis=-1, keepdims=True)
    return inv_std * (scaled - first_mean - normed * second_mean)


def distributed_plan(
    pair_map,
    cotangent,
    lengths,
    norm_gains,
    edge_weight,
    mult_gate_weight,
    mult_out_weight,
    attention_weight,
    bias_weight,
    attention_out_weight,
):
    row_count, full_size, channels = pair_map.shape
    inner_width = HEADS * HEAD_DIM
    head_scale = 1.0 / math.sqrt(HEAD_DIM)
    first_row = lax.axis_index("dap") * row_count
    real_count = lengths[0]
    valid_all = (jnp.arange(full_size) < real_count).astype(jnp.float32)
    valid_rows = (first_row + jnp.arange(row_count) < real_count).astype(jnp.float32)
    mask_pair = (valid_rows[:, None] * valid_all[None, :])[:, :, None]
    pair_f32 = pair_map.astype(jnp.float32)
    normed_full, hat_in, scale_in = norm_forward(pair_f32, norm_gains[0])
    normed_x = normed_full.astype(jnp.bfloat16)
    projected = jnp.einsum("rnc,cf->rnf", normed_x, edge_weight, preferred_element_type=jnp.float32)
    left_gate = projected[..., :channels]
    left_value = projected[..., channels : 2 * channels]
    right_gate = projected[..., 2 * channels : 3 * channels]
    right_value = projected[..., 3 * channels :]
    left_sig = jax.nn.sigmoid(left_gate)
    right_sig = jax.nn.sigmoid(right_gate)
    left_edges = (mask_pair * left_sig * left_value).astype(jnp.bfloat16)
    right_edges = (mask_pair * right_sig * right_value).astype(jnp.bfloat16)
    product = jnp.einsum(
        "ikc,jkc->ijc",
        left_edges,
        lax.all_gather(right_edges, "dap", axis=0, tiled=True),
        preferred_element_type=jnp.float32,
    )
    update_full, hat_mid, scale_mid = norm_forward(product, norm_gains[1])
    update = update_full.astype(jnp.bfloat16)
    edge_out = jnp.einsum(
        "rnc,cf->rnf", update, mult_out_weight, preferred_element_type=jnp.float32
    )
    gate_sig = jax.nn.sigmoid(
        jnp.einsum("rnc,cf->rnf", normed_x, mult_gate_weight, preferred_element_type=jnp.float32)
    )
    middle = pair_f32 + gate_sig * edge_out
    normed_mid, hat_attn, scale_attn = norm_forward(middle, norm_gains[2])
    normed_y = normed_mid.astype(jnp.bfloat16)
    bias_local = jnp.einsum(
        "kic,ch->hki", normed_y, bias_weight, preferred_element_type=jnp.float32
    ).astype(jnp.bfloat16)
    bias_whole = lax.all_gather(bias_local, "dap", axis=1, tiled=True)
    bias_query = jnp.swapaxes(bias_whole, 1, 2).astype(jnp.float32)
    column_y, column_cot = (
        lax.all_to_all(normed_y, "dap", split_axis=1, concat_axis=0, tiled=True),
        lax.all_to_all(cotangent, "dap", split_axis=1, concat_axis=0, tiled=True),
    )
    packed = jnp.einsum(
        "ijc,cf->ijf", column_y, attention_weight, preferred_element_type=jnp.float32
    )
    packed = packed.reshape(full_size, row_count, 4, HEADS, HEAD_DIM)
    query_vectors = (packed[:, :, 0] * head_scale).astype(jnp.bfloat16)
    key_vectors = packed[:, :, 1].astype(jnp.bfloat16)
    value_vectors = packed[:, :, 2].astype(jnp.bfloat16)
    att_gate = jax.nn.sigmoid(packed[:, :, 3])
    scores = (
        jnp.einsum(
            "ijhd,kjhd->jhik", query_vectors, key_vectors, preferred_element_type=jnp.float32
        )
        + bias_query[None]
    )
    exp_scores = valid_all * jnp.exp(scores)
    attention = exp_scores / jnp.sum(exp_scores, axis=-1, keepdims=True)
    attention_half = attention.astype(jnp.bfloat16)
    attended = jnp.einsum(
        "jhik,kjhd->ijhd", attention_half, value_vectors, preferred_element_type=jnp.float32
    )
    gated = (att_gate * attended).astype(jnp.bfloat16).reshape(full_size, row_count, inner_width)
    part_attn_out = jnp.einsum("ijf,ijc->fc", gated, column_cot, preferred_element_type=jnp.float32)
    grad_gated = jnp.einsum(
        "ijc,fc->ijf", column_cot, attention_out_weight, preferred_element_type=jnp.float32
    )
    grad_gated = grad_gated.reshape(full_size, row_count, HEADS, HEAD_DIM)
    grad_att = (grad_gated * att_gate).astype(jnp.bfloat16)
    grad_gate_pre = grad_gated * attended * att_gate * (1.0 - att_gate)
    grad_attention = jnp.einsum(
        "ijhd,kjhd->jhik", grad_att, value_vectors, preferred_element_type=jnp.float32
    )
    row_dots = jnp.transpose(jnp.sum(grad_att.astype(jnp.float32) * attended, axis=-1), (1, 2, 0))
    grad_scores = attention * (grad_attention - row_dots[..., None])
    scores_half = grad_scores.astype(jnp.bfloat16)
    grad_query = jnp.einsum(
        "jhik,kjhd->ijhd", scores_half, key_vectors, preferred_element_type=jnp.float32
    )
    grad_key = jnp.einsum(
        "jhik,ijhd->kjhd", scores_half, query_vectors, preferred_element_type=jnp.float32
    )
    grad_value = jnp.einsum(
        "jhik,ijhd->kjhd", attention_half, grad_att, preferred_element_type=jnp.float32
    )
    grad_packed = jnp.stack([grad_query * head_scale, grad_key, grad_value, grad_gate_pre], axis=2)
    grad_packed = grad_packed.reshape(full_size, row_count, 4 * inner_width).astype(jnp.bfloat16)
    part_attention = jnp.einsum(
        "ijc,ijf->cf", column_y, grad_packed, preferred_element_type=jnp.float32
    )
    column_grad = jnp.einsum(
        "ijf,cf->ijc", grad_packed, attention_weight, preferred_element_type=jnp.float32
    ).astype(jnp.bfloat16)
    row_grad = lax.all_to_all(column_grad, "dap", split_axis=0, concat_axis=1, tiled=True)
    score_sums = jnp.sum(grad_scores, axis=0)
    taken = score_sums
    bias_half = lax.psum_scatter(
        jnp.transpose(taken, (2, 0, 1)), "dap", scatter_dimension=0, tiled=True
    ).astype(jnp.bfloat16)
    part_bias = jnp.einsum("kic,khi->ch", normed_y, bias_half, preferred_element_type=jnp.float32)
    grad_normed_y = row_grad.astype(jnp.float32) + jnp.einsum(
        "khi,ch->kic", bias_half, bias_weight, preferred_element_type=jnp.float32
    )
    part_gain_attn = jnp.sum(grad_normed_y * hat_attn, axis=(0, 1))
    grad_middle = cotangent.astype(jnp.float32) + norm_backward(
        grad_normed_y, hat_attn, scale_attn, norm_gains[2]
    )
    grad_edge_out = (grad_middle * gate_sig).astype(jnp.bfloat16)
    grad_gate = (grad_middle * edge_out * gate_sig * (1.0 - gate_sig)).astype(jnp.bfloat16)
    part_mult_out = jnp.einsum(
        "rnc,rnf->cf", update, grad_edge_out, preferred_element_type=jnp.float32
    )
    part_mult_gate = jnp.einsum(
        "rnc,rnf->cf", normed_x, grad_gate, preferred_element_type=jnp.float32
    )
    grad_update = jnp.einsum(
        "rnf,cf->rnc", grad_edge_out, mult_out_weight, preferred_element_type=jnp.float32
    )
    part_gain_mid = jnp.sum(grad_update * hat_mid, axis=(0, 1))
    grad_product = norm_backward(grad_update, hat_mid, scale_mid, norm_gains[1]).astype(
        jnp.bfloat16
    )
    taken = grad_product
    grad_left = jnp.einsum(
        "ijc,jkc->ikc",
        taken,
        lax.all_gather(right_edges, "dap", axis=0, tiled=True),
        preferred_element_type=jnp.float32,
    )
    grad_cols = lax.all_to_all(grad_product, "dap", split_axis=1, concat_axis=0, tiled=True)
    taken = grad_cols
    grad_right = jnp.einsum(
        "ijc,ikc->jkc",
        taken,
        lax.all_gather(left_edges, "dap", axis=0, tiled=True),
        preferred_element_type=jnp.float32,
    )
    grad_proj = jnp.concatenate(
        [
            grad_left * mask_pair * left_value * left_sig * (1.0 - left_sig),
            grad_left * mask_pair * left_sig,
            grad_right * mask_pair * right_value * right_sig * (1.0 - right_sig),
            grad_right * mask_pair * right_sig,
        ],
        axis=-1,
    ).astype(jnp.bfloat16)
    part_edge = jnp.einsum("rnc,rnf->cf", normed_x, grad_proj, preferred_element_type=jnp.float32)
    grad_normed_x = jnp.einsum(
        "rnf,cf->rnc", grad_proj, edge_weight, preferred_element_type=jnp.float32
    )
    grad_normed_x = grad_normed_x + jnp.einsum(
        "rnf,cf->rnc", grad_gate, mult_gate_weight, preferred_element_type=jnp.float32
    )
    part_gain_in = jnp.sum(grad_normed_x * hat_in, axis=(0, 1))
    grad_pair = (
        grad_middle + norm_backward(grad_normed_x, hat_in, scale_in, norm_gains[0])
    ).astype(jnp.bfloat16)
    totals = lax.psum(
        (
            part_gain_in,
            part_gain_mid,
            part_edge,
            part_mult_gate,
            part_mult_out,
            part_gain_attn,
            part_attention,
            part_bias,
            part_attn_out,
        ),
        "dap",
    )
    (
        gain_in_sum,
        gain_mid_sum,
        edge_sum,
        mult_gate_sum,
        mult_out_sum,
        gain_attn_sum,
        attention_sum,
        bias_sum,
        attn_out_sum,
    ) = totals
    inverse = 1.0 / full_size
    grad_gains = jnp.stack([gain_in_sum, gain_mid_sum, gain_attn_sum]) * inverse
    return (
        grad_pair,
        grad_gains,
        edge_sum * inverse,
        mult_gate_sum * inverse,
        mult_out_sum * inverse,
        attention_sum * inverse,
        bias_sum * inverse,
        attn_out_sum * inverse,
    )


ROW_BLOCK = 8
VMEM_SLACK = 8 * 2**20
VMEM_SHARE = 32 * 2**20
HALF = jnp.bfloat16
FULL = jnp.float32


def dot_nn(left, right):
    return lax.dot_general(left, right, (((1,), (0,)), ((), ())), preferred_element_type=FULL)


def dot_nt(left, right):
    return lax.dot_general(left, right, (((1,), (1,)), ((), ())), preferred_element_type=FULL)


def dot_tn(left, right):
    return lax.dot_general(left, right, (((0,), (0,)), ((), ())), preferred_element_type=FULL)


def dot_wide(values, ones):
    high = values.astype(HALF)
    low = (values - high.astype(FULL)).astype(HALF)
    return dot_nn(jnp.concatenate([high, low], axis=1), jnp.concatenate([ones, ones], axis=0))


def lane_mean(values):
    return jnp.mean(values, axis=-1, keepdims=True)


def sigmoid(values):
    return pltpu.reciprocal(1.0 + jnp.exp(-values), approx=True)


def head_blocks(row_width, col_width, dtype):
    shape = (HEADS * row_width, HEADS * col_width)
    row = lax.broadcasted_iota(jnp.int32, shape, 0)
    col = lax.broadcasted_iota(jnp.int32, shape, 1)
    same = None
    for h in range(HEADS):
        here = (row >= h * row_width) & (row < (h + 1) * row_width)
        here = here & (col >= h * col_width) & (col < (h + 1) * col_width)
        same = here if same is None else same | here
    return jnp.where(same, 1.0, 0.0).astype(dtype)


def place_rows(target, part, near_ref, far_ref, masks):
    me = lax.axis_index("dap")
    cells = target.shape[0] // (2 * len(masks))
    for other, blocks in enumerate((near_ref, far_ref)):
        for at, mask in enumerate(masks):
            place = pl.ds(pl.multiple_of((me ^ mask ^ other) * cells, cells), cells)
            target[place, :] = blocks[at, part].reshape(cells, target.shape[1]).astype(FULL)


def block_tools(size):
    block = ROW_BLOCK * size

    def rows_of(at):
        return pl.ds(pl.multiple_of(at * block, block), block)

    def columns_of(ref, at):
        return jnp.concatenate(
            [ref[pl.ds(at * ROW_BLOCK + a, size, stride=size), :] for a in range(ROW_BLOCK)], axis=0
        )

    return rows_of, columns_of


def outer_sum(size, at, row_ref, row_stride, block_stride, block_ref):
    sums = [jnp.zeros((size, block_ref.shape[1]), FULL)] * ROW_BLOCK
    for k in range(size):
        whole = block_ref[k * size : (k + 1) * size, :]
        for a in range(ROW_BLOCK):
            row = (at * ROW_BLOCK + a) * block_stride + k * row_stride
            sums[a] = sums[a] + row_ref[pl.ds(row, 1), :] * whole
    return jnp.concatenate(sums, axis=0)


def same_cell_of(size):
    row = lax.broadcasted_iota(jnp.int32, (size, HEADS * size), 0)
    lane = lax.broadcasted_iota(jnp.int32, (size, HEADS * size), 1)
    same = lane == row
    for h in range(1, HEADS):
        same = same | (lane == row + h * size)
    return jnp.where(same, 1.0, 0.0)


def real_lanes(size, real):
    lane = lax.broadcasted_iota(jnp.int32, (1, HEADS * size), 1)
    inside = lane < real
    for h in range(1, HEADS):
        inside = inside | ((lane >= h * size) & (lane < h * size + real))
    return jnp.where(inside, 1.0, 0.0)


def spread_bias_weight(target, bias_w_ref, size):
    bias_rows = bias_w_ref[...].astype(FULL)
    for h in range(HEADS):
        target[h * size : (h + 1) * size, :] = jnp.broadcast_to(
            bias_rows[h : h + 1], (size, bias_rows.shape[1])
        ).astype(HALF)


def multiply_kernel(
    size,
    masks,
    near_ref,
    far_ref,
    lengths_ref,
    gains_ref,
    edge_w_ref,
    gate_w_ref,
    out_w_ref,
    left_ref,
    right_ref,
    left_a_ref,
    left_b_ref,
    right_a_ref,
    right_b_ref,
    gate_ref,
    hat_mid_ref,
    scale_mid_ref,
    edge_out_ref,
    hat_y_ref,
    scale_y_ref,
    y_ref,
    x_half_ref,
    update_ref,
    pair_ref,
    right_t_ref,
):
    channels = gains_ref.shape[1]
    block = ROW_BLOCK * size
    blocks = size // ROW_BLOCK
    rows_of, columns_of = block_tools(size)
    real = lengths_ref[0]
    gain_x = gains_ref[0:1, :]
    gain_mid = gains_ref[1:2, :]
    gain_y = gains_ref[2:3, :]
    place_rows(pair_ref, 0, near_ref, far_ref, masks)

    def project(at, carry):
        rows = rows_of(at)
        hat, _ = kernel_norm(pair_ref[rows, :])
        normed = (hat * gain_x).astype(HALF)
        x_half_ref[rows, :] = normed
        projected = dot_nn(normed, edge_w_ref[...])
        gate_ref[rows, :] = sigmoid(dot_nn(normed, gate_w_ref[...]))
        shape = (ROW_BLOCK, size, channels)
        row = lax.broadcasted_iota(jnp.int32, shape, 0) + at * ROW_BLOCK
        col = lax.broadcasted_iota(jnp.int32, shape, 1)
        mask = jnp.where((row < real) & (col < real), 1.0, 0.0).reshape(block, channels)
        for side, (edge, first, second) in enumerate(
            ((left_ref, left_a_ref, left_b_ref), (right_ref, right_a_ref, right_b_ref))
        ):
            base = 2 * side * channels
            sig = sigmoid(projected[:, base : base + channels])
            value = projected[:, base + channels : base + 2 * channels]
            masked = mask * sig
            product = masked * value
            edge[rows, :] = product.astype(HALF).astype(FULL)
            first[rows, :] = product * (1.0 - sig)
            second[rows, :] = masked
        return carry

    lax.fori_loop(0, blocks, project, 0)

    def turn(at, carry):
        right_t_ref[rows_of(at), :] = columns_of(right_ref, at)
        return carry

    lax.fori_loop(0, blocks, turn, 0)

    def multiply(at, carry):
        rows = rows_of(at)
        product = outer_sum(size, at, left_ref, 1, size, right_t_ref)
        hat, scale = kernel_norm(product)
        hat_mid_ref[rows, :] = hat
        scale_mid_ref[rows, :] = jnp.broadcast_to(scale, hat.shape)
        update = (hat * gain_mid).astype(HALF)
        update_ref[rows, :] = update
        edge_out = dot_nn(update, out_w_ref[...])
        edge_out_ref[rows, :] = edge_out
        middle = pair_ref[rows, :] + gate_ref[rows, :] * edge_out
        hat, scale = kernel_norm(middle)
        hat_y_ref[rows, :] = hat
        scale_y_ref[rows, :] = jnp.broadcast_to(scale, hat.shape)
        y_ref[rows, :] = hat * gain_y
        return carry

    lax.fori_loop(0, blocks, multiply, 0)


def project_kernel(
    size,
    y_ref,
    att_w_ref,
    bias_w_ref,
    att_gate_ref,
    bias_ref,
    y_t_ref,
    query_ref,
    key_ref,
    value_ref,
    bias_rep_ref,
):
    channels = y_ref.shape[1]
    lanes = HEADS * size
    head_scale = 1.0 / math.sqrt(HEAD_DIM)
    rows_of, columns_of = block_tools(size)
    same_cell = same_cell_of(size)
    spread_bias_weight(bias_rep_ref, bias_w_ref, size)

    def prepare(at, carry):
        rows = rows_of(at)
        y = columns_of(y_ref, at).astype(HALF)
        y_t_ref[rows, :] = y
        packed = dot_nn(y, att_w_ref[...])
        query_ref[rows, :] = (packed[:, :channels] * head_scale).astype(HALF)
        key_ref[rows, :] = packed[:, channels : 2 * channels].astype(HALF)
        value_ref[rows, :] = packed[:, 2 * channels : 3 * channels].astype(HALF)
        att_gate_ref[rows, :] = sigmoid(packed[:, 3 * channels :])
        spread = dot_nt(y, bias_rep_ref[...]).astype(HALF).astype(FULL)
        spread = spread.reshape(ROW_BLOCK, size, lanes) * same_cell[None]
        bias_ref[pl.ds(at * ROW_BLOCK, ROW_BLOCK), :] = jnp.sum(spread, axis=1)
        return carry

    lax.fori_loop(0, size // ROW_BLOCK, prepare, 0)


def attend_kernel(
    size,
    masks,
    near_ref,
    far_ref,
    lengths_ref,
    att_w_ref,
    att_out_w_ref,
    att_gate_ref,
    bias_ref,
    y_t_ref,
    query_ref,
    key_ref,
    value_ref,
    bias_rep_ref,
    cot_ref,
    grad_y_ref,
    grad_att_w_ref,
    grad_bias_ref,
    grad_att_out_ref,
    gain_part_ref,
    cot_t_ref,
    gated_ref,
    grad_packed_ref,
    bias_grad_ref,
):
    channels = cot_ref.shape[1]
    block = ROW_BLOCK * size
    blocks = size // ROW_BLOCK
    lanes = HEADS * size
    head_scale = 1.0 / math.sqrt(HEAD_DIM)
    rows_of, columns_of = block_tools(size)
    same_cell = same_cell_of(size)
    valid = real_lanes(size, lengths_ref[0])
    place_rows(cot_ref, 1, near_ref, far_ref, masks)

    head_mask = head_blocks(size, HEAD_DIM, HALF)
    head_mask_full = head_blocks(size, HEAD_DIM, FULL)
    no_mask = jnp.zeros((lanes, channels), HALF)
    no_rows = jnp.zeros((size, channels), HALF)
    key_ones = head_blocks(size, size, HALF)
    dim_ones = head_blocks(HEAD_DIM, size, HALF)

    def attend(at, score_sum):
        rows = rows_of(at)
        parts = [slice(a * size, (a + 1) * size) for a in range(ROW_BLOCK)]
        query, key, value = (ref[rows, :] for ref in (query_ref, key_ref, value_ref))
        gate = att_gate_ref[rows, :]
        cot = columns_of(cot_ref, at).astype(HALF)
        cot_t_ref[rows, :] = cot
        grad_gated = dot_nt(cot, att_out_w_ref[...])
        grad_att = (grad_gated * gate).astype(HALF)
        keys = [jnp.concatenate([key[p]] * HEADS, axis=0) * head_mask for p in parts]
        values = [jnp.concatenate([value[p]] * HEADS, axis=0) * head_mask for p in parts]
        bias = bias_ref[...]

        def products(p, a):
            both = jnp.concatenate(
                [
                    jnp.concatenate([keys[a], no_mask], axis=1),
                    jnp.concatenate([no_mask, values[a]], axis=1),
                ],
                axis=0,
            )
            return dot_nt(jnp.concatenate([query[p], grad_att[p]], axis=1), both)

        pairs = [products(p, a) for a, p in enumerate(parts)]
        scores = jnp.concatenate([pair[:, :lanes] + bias for pair in pairs], axis=0)
        grad_attention = jnp.concatenate([pair[:, lanes:] for pair in pairs], axis=0)
        exp_scores = valid * jnp.exp(scores)
        attention = exp_scores / dot_wide(exp_scores, key_ones)
        attention_half = attention.astype(HALF)
        attended = jnp.concatenate(
            [dot_nn(attention_half[p], values[a]) for a, p in enumerate(parts)], axis=0
        )
        row_dots = dot_wide(grad_att.astype(FULL) * attended, dim_ones)
        grad_scores = attention * (grad_attention - row_dots)
        scores_half = grad_scores.astype(HALF)
        for p in parts:
            score_sum = score_sum + grad_scores[p]
        grad_query = jnp.concatenate(
            [dot_nn(scores_half[p], keys[a]) for a, p in enumerate(parts)], axis=0
        )

        def key_sums(p):
            weights = jnp.concatenate([scores_half[p], attention_half[p]], axis=0)
            vectors = jnp.concatenate(
                [
                    jnp.concatenate([query[p], no_rows], axis=1),
                    jnp.concatenate([no_rows, grad_att[p]], axis=1),
                ],
                axis=0,
            )
            whole = dot_tn(weights, vectors)
            masked = [whole[:, :channels] * head_mask_full, whole[:, channels:] * head_mask_full]
            return [sum(part[h * size : (h + 1) * size] for h in range(HEADS)) for part in masked]

        per_key = [key_sums(p) for p in parts]
        grad_key = jnp.concatenate([pair[0] for pair in per_key], axis=0)
        grad_value = jnp.concatenate([pair[1] for pair in per_key], axis=0)
        gated = gate * attended
        gated_ref[rows, :] = gated.astype(HALF)
        grad_gate_pre = grad_gated * gated * (1.0 - gate)
        grad_packed = jnp.concatenate(
            [
                (grad_query * head_scale).astype(HALF),
                grad_key.astype(HALF),
                grad_value.astype(HALF),
                grad_gate_pre.astype(HALF),
            ],
            axis=1,
        )
        grad_packed_ref[rows, : 4 * channels] = grad_packed
        grad_y_ref[rows, :] = dot_nt(grad_packed, att_w_ref[...])
        return score_sum

    score_sum = lax.fori_loop(0, blocks, attend, jnp.zeros((size, lanes), FULL), unroll=2)
    bias_grad_ref[...] = score_sum.astype(HALF).astype(FULL)

    def spread_bias(at, carry):
        rows = rows_of(at)
        part = bias_grad_ref[pl.ds(at * ROW_BLOCK, ROW_BLOCK), :]
        spread = (part[:, None, :] * same_cell[None]).reshape(block, lanes).astype(HALF)
        grad_packed_ref[rows, 4 * channels :] = spread
        grad_y_ref[rows, :] += dot_nn(spread, bias_rep_ref[...])
        return carry

    lax.fori_loop(0, blocks, spread_bias, 0)

    inverse = 1.0 / size
    y_sum = dot_tn(y_t_ref[...], grad_packed_ref[...]) * inverse
    att_sum, bias_sum = y_sum[:, : 4 * channels], jnp.transpose(y_sum[:, 4 * channels :])
    grad_att_w_ref[...] = att_sum
    grad_att_out_ref[...] = dot_tn(gated_ref[...], cot_t_ref[...]) * inverse
    for h in range(HEADS):
        grad_bias_ref[h : h + 1, :] = jnp.sum(
            bias_sum[h * size : (h + 1) * size], axis=0, keepdims=True
        )
    bias_part = jnp.sum(bias_rep_ref[...].astype(FULL) * bias_sum, axis=0, keepdims=True)
    gain_part_ref[...] = gain_sum(((att_w_ref[...], att_sum),)) + bias_part


def gain_sum(pairs):
    total = sum(jnp.sum(weight.astype(FULL) * grad, axis=1, keepdims=True) for weight, grad in pairs)
    channels = total.shape[0]
    return jnp.transpose(jnp.broadcast_to(total, (channels, channels)))[0:1, :]


def edges_kernel(
    size,
    devices,
    pair_ref,
    gains_ref,
    edge_w_ref,
    gate_w_ref,
    out_w_ref,
    left_ref,
    right_ref,
    left_a_ref,
    left_b_ref,
    right_a_ref,
    right_b_ref,
    gate_ref,
    hat_mid_ref,
    scale_mid_ref,
    edge_out_ref,
    hat_y_ref,
    scale_y_ref,
    x_half_ref,
    update_ref,
    cot_ref,
    grad_y_ref,
    gain_part_ref,
    grad_pair_ref,
    grad_gains_ref,
    grad_edge_ref,
    grad_gate_w_ref,
    grad_out_w_ref,
    grad_middle_ref,
    grad_product_ref,
    grad_proj_ref,
    x_sum_ref,
    out_sum_ref,
):
    channels = gains_ref.shape[1]
    blocks = size // ROW_BLOCK
    rows_of, columns_of = block_tools(size)
    gain_x = gains_ref[0:1, :]
    gain_mid = gains_ref[1:2, :]
    gain_y = gains_ref[2:3, :]

    x_sum_ref[...] = jnp.zeros(x_sum_ref.shape, FULL)
    out_sum_ref[...] = jnp.zeros(out_sum_ref.shape, FULL)

    def middle_back(at, carry):
        rows = rows_of(at)
        grad_y = columns_of(grad_y_ref, at)
        grad_middle = cot_ref[rows, :] + kernel_norm_back(
            grad_y, hat_y_ref[rows, :], scale_y_ref[rows, :], gain_y
        )
        grad_middle_ref[rows, :] = grad_middle
        gate = gate_ref[rows, :]
        gated = grad_middle * gate
        grad_edge_out = gated.astype(HALF)
        grad_gate = (gated * edge_out_ref[rows, :] * (1.0 - gate)).astype(HALF)
        grad_proj_ref[rows, 4 * channels :] = grad_gate
        x_sum_ref[:, 4 * channels :] += dot_tn(x_half_ref[rows, :], grad_gate)
        out_sum_ref[...] += dot_tn(update_ref[rows, :], grad_edge_out)
        grad_update = dot_nt(grad_edge_out, out_w_ref[...])
        grad_product = kernel_norm_back(grad_update, hat_mid_ref[rows, :], scale_mid_ref[rows, :], gain_mid)
        grad_product_ref[rows, :] = grad_product.astype(HALF).astype(FULL)
        return carry

    lax.fori_loop(0, blocks, middle_back, 0)

    def edges_back(at, carry):
        rows = rows_of(at)
        x_half = x_half_ref[rows, :]
        for side, (first_ref, second_ref, strides, other_ref) in enumerate(
            (
                (left_a_ref, left_b_ref, (1, size), right_ref),
                (right_a_ref, right_b_ref, (size, 1), left_ref),
            )
        ):
            grad = outer_sum(size, at, grad_product_ref, *strides, other_ref)
            both = jnp.concatenate(
                [(grad * first_ref[rows, :]).astype(HALF), (grad * second_ref[rows, :]).astype(HALF)], axis=1
            )
            place = slice(2 * side * channels, 2 * (side + 1) * channels)
            grad_proj_ref[rows, place] = both
            x_sum_ref[:, place] += dot_tn(x_half, both)
        return carry

    lax.fori_loop(0, blocks, edges_back, 0)

    inverse = 1.0 / size
    x_sum = x_sum_ref[...] * inverse
    edge_sum, gate_sum = x_sum[:, : 4 * channels], x_sum[:, 4 * channels :]
    grad_edge_ref[...] = edge_sum
    grad_gate_w_ref[...] = gate_sum
    out_sum = out_sum_ref[...] * inverse
    grad_out_w_ref[...] = out_sum
    grad_gains_ref[0:1, :] = gain_sum(((edge_w_ref[...], edge_sum), (gate_w_ref[...], gate_sum))) / gain_x
    grad_gains_ref[1:2, :] = gain_sum(((out_w_ref[...], out_sum),)) / gain_mid
    grad_gains_ref[2:3, :] = gain_part_ref[...] / gain_y

    own_cells = size * size // devices
    own = pl.ds(pl.multiple_of(lax.axis_index("dap") * own_cells, own_cells), own_cells)
    hat, scale = kernel_norm(pair_ref[...].reshape(own_cells, channels).astype(FULL))
    grad_x = dot_nt(grad_proj_ref[own, : 4 * channels], edge_w_ref[...])
    grad_x = grad_x + dot_nt(grad_proj_ref[own, 4 * channels :], gate_w_ref[...])
    grad_pair = grad_middle_ref[own, :] + kernel_norm_back(grad_x, hat, scale, gain_x)
    grad_pair_ref[...] = grad_pair.astype(grad_pair_ref.dtype)


def kernel_norm(values):
    center = values - lane_mean(values)
    scale = lax.rsqrt(lane_mean(center * center) + epsilon)
    return center * scale, scale


def kernel_norm_back(grad_out, hat, scale, gain):
    scaled = grad_out * gain
    return scale * (scaled - lane_mean(scaled) - hat * lane_mean(scaled * hat))


def bytes_of(arrays):
    return sum(math.prod(shape) * jnp.dtype(dtype).itemsize for shape, dtype in arrays)


def run_kernel(kernel, operands, outs, scratch, seconds, lengths_at=None):
    vmem = pl.BlockSpec(memory_space=pltpu.VMEM)
    in_specs = [vmem] * len(operands)
    if lengths_at is not None:
        in_specs[lengths_at] = pl.BlockSpec(memory_space=pltpu.SMEM)
    return pl.pallas_call(
        kernel,
        out_shape=[jax.ShapeDtypeStruct(*out) for out in outs],
        in_specs=in_specs,
        out_specs=[vmem] * len(outs),
        scratch_shapes=[pltpu.VMEM(*part) for part in scratch],
        compiler_params=pltpu.CompilerParams(vmem_limit_bytes=bytes_of(scratch) + VMEM_SLACK),
        cost_estimate=pl.CostEstimate(flops=0, bytes_accessed=int(seconds * 3.6e12), transcendentals=0),
    )(*operands)


def replicated_plan(
    axis_size,
    pair_map,
    cotangent,
    lengths,
    norm_gains,
    edge_weight,
    mult_gate_weight,
    mult_out_weight,
    attention_weight,
    bias_weight,
    attention_out_weight,
):
    _, size, channels = pair_map.shape
    cells, lanes = size * size, HEADS * size
    bits = axis_size.bit_length() - 1
    far_step = 1 << (bits - 1)
    near_steps = range(2, far_step, 2)

    def swapped(held, mask):
        return lax.ppermute(held, "dap", [(d, d ^ mask) for d in range(axis_size)])

    own = jnp.stack([pair_map, cotangent])
    held = jnp.stack([own, swapped(own, far_step)])
    masks = [0, far_step]
    near = jnp.concatenate([held] + [swapped(held, step) for step in near_steps], axis=0)
    masks = masks + [mask ^ step for step in near_steps for mask in masks]
    far = swapped(near, 1)

    full, half = ((cells, channels), FULL), ((cells, channels), HALF)
    square, wide = ((channels, channels), FULL), ((channels, 4 * channels), FULL)
    *kept, y, x_half, update = run_kernel(
        functools.partial(multiply_kernel, size, masks),
        (near, far, lengths, norm_gains, edge_weight, mult_gate_weight, mult_out_weight),
        [full] * 13 + [half] * 2,
        [full] * 2,
        5e-6,
        2,
    )
    projections = run_kernel(
        functools.partial(project_kernel, size),
        (y, attention_weight, bias_weight.T),
        [full, ((size, lanes), FULL)] + [half] * 4 + [((lanes, channels), HALF)],
        [],
        2e-6,
    )
    cot, grad_y, grad_att_w, grad_bias, grad_att_out, gain_part = run_kernel(
        functools.partial(attend_kernel, size, masks),
        (near, far, lengths, attention_weight, attention_out_weight, *projections),
        [full, full, wide, ((HEADS, channels), FULL), square, ((1, channels), FULL)],
        [half] * 2 + [((cells, 4 * channels + lanes), HALF), ((size, lanes), FULL)],
        7e-6,
        2,
    )
    grad_pair, grad_gains, grad_edge, grad_gate_w, grad_out_w = run_kernel(
        functools.partial(edges_kernel, size, axis_size),
        (pair_map, norm_gains, edge_weight, mult_gate_weight, mult_out_weight, *kept, x_half, update, cot, grad_y, gain_part),
        [((cells // axis_size, channels), HALF), ((3, channels), FULL), wide, square, square],
        [full] * 2 + [((cells, 5 * channels), HALF), ((channels, 5 * channels), FULL), square],
        6e-6,
    )
    return (
        grad_pair.reshape(pair_map.shape),
        grad_gains,
        grad_edge,
        grad_gate_w,
        grad_out_w,
        grad_att_w,
        grad_bias.T,
        grad_att_out,
    )


def per_device(axis_size, pair_map, *rest):
    _, size, channels = pair_map.shape
    fits = size % ROW_BLOCK == 0 and 25 * bytes_of([((size, size, channels), FULL)]) <= VMEM_SHARE
    if fits and axis_size >= 8 and axis_size & (axis_size - 1) == 0:
        return replicated_plan(axis_size, pair_map, *rest)
    return distributed_plan(pair_map, *rest)


def solution(mesh):
    return jax.shard_map(
        functools.partial(per_device, mesh.shape["dap"]),
        mesh=mesh,
        in_specs=(
            P(("groups", "dap"), None, None),
            P(("groups", "dap"), None, None),
            P("groups"),
            P(),
            P(),
            P(),
            P(),
            P(),
            P(),
            P(),
        ),
        out_specs=(
            P(("groups", "dap"), None, None),
            P("groups", None),
            P("groups", None),
            P("groups", None),
            P("groups", None),
            P("groups", None),
            P("groups", None),
            P("groups", None),
        ),
        check_vma=False,
    )
```

```python
import functools
import math

import jax
import jax.numpy as jnp
from jax import lax
from jax.experimental import pallas as pl
from jax.experimental.pallas import tpu as pltpu
from jax.sharding import PartitionSpec as P

HEADS = 4
HEAD_DIM = 32


epsilon = 1e-05


def norm_forward(values, gain_row):
    center = values - jnp.mean(values, axis=-1, keepdims=True)
    inv_std = lax.rsqrt(jnp.mean(center * center, axis=-1, keepdims=True) + epsilon)
    normed = center * inv_std
    return (normed * gain_row, normed, inv_std)


def norm_backward(grad_out, normed, inv_std, gain_row):
    scaled = grad_out * gain_row
    first_mean = jnp.mean(scaled, axis=-1, keepdims=True)
    second_mean = jnp.mean(scaled * normed, axis=-1, keepdims=True)
    return inv_std * (scaled - first_mean - normed * second_mean)


def distributed_plan(
    pair_map,
    cotangent,
    lengths,
    norm_gains,
    edge_weight,
    mult_gate_weight,
    mult_out_weight,
    attention_weight,
    bias_weight,
    attention_out_weight,
):
    row_count, full_size, channels = pair_map.shape
    inner_width = HEADS * HEAD_DIM
    head_scale = 1.0 / math.sqrt(HEAD_DIM)
    first_row = lax.axis_index("dap") * row_count
    real_count = lengths[0]
    valid_all = (jnp.arange(full_size) < real_count).astype(jnp.float32)
    valid_rows = (first_row + jnp.arange(row_count) < real_count).astype(jnp.float32)
    mask_pair = (valid_rows[:, None] * valid_all[None, :])[:, :, None]
    pair_f32 = pair_map.astype(jnp.float32)
    normed_full, hat_in, scale_in = norm_forward(pair_f32, norm_gains[0])
    normed_x = normed_full.astype(jnp.bfloat16)
    projected = jnp.einsum("rnc,cf->rnf", normed_x, edge_weight, preferred_element_type=jnp.float32)
    left_gate = projected[..., :channels]
    left_value = projected[..., channels : 2 * channels]
    right_gate = projected[..., 2 * channels : 3 * channels]
    right_value = projected[..., 3 * channels :]
    left_sig = jax.nn.sigmoid(left_gate)
    right_sig = jax.nn.sigmoid(right_gate)
    left_edges = (mask_pair * left_sig * left_value).astype(jnp.bfloat16)
    right_edges = (mask_pair * right_sig * right_value).astype(jnp.bfloat16)
    product = jnp.einsum(
        "ikc,jkc->ijc",
        left_edges,
        lax.all_gather(right_edges, "dap", axis=0, tiled=True),
        preferred_element_type=jnp.float32,
    )
    update_full, hat_mid, scale_mid = norm_forward(product, norm_gains[1])
    update = update_full.astype(jnp.bfloat16)
    edge_out = jnp.einsum(
        "rnc,cf->rnf", update, mult_out_weight, preferred_element_type=jnp.float32
    )
    gate_sig = jax.nn.sigmoid(
        jnp.einsum("rnc,cf->rnf", normed_x, mult_gate_weight, preferred_element_type=jnp.float32)
    )
    middle = pair_f32 + gate_sig * edge_out
    normed_mid, hat_attn, scale_attn = norm_forward(middle, norm_gains[2])
    normed_y = normed_mid.astype(jnp.bfloat16)
    bias_local = jnp.einsum(
        "kic,ch->hki", normed_y, bias_weight, preferred_element_type=jnp.float32
    ).astype(jnp.bfloat16)
    bias_whole = lax.all_gather(bias_local, "dap", axis=1, tiled=True)
    bias_query = jnp.swapaxes(bias_whole, 1, 2).astype(jnp.float32)
    column_y, column_cot = (
        lax.all_to_all(normed_y, "dap", split_axis=1, concat_axis=0, tiled=True),
        lax.all_to_all(cotangent, "dap", split_axis=1, concat_axis=0, tiled=True),
    )
    packed = jnp.einsum(
        "ijc,cf->ijf", column_y, attention_weight, preferred_element_type=jnp.float32
    )
    packed = packed.reshape(full_size, row_count, 4, HEADS, HEAD_DIM)
    query_vectors = (packed[:, :, 0] * head_scale).astype(jnp.bfloat16)
    key_vectors = packed[:, :, 1].astype(jnp.bfloat16)
    value_vectors = packed[:, :, 2].astype(jnp.bfloat16)
    att_gate = jax.nn.sigmoid(packed[:, :, 3])
    scores = (
        jnp.einsum(
            "ijhd,kjhd->jhik", query_vectors, key_vectors, preferred_element_type=jnp.float32
        )
        + bias_query[None]
    )
    exp_scores = valid_all * jnp.exp(scores)
    attention = exp_scores / jnp.sum(exp_scores, axis=-1, keepdims=True)
    attention_half = attention.astype(jnp.bfloat16)
    attended = jnp.einsum(
        "jhik,kjhd->ijhd", attention_half, value_vectors, preferred_element_type=jnp.float32
    )
    gated = (att_gate * attended).astype(jnp.bfloat16).reshape(full_size, row_count, inner_width)
    part_attn_out = jnp.einsum("ijf,ijc->fc", gated, column_cot, preferred_element_type=jnp.float32)
    grad_gated = jnp.einsum(
        "ijc,fc->ijf", column_cot, attention_out_weight, preferred_element_type=jnp.float32
    )
    grad_gated = grad_gated.reshape(full_size, row_count, HEADS, HEAD_DIM)
    grad_att = (grad_gated * att_gate).astype(jnp.bfloat16)
    grad_gate_pre = grad_gated * attended * att_gate * (1.0 - att_gate)
    grad_attention = jnp.einsum(
        "ijhd,kjhd->jhik", grad_att, value_vectors, preferred_element_type=jnp.float32
    )
    row_dots = jnp.transpose(jnp.sum(grad_att.astype(jnp.float32) * attended, axis=-1), (1, 2, 0))
    grad_scores = attention * (grad_attention - row_dots[..., None])
    scores_half = grad_scores.astype(jnp.bfloat16)
    grad_query = jnp.einsum(
        "jhik,kjhd->ijhd", scores_half, key_vectors, preferred_element_type=jnp.float32
    )
    grad_key = jnp.einsum(
        "jhik,ijhd->kjhd", scores_half, query_vectors, preferred_element_type=jnp.float32
    )
    grad_value = jnp.einsum(
        "jhik,ijhd->kjhd", attention_half, grad_att, preferred_element_type=jnp.float32
    )
    grad_packed = jnp.stack([grad_query * head_scale, grad_key, grad_value, grad_gate_pre], axis=2)
    grad_packed = grad_packed.reshape(full_size, row_count, 4 * inner_width).astype(jnp.bfloat16)
    part_attention = jnp.einsum(
        "ijc,ijf->cf", column_y, grad_packed, preferred_element_type=jnp.float32
    )
    column_grad = jnp.einsum(
        "ijf,cf->ijc", grad_packed, attention_weight, preferred_element_type=jnp.float32
    ).astype(jnp.bfloat16)
    row_grad = lax.all_to_all(column_grad, "dap", split_axis=0, concat_axis=1, tiled=True)
    score_sums = jnp.sum(grad_scores, axis=0)
    taken = score_sums
    bias_half = lax.psum_scatter(
        jnp.transpose(taken, (2, 0, 1)), "dap", scatter_dimension=0, tiled=True
    ).astype(jnp.bfloat16)
    part_bias = jnp.einsum("kic,khi->ch", normed_y, bias_half, preferred_element_type=jnp.float32)
    grad_normed_y = row_grad.astype(jnp.float32) + jnp.einsum(
        "khi,ch->kic", bias_half, bias_weight, preferred_element_type=jnp.float32
    )
    part_gain_attn = jnp.sum(grad_normed_y * hat_attn, axis=(0, 1))
    grad_middle = cotangent.astype(jnp.float32) + norm_backward(
        grad_normed_y, hat_attn, scale_attn, norm_gains[2]
    )
    grad_edge_out = (grad_middle * gate_sig).astype(jnp.bfloat16)
    grad_gate = (grad_middle * edge_out * gate_sig * (1.0 - gate_sig)).astype(jnp.bfloat16)
    part_mult_out = jnp.einsum(
        "rnc,rnf->cf", update, grad_edge_out, preferred_element_type=jnp.float32
    )
    part_mult_gate = jnp.einsum(
        "rnc,rnf->cf", normed_x, grad_gate, preferred_element_type=jnp.float32
    )
    grad_update = jnp.einsum(
        "rnf,cf->rnc", grad_edge_out, mult_out_weight, preferred_element_type=jnp.float32
    )
    part_gain_mid = jnp.sum(grad_update * hat_mid, axis=(0, 1))
    grad_product = norm_backward(grad_update, hat_mid, scale_mid, norm_gains[1]).astype(
        jnp.bfloat16
    )
    taken = grad_product
    grad_left = jnp.einsum(
        "ijc,jkc->ikc",
        taken,
        lax.all_gather(right_edges, "dap", axis=0, tiled=True),
        preferred_element_type=jnp.float32,
    )
    grad_cols = lax.all_to_all(grad_product, "dap", split_axis=1, concat_axis=0, tiled=True)
    taken = grad_cols
    grad_right = jnp.einsum(
        "ijc,ikc->jkc",
        taken,
        lax.all_gather(left_edges, "dap", axis=0, tiled=True),
        preferred_element_type=jnp.float32,
    )
    grad_proj = jnp.concatenate(
        [
            grad_left * mask_pair * left_value * left_sig * (1.0 - left_sig),
            grad_left * mask_pair * left_sig,
            grad_right * mask_pair * right_value * right_sig * (1.0 - right_sig),
            grad_right * mask_pair * right_sig,
        ],
        axis=-1,
    ).astype(jnp.bfloat16)
    part_edge = jnp.einsum("rnc,rnf->cf", normed_x, grad_proj, preferred_element_type=jnp.float32)
    grad_normed_x = jnp.einsum(
        "rnf,cf->rnc", grad_proj, edge_weight, preferred_element_type=jnp.float32
    )
    grad_normed_x = grad_normed_x + jnp.einsum(
        "rnf,cf->rnc", grad_gate, mult_gate_weight, preferred_element_type=jnp.float32
    )
    part_gain_in = jnp.sum(grad_normed_x * hat_in, axis=(0, 1))
    grad_pair = (
        grad_middle + norm_backward(grad_normed_x, hat_in, scale_in, norm_gains[0])
    ).astype(jnp.bfloat16)
    totals = lax.psum(
        (
            part_gain_in,
            part_gain_mid,
            part_edge,
            part_mult_gate,
            part_mult_out,
            part_gain_attn,
            part_attention,
            part_bias,
            part_attn_out,
        ),
        "dap",
    )
    (
        gain_in_sum,
        gain_mid_sum,
        edge_sum,
        mult_gate_sum,
        mult_out_sum,
        gain_attn_sum,
        attention_sum,
        bias_sum,
        attn_out_sum,
    ) = totals
    inverse = 1.0 / full_size
    grad_gains = jnp.stack([gain_in_sum, gain_mid_sum, gain_attn_sum]) * inverse
    return (
        grad_pair,
        grad_gains,
        edge_sum * inverse,
        mult_gate_sum * inverse,
        mult_out_sum * inverse,
        attention_sum * inverse,
        bias_sum * inverse,
        attn_out_sum * inverse,
    )


ROW_BLOCK = 8
VMEM_SLACK = 8 * 2**20
VMEM_SHARE = 32 * 2**20
HALF = jnp.bfloat16
FULL = jnp.float32


def dot_nn(left, right):
    return lax.dot_general(left, right, (((1,), (0,)), ((), ())), preferred_element_type=FULL)


def dot_nt(left, right):
    return lax.dot_general(left, right, (((1,), (1,)), ((), ())), preferred_element_type=FULL)


def dot_tn(left, right):
    return lax.dot_general(left, right, (((0,), (0,)), ((), ())), preferred_element_type=FULL)


def dot_wide(values, ones):
    high = values.astype(HALF)
    low = (values - high.astype(FULL)).astype(HALF)
    return dot_nn(jnp.concatenate([high, low], axis=1), jnp.concatenate([ones, ones], axis=0))


def lane_mean(values):
    return jnp.mean(values, axis=-1, keepdims=True)


def sigmoid(values):
    return pltpu.reciprocal(1.0 + jnp.exp(-values), approx=True)


def head_blocks(row_width, col_width, dtype):
    shape = (HEADS * row_width, HEADS * col_width)
    row = lax.broadcasted_iota(jnp.int32, shape, 0)
    col = lax.broadcasted_iota(jnp.int32, shape, 1)
    same = None
    for h in range(HEADS):
        here = (row >= h * row_width) & (row < (h + 1) * row_width)
        here = here & (col >= h * col_width) & (col < (h + 1) * col_width)
        same = here if same is None else same | here
    return jnp.where(same, 1.0, 0.0).astype(dtype)


def place_rows(target, part, near_ref, far_ref, masks):
    me = lax.axis_index("dap")
    cells = target.shape[0] // (2 * len(masks))
    for other, blocks in enumerate((near_ref, far_ref)):
        for at, mask in enumerate(masks):
            place = pl.ds(pl.multiple_of((me ^ mask ^ other) * cells, cells), cells)
            target[place, :] = blocks[at, part].reshape(cells, target.shape[1]).astype(FULL)


def block_tools(size):
    block = ROW_BLOCK * size

    def rows_of(at):
        return pl.ds(pl.multiple_of(at * block, block), block)

    def columns_of(ref, at):
        return jnp.concatenate(
            [ref[pl.ds(at * ROW_BLOCK + a, size, stride=size), :] for a in range(ROW_BLOCK)], axis=0
        )

    return rows_of, columns_of


def outer_sum(size, at, row_ref, row_stride, block_stride, block_ref):
    sums = [jnp.zeros((size, block_ref.shape[1]), FULL)] * ROW_BLOCK
    for k in range(size):
        whole = block_ref[k * size : (k + 1) * size, :]
        for a in range(ROW_BLOCK):
            row = (at * ROW_BLOCK + a) * block_stride + k * row_stride
            sums[a] = sums[a] + row_ref[pl.ds(row, 1), :] * whole
    return jnp.concatenate(sums, axis=0)


def same_cell_of(size):
    row = lax.broadcasted_iota(jnp.int32, (size, HEADS * size), 0)
    lane = lax.broadcasted_iota(jnp.int32, (size, HEADS * size), 1)
    same = lane == row
    for h in range(1, HEADS):
        same = same | (lane == row + h * size)
    return jnp.where(same, 1.0, 0.0)


def real_lanes(size, real):
    lane = lax.broadcasted_iota(jnp.int32, (1, HEADS * size), 1)
    inside = lane < real
    for h in range(1, HEADS):
        inside = inside | ((lane >= h * size) & (lane < h * size + real))
    return jnp.where(inside, 1.0, 0.0)


def spread_bias_weight(target, bias_w_ref, size):
    bias_rows = bias_w_ref[...].astype(FULL)
    for h in range(HEADS):
        target[h * size : (h + 1) * size, :] = jnp.broadcast_to(
            bias_rows[h : h + 1], (size, bias_rows.shape[1])
        ).astype(HALF)


def multiply_kernel(
    size,
    masks,
    near_ref,
    far_ref,
    lengths_ref,
    gains_ref,
    edge_w_ref,
    gate_w_ref,
    out_w_ref,
    left_ref,
    right_ref,
    left_a_ref,
    left_b_ref,
    right_a_ref,
    right_b_ref,
    gate_ref,
    hat_mid_ref,
    scale_mid_ref,
    edge_out_ref,
    hat_y_ref,
    scale_y_ref,
    y_ref,
    x_half_ref,
    update_ref,
    pair_ref,
    right_t_ref,
):
    channels = gains_ref.shape[1]
    block = ROW_BLOCK * size
    blocks = size // ROW_BLOCK
    rows_of, columns_of = block_tools(size)
    real = lengths_ref[0]
    gain_x = gains_ref[0:1, :]
    gain_mid = gains_ref[1:2, :]
    gain_y = gains_ref[2:3, :]
    place_rows(pair_ref, 0, near_ref, far_ref, masks)

    def project(at, carry):
        rows = rows_of(at)
        hat, _ = kernel_norm(pair_ref[rows, :])
        normed = (hat * gain_x).astype(HALF)
        x_half_ref[rows, :] = normed
        projected = dot_nn(normed, edge_w_ref[...])
        gate_ref[rows, :] = sigmoid(dot_nn(normed, gate_w_ref[...]))
        shape = (ROW_BLOCK, size, channels)
        row = lax.broadcasted_iota(jnp.int32, shape, 0) + at * ROW_BLOCK
        col = lax.broadcasted_iota(jnp.int32, shape, 1)
        mask = jnp.where((row < real) & (col < real), 1.0, 0.0).reshape(block, channels)
        for side, (edge, first, second) in enumerate(
            ((left_ref, left_a_ref, left_b_ref), (right_ref, right_a_ref, right_b_ref))
        ):
            base = 2 * side * channels
            sig = sigmoid(projected[:, base : base + channels])
            value = projected[:, base + channels : base + 2 * channels]
            masked = mask * sig
            product = masked * value
            edge[rows, :] = product.astype(HALF).astype(FULL)
            first[rows, :] = product * (1.0 - sig)
            second[rows, :] = masked
        return carry

    lax.fori_loop(0, blocks, project, 0, unroll=2)

    def turn(at, carry):
        right_t_ref[rows_of(at), :] = columns_of(right_ref, at)
        return carry

    lax.fori_loop(0, blocks, turn, 0, unroll=2)

    def multiply(at, carry):
        rows = rows_of(at)
        product = outer_sum(size, at, left_ref, 1, size, right_t_ref)
        hat, scale = kernel_norm(product)
        hat_mid_ref[rows, :] = hat
        scale_mid_ref[rows, :] = jnp.broadcast_to(scale, hat.shape)
        update = (hat * gain_mid).astype(HALF)
        update_ref[rows, :] = update
        edge_out = dot_nn(update, out_w_ref[...])
        edge_out_ref[rows, :] = edge_out
        middle = pair_ref[rows, :] + gate_ref[rows, :] * edge_out
        hat, scale = kernel_norm(middle)
        hat_y_ref[rows, :] = hat
        scale_y_ref[rows, :] = jnp.broadcast_to(scale, hat.shape)
        y_ref[rows, :] = hat * gain_y
        return carry

    lax.fori_loop(0, blocks, multiply, 0, unroll=2)


def project_kernel(
    size,
    y_ref,
    att_w_ref,
    bias_w_ref,
    att_gate_ref,
    bias_ref,
    y_t_ref,
    query_ref,
    key_ref,
    value_ref,
    bias_rep_ref,
):
    channels = y_ref.shape[1]
    lanes = HEADS * size
    head_scale = 1.0 / math.sqrt(HEAD_DIM)
    rows_of, columns_of = block_tools(size)
    same_cell = same_cell_of(size)
    spread_bias_weight(bias_rep_ref, bias_w_ref, size)

    def prepare(at, carry):
        rows = rows_of(at)
        y = columns_of(y_ref, at).astype(HALF)
        y_t_ref[rows, :] = y
        packed = dot_nn(y, att_w_ref[...])
        query_ref[rows, :] = (packed[:, :channels] * head_scale).astype(HALF)
        key_ref[rows, :] = packed[:, channels : 2 * channels].astype(HALF)
        value_ref[rows, :] = packed[:, 2 * channels : 3 * channels].astype(HALF)
        att_gate_ref[rows, :] = sigmoid(packed[:, 3 * channels :])
        spread = dot_nt(y, bias_rep_ref[...]).astype(HALF).astype(FULL)
        spread = spread.reshape(ROW_BLOCK, size, lanes) * same_cell[None]
        bias_ref[pl.ds(at * ROW_BLOCK, ROW_BLOCK), :] = jnp.sum(spread, axis=1)
        return carry

    lax.fori_loop(0, size // ROW_BLOCK, prepare, 0, unroll=2)


def attend_kernel(
    size,
    masks,
    near_ref,
    far_ref,
    lengths_ref,
    att_w_ref,
    att_out_w_ref,
    att_gate_ref,
    bias_ref,
    y_t_ref,
    query_ref,
    key_ref,
    value_ref,
    bias_rep_ref,
    cot_ref,
    grad_y_ref,
    grad_att_w_ref,
    grad_bias_ref,
    grad_att_out_ref,
    gain_part_ref,
    cot_t_ref,
    gated_ref,
    grad_packed_ref,
    bias_grad_ref,
):
    channels = cot_ref.shape[1]
    block = ROW_BLOCK * size
    blocks = size // ROW_BLOCK
    lanes = HEADS * size
    head_scale = 1.0 / math.sqrt(HEAD_DIM)
    rows_of, columns_of = block_tools(size)
    same_cell = same_cell_of(size)
    valid = real_lanes(size, lengths_ref[0])
    place_rows(cot_ref, 1, near_ref, far_ref, masks)

    head_mask = head_blocks(size, HEAD_DIM, HALF)
    head_mask_full = head_blocks(size, HEAD_DIM, FULL)
    no_mask = jnp.zeros((lanes, channels), HALF)
    no_rows = jnp.zeros((size, channels), HALF)
    key_ones = head_blocks(size, size, HALF)
    dim_ones = head_blocks(HEAD_DIM, size, HALF)

    def attend(at, score_sum):
        rows = rows_of(at)
        parts = [slice(a * size, (a + 1) * size) for a in range(ROW_BLOCK)]
        query, key, value = (ref[rows, :] for ref in (query_ref, key_ref, value_ref))
        gate = att_gate_ref[rows, :]
        cot = columns_of(cot_ref, at).astype(HALF)
        cot_t_ref[rows, :] = cot
        grad_gated = dot_nt(cot, att_out_w_ref[...])
        grad_att = (grad_gated * gate).astype(HALF)
        keys = [jnp.concatenate([key[p]] * HEADS, axis=0) * head_mask for p in parts]
        values = [jnp.concatenate([value[p]] * HEADS, axis=0) * head_mask for p in parts]
        bias = bias_ref[...]

        def products(p, a):
            both = jnp.concatenate(
                [
                    jnp.concatenate([keys[a], no_mask], axis=1),
                    jnp.concatenate([no_mask, values[a]], axis=1),
                ],
                axis=0,
            )
            return dot_nt(jnp.concatenate([query[p], grad_att[p]], axis=1), both)

        pairs = [products(p, a) for a, p in enumerate(parts)]
        scores = jnp.concatenate([pair[:, :lanes] + bias for pair in pairs], axis=0)
        grad_attention = jnp.concatenate([pair[:, lanes:] for pair in pairs], axis=0)
        exp_scores = valid * jnp.exp(scores)
        attention = exp_scores / dot_wide(exp_scores, key_ones)
        attention_half = attention.astype(HALF)
        attended = jnp.concatenate(
            [dot_nn(attention_half[p], values[a]) for a, p in enumerate(parts)], axis=0
        )
        row_dots = dot_wide(grad_att.astype(FULL) * attended, dim_ones)
        grad_scores = attention * (grad_attention - row_dots)
        scores_half = grad_scores.astype(HALF)
        for p in parts:
            score_sum = score_sum + grad_scores[p]
        grad_query = jnp.concatenate(
            [dot_nn(scores_half[p], keys[a]) for a, p in enumerate(parts)], axis=0
        )

        def key_sums(p):
            weights = jnp.concatenate([scores_half[p], attention_half[p]], axis=0)
            vectors = jnp.concatenate(
                [
                    jnp.concatenate([query[p], no_rows], axis=1),
                    jnp.concatenate([no_rows, grad_att[p]], axis=1),
                ],
                axis=0,
            )
            whole = dot_tn(weights, vectors)
            masked = [whole[:, :channels] * head_mask_full, whole[:, channels:] * head_mask_full]
            return [sum(part[h * size : (h + 1) * size] for h in range(HEADS)) for part in masked]

        per_key = [key_sums(p) for p in parts]
        grad_key = jnp.concatenate([pair[0] for pair in per_key], axis=0)
        grad_value = jnp.concatenate([pair[1] for pair in per_key], axis=0)
        gated = gate * attended
        gated_ref[rows, :] = gated.astype(HALF)
        grad_gate_pre = grad_gated * gated * (1.0 - gate)
        grad_packed = jnp.concatenate(
            [
                (grad_query * head_scale).astype(HALF),
                grad_key.astype(HALF),
                grad_value.astype(HALF),
                grad_gate_pre.astype(HALF),
            ],
            axis=1,
        )
        grad_packed_ref[rows, : 4 * channels] = grad_packed
        grad_y_ref[rows, :] = dot_nt(grad_packed, att_w_ref[...])
        return score_sum

    score_sum = lax.fori_loop(0, blocks, attend, jnp.zeros((size, lanes), FULL), unroll=4)
    bias_grad_ref[...] = score_sum.astype(HALF).astype(FULL)

    def spread_bias(at, carry):
        rows = rows_of(at)
        part = bias_grad_ref[pl.ds(at * ROW_BLOCK, ROW_BLOCK), :]
        spread = (part[:, None, :] * same_cell[None]).reshape(block, lanes).astype(HALF)
        grad_packed_ref[rows, 4 * channels :] = spread
        grad_y_ref[rows, :] += dot_nn(spread, bias_rep_ref[...])
        return carry

    lax.fori_loop(0, blocks, spread_bias, 0, unroll=2)

    inverse = 1.0 / size
    y_sum = dot_tn(y_t_ref[...], grad_packed_ref[...]) * inverse
    att_sum, bias_sum = y_sum[:, : 4 * channels], jnp.transpose(y_sum[:, 4 * channels :])
    grad_att_w_ref[...] = att_sum
    grad_att_out_ref[...] = dot_tn(gated_ref[...], cot_t_ref[...]) * inverse
    for h in range(HEADS):
        grad_bias_ref[h : h + 1, :] = jnp.sum(
            bias_sum[h * size : (h + 1) * size], axis=0, keepdims=True
        )
    bias_part = jnp.sum(bias_rep_ref[...].astype(FULL) * bias_sum, axis=0, keepdims=True)
    gain_part_ref[...] = gain_sum(((att_w_ref[...], att_sum),)) + bias_part


def gain_sum(pairs):
    total = sum(jnp.sum(weight.astype(FULL) * grad, axis=1, keepdims=True) for weight, grad in pairs)
    channels = total.shape[0]
    return jnp.transpose(jnp.broadcast_to(total, (channels, channels)))[0:1, :]


def edges_kernel(
    size,
    devices,
    pair_ref,
    gains_ref,
    edge_w_ref,
    gate_w_ref,
    out_w_ref,
    left_ref,
    right_ref,
    left_a_ref,
    left_b_ref,
    right_a_ref,
    right_b_ref,
    gate_ref,
    hat_mid_ref,
    scale_mid_ref,
    edge_out_ref,
    hat_y_ref,
    scale_y_ref,
    x_half_ref,
    update_ref,
    cot_ref,
    grad_y_ref,
    gain_part_ref,
    grad_pair_ref,
    grad_gains_ref,
    grad_edge_ref,
    grad_gate_w_ref,
    grad_out_w_ref,
    grad_middle_ref,
    grad_product_ref,
    grad_proj_ref,
    x_sum_ref,
    out_sum_ref,
):
    channels = gains_ref.shape[1]
    blocks = size // ROW_BLOCK
    rows_of, columns_of = block_tools(size)
    gain_x = gains_ref[0:1, :]
    gain_mid = gains_ref[1:2, :]
    gain_y = gains_ref[2:3, :]

    x_sum_ref[...] = jnp.zeros(x_sum_ref.shape, FULL)
    out_sum_ref[...] = jnp.zeros(out_sum_ref.shape, FULL)

    def middle_back(at, carry):
        rows = rows_of(at)
        grad_y = columns_of(grad_y_ref, at)
        grad_middle = cot_ref[rows, :] + kernel_norm_back(
            grad_y, hat_y_ref[rows, :], scale_y_ref[rows, :], gain_y
        )
        grad_middle_ref[rows, :] = grad_middle
        gate = gate_ref[rows, :]
        gated = grad_middle * gate
        grad_edge_out = gated.astype(HALF)
        grad_gate = (gated * edge_out_ref[rows, :] * (1.0 - gate)).astype(HALF)
        grad_proj_ref[rows, 4 * channels :] = grad_gate
        x_sum_ref[:, 4 * channels :] += dot_tn(x_half_ref[rows, :], grad_gate)
        out_sum_ref[...] += dot_tn(update_ref[rows, :], grad_edge_out)
        grad_update = dot_nt(grad_edge_out, out_w_ref[...])
        grad_product = kernel_norm_back(grad_update, hat_mid_ref[rows, :], scale_mid_ref[rows, :], gain_mid)
        grad_product_ref[rows, :] = grad_product.astype(HALF).astype(FULL)
        return carry

    lax.fori_loop(0, blocks, middle_back, 0, unroll=2)

    def edges_back(at, carry):
        rows = rows_of(at)
        x_half = x_half_ref[rows, :]
        for side, (first_ref, second_ref, strides, other_ref) in enumerate(
            (
                (left_a_ref, left_b_ref, (1, size), right_ref),
                (right_a_ref, right_b_ref, (size, 1), left_ref),
            )
        ):
            grad = outer_sum(size, at, grad_product_ref, *strides, other_ref)
            both = jnp.concatenate(
                [(grad * first_ref[rows, :]).astype(HALF), (grad * second_ref[rows, :]).astype(HALF)], axis=1
            )
            place = slice(2 * side * channels, 2 * (side + 1) * channels)
            grad_proj_ref[rows, place] = both
            x_sum_ref[:, place] += dot_tn(x_half, both)
        return carry

    lax.fori_loop(0, blocks, edges_back, 0, unroll=2)

    inverse = 1.0 / size
    x_sum = x_sum_ref[...] * inverse
    edge_sum, gate_sum = x_sum[:, : 4 * channels], x_sum[:, 4 * channels :]
    grad_edge_ref[...] = edge_sum
    grad_gate_w_ref[...] = gate_sum
    out_sum = out_sum_ref[...] * inverse
    grad_out_w_ref[...] = out_sum
    grad_gains_ref[0:1, :] = gain_sum(((edge_w_ref[...], edge_sum), (gate_w_ref[...], gate_sum))) / gain_x
    grad_gains_ref[1:2, :] = gain_sum(((out_w_ref[...], out_sum),)) / gain_mid
    grad_gains_ref[2:3, :] = gain_part_ref[...] / gain_y

    own_cells = size * size // devices
    own = pl.ds(pl.multiple_of(lax.axis_index("dap") * own_cells, own_cells), own_cells)
    hat, scale = kernel_norm(pair_ref[...].reshape(own_cells, channels).astype(FULL))
    grad_x = dot_nt(grad_proj_ref[own, : 4 * channels], edge_w_ref[...])
    grad_x = grad_x + dot_nt(grad_proj_ref[own, 4 * channels :], gate_w_ref[...])
    grad_pair = grad_middle_ref[own, :] + kernel_norm_back(grad_x, hat, scale, gain_x)
    grad_pair_ref[...] = grad_pair.astype(grad_pair_ref.dtype)


def kernel_norm(values):
    center = values - lane_mean(values)
    scale = lax.rsqrt(lane_mean(center * center) + epsilon)
    return center * scale, scale


def kernel_norm_back(grad_out, hat, scale, gain):
    scaled = grad_out * gain
    return scale * (scaled - lane_mean(scaled) - hat * lane_mean(scaled * hat))


def bytes_of(arrays):
    return sum(math.prod(shape) * jnp.dtype(dtype).itemsize for shape, dtype in arrays)


def run_kernel(kernel, operands, outs, scratch, seconds, lengths_at=None):
    vmem = pl.BlockSpec(memory_space=pltpu.VMEM)
    in_specs = [vmem] * len(operands)
    if lengths_at is not None:
        in_specs[lengths_at] = pl.BlockSpec(memory_space=pltpu.SMEM)
    return pl.pallas_call(
        kernel,
        out_shape=[jax.ShapeDtypeStruct(*out) for out in outs],
        in_specs=in_specs,
        out_specs=[vmem] * len(outs),
        scratch_shapes=[pltpu.VMEM(*part) for part in scratch],
        compiler_params=pltpu.CompilerParams(vmem_limit_bytes=bytes_of(scratch) + VMEM_SLACK),
        cost_estimate=pl.CostEstimate(flops=0, bytes_accessed=int(seconds * 3.6e12), transcendentals=0),
    )(*operands)


def replicated_plan(
    axis_size,
    pair_map,
    cotangent,
    lengths,
    norm_gains,
    edge_weight,
    mult_gate_weight,
    mult_out_weight,
    attention_weight,
    bias_weight,
    attention_out_weight,
):
    _, size, channels = pair_map.shape
    cells, lanes = size * size, HEADS * size
    bits = axis_size.bit_length() - 1
    far_step = 1 << (bits - 1)
    near_steps = range(2, far_step, 2)

    def swapped(held, mask):
        return lax.ppermute(held, "dap", [(d, d ^ mask) for d in range(axis_size)])

    own = jnp.stack([pair_map, cotangent])
    held = jnp.stack([own, swapped(own, far_step)])
    masks = [0, far_step]
    near = jnp.concatenate([held] + [swapped(held, step) for step in near_steps], axis=0)
    masks = masks + [mask ^ step for step in near_steps for mask in masks]
    far = swapped(near, 1)

    full, half = ((cells, channels), FULL), ((cells, channels), HALF)
    square, wide = ((channels, channels), FULL), ((channels, 4 * channels), FULL)
    *kept, y, x_half, update = run_kernel(
        functools.partial(multiply_kernel, size, masks),
        (near, far, lengths, norm_gains, edge_weight, mult_gate_weight, mult_out_weight),
        [full] * 13 + [half] * 2,
        [full] * 2,
        5e-6,
        2,
    )
    projections = run_kernel(
        functools.partial(project_kernel, size),
        (y, attention_weight, bias_weight.T),
        [full, ((size, lanes), FULL)] + [half] * 4 + [((lanes, channels), HALF)],
        [],
        2e-6,
    )
    cot, grad_y, grad_att_w, grad_bias, grad_att_out, gain_part = run_kernel(
        functools.partial(attend_kernel, size, masks),
        (near, far, lengths, attention_weight, attention_out_weight, *projections),
        [full, full, wide, ((HEADS, channels), FULL), square, ((1, channels), FULL)],
        [half] * 2 + [((cells, 4 * channels + lanes), HALF), ((size, lanes), FULL)],
        7e-6,
        2,
    )
    grad_pair, grad_gains, grad_edge, grad_gate_w, grad_out_w = run_kernel(
        functools.partial(edges_kernel, size, axis_size),
        (pair_map, norm_gains, edge_weight, mult_gate_weight, mult_out_weight, *kept, x_half, update, cot, grad_y, gain_part),
        [((cells // axis_size, channels), HALF), ((3, channels), FULL), wide, square, square],
        [full] * 2 + [((cells, 5 * channels), HALF), ((channels, 5 * channels), FULL), square],
        6e-6,
    )
    return (
        grad_pair.reshape(pair_map.shape),
        grad_gains,
        grad_edge,
        grad_gate_w,
        grad_out_w,
        grad_att_w,
        grad_bias.T,
        grad_att_out,
    )


def per_device(axis_size, pair_map, *rest):
    _, size, channels = pair_map.shape
    fits = size % ROW_BLOCK == 0 and 25 * bytes_of([((size, size, channels), FULL)]) <= VMEM_SHARE
    if fits and axis_size >= 8 and axis_size & (axis_size - 1) == 0:
        return replicated_plan(axis_size, pair_map, *rest)
    return distributed_plan(pair_map, *rest)


def solution(mesh):
    return jax.shard_map(
        functools.partial(per_device, mesh.shape["dap"]),
        mesh=mesh,
        in_specs=(
            P(("groups", "dap"), None, None),
            P(("groups", "dap"), None, None),
            P("groups"),
            P(),
            P(),
            P(),
            P(),
            P(),
            P(),
            P(),
        ),
        out_specs=(
            P(("groups", "dap"), None, None),
            P("groups", None),
            P("groups", None),
            P("groups", None),
            P("groups", None),
            P("groups", None),
            P("groups", None),
            P("groups", None),
        ),
        check_vma=False,
    )
```

```python
import functools
import math

import jax
import jax.numpy as jnp
from jax import lax
from jax.experimental import pallas as pl
from jax.experimental.pallas import tpu as pltpu
from jax.sharding import PartitionSpec as P

HEADS = 4
HEAD_DIM = 32


epsilon = 1e-05


def norm_forward(values, gain_row):
    center = values - jnp.mean(values, axis=-1, keepdims=True)
    inv_std = lax.rsqrt(jnp.mean(center * center, axis=-1, keepdims=True) + epsilon)
    normed = center * inv_std
    return (normed * gain_row, normed, inv_std)


def norm_backward(grad_out, normed, inv_std, gain_row):
    scaled = grad_out * gain_row
    first_mean = jnp.mean(scaled, axis=-1, keepdims=True)
    second_mean = jnp.mean(scaled * normed, axis=-1, keepdims=True)
    return inv_std * (scaled - first_mean - normed * second_mean)


def distributed_plan(
    pair_map,
    cotangent,
    lengths,
    norm_gains,
    edge_weight,
    mult_gate_weight,
    mult_out_weight,
    attention_weight,
    bias_weight,
    attention_out_weight,
):
    row_count, full_size, channels = pair_map.shape
    inner_width = HEADS * HEAD_DIM
    head_scale = 1.0 / math.sqrt(HEAD_DIM)
    first_row = lax.axis_index("dap") * row_count
    real_count = lengths[0]
    valid_all = (jnp.arange(full_size) < real_count).astype(jnp.float32)
    valid_rows = (first_row + jnp.arange(row_count) < real_count).astype(jnp.float32)
    mask_pair = (valid_rows[:, None] * valid_all[None, :])[:, :, None]
    pair_f32 = pair_map.astype(jnp.float32)
    normed_full, hat_in, scale_in = norm_forward(pair_f32, norm_gains[0])
    normed_x = normed_full.astype(jnp.bfloat16)
    projected = jnp.einsum("rnc,cf->rnf", normed_x, edge_weight, preferred_element_type=jnp.float32)
    left_gate = projected[..., :channels]
    left_value = projected[..., channels : 2 * channels]
    right_gate = projected[..., 2 * channels : 3 * channels]
    right_value = projected[..., 3 * channels :]
    left_sig = jax.nn.sigmoid(left_gate)
    right_sig = jax.nn.sigmoid(right_gate)
    left_edges = (mask_pair * left_sig * left_value).astype(jnp.bfloat16)
    right_edges = (mask_pair * right_sig * right_value).astype(jnp.bfloat16)
    product = jnp.einsum(
        "ikc,jkc->ijc",
        left_edges,
        lax.all_gather(right_edges, "dap", axis=0, tiled=True),
        preferred_element_type=jnp.float32,
    )
    update_full, hat_mid, scale_mid = norm_forward(product, norm_gains[1])
    update = update_full.astype(jnp.bfloat16)
    edge_out = jnp.einsum(
        "rnc,cf->rnf", update, mult_out_weight, preferred_element_type=jnp.float32
    )
    gate_sig = jax.nn.sigmoid(
        jnp.einsum("rnc,cf->rnf", normed_x, mult_gate_weight, preferred_element_type=jnp.float32)
    )
    middle = pair_f32 + gate_sig * edge_out
    normed_mid, hat_attn, scale_attn = norm_forward(middle, norm_gains[2])
    normed_y = normed_mid.astype(jnp.bfloat16)
    bias_local = jnp.einsum(
        "kic,ch->hki", normed_y, bias_weight, preferred_element_type=jnp.float32
    ).astype(jnp.bfloat16)
    bias_whole = lax.all_gather(bias_local, "dap", axis=1, tiled=True)
    bias_query = jnp.swapaxes(bias_whole, 1, 2).astype(jnp.float32)
    column_y, column_cot = (
        lax.all_to_all(normed_y, "dap", split_axis=1, concat_axis=0, tiled=True),
        lax.all_to_all(cotangent, "dap", split_axis=1, concat_axis=0, tiled=True),
    )
    packed = jnp.einsum(
        "ijc,cf->ijf", column_y, attention_weight, preferred_element_type=jnp.float32
    )
    packed = packed.reshape(full_size, row_count, 4, HEADS, HEAD_DIM)
    query_vectors = (packed[:, :, 0] * head_scale).astype(jnp.bfloat16)
    key_vectors = packed[:, :, 1].astype(jnp.bfloat16)
    value_vectors = packed[:, :, 2].astype(jnp.bfloat16)
    att_gate = jax.nn.sigmoid(packed[:, :, 3])
    scores = (
        jnp.einsum(
            "ijhd,kjhd->jhik", query_vectors, key_vectors, preferred_element_type=jnp.float32
        )
        + bias_query[None]
    )
    exp_scores = valid_all * jnp.exp(scores)
    attention = exp_scores / jnp.sum(exp_scores, axis=-1, keepdims=True)
    attention_half = attention.astype(jnp.bfloat16)
    attended = jnp.einsum(
        "jhik,kjhd->ijhd", attention_half, value_vectors, preferred_element_type=jnp.float32
    )
    gated = (att_gate * attended).astype(jnp.bfloat16).reshape(full_size, row_count, inner_width)
    part_attn_out = jnp.einsum("ijf,ijc->fc", gated, column_cot, preferred_element_type=jnp.float32)
    grad_gated = jnp.einsum(
        "ijc,fc->ijf", column_cot, attention_out_weight, preferred_element_type=jnp.float32
    )
    grad_gated = grad_gated.reshape(full_size, row_count, HEADS, HEAD_DIM)
    grad_att = (grad_gated * att_gate).astype(jnp.bfloat16)
    grad_gate_pre = grad_gated * attended * att_gate * (1.0 - att_gate)
    grad_attention = jnp.einsum(
        "ijhd,kjhd->jhik", grad_att, value_vectors, preferred_element_type=jnp.float32
    )
    row_dots = jnp.transpose(jnp.sum(grad_att.astype(jnp.float32) * attended, axis=-1), (1, 2, 0))
    grad_scores = attention * (grad_attention - row_dots[..., None])
    scores_half = grad_scores.astype(jnp.bfloat16)
    grad_query = jnp.einsum(
        "jhik,kjhd->ijhd", scores_half, key_vectors, preferred_element_type=jnp.float32
    )
    grad_key = jnp.einsum(
        "jhik,ijhd->kjhd", scores_half, query_vectors, preferred_element_type=jnp.float32
    )
    grad_value = jnp.einsum(
        "jhik,ijhd->kjhd", attention_half, grad_att, preferred_element_type=jnp.float32
    )
    grad_packed = jnp.stack([grad_query * head_scale, grad_key, grad_value, grad_gate_pre], axis=2)
    grad_packed = grad_packed.reshape(full_size, row_count, 4 * inner_width).astype(jnp.bfloat16)
    part_attention = jnp.einsum(
        "ijc,ijf->cf", column_y, grad_packed, preferred_element_type=jnp.float32
    )
    column_grad = jnp.einsum(
        "ijf,cf->ijc", grad_packed, attention_weight, preferred_element_type=jnp.float32
    ).astype(jnp.bfloat16)
    row_grad = lax.all_to_all(column_grad, "dap", split_axis=0, concat_axis=1, tiled=True)
    score_sums = jnp.sum(grad_scores, axis=0)
    taken = score_sums
    bias_half = lax.psum_scatter(
        jnp.transpose(taken, (2, 0, 1)), "dap", scatter_dimension=0, tiled=True
    ).astype(jnp.bfloat16)
    part_bias = jnp.einsum("kic,khi->ch", normed_y, bias_half, preferred_element_type=jnp.float32)
    grad_normed_y = row_grad.astype(jnp.float32) + jnp.einsum(
        "khi,ch->kic", bias_half, bias_weight, preferred_element_type=jnp.float32
    )
    part_gain_attn = jnp.sum(grad_normed_y * hat_attn, axis=(0, 1))
    grad_middle = cotangent.astype(jnp.float32) + norm_backward(
        grad_normed_y, hat_attn, scale_attn, norm_gains[2]
    )
    grad_edge_out = (grad_middle * gate_sig).astype(jnp.bfloat16)
    grad_gate = (grad_middle * edge_out * gate_sig * (1.0 - gate_sig)).astype(jnp.bfloat16)
    part_mult_out = jnp.einsum(
        "rnc,rnf->cf", update, grad_edge_out, preferred_element_type=jnp.float32
    )
    part_mult_gate = jnp.einsum(
        "rnc,rnf->cf", normed_x, grad_gate, preferred_element_type=jnp.float32
    )
    grad_update = jnp.einsum(
        "rnf,cf->rnc", grad_edge_out, mult_out_weight, preferred_element_type=jnp.float32
    )
    part_gain_mid = jnp.sum(grad_update * hat_mid, axis=(0, 1))
    grad_product = norm_backward(grad_update, hat_mid, scale_mid, norm_gains[1]).astype(
        jnp.bfloat16
    )
    taken = grad_product
    grad_left = jnp.einsum(
        "ijc,jkc->ikc",
        taken,
        lax.all_gather(right_edges, "dap", axis=0, tiled=True),
        preferred_element_type=jnp.float32,
    )
    grad_cols = lax.all_to_all(grad_product, "dap", split_axis=1, concat_axis=0, tiled=True)
    taken = grad_cols
    grad_right = jnp.einsum(
        "ijc,ikc->jkc",
        taken,
        lax.all_gather(left_edges, "dap", axis=0, tiled=True),
        preferred_element_type=jnp.float32,
    )
    grad_proj = jnp.concatenate(
        [
            grad_left * mask_pair * left_value * left_sig * (1.0 - left_sig),
            grad_left * mask_pair * left_sig,
            grad_right * mask_pair * right_value * right_sig * (1.0 - right_sig),
            grad_right * mask_pair * right_sig,
        ],
        axis=-1,
    ).astype(jnp.bfloat16)
    part_edge = jnp.einsum("rnc,rnf->cf", normed_x, grad_proj, preferred_element_type=jnp.float32)
    grad_normed_x = jnp.einsum(
        "rnf,cf->rnc", grad_proj, edge_weight, preferred_element_type=jnp.float32
    )
    grad_normed_x = grad_normed_x + jnp.einsum(
        "rnf,cf->rnc", grad_gate, mult_gate_weight, preferred_element_type=jnp.float32
    )
    part_gain_in = jnp.sum(grad_normed_x * hat_in, axis=(0, 1))
    grad_pair = (
        grad_middle + norm_backward(grad_normed_x, hat_in, scale_in, norm_gains[0])
    ).astype(jnp.bfloat16)
    totals = lax.psum(
        (
            part_gain_in,
            part_gain_mid,
            part_edge,
            part_mult_gate,
            part_mult_out,
            part_gain_attn,
            part_attention,
            part_bias,
            part_attn_out,
        ),
        "dap",
    )
    (
        gain_in_sum,
        gain_mid_sum,
        edge_sum,
        mult_gate_sum,
        mult_out_sum,
        gain_attn_sum,
        attention_sum,
        bias_sum,
        attn_out_sum,
    ) = totals
    inverse = 1.0 / full_size
    grad_gains = jnp.stack([gain_in_sum, gain_mid_sum, gain_attn_sum]) * inverse
    return (
        grad_pair,
        grad_gains,
        edge_sum * inverse,
        mult_gate_sum * inverse,
        mult_out_sum * inverse,
        attention_sum * inverse,
        bias_sum * inverse,
        attn_out_sum * inverse,
    )


ROW_BLOCK = 8
VMEM_SLACK = 8 * 2**20
VMEM_SHARE = 32 * 2**20
HALF = jnp.bfloat16
FULL = jnp.float32


def dot_nn(left, right):
    return lax.dot_general(left, right, (((1,), (0,)), ((), ())), preferred_element_type=FULL)


def dot_nt(left, right):
    return lax.dot_general(left, right, (((1,), (1,)), ((), ())), preferred_element_type=FULL)


def dot_tn(left, right):
    return lax.dot_general(left, right, (((0,), (0,)), ((), ())), preferred_element_type=FULL)


def dot_wide(values, ones):
    high = values.astype(HALF)
    low = (values - high.astype(FULL)).astype(HALF)
    return dot_nn(jnp.concatenate([high, low], axis=1), jnp.concatenate([ones, ones], axis=0))


def lane_mean(values):
    return jnp.mean(values, axis=-1, keepdims=True)


def sigmoid(values):
    return pltpu.reciprocal(1.0 + jnp.exp(-values), approx=True)


def head_blocks(row_width, col_width, dtype):
    shape = (HEADS * row_width, HEADS * col_width)
    row = lax.broadcasted_iota(jnp.int32, shape, 0)
    col = lax.broadcasted_iota(jnp.int32, shape, 1)
    same = None
    for h in range(HEADS):
        here = (row >= h * row_width) & (row < (h + 1) * row_width)
        here = here & (col >= h * col_width) & (col < (h + 1) * col_width)
        same = here if same is None else same | here
    return jnp.where(same, 1.0, 0.0).astype(dtype)


def place_rows(target, part, near_ref, far_ref, masks):
    me = lax.axis_index("dap")
    cells = target.shape[0] // (2 * len(masks))
    for other, blocks in enumerate((near_ref, far_ref)):
        for at, mask in enumerate(masks):
            place = pl.ds(pl.multiple_of((me ^ mask ^ other) * cells, cells), cells)
            target[place, :] = blocks[at, part].reshape(cells, target.shape[1]).astype(FULL)


def block_tools(size):
    block = ROW_BLOCK * size

    def rows_of(at):
        return pl.ds(pl.multiple_of(at * block, block), block)

    def columns_of(ref, at):
        return jnp.concatenate(
            [ref[pl.ds(at * ROW_BLOCK + a, size, stride=size), :] for a in range(ROW_BLOCK)], axis=0
        )

    return rows_of, columns_of


def outer_sum(size, at, row_ref, row_stride, block_stride, block_ref):
    sums = [jnp.zeros((size, block_ref.shape[1]), FULL)] * ROW_BLOCK
    for k in range(size):
        whole = block_ref[k * size : (k + 1) * size, :]
        for a in range(ROW_BLOCK):
            row = (at * ROW_BLOCK + a) * block_stride + k * row_stride
            sums[a] = sums[a] + row_ref[pl.ds(row, 1), :] * whole
    return jnp.concatenate(sums, axis=0)


def same_cell_of(size):
    row = lax.broadcasted_iota(jnp.int32, (size, HEADS * size), 0)
    lane = lax.broadcasted_iota(jnp.int32, (size, HEADS * size), 1)
    same = lane == row
    for h in range(1, HEADS):
        same = same | (lane == row + h * size)
    return jnp.where(same, 1.0, 0.0)


def real_lanes(size, real):
    lane = lax.broadcasted_iota(jnp.int32, (1, HEADS * size), 1)
    inside = lane < real
    for h in range(1, HEADS):
        inside = inside | ((lane >= h * size) & (lane < h * size + real))
    return jnp.where(inside, 1.0, 0.0)


def spread_bias_weight(target, bias_w_ref, size):
    bias_rows = bias_w_ref[...].astype(FULL)
    for h in range(HEADS):
        target[h * size : (h + 1) * size, :] = jnp.broadcast_to(
            bias_rows[h : h + 1], (size, bias_rows.shape[1])
        ).astype(HALF)


def multiply_kernel(
    size,
    masks,
    near_ref,
    far_ref,
    lengths_ref,
    gains_ref,
    edge_w_ref,
    gate_w_ref,
    out_w_ref,
    left_ref,
    right_ref,
    left_a_ref,
    left_b_ref,
    right_a_ref,
    right_b_ref,
    gate_ref,
    hat_mid_ref,
    scale_mid_ref,
    edge_out_ref,
    hat_y_ref,
    scale_y_ref,
    y_ref,
    x_half_ref,
    update_ref,
    pair_ref,
    right_t_ref,
):
    channels = gains_ref.shape[1]
    block = ROW_BLOCK * size
    blocks = size // ROW_BLOCK
    rows_of, columns_of = block_tools(size)
    real = lengths_ref[0]
    gain_x = gains_ref[0:1, :]
    gain_mid = gains_ref[1:2, :]
    gain_y = gains_ref[2:3, :]
    place_rows(pair_ref, 0, near_ref, far_ref, masks)

    def project(at, carry):
        rows = rows_of(at)
        hat, _ = kernel_norm(pair_ref[rows, :])
        normed = (hat * gain_x).astype(HALF)
        x_half_ref[rows, :] = normed
        projected = dot_nn(normed, edge_w_ref[...])
        gate_ref[rows, :] = sigmoid(dot_nn(normed, gate_w_ref[...]))
        shape = (ROW_BLOCK, size, channels)
        row = lax.broadcasted_iota(jnp.int32, shape, 0) + at * ROW_BLOCK
        col = lax.broadcasted_iota(jnp.int32, shape, 1)
        mask = jnp.where((row < real) & (col < real), 1.0, 0.0).reshape(block, channels)
        for side, (edge, first, second) in enumerate(
            ((left_ref, left_a_ref, left_b_ref), (right_ref, right_a_ref, right_b_ref))
        ):
            base = 2 * side * channels
            sig = sigmoid(projected[:, base : base + channels])
            value = projected[:, base + channels : base + 2 * channels]
            masked = mask * sig
            product = masked * value
            edge[rows, :] = product.astype(HALF).astype(FULL)
            first[rows, :] = product * (1.0 - sig)
            second[rows, :] = masked
        return carry

    lax.fori_loop(0, blocks, project, 0, unroll=4)

    def turn(at, carry):
        right_t_ref[rows_of(at), :] = columns_of(right_ref, at)
        return carry

    lax.fori_loop(0, blocks, turn, 0, unroll=4)

    def multiply(at, carry):
        rows = rows_of(at)
        product = outer_sum(size, at, left_ref, 1, size, right_t_ref)
        hat, scale = kernel_norm(product)
        hat_mid_ref[rows, :] = hat
        scale_mid_ref[rows, :] = jnp.broadcast_to(scale, hat.shape)
        update = (hat * gain_mid).astype(HALF)
        update_ref[rows, :] = update
        edge_out = dot_nn(update, out_w_ref[...])
        edge_out_ref[rows, :] = edge_out
        middle = pair_ref[rows, :] + gate_ref[rows, :] * edge_out
        hat, scale = kernel_norm(middle)
        hat_y_ref[rows, :] = hat
        scale_y_ref[rows, :] = jnp.broadcast_to(scale, hat.shape)
        y_ref[rows, :] = hat * gain_y
        return carry

    lax.fori_loop(0, blocks, multiply, 0, unroll=4)


def project_kernel(
    size,
    y_ref,
    att_w_ref,
    bias_w_ref,
    att_gate_ref,
    bias_ref,
    y_t_ref,
    query_ref,
    key_ref,
    value_ref,
    bias_rep_ref,
):
    channels = y_ref.shape[1]
    lanes = HEADS * size
    head_scale = 1.0 / math.sqrt(HEAD_DIM)
    rows_of, columns_of = block_tools(size)
    same_cell = same_cell_of(size)
    spread_bias_weight(bias_rep_ref, bias_w_ref, size)

    def prepare(at, carry):
        rows = rows_of(at)
        y = columns_of(y_ref, at).astype(HALF)
        y_t_ref[rows, :] = y
        packed = dot_nn(y, att_w_ref[...])
        query_ref[rows, :] = (packed[:, :channels] * head_scale).astype(HALF)
        key_ref[rows, :] = packed[:, channels : 2 * channels].astype(HALF)
        value_ref[rows, :] = packed[:, 2 * channels : 3 * channels].astype(HALF)
        att_gate_ref[rows, :] = sigmoid(packed[:, 3 * channels :])
        spread = dot_nt(y, bias_rep_ref[...]).astype(HALF).astype(FULL)
        spread = spread.reshape(ROW_BLOCK, size, lanes) * same_cell[None]
        bias_ref[pl.ds(at * ROW_BLOCK, ROW_BLOCK), :] = jnp.sum(spread, axis=1)
        return carry

    lax.fori_loop(0, size // ROW_BLOCK, prepare, 0, unroll=4)


def attend_kernel(
    size,
    masks,
    near_ref,
    far_ref,
    lengths_ref,
    att_w_ref,
    att_out_w_ref,
    att_gate_ref,
    bias_ref,
    y_t_ref,
    query_ref,
    key_ref,
    value_ref,
    bias_rep_ref,
    cot_ref,
    grad_y_ref,
    grad_att_w_ref,
    grad_bias_ref,
    grad_att_out_ref,
    gain_part_ref,
    cot_t_ref,
    gated_ref,
    grad_packed_ref,
    bias_grad_ref,
):
    channels = cot_ref.shape[1]
    block = ROW_BLOCK * size
    blocks = size // ROW_BLOCK
    lanes = HEADS * size
    head_scale = 1.0 / math.sqrt(HEAD_DIM)
    rows_of, columns_of = block_tools(size)
    same_cell = same_cell_of(size)
    valid = real_lanes(size, lengths_ref[0])
    place_rows(cot_ref, 1, near_ref, far_ref, masks)

    head_mask = head_blocks(size, HEAD_DIM, HALF)
    head_mask_full = head_blocks(size, HEAD_DIM, FULL)
    no_mask = jnp.zeros((lanes, channels), HALF)
    no_rows = jnp.zeros((size, channels), HALF)
    key_ones = head_blocks(size, size, HALF)
    dim_ones = head_blocks(HEAD_DIM, size, HALF)

    def attend(at, score_sum):
        rows = rows_of(at)
        parts = [slice(a * size, (a + 1) * size) for a in range(ROW_BLOCK)]
        query, key, value = (ref[rows, :] for ref in (query_ref, key_ref, value_ref))
        gate = att_gate_ref[rows, :]
        cot = columns_of(cot_ref, at).astype(HALF)
        cot_t_ref[rows, :] = cot
        grad_gated = dot_nt(cot, att_out_w_ref[...])
        grad_att = (grad_gated * gate).astype(HALF)
        keys = [jnp.concatenate([key[p]] * HEADS, axis=0) * head_mask for p in parts]
        values = [jnp.concatenate([value[p]] * HEADS, axis=0) * head_mask for p in parts]
        bias = bias_ref[...]

        def products(p, a):
            both = jnp.concatenate(
                [
                    jnp.concatenate([keys[a], no_mask], axis=1),
                    jnp.concatenate([no_mask, values[a]], axis=1),
                ],
                axis=0,
            )
            return dot_nt(jnp.concatenate([query[p], grad_att[p]], axis=1), both)

        pairs = [products(p, a) for a, p in enumerate(parts)]
        scores = jnp.concatenate([pair[:, :lanes] + bias for pair in pairs], axis=0)
        grad_attention = jnp.concatenate([pair[:, lanes:] for pair in pairs], axis=0)
        exp_scores = valid * jnp.exp(scores)
        attention = exp_scores / dot_wide(exp_scores, key_ones)
        attention_half = attention.astype(HALF)
        attended = jnp.concatenate(
            [dot_nn(attention_half[p], values[a]) for a, p in enumerate(parts)], axis=0
        )
        row_dots = dot_wide(grad_att.astype(FULL) * attended, dim_ones)
        grad_scores = attention * (grad_attention - row_dots)
        scores_half = grad_scores.astype(HALF)
        for p in parts:
            score_sum = score_sum + grad_scores[p]
        grad_query = jnp.concatenate(
            [dot_nn(scores_half[p], keys[a]) for a, p in enumerate(parts)], axis=0
        )

        def key_sums(p):
            weights = jnp.concatenate([scores_half[p], attention_half[p]], axis=0)
            vectors = jnp.concatenate(
                [
                    jnp.concatenate([query[p], no_rows], axis=1),
                    jnp.concatenate([no_rows, grad_att[p]], axis=1),
                ],
                axis=0,
            )
            whole = dot_tn(weights, vectors)
            masked = [whole[:, :channels] * head_mask_full, whole[:, channels:] * head_mask_full]
            return [sum(part[h * size : (h + 1) * size] for h in range(HEADS)) for part in masked]

        per_key = [key_sums(p) for p in parts]
        grad_key = jnp.concatenate([pair[0] for pair in per_key], axis=0)
        grad_value = jnp.concatenate([pair[1] for pair in per_key], axis=0)
        gated = gate * attended
        gated_ref[rows, :] = gated.astype(HALF)
        grad_gate_pre = grad_gated * gated * (1.0 - gate)
        grad_packed = jnp.concatenate(
            [
                (grad_query * head_scale).astype(HALF),
                grad_key.astype(HALF),
                grad_value.astype(HALF),
                grad_gate_pre.astype(HALF),
            ],
            axis=1,
        )
        grad_packed_ref[rows, : 4 * channels] = grad_packed
        grad_y_ref[rows, :] = dot_nt(grad_packed, att_w_ref[...])
        return score_sum

    score_sum = lax.fori_loop(0, blocks, attend, jnp.zeros((size, lanes), FULL), unroll=4)
    bias_grad_ref[...] = score_sum.astype(HALF).astype(FULL)

    def spread_bias(at, carry):
        rows = rows_of(at)
        part = bias_grad_ref[pl.ds(at * ROW_BLOCK, ROW_BLOCK), :]
        spread = (part[:, None, :] * same_cell[None]).reshape(block, lanes).astype(HALF)
        grad_packed_ref[rows, 4 * channels :] = spread
        grad_y_ref[rows, :] += dot_nn(spread, bias_rep_ref[...])
        return carry

    lax.fori_loop(0, blocks, spread_bias, 0, unroll=4)

    inverse = 1.0 / size
    y_sum = dot_tn(y_t_ref[...], grad_packed_ref[...]) * inverse
    att_sum, bias_sum = y_sum[:, : 4 * channels], jnp.transpose(y_sum[:, 4 * channels :])
    grad_att_w_ref[...] = att_sum
    grad_att_out_ref[...] = dot_tn(gated_ref[...], cot_t_ref[...]) * inverse
    for h in range(HEADS):
        grad_bias_ref[h : h + 1, :] = jnp.sum(
            bias_sum[h * size : (h + 1) * size], axis=0, keepdims=True
        )
    bias_part = jnp.sum(bias_rep_ref[...].astype(FULL) * bias_sum, axis=0, keepdims=True)
    gain_part_ref[...] = gain_sum(((att_w_ref[...], att_sum),)) + bias_part


def gain_sum(pairs):
    total = sum(jnp.sum(weight.astype(FULL) * grad, axis=1, keepdims=True) for weight, grad in pairs)
    channels = total.shape[0]
    return jnp.transpose(jnp.broadcast_to(total, (channels, channels)))[0:1, :]


def edges_kernel(
    size,
    devices,
    pair_ref,
    gains_ref,
    edge_w_ref,
    gate_w_ref,
    out_w_ref,
    left_ref,
    right_ref,
    left_a_ref,
    left_b_ref,
    right_a_ref,
    right_b_ref,
    gate_ref,
    hat_mid_ref,
    scale_mid_ref,
    edge_out_ref,
    hat_y_ref,
    scale_y_ref,
    x_half_ref,
    update_ref,
    cot_ref,
    grad_y_ref,
    gain_part_ref,
    grad_pair_ref,
    grad_gains_ref,
    grad_edge_ref,
    grad_gate_w_ref,
    grad_out_w_ref,
    grad_middle_ref,
    grad_product_ref,
    grad_proj_ref,
    x_sum_ref,
    out_sum_ref,
):
    channels = gains_ref.shape[1]
    blocks = size // ROW_BLOCK
    rows_of, columns_of = block_tools(size)
    gain_x = gains_ref[0:1, :]
    gain_mid = gains_ref[1:2, :]
    gain_y = gains_ref[2:3, :]

    x_sum_ref[...] = jnp.zeros(x_sum_ref.shape, FULL)
    out_sum_ref[...] = jnp.zeros(out_sum_ref.shape, FULL)

    def middle_back(at, carry):
        rows = rows_of(at)
        grad_y = columns_of(grad_y_ref, at)
        grad_middle = cot_ref[rows, :] + kernel_norm_back(
            grad_y, hat_y_ref[rows, :], scale_y_ref[rows, :], gain_y
        )
        grad_middle_ref[rows, :] = grad_middle
        gate = gate_ref[rows, :]
        gated = grad_middle * gate
        grad_edge_out = gated.astype(HALF)
        grad_gate = (gated * edge_out_ref[rows, :] * (1.0 - gate)).astype(HALF)
        grad_proj_ref[rows, 4 * channels :] = grad_gate
        x_sum_ref[:, 4 * channels :] += dot_tn(x_half_ref[rows, :], grad_gate)
        out_sum_ref[...] += dot_tn(update_ref[rows, :], grad_edge_out)
        grad_update = dot_nt(grad_edge_out, out_w_ref[...])
        grad_product = kernel_norm_back(grad_update, hat_mid_ref[rows, :], scale_mid_ref[rows, :], gain_mid)
        grad_product_ref[rows, :] = grad_product.astype(HALF).astype(FULL)
        return carry

    lax.fori_loop(0, blocks, middle_back, 0, unroll=4)

    def edges_back(at, carry):
        rows = rows_of(at)
        x_half = x_half_ref[rows, :]
        for side, (first_ref, second_ref, strides, other_ref) in enumerate(
            (
                (left_a_ref, left_b_ref, (1, size), right_ref),
                (right_a_ref, right_b_ref, (size, 1), left_ref),
            )
        ):
            grad = outer_sum(size, at, grad_product_ref, *strides, other_ref)
            both = jnp.concatenate(
                [(grad * first_ref[rows, :]).astype(HALF), (grad * second_ref[rows, :]).astype(HALF)], axis=1
            )
            place = slice(2 * side * channels, 2 * (side + 1) * channels)
            grad_proj_ref[rows, place] = both
            x_sum_ref[:, place] += dot_tn(x_half, both)
        return carry

    lax.fori_loop(0, blocks, edges_back, 0, unroll=4)

    inverse = 1.0 / size
    x_sum = x_sum_ref[...] * inverse
    edge_sum, gate_sum = x_sum[:, : 4 * channels], x_sum[:, 4 * channels :]
    grad_edge_ref[...] = edge_sum
    grad_gate_w_ref[...] = gate_sum
    out_sum = out_sum_ref[...] * inverse
    grad_out_w_ref[...] = out_sum
    grad_gains_ref[0:1, :] = gain_sum(((edge_w_ref[...], edge_sum), (gate_w_ref[...], gate_sum))) / gain_x
    grad_gains_ref[1:2, :] = gain_sum(((out_w_ref[...], out_sum),)) / gain_mid
    grad_gains_ref[2:3, :] = gain_part_ref[...] / gain_y

    own_cells = size * size // devices
    own = pl.ds(pl.multiple_of(lax.axis_index("dap") * own_cells, own_cells), own_cells)
    hat, scale = kernel_norm(pair_ref[...].reshape(own_cells, channels).astype(FULL))
    grad_x = dot_nt(grad_proj_ref[own, : 4 * channels], edge_w_ref[...])
    grad_x = grad_x + dot_nt(grad_proj_ref[own, 4 * channels :], gate_w_ref[...])
    grad_pair = grad_middle_ref[own, :] + kernel_norm_back(grad_x, hat, scale, gain_x)
    grad_pair_ref[...] = grad_pair.astype(grad_pair_ref.dtype)


def kernel_norm(values):
    center = values - lane_mean(values)
    scale = lax.rsqrt(lane_mean(center * center) + epsilon)
    return center * scale, scale


def kernel_norm_back(grad_out, hat, scale, gain):
    scaled = grad_out * gain
    return scale * (scaled - lane_mean(scaled) - hat * lane_mean(scaled * hat))


def bytes_of(arrays):
    return sum(math.prod(shape) * jnp.dtype(dtype).itemsize for shape, dtype in arrays)


def run_kernel(kernel, operands, outs, scratch, seconds, lengths_at=None):
    vmem = pl.BlockSpec(memory_space=pltpu.VMEM)
    in_specs = [vmem] * len(operands)
    if lengths_at is not None:
        in_specs[lengths_at] = pl.BlockSpec(memory_space=pltpu.SMEM)
    return pl.pallas_call(
        kernel,
        out_shape=[jax.ShapeDtypeStruct(*out) for out in outs],
        in_specs=in_specs,
        out_specs=[vmem] * len(outs),
        scratch_shapes=[pltpu.VMEM(*part) for part in scratch],
        compiler_params=pltpu.CompilerParams(vmem_limit_bytes=bytes_of(scratch) + VMEM_SLACK),
        cost_estimate=pl.CostEstimate(flops=0, bytes_accessed=int(seconds * 3.6e12), transcendentals=0),
    )(*operands)


def replicated_plan(
    axis_size,
    pair_map,
    cotangent,
    lengths,
    norm_gains,
    edge_weight,
    mult_gate_weight,
    mult_out_weight,
    attention_weight,
    bias_weight,
    attention_out_weight,
):
    _, size, channels = pair_map.shape
    cells, lanes = size * size, HEADS * size
    bits = axis_size.bit_length() - 1
    far_step = 1 << (bits - 1)
    near_steps = range(2, far_step, 2)

    def swapped(held, mask):
        return lax.ppermute(held, "dap", [(d, d ^ mask) for d in range(axis_size)])

    own = jnp.stack([pair_map, cotangent])
    held = jnp.stack([own, swapped(own, far_step)])
    masks = [0, far_step]
    near = jnp.concatenate([held] + [swapped(held, step) for step in near_steps], axis=0)
    masks = masks + [mask ^ step for step in near_steps for mask in masks]
    far = swapped(near, 1)

    full, half = ((cells, channels), FULL), ((cells, channels), HALF)
    square, wide = ((channels, channels), FULL), ((channels, 4 * channels), FULL)
    *kept, y, x_half, update = run_kernel(
        functools.partial(multiply_kernel, size, masks),
        (near, far, lengths, norm_gains, edge_weight, mult_gate_weight, mult_out_weight),
        [full] * 13 + [half] * 2,
        [full] * 2,
        5e-6,
        2,
    )
    projections = run_kernel(
        functools.partial(project_kernel, size),
        (y, attention_weight, bias_weight.T),
        [full, ((size, lanes), FULL)] + [half] * 4 + [((lanes, channels), HALF)],
        [],
        2e-6,
    )
    cot, grad_y, grad_att_w, grad_bias, grad_att_out, gain_part = run_kernel(
        functools.partial(attend_kernel, size, masks),
        (near, far, lengths, attention_weight, attention_out_weight, *projections),
        [full, full, wide, ((HEADS, channels), FULL), square, ((1, channels), FULL)],
        [half] * 2 + [((cells, 4 * channels + lanes), HALF), ((size, lanes), FULL)],
        7e-6,
        2,
    )
    grad_pair, grad_gains, grad_edge, grad_gate_w, grad_out_w = run_kernel(
        functools.partial(edges_kernel, size, axis_size),
        (pair_map, norm_gains, edge_weight, mult_gate_weight, mult_out_weight, *kept, x_half, update, cot, grad_y, gain_part),
        [((cells // axis_size, channels), HALF), ((3, channels), FULL), wide, square, square],
        [full] * 2 + [((cells, 5 * channels), HALF), ((channels, 5 * channels), FULL), square],
        6e-6,
    )
    return (
        grad_pair.reshape(pair_map.shape),
        grad_gains,
        grad_edge,
        grad_gate_w,
        grad_out_w,
        grad_att_w,
        grad_bias.T,
        grad_att_out,
    )


def per_device(axis_size, pair_map, *rest):
    _, size, channels = pair_map.shape
    fits = size % ROW_BLOCK == 0 and 25 * bytes_of([((size, size, channels), FULL)]) <= VMEM_SHARE
    if fits and axis_size >= 8 and axis_size & (axis_size - 1) == 0:
        return replicated_plan(axis_size, pair_map, *rest)
    return distributed_plan(pair_map, *rest)


def solution(mesh):
    return jax.shard_map(
        functools.partial(per_device, mesh.shape["dap"]),
        mesh=mesh,
        in_specs=(
            P(("groups", "dap"), None, None),
            P(("groups", "dap"), None, None),
            P("groups"),
            P(),
            P(),
            P(),
            P(),
            P(),
            P(),
            P(),
        ),
        out_specs=(
            P(("groups", "dap"), None, None),
            P("groups", None),
            P("groups", None),
            P("groups", None),
            P("groups", None),
            P("groups", None),
            P("groups", None),
            P("groups", None),
        ),
        check_vma=False,
    )
```

```python
import functools
import math

import jax
import jax.numpy as jnp
from jax import lax
from jax.experimental import pallas as pl
from jax.experimental.pallas import tpu as pltpu
from jax.sharding import PartitionSpec as P

HEADS = 4
HEAD_DIM = 32


epsilon = 1e-05


def norm_forward(values, gain_row):
    center = values - jnp.mean(values, axis=-1, keepdims=True)
    inv_std = lax.rsqrt(jnp.mean(center * center, axis=-1, keepdims=True) + epsilon)
    normed = center * inv_std
    return (normed * gain_row, normed, inv_std)


def norm_backward(grad_out, normed, inv_std, gain_row):
    scaled = grad_out * gain_row
    first_mean = jnp.mean(scaled, axis=-1, keepdims=True)
    second_mean = jnp.mean(scaled * normed, axis=-1, keepdims=True)
    return inv_std * (scaled - first_mean - normed * second_mean)


def distributed_plan(
    pair_map,
    cotangent,
    lengths,
    norm_gains,
    edge_weight,
    mult_gate_weight,
    mult_out_weight,
    attention_weight,
    bias_weight,
    attention_out_weight,
):
    row_count, full_size, channels = pair_map.shape
    inner_width = HEADS * HEAD_DIM
    head_scale = 1.0 / math.sqrt(HEAD_DIM)
    first_row = lax.axis_index("dap") * row_count
    real_count = lengths[0]
    valid_all = (jnp.arange(full_size) < real_count).astype(jnp.float32)
    valid_rows = (first_row + jnp.arange(row_count) < real_count).astype(jnp.float32)
    mask_pair = (valid_rows[:, None] * valid_all[None, :])[:, :, None]
    pair_f32 = pair_map.astype(jnp.float32)
    normed_full, hat_in, scale_in = norm_forward(pair_f32, norm_gains[0])
    normed_x = normed_full.astype(jnp.bfloat16)
    projected = jnp.einsum("rnc,cf->rnf", normed_x, edge_weight, preferred_element_type=jnp.float32)
    left_gate = projected[..., :channels]
    left_value = projected[..., channels : 2 * channels]
    right_gate = projected[..., 2 * channels : 3 * channels]
    right_value = projected[..., 3 * channels :]
    left_sig = jax.nn.sigmoid(left_gate)
    right_sig = jax.nn.sigmoid(right_gate)
    left_edges = (mask_pair * left_sig * left_value).astype(jnp.bfloat16)
    right_edges = (mask_pair * right_sig * right_value).astype(jnp.bfloat16)
    product = jnp.einsum(
        "ikc,jkc->ijc",
        left_edges,
        lax.all_gather(right_edges, "dap", axis=0, tiled=True),
        preferred_element_type=jnp.float32,
    )
    update_full, hat_mid, scale_mid = norm_forward(product, norm_gains[1])
    update = update_full.astype(jnp.bfloat16)
    edge_out = jnp.einsum(
        "rnc,cf->rnf", update, mult_out_weight, preferred_element_type=jnp.float32
    )
    gate_sig = jax.nn.sigmoid(
        jnp.einsum("rnc,cf->rnf", normed_x, mult_gate_weight, preferred_element_type=jnp.float32)
    )
    middle = pair_f32 + gate_sig * edge_out
    normed_mid, hat_attn, scale_attn = norm_forward(middle, norm_gains[2])
    normed_y = normed_mid.astype(jnp.bfloat16)
    bias_local = jnp.einsum(
        "kic,ch->hki", normed_y, bias_weight, preferred_element_type=jnp.float32
    ).astype(jnp.bfloat16)
    bias_whole = lax.all_gather(bias_local, "dap", axis=1, tiled=True)
    bias_query = jnp.swapaxes(bias_whole, 1, 2).astype(jnp.float32)
    column_y, column_cot = (
        lax.all_to_all(normed_y, "dap", split_axis=1, concat_axis=0, tiled=True),
        lax.all_to_all(cotangent, "dap", split_axis=1, concat_axis=0, tiled=True),
    )
    packed = jnp.einsum(
        "ijc,cf->ijf", column_y, attention_weight, preferred_element_type=jnp.float32
    )
    packed = packed.reshape(full_size, row_count, 4, HEADS, HEAD_DIM)
    query_vectors = (packed[:, :, 0] * head_scale).astype(jnp.bfloat16)
    key_vectors = packed[:, :, 1].astype(jnp.bfloat16)
    value_vectors = packed[:, :, 2].astype(jnp.bfloat16)
    att_gate = jax.nn.sigmoid(packed[:, :, 3])
    scores = (
        jnp.einsum(
            "ijhd,kjhd->jhik", query_vectors, key_vectors, preferred_element_type=jnp.float32
        )
        + bias_query[None]
    )
    exp_scores = valid_all * jnp.exp(scores)
    attention = exp_scores / jnp.sum(exp_scores, axis=-1, keepdims=True)
    attention_half = attention.astype(jnp.bfloat16)
    attended = jnp.einsum(
        "jhik,kjhd->ijhd", attention_half, value_vectors, preferred_element_type=jnp.float32
    )
    gated = (att_gate * attended).astype(jnp.bfloat16).reshape(full_size, row_count, inner_width)
    part_attn_out = jnp.einsum("ijf,ijc->fc", gated, column_cot, preferred_element_type=jnp.float32)
    grad_gated = jnp.einsum(
        "ijc,fc->ijf", column_cot, attention_out_weight, preferred_element_type=jnp.float32
    )
    grad_gated = grad_gated.reshape(full_size, row_count, HEADS, HEAD_DIM)
    grad_att = (grad_gated * att_gate).astype(jnp.bfloat16)
    grad_gate_pre = grad_gated * attended * att_gate * (1.0 - att_gate)
    grad_attention = jnp.einsum(
        "ijhd,kjhd->jhik", grad_att, value_vectors, preferred_element_type=jnp.float32
    )
    row_dots = jnp.transpose(jnp.sum(grad_att.astype(jnp.float32) * attended, axis=-1), (1, 2, 0))
    grad_scores = attention * (grad_attention - row_dots[..., None])
    scores_half = grad_scores.astype(jnp.bfloat16)
    grad_query = jnp.einsum(
        "jhik,kjhd->ijhd", scores_half, key_vectors, preferred_element_type=jnp.float32
    )
    grad_key = jnp.einsum(
        "jhik,ijhd->kjhd", scores_half, query_vectors, preferred_element_type=jnp.float32
    )
    grad_value = jnp.einsum(
        "jhik,ijhd->kjhd", attention_half, grad_att, preferred_element_type=jnp.float32
    )
    grad_packed = jnp.stack([grad_query * head_scale, grad_key, grad_value, grad_gate_pre], axis=2)
    grad_packed = grad_packed.reshape(full_size, row_count, 4 * inner_width).astype(jnp.bfloat16)
    part_attention = jnp.einsum(
        "ijc,ijf->cf", column_y, grad_packed, preferred_element_type=jnp.float32
    )
    column_grad = jnp.einsum(
        "ijf,cf->ijc", grad_packed, attention_weight, preferred_element_type=jnp.float32
    ).astype(jnp.bfloat16)
    row_grad = lax.all_to_all(column_grad, "dap", split_axis=0, concat_axis=1, tiled=True)
    score_sums = jnp.sum(grad_scores, axis=0)
    taken = score_sums
    bias_half = lax.psum_scatter(
        jnp.transpose(taken, (2, 0, 1)), "dap", scatter_dimension=0, tiled=True
    ).astype(jnp.bfloat16)
    part_bias = jnp.einsum("kic,khi->ch", normed_y, bias_half, preferred_element_type=jnp.float32)
    grad_normed_y = row_grad.astype(jnp.float32) + jnp.einsum(
        "khi,ch->kic", bias_half, bias_weight, preferred_element_type=jnp.float32
    )
    part_gain_attn = jnp.sum(grad_normed_y * hat_attn, axis=(0, 1))
    grad_middle = cotangent.astype(jnp.float32) + norm_backward(
        grad_normed_y, hat_attn, scale_attn, norm_gains[2]
    )
    grad_edge_out = (grad_middle * gate_sig).astype(jnp.bfloat16)
    grad_gate = (grad_middle * edge_out * gate_sig * (1.0 - gate_sig)).astype(jnp.bfloat16)
    part_mult_out = jnp.einsum(
        "rnc,rnf->cf", update, grad_edge_out, preferred_element_type=jnp.float32
    )
    part_mult_gate = jnp.einsum(
        "rnc,rnf->cf", normed_x, grad_gate, preferred_element_type=jnp.float32
    )
    grad_update = jnp.einsum(
        "rnf,cf->rnc", grad_edge_out, mult_out_weight, preferred_element_type=jnp.float32
    )
    part_gain_mid = jnp.sum(grad_update * hat_mid, axis=(0, 1))
    grad_product = norm_backward(grad_update, hat_mid, scale_mid, norm_gains[1]).astype(
        jnp.bfloat16
    )
    taken = grad_product
    grad_left = jnp.einsum(
        "ijc,jkc->ikc",
        taken,
        lax.all_gather(right_edges, "dap", axis=0, tiled=True),
        preferred_element_type=jnp.float32,
    )
    grad_cols = lax.all_to_all(grad_product, "dap", split_axis=1, concat_axis=0, tiled=True)
    taken = grad_cols
    grad_right = jnp.einsum(
        "ijc,ikc->jkc",
        taken,
        lax.all_gather(left_edges, "dap", axis=0, tiled=True),
        preferred_element_type=jnp.float32,
    )
    grad_proj = jnp.concatenate(
        [
            grad_left * mask_pair * left_value * left_sig * (1.0 - left_sig),
            grad_left * mask_pair * left_sig,
            grad_right * mask_pair * right_value * right_sig * (1.0 - right_sig),
            grad_right * mask_pair * right_sig,
        ],
        axis=-1,
    ).astype(jnp.bfloat16)
    part_edge = jnp.einsum("rnc,rnf->cf", normed_x, grad_proj, preferred_element_type=jnp.float32)
    grad_normed_x = jnp.einsum(
        "rnf,cf->rnc", grad_proj, edge_weight, preferred_element_type=jnp.float32
    )
    grad_normed_x = grad_normed_x + jnp.einsum(
        "rnf,cf->rnc", grad_gate, mult_gate_weight, preferred_element_type=jnp.float32
    )
    part_gain_in = jnp.sum(grad_normed_x * hat_in, axis=(0, 1))
    grad_pair = (
        grad_middle + norm_backward(grad_normed_x, hat_in, scale_in, norm_gains[0])
    ).astype(jnp.bfloat16)
    totals = lax.psum(
        (
            part_gain_in,
            part_gain_mid,
            part_edge,
            part_mult_gate,
            part_mult_out,
            part_gain_attn,
            part_attention,
            part_bias,
            part_attn_out,
        ),
        "dap",
    )
    (
        gain_in_sum,
        gain_mid_sum,
        edge_sum,
        mult_gate_sum,
        mult_out_sum,
        gain_attn_sum,
        attention_sum,
        bias_sum,
        attn_out_sum,
    ) = totals
    inverse = 1.0 / full_size
    grad_gains = jnp.stack([gain_in_sum, gain_mid_sum, gain_attn_sum]) * inverse
    return (
        grad_pair,
        grad_gains,
        edge_sum * inverse,
        mult_gate_sum * inverse,
        mult_out_sum * inverse,
        attention_sum * inverse,
        bias_sum * inverse,
        attn_out_sum * inverse,
    )


ROW_BLOCK = 8
VMEM_SLACK = 8 * 2**20
VMEM_SHARE = 32 * 2**20
HALF = jnp.bfloat16
FULL = jnp.float32


def dot_nn(left, right):
    return lax.dot_general(left, right, (((1,), (0,)), ((), ())), preferred_element_type=FULL)


def dot_nt(left, right):
    return lax.dot_general(left, right, (((1,), (1,)), ((), ())), preferred_element_type=FULL)


def dot_tn(left, right):
    return lax.dot_general(left, right, (((0,), (0,)), ((), ())), preferred_element_type=FULL)


def dot_wide(values, ones):
    high = values.astype(HALF)
    low = (values - high.astype(FULL)).astype(HALF)
    return dot_nn(jnp.concatenate([high, low], axis=1), jnp.concatenate([ones, ones], axis=0))


def lane_mean(values):
    return jnp.mean(values, axis=-1, keepdims=True)


def sigmoid(values):
    return pltpu.reciprocal(1.0 + jnp.exp(-values), approx=True)


def head_blocks(row_width, col_width, dtype):
    shape = (HEADS * row_width, HEADS * col_width)
    row = lax.broadcasted_iota(jnp.int32, shape, 0)
    col = lax.broadcasted_iota(jnp.int32, shape, 1)
    same = None
    for h in range(HEADS):
        here = (row >= h * row_width) & (row < (h + 1) * row_width)
        here = here & (col >= h * col_width) & (col < (h + 1) * col_width)
        same = here if same is None else same | here
    return jnp.where(same, 1.0, 0.0).astype(dtype)


def place_rows(target, part, near_ref, far_ref, masks):
    me = lax.axis_index("dap")
    cells = target.shape[0] // (2 * len(masks))
    for other, blocks in enumerate((near_ref, far_ref)):
        for at, mask in enumerate(masks):
            place = pl.ds(pl.multiple_of((me ^ mask ^ other) * cells, cells), cells)
            target[place, :] = blocks[at, part].reshape(cells, target.shape[1]).astype(FULL)


def block_tools(size):
    block = ROW_BLOCK * size

    def rows_of(at):
        return pl.ds(pl.multiple_of(at * block, block), block)

    def columns_of(ref, at):
        return jnp.concatenate(
            [ref[pl.ds(at * ROW_BLOCK + a, size, stride=size), :] for a in range(ROW_BLOCK)], axis=0
        )

    return rows_of, columns_of


def outer_sum(size, at, row_ref, row_stride, block_stride, block_ref):
    sums = [jnp.zeros((size, block_ref.shape[1]), FULL)] * ROW_BLOCK
    for k in range(size):
        whole = block_ref[k * size : (k + 1) * size, :]
        for a in range(ROW_BLOCK):
            row = (at * ROW_BLOCK + a) * block_stride + k * row_stride
            sums[a] = sums[a] + row_ref[pl.ds(row, 1), :] * whole
    return jnp.concatenate(sums, axis=0)


def same_cell_of(size):
    row = lax.broadcasted_iota(jnp.int32, (size, HEADS * size), 0)
    lane = lax.broadcasted_iota(jnp.int32, (size, HEADS * size), 1)
    same = lane == row
    for h in range(1, HEADS):
        same = same | (lane == row + h * size)
    return jnp.where(same, 1.0, 0.0)


def real_lanes(size, real):
    lane = lax.broadcasted_iota(jnp.int32, (1, HEADS * size), 1)
    inside = lane < real
    for h in range(1, HEADS):
        inside = inside | ((lane >= h * size) & (lane < h * size + real))
    return jnp.where(inside, 1.0, 0.0)


def spread_bias_weight(target, bias_w_ref, size):
    bias_rows = bias_w_ref[...].astype(FULL)
    for h in range(HEADS):
        target[h * size : (h + 1) * size, :] = jnp.broadcast_to(
            bias_rows[h : h + 1], (size, bias_rows.shape[1])
        ).astype(HALF)


def multiply_kernel(
    size,
    masks,
    near_ref,
    far_ref,
    lengths_ref,
    gains_ref,
    edge_w_ref,
    gate_w_ref,
    out_w_ref,
    left_ref,
    right_ref,
    left_a_ref,
    left_b_ref,
    right_a_ref,
    right_b_ref,
    gate_ref,
    hat_mid_ref,
    scale_mid_ref,
    edge_out_ref,
    hat_y_ref,
    scale_y_ref,
    y_ref,
    x_half_ref,
    update_ref,
    pair_ref,
    right_t_ref,
):
    channels = gains_ref.shape[1]
    block = ROW_BLOCK * size
    blocks = size // ROW_BLOCK
    rows_of, columns_of = block_tools(size)
    real = lengths_ref[0]
    gain_x = gains_ref[0:1, :]
    gain_mid = gains_ref[1:2, :]
    gain_y = gains_ref[2:3, :]
    place_rows(pair_ref, 0, near_ref, far_ref, masks)

    def project(at, carry):
        rows = rows_of(at)
        hat, _ = kernel_norm(pair_ref[rows, :])
        normed = (hat * gain_x).astype(HALF)
        x_half_ref[rows, :] = normed
        projected = dot_nn(normed, edge_w_ref[...])
        gate_ref[rows, :] = sigmoid(dot_nn(normed, gate_w_ref[...]))
        shape = (ROW_BLOCK, size, channels)
        row = lax.broadcasted_iota(jnp.int32, shape, 0) + at * ROW_BLOCK
        col = lax.broadcasted_iota(jnp.int32, shape, 1)
        mask = jnp.where((row < real) & (col < real), 1.0, 0.0).reshape(block, channels)
        for side, (edge, first, second) in enumerate(
            ((left_ref, left_a_ref, left_b_ref), (right_ref, right_a_ref, right_b_ref))
        ):
            base = 2 * side * channels
            sig = sigmoid(projected[:, base : base + channels])
            value = projected[:, base + channels : base + 2 * channels]
            masked = mask * sig
            product = masked * value
            edge[rows, :] = product.astype(HALF).astype(FULL)
            first[rows, :] = product * (1.0 - sig)
            second[rows, :] = masked
        return carry

    lax.fori_loop(0, blocks, project, 0, unroll=4)

    def turn(at, carry):
        right_t_ref[rows_of(at), :] = columns_of(right_ref, at)
        return carry

    lax.fori_loop(0, blocks, turn, 0, unroll=4)

    def multiply(at, carry):
        rows = rows_of(at)
        product = outer_sum(size, at, left_ref, 1, size, right_t_ref)
        hat, scale = kernel_norm(product)
        hat_mid_ref[rows, :] = hat
        scale_mid_ref[rows, :] = jnp.broadcast_to(scale, hat.shape)
        update = (hat * gain_mid).astype(HALF)
        update_ref[rows, :] = update
        edge_out = dot_nn(update, out_w_ref[...])
        edge_out_ref[rows, :] = edge_out
        middle = pair_ref[rows, :] + gate_ref[rows, :] * edge_out
        hat, scale = kernel_norm(middle)
        hat_y_ref[rows, :] = hat
        scale_y_ref[rows, :] = jnp.broadcast_to(scale, hat.shape)
        y_ref[rows, :] = hat * gain_y
        return carry

    lax.fori_loop(0, blocks, multiply, 0, unroll=4)


def project_kernel(
    size,
    y_ref,
    att_w_ref,
    bias_w_ref,
    att_gate_ref,
    bias_ref,
    y_t_ref,
    query_ref,
    key_ref,
    value_ref,
    bias_rep_ref,
):
    channels = y_ref.shape[1]
    lanes = HEADS * size
    head_scale = 1.0 / math.sqrt(HEAD_DIM)
    rows_of, columns_of = block_tools(size)
    same_cell = same_cell_of(size)
    spread_bias_weight(bias_rep_ref, bias_w_ref, size)

    def prepare(at, carry):
        rows = rows_of(at)
        y = columns_of(y_ref, at).astype(HALF)
        y_t_ref[rows, :] = y
        packed = dot_nn(y, att_w_ref[...])
        query_ref[rows, :] = (packed[:, :channels] * head_scale).astype(HALF)
        key_ref[rows, :] = packed[:, channels : 2 * channels].astype(HALF)
        value_ref[rows, :] = packed[:, 2 * channels : 3 * channels].astype(HALF)
        att_gate_ref[rows, :] = sigmoid(packed[:, 3 * channels :])
        spread = dot_nt(y, bias_rep_ref[...]).astype(HALF).astype(FULL)
        spread = spread.reshape(ROW_BLOCK, size, lanes) * same_cell[None]
        bias_ref[pl.ds(at * ROW_BLOCK, ROW_BLOCK), :] = jnp.sum(spread, axis=1)
        return carry

    lax.fori_loop(0, size // ROW_BLOCK, prepare, 0, unroll=4)


def attend_kernel(
    size,
    masks,
    near_ref,
    far_ref,
    lengths_ref,
    att_w_ref,
    att_out_w_ref,
    att_gate_ref,
    bias_ref,
    y_t_ref,
    query_ref,
    key_ref,
    value_ref,
    bias_rep_ref,
    cot_ref,
    grad_y_ref,
    grad_att_w_ref,
    grad_bias_ref,
    grad_att_out_ref,
    gain_part_ref,
    cot_t_ref,
    gated_ref,
    grad_packed_ref,
    bias_grad_ref,
):
    channels = cot_ref.shape[1]
    block = ROW_BLOCK * size
    blocks = size // ROW_BLOCK
    lanes = HEADS * size
    head_scale = 1.0 / math.sqrt(HEAD_DIM)
    rows_of, columns_of = block_tools(size)
    same_cell = same_cell_of(size)
    valid = real_lanes(size, lengths_ref[0])
    place_rows(cot_ref, 1, near_ref, far_ref, masks)

    head_mask = head_blocks(size, HEAD_DIM, HALF)
    head_mask_full = head_blocks(size, HEAD_DIM, FULL)
    no_mask = jnp.zeros((lanes, channels), HALF)
    no_rows = jnp.zeros((size, channels), HALF)
    key_ones = head_blocks(size, size, HALF)
    dim_ones = head_blocks(HEAD_DIM, size, HALF)

    def attend(at, score_sum):
        rows = rows_of(at)
        parts = [slice(a * size, (a + 1) * size) for a in range(ROW_BLOCK)]
        query, key, value = (ref[rows, :] for ref in (query_ref, key_ref, value_ref))
        gate = att_gate_ref[rows, :]
        cot = columns_of(cot_ref, at).astype(HALF)
        cot_t_ref[rows, :] = cot
        grad_gated = dot_nt(cot, att_out_w_ref[...])
        grad_att = (grad_gated * gate).astype(HALF)
        keys = [jnp.concatenate([key[p]] * HEADS, axis=0) * head_mask for p in parts]
        values = [jnp.concatenate([value[p]] * HEADS, axis=0) * head_mask for p in parts]
        bias = bias_ref[...]

        def products(p, a):
            both = jnp.concatenate(
                [
                    jnp.concatenate([keys[a], no_mask], axis=1),
                    jnp.concatenate([no_mask, values[a]], axis=1),
                ],
                axis=0,
            )
            return dot_nt(jnp.concatenate([query[p], grad_att[p]], axis=1), both)

        pairs = [products(p, a) for a, p in enumerate(parts)]
        scores = jnp.concatenate([pair[:, :lanes] + bias for pair in pairs], axis=0)
        grad_attention = jnp.concatenate([pair[:, lanes:] for pair in pairs], axis=0)
        exp_scores = valid * jnp.exp(scores)
        attention = exp_scores / dot_wide(exp_scores, key_ones)
        attention_half = attention.astype(HALF)
        attended = jnp.concatenate(
            [dot_nn(attention_half[p], values[a]) for a, p in enumerate(parts)], axis=0
        )
        row_dots = dot_wide(grad_att.astype(FULL) * attended, dim_ones)
        grad_scores = attention * (grad_attention - row_dots)
        scores_half = grad_scores.astype(HALF)
        for p in parts:
            score_sum = score_sum + grad_scores[p]
        grad_query = jnp.concatenate(
            [dot_nn(scores_half[p], keys[a]) for a, p in enumerate(parts)], axis=0
        )

        def key_sums(p):
            weights = jnp.concatenate([scores_half[p], attention_half[p]], axis=0)
            vectors = jnp.concatenate(
                [
                    jnp.concatenate([query[p], no_rows], axis=1),
                    jnp.concatenate([no_rows, grad_att[p]], axis=1),
                ],
                axis=0,
            )
            whole = dot_tn(weights, vectors)
            masked = [whole[:, :channels] * head_mask_full, whole[:, channels:] * head_mask_full]
            return [sum(part[h * size : (h + 1) * size] for h in range(HEADS)) for part in masked]

        per_key = [key_sums(p) for p in parts]
        grad_key = jnp.concatenate([pair[0] for pair in per_key], axis=0)
        grad_value = jnp.concatenate([pair[1] for pair in per_key], axis=0)
        gated = gate * attended
        gated_ref[rows, :] = gated.astype(HALF)
        grad_gate_pre = grad_gated * gated * (1.0 - gate)
        grad_packed = jnp.concatenate(
            [
                (grad_query * head_scale).astype(HALF),
                grad_key.astype(HALF),
                grad_value.astype(HALF),
                grad_gate_pre.astype(HALF),
            ],
            axis=1,
        )
        grad_packed_ref[rows, : 4 * channels] = grad_packed
        grad_y_ref[rows, :] = dot_nt(grad_packed, att_w_ref[...])
        return score_sum

    score_sum = lax.fori_loop(0, blocks, attend, jnp.zeros((size, lanes), FULL), unroll=4)
    bias_grad_ref[...] = score_sum.astype(HALF).astype(FULL)

    def spread_bias(at, carry):
        rows = rows_of(at)
        part = bias_grad_ref[pl.ds(at * ROW_BLOCK, ROW_BLOCK), :]
        spread = (part[:, None, :] * same_cell[None]).reshape(block, lanes).astype(HALF)
        grad_packed_ref[rows, 4 * channels :] = spread
        grad_y_ref[rows, :] += dot_nn(spread, bias_rep_ref[...])
        return carry

    lax.fori_loop(0, blocks, spread_bias, 0, unroll=4)

    inverse = 1.0 / size
    y_sum = dot_tn(y_t_ref[...], grad_packed_ref[...]) * inverse
    att_sum, bias_sum = y_sum[:, : 4 * channels], jnp.transpose(y_sum[:, 4 * channels :])
    grad_att_w_ref[...] = att_sum
    grad_att_out_ref[...] = dot_tn(gated_ref[...], cot_t_ref[...]) * inverse
    for h in range(HEADS):
        grad_bias_ref[h : h + 1, :] = jnp.sum(
            bias_sum[h * size : (h + 1) * size], axis=0, keepdims=True
        )
    bias_part = jnp.sum(bias_rep_ref[...].astype(FULL) * bias_sum, axis=0, keepdims=True)
    gain_part_ref[...] = gain_sum(((att_w_ref[...], att_sum),)) + bias_part


def gain_sum(pairs):
    total = sum(jnp.sum(weight.astype(FULL) * grad, axis=1, keepdims=True) for weight, grad in pairs)
    channels = total.shape[0]
    return jnp.transpose(jnp.broadcast_to(total, (channels, channels)))[0:1, :]


def edges_kernel(
    size,
    devices,
    pair_ref,
    gains_ref,
    edge_w_ref,
    gate_w_ref,
    out_w_ref,
    left_ref,
    right_ref,
    left_a_ref,
    left_b_ref,
    right_a_ref,
    right_b_ref,
    gate_ref,
    hat_mid_ref,
    scale_mid_ref,
    edge_out_ref,
    hat_y_ref,
    scale_y_ref,
    x_half_ref,
    update_ref,
    cot_ref,
    grad_y_ref,
    gain_part_ref,
    grad_pair_ref,
    grad_gains_ref,
    grad_edge_ref,
    grad_gate_w_ref,
    grad_out_w_ref,
    grad_middle_ref,
    grad_product_ref,
    grad_proj_ref,
    x_sum_ref,
    out_sum_ref,
):
    channels = gains_ref.shape[1]
    blocks = size // ROW_BLOCK
    rows_of, columns_of = block_tools(size)
    gain_x = gains_ref[0:1, :]
    gain_mid = gains_ref[1:2, :]
    gain_y = gains_ref[2:3, :]

    x_sum_ref[...] = jnp.zeros(x_sum_ref.shape, FULL)
    out_sum_ref[...] = jnp.zeros(out_sum_ref.shape, FULL)

    def middle_back(at, carry):
        rows = rows_of(at)
        grad_y = columns_of(grad_y_ref, at)
        grad_middle = cot_ref[rows, :] + kernel_norm_back(
            grad_y, hat_y_ref[rows, :], scale_y_ref[rows, :], gain_y
        )
        grad_middle_ref[rows, :] = grad_middle
        gate = gate_ref[rows, :]
        gated = grad_middle * gate
        grad_edge_out = gated.astype(HALF)
        grad_gate = (gated * edge_out_ref[rows, :] * (1.0 - gate)).astype(HALF)
        grad_proj_ref[rows, 4 * channels :] = grad_gate
        x_sum_ref[:, 4 * channels :] += dot_tn(x_half_ref[rows, :], grad_gate)
        out_sum_ref[...] += dot_tn(update_ref[rows, :], grad_edge_out)
        grad_update = dot_nt(grad_edge_out, out_w_ref[...])
        grad_product = kernel_norm_back(grad_update, hat_mid_ref[rows, :], scale_mid_ref[rows, :], gain_mid)
        grad_product_ref[rows, :] = grad_product.astype(HALF).astype(FULL)
        return carry

    lax.fori_loop(0, blocks, middle_back, 0, unroll=4)

    def edges_back(at, carry):
        rows = rows_of(at)
        x_half = x_half_ref[rows, :]
        for side, (first_ref, second_ref, strides, other_ref) in enumerate(
            (
                (left_a_ref, left_b_ref, (1, size), right_ref),
                (right_a_ref, right_b_ref, (size, 1), left_ref),
            )
        ):
            grad = outer_sum(size, at, grad_product_ref, *strides, other_ref)
            both = jnp.concatenate(
                [(grad * first_ref[rows, :]).astype(HALF), (grad * second_ref[rows, :]).astype(HALF)], axis=1
            )
            place = slice(2 * side * channels, 2 * (side + 1) * channels)
            grad_proj_ref[rows, place] = both
            x_sum_ref[:, place] += dot_tn(x_half, both)
        return carry

    lax.fori_loop(0, blocks, edges_back, 0, unroll=4)

    inverse = 1.0 / size
    x_sum = x_sum_ref[...] * inverse
    edge_sum, gate_sum = x_sum[:, : 4 * channels], x_sum[:, 4 * channels :]
    grad_edge_ref[...] = edge_sum
    grad_gate_w_ref[...] = gate_sum
    out_sum = out_sum_ref[...] * inverse
    grad_out_w_ref[...] = out_sum
    grad_gains_ref[0:1, :] = gain_sum(((edge_w_ref[...], edge_sum), (gate_w_ref[...], gate_sum))) / gain_x
    grad_gains_ref[1:2, :] = gain_sum(((out_w_ref[...], out_sum),)) / gain_mid
    grad_gains_ref[2:3, :] = gain_part_ref[...] / gain_y

    own_cells = size * size // devices
    own = pl.ds(pl.multiple_of(lax.axis_index("dap") * own_cells, own_cells), own_cells)
    hat, scale = kernel_norm(pair_ref[...].reshape(own_cells, channels).astype(FULL))
    grad_x = dot_nt(grad_proj_ref[own, : 4 * channels], edge_w_ref[...])
    grad_x = grad_x + dot_nt(grad_proj_ref[own, 4 * channels :], gate_w_ref[...])
    grad_pair = grad_middle_ref[own, :] + kernel_norm_back(grad_x, hat, scale, gain_x)
    grad_pair_ref[...] = grad_pair.astype(grad_pair_ref.dtype)


def kernel_norm(values):
    center = values - lane_mean(values)
    scale = lax.rsqrt(lane_mean(center * center) + epsilon)
    return center * scale, scale


def kernel_norm_back(grad_out, hat, scale, gain):
    scaled = grad_out * gain
    return scale * (scaled - lane_mean(scaled) - hat * lane_mean(scaled * hat))


def bytes_of(arrays):
    return sum(math.prod(shape) * jnp.dtype(dtype).itemsize for shape, dtype in arrays)


def kernel_scratch(size, channels):
    cells, lanes = size * size, HEADS * size
    full, half = ((cells, channels), FULL), ((cells, channels), HALF)
    square, wide = ((channels, channels), FULL), ((channels, 4 * channels), FULL)
    return {
        "kept": [full] * 12,
        "y": [full],
        "halves": [half] * 2,
        "multiply": [full] * 2,
        "projections": [full, ((size, lanes), FULL)] + [half] * 4 + [((lanes, channels), HALF)],
        "shared": [full] * 2,
        "sums": [wide, square, ((1, channels), FULL)],
        "attend": [half] * 2 + [((cells, 4 * channels + lanes), HALF), ((size, lanes), FULL)],
        "edges": [full] * 2 + [((cells, 5 * channels), HALF), ((channels, 5 * channels), FULL), square],
    }


def whole_kernel(
    size,
    masks,
    near_ref,
    far_ref,
    lengths_ref,
    gains_ref,
    edge_w_ref,
    gate_w_ref,
    out_w_ref,
    att_w_ref,
    bias_w_ref,
    att_out_w_ref,
    grad_pair_ref,
    grad_gains_ref,
    grad_edge_ref,
    grad_gate_w_ref,
    grad_out_w_ref,
    grad_att_w_ref,
    grad_bias_ref,
    grad_att_out_ref,
    *scratch,
):
    part, at = {}, 0
    for name, arrays in kernel_scratch(size, 1).items():
        part[name] = scratch[at : at + len(arrays)]
        at += len(arrays)
    sent = scratch[at]
    weights = (edge_w_ref, gate_w_ref, out_w_ref)
    multiply_kernel(
        size, masks, near_ref, far_ref, lengths_ref, gains_ref, *weights, *part["kept"], *part["y"], *part["halves"], *part["multiply"]
    )
    project_kernel(size, *part["y"], att_w_ref, bias_w_ref, *part["projections"])
    att_sum_ref, att_out_sum_ref, gain_part_ref = part["sums"]
    attend_kernel(
        size,
        masks,
        near_ref,
        far_ref,
        lengths_ref,
        att_w_ref,
        att_out_w_ref,
        *part["projections"],
        *part["shared"],
        att_sum_ref,
        grad_bias_ref,
        att_out_sum_ref,
        gain_part_ref,
        *part["attend"],
    )
    copies = [
        pltpu.make_async_copy(source, target, sent.at[slot])
        for slot, (source, target) in enumerate(((att_sum_ref, grad_att_w_ref), (att_out_sum_ref, grad_att_out_ref)))
    ]
    for copy in copies:
        copy.start()
    edges_kernel(
        size,
        2 * len(masks),
        near_ref.at[0, 0],
        gains_ref,
        *weights,
        *part["kept"],
        *part["halves"],
        *part["shared"],
        gain_part_ref,
        grad_pair_ref,
        grad_gains_ref,
        grad_edge_ref,
        grad_gate_w_ref,
        grad_out_w_ref,
        *part["edges"],
    )
    for copy in copies:
        copy.wait()


def replicated_plan(
    axis_size,
    pair_map,
    cotangent,
    lengths,
    norm_gains,
    edge_weight,
    mult_gate_weight,
    mult_out_weight,
    attention_weight,
    bias_weight,
    attention_out_weight,
):
    _, size, channels = pair_map.shape
    cells = size * size
    bits = axis_size.bit_length() - 1
    far_step = 1 << (bits - 1)
    near_steps = range(2, far_step, 2)

    def swapped(held, mask):
        return lax.ppermute(held, "dap", [(d, d ^ mask) for d in range(axis_size)])

    own = jnp.stack([pair_map, cotangent])
    held = jnp.stack([own, swapped(own, far_step)])
    masks = [0, far_step]
    near = jnp.concatenate([held] + [swapped(held, step) for step in near_steps], axis=0)
    masks = masks + [mask ^ step for step in near_steps for mask in masks]
    far = swapped(near, 1)

    square, wide = ((channels, channels), FULL), ((channels, 4 * channels), FULL)
    outs = [((cells // axis_size, channels), HALF), ((3, channels), FULL), wide, square, square]
    outs += [wide, ((HEADS, channels), FULL), square]
    scratch = sum(kernel_scratch(size, channels).values(), [])
    vmem = pl.BlockSpec(memory_space=pltpu.VMEM)
    smem = pl.BlockSpec(memory_space=pltpu.SMEM)
    anywhere = pl.BlockSpec(memory_space=pl.ANY)
    results = pl.pallas_call(
        functools.partial(whole_kernel, size, masks),
        out_shape=[jax.ShapeDtypeStruct(*out) for out in outs],
        in_specs=[vmem, vmem, smem] + [vmem] * 7,
        out_specs=[vmem] * 5 + [anywhere, vmem, anywhere],
        scratch_shapes=[pltpu.VMEM(*part) for part in scratch] + [pltpu.SemaphoreType.DMA((2,))],
        compiler_params=pltpu.CompilerParams(vmem_limit_bytes=bytes_of(scratch) + VMEM_SLACK),
    )(
        near,
        far,
        lengths,
        norm_gains,
        edge_weight,
        mult_gate_weight,
        mult_out_weight,
        attention_weight,
        bias_weight.T,
        attention_out_weight,
    )
    return (results[0].reshape(pair_map.shape), *results[1:6], results[6].T, results[7])


def per_device(axis_size, pair_map, *rest):
    _, size, channels = pair_map.shape
    scratch = sum(kernel_scratch(size, channels).values(), [])
    fits = size % ROW_BLOCK == 0 and bytes_of(scratch) <= VMEM_SHARE
    if fits and axis_size >= 8 and axis_size & (axis_size - 1) == 0:
        return replicated_plan(axis_size, pair_map, *rest)
    return distributed_plan(pair_map, *rest)


def solution(mesh):
    return jax.shard_map(
        functools.partial(per_device, mesh.shape["dap"]),
        mesh=mesh,
        in_specs=(
            P(("groups", "dap"), None, None),
            P(("groups", "dap"), None, None),
            P("groups"),
            P(),
            P(),
            P(),
            P(),
            P(),
            P(),
            P(),
        ),
        out_specs=(
            P(("groups", "dap"), None, None),
            P("groups", None),
            P("groups", None),
            P("groups", None),
            P("groups", None),
            P("groups", None),
            P("groups", None),
            P("groups", None),
        ),
        check_vma=False,
    )
```

```python
import functools
import math

import jax
import jax.numpy as jnp
from jax import lax
from jax.experimental import pallas as pl
from jax.experimental.pallas import tpu as pltpu
from jax.sharding import PartitionSpec as P

HEADS = 4
HEAD_DIM = 32


epsilon = 1e-05


def norm_forward(values, gain_row):
    center = values - jnp.mean(values, axis=-1, keepdims=True)
    inv_std = lax.rsqrt(jnp.mean(center * center, axis=-1, keepdims=True) + epsilon)
    normed = center * inv_std
    return (normed * gain_row, normed, inv_std)


def norm_backward(grad_out, normed, inv_std, gain_row):
    scaled = grad_out * gain_row
    first_mean = jnp.mean(scaled, axis=-1, keepdims=True)
    second_mean = jnp.mean(scaled * normed, axis=-1, keepdims=True)
    return inv_std * (scaled - first_mean - normed * second_mean)


def distributed_plan(
    pair_map,
    cotangent,
    lengths,
    norm_gains,
    edge_weight,
    mult_gate_weight,
    mult_out_weight,
    attention_weight,
    bias_weight,
    attention_out_weight,
):
    row_count, full_size, channels = pair_map.shape
    inner_width = HEADS * HEAD_DIM
    head_scale = 1.0 / math.sqrt(HEAD_DIM)
    first_row = lax.axis_index("dap") * row_count
    real_count = lengths[0]
    valid_all = (jnp.arange(full_size) < real_count).astype(jnp.float32)
    valid_rows = (first_row + jnp.arange(row_count) < real_count).astype(jnp.float32)
    mask_pair = (valid_rows[:, None] * valid_all[None, :])[:, :, None]
    pair_f32 = pair_map.astype(jnp.float32)
    normed_full, hat_in, scale_in = norm_forward(pair_f32, norm_gains[0])
    normed_x = normed_full.astype(jnp.bfloat16)
    projected = jnp.einsum("rnc,cf->rnf", normed_x, edge_weight, preferred_element_type=jnp.float32)
    left_gate = projected[..., :channels]
    left_value = projected[..., channels : 2 * channels]
    right_gate = projected[..., 2 * channels : 3 * channels]
    right_value = projected[..., 3 * channels :]
    left_sig = jax.nn.sigmoid(left_gate)
    right_sig = jax.nn.sigmoid(right_gate)
    left_edges = (mask_pair * left_sig * left_value).astype(jnp.bfloat16)
    right_edges = (mask_pair * right_sig * right_value).astype(jnp.bfloat16)
    product = jnp.einsum(
        "ikc,jkc->ijc",
        left_edges,
        lax.all_gather(right_edges, "dap", axis=0, tiled=True),
        preferred_element_type=jnp.float32,
    )
    update_full, hat_mid, scale_mid = norm_forward(product, norm_gains[1])
    update = update_full.astype(jnp.bfloat16)
    edge_out = jnp.einsum(
        "rnc,cf->rnf", update, mult_out_weight, preferred_element_type=jnp.float32
    )
    gate_sig = jax.nn.sigmoid(
        jnp.einsum("rnc,cf->rnf", normed_x, mult_gate_weight, preferred_element_type=jnp.float32)
    )
    middle = pair_f32 + gate_sig * edge_out
    normed_mid, hat_attn, scale_attn = norm_forward(middle, norm_gains[2])
    normed_y = normed_mid.astype(jnp.bfloat16)
    bias_local = jnp.einsum(
        "kic,ch->hki", normed_y, bias_weight, preferred_element_type=jnp.float32
    ).astype(jnp.bfloat16)
    bias_whole = lax.all_gather(bias_local, "dap", axis=1, tiled=True)
    bias_query = jnp.swapaxes(bias_whole, 1, 2).astype(jnp.float32)
    column_y, column_cot = (
        lax.all_to_all(normed_y, "dap", split_axis=1, concat_axis=0, tiled=True),
        lax.all_to_all(cotangent, "dap", split_axis=1, concat_axis=0, tiled=True),
    )
    packed = jnp.einsum(
        "ijc,cf->ijf", column_y, attention_weight, preferred_element_type=jnp.float32
    )
    packed = packed.reshape(full_size, row_count, 4, HEADS, HEAD_DIM)
    query_vectors = (packed[:, :, 0] * head_scale).astype(jnp.bfloat16)
    key_vectors = packed[:, :, 1].astype(jnp.bfloat16)
    value_vectors = packed[:, :, 2].astype(jnp.bfloat16)
    att_gate = jax.nn.sigmoid(packed[:, :, 3])
    scores = (
        jnp.einsum(
            "ijhd,kjhd->jhik", query_vectors, key_vectors, preferred_element_type=jnp.float32
        )
        + bias_query[None]
    )
    exp_scores = valid_all * jnp.exp(scores)
    attention = exp_scores / jnp.sum(exp_scores, axis=-1, keepdims=True)
    attention_half = attention.astype(jnp.bfloat16)
    attended = jnp.einsum(
        "jhik,kjhd->ijhd", attention_half, value_vectors, preferred_element_type=jnp.float32
    )
    gated = (att_gate * attended).astype(jnp.bfloat16).reshape(full_size, row_count, inner_width)
    part_attn_out = jnp.einsum("ijf,ijc->fc", gated, column_cot, preferred_element_type=jnp.float32)
    grad_gated = jnp.einsum(
        "ijc,fc->ijf", column_cot, attention_out_weight, preferred_element_type=jnp.float32
    )
    grad_gated = grad_gated.reshape(full_size, row_count, HEADS, HEAD_DIM)
    grad_att = (grad_gated * att_gate).astype(jnp.bfloat16)
    grad_gate_pre = grad_gated * attended * att_gate * (1.0 - att_gate)
    grad_attention = jnp.einsum(
        "ijhd,kjhd->jhik", grad_att, value_vectors, preferred_element_type=jnp.float32
    )
    row_dots = jnp.transpose(jnp.sum(grad_att.astype(jnp.float32) * attended, axis=-1), (1, 2, 0))
    grad_scores = attention * (grad_attention - row_dots[..., None])
    scores_half = grad_scores.astype(jnp.bfloat16)
    grad_query = jnp.einsum(
        "jhik,kjhd->ijhd", scores_half, key_vectors, preferred_element_type=jnp.float32
    )
    grad_key = jnp.einsum(
        "jhik,ijhd->kjhd", scores_half, query_vectors, preferred_element_type=jnp.float32
    )
    grad_value = jnp.einsum(
        "jhik,ijhd->kjhd", attention_half, grad_att, preferred_element_type=jnp.float32
    )
    grad_packed = jnp.stack([grad_query * head_scale, grad_key, grad_value, grad_gate_pre], axis=2)
    grad_packed = grad_packed.reshape(full_size, row_count, 4 * inner_width).astype(jnp.bfloat16)
    part_attention = jnp.einsum(
        "ijc,ijf->cf", column_y, grad_packed, preferred_element_type=jnp.float32
    )
    column_grad = jnp.einsum(
        "ijf,cf->ijc", grad_packed, attention_weight, preferred_element_type=jnp.float32
    ).astype(jnp.bfloat16)
    row_grad = lax.all_to_all(column_grad, "dap", split_axis=0, concat_axis=1, tiled=True)
    score_sums = jnp.sum(grad_scores, axis=0)
    taken = score_sums
    bias_half = lax.psum_scatter(
        jnp.transpose(taken, (2, 0, 1)), "dap", scatter_dimension=0, tiled=True
    ).astype(jnp.bfloat16)
    part_bias = jnp.einsum("kic,khi->ch", normed_y, bias_half, preferred_element_type=jnp.float32)
    grad_normed_y = row_grad.astype(jnp.float32) + jnp.einsum(
        "khi,ch->kic", bias_half, bias_weight, preferred_element_type=jnp.float32
    )
    part_gain_attn = jnp.sum(grad_normed_y * hat_attn, axis=(0, 1))
    grad_middle = cotangent.astype(jnp.float32) + norm_backward(
        grad_normed_y, hat_attn, scale_attn, norm_gains[2]
    )
    grad_edge_out = (grad_middle * gate_sig).astype(jnp.bfloat16)
    grad_gate = (grad_middle * edge_out * gate_sig * (1.0 - gate_sig)).astype(jnp.bfloat16)
    part_mult_out = jnp.einsum(
        "rnc,rnf->cf", update, grad_edge_out, preferred_element_type=jnp.float32
    )
    part_mult_gate = jnp.einsum(
        "rnc,rnf->cf", normed_x, grad_gate, preferred_element_type=jnp.float32
    )
    grad_update = jnp.einsum(
        "rnf,cf->rnc", grad_edge_out, mult_out_weight, preferred_element_type=jnp.float32
    )
    part_gain_mid = jnp.sum(grad_update * hat_mid, axis=(0, 1))
    grad_product = norm_backward(grad_update, hat_mid, scale_mid, norm_gains[1]).astype(
        jnp.bfloat16
    )
    taken = grad_product
    grad_left = jnp.einsum(
        "ijc,jkc->ikc",
        taken,
        lax.all_gather(right_edges, "dap", axis=0, tiled=True),
        preferred_element_type=jnp.float32,
    )
    grad_cols = lax.all_to_all(grad_product, "dap", split_axis=1, concat_axis=0, tiled=True)
    taken = grad_cols
    grad_right = jnp.einsum(
        "ijc,ikc->jkc",
        taken,
        lax.all_gather(left_edges, "dap", axis=0, tiled=True),
        preferred_element_type=jnp.float32,
    )
    grad_proj = jnp.concatenate(
        [
            grad_left * mask_pair * left_value * left_sig * (1.0 - left_sig),
            grad_left * mask_pair * left_sig,
            grad_right * mask_pair * right_value * right_sig * (1.0 - right_sig),
            grad_right * mask_pair * right_sig,
        ],
        axis=-1,
    ).astype(jnp.bfloat16)
    part_edge = jnp.einsum("rnc,rnf->cf", normed_x, grad_proj, preferred_element_type=jnp.float32)
    grad_normed_x = jnp.einsum(
        "rnf,cf->rnc", grad_proj, edge_weight, preferred_element_type=jnp.float32
    )
    grad_normed_x = grad_normed_x + jnp.einsum(
        "rnf,cf->rnc", grad_gate, mult_gate_weight, preferred_element_type=jnp.float32
    )
    part_gain_in = jnp.sum(grad_normed_x * hat_in, axis=(0, 1))
    grad_pair = (
        grad_middle + norm_backward(grad_normed_x, hat_in, scale_in, norm_gains[0])
    ).astype(jnp.bfloat16)
    totals = lax.psum(
        (
            part_gain_in,
            part_gain_mid,
            part_edge,
            part_mult_gate,
            part_mult_out,
            part_gain_attn,
            part_attention,
            part_bias,
            part_attn_out,
        ),
        "dap",
    )
    (
        gain_in_sum,
        gain_mid_sum,
        edge_sum,
        mult_gate_sum,
        mult_out_sum,
        gain_attn_sum,
        attention_sum,
        bias_sum,
        attn_out_sum,
    ) = totals
    inverse = 1.0 / full_size
    grad_gains = jnp.stack([gain_in_sum, gain_mid_sum, gain_attn_sum]) * inverse
    return (
        grad_pair,
        grad_gains,
        edge_sum * inverse,
        mult_gate_sum * inverse,
        mult_out_sum * inverse,
        attention_sum * inverse,
        bias_sum * inverse,
        attn_out_sum * inverse,
    )


ROW_BLOCK = 8
VMEM_SLACK = 8 * 2**20
VMEM_SHARE = 32 * 2**20
HALF = jnp.bfloat16
FULL = jnp.float32


def dot_nn(left, right):
    return lax.dot_general(left, right, (((1,), (0,)), ((), ())), preferred_element_type=FULL)


def dot_nt(left, right):
    return lax.dot_general(left, right, (((1,), (1,)), ((), ())), preferred_element_type=FULL)


def dot_tn(left, right):
    return lax.dot_general(left, right, (((0,), (0,)), ((), ())), preferred_element_type=FULL)


def dot_wide(values, ones):
    high = values.astype(HALF)
    low = (values - high.astype(FULL)).astype(HALF)
    return dot_nn(jnp.concatenate([high, low], axis=1), jnp.concatenate([ones, ones], axis=0))


def lane_mean(values):
    return jnp.mean(values, axis=-1, keepdims=True)


def sigmoid(values):
    return pltpu.reciprocal(1.0 + jnp.exp(-values), approx=True)


def head_blocks(row_width, col_width, dtype):
    shape = (HEADS * row_width, HEADS * col_width)
    row = lax.broadcasted_iota(jnp.int32, shape, 0)
    col = lax.broadcasted_iota(jnp.int32, shape, 1)
    same = None
    for h in range(HEADS):
        here = (row >= h * row_width) & (row < (h + 1) * row_width)
        here = here & (col >= h * col_width) & (col < (h + 1) * col_width)
        same = here if same is None else same | here
    return jnp.where(same, 1.0, 0.0).astype(dtype)


def place_rows(target, part, sources, masks):
    me = lax.axis_index("dap")
    cells = target.shape[0] // (2 * len(masks))

    def place(source):
        for at, mask in enumerate(masks):
            start = (me - lax.rem(me, 2)) ^ mask
            for core in range(2):
                place = pl.ds(pl.multiple_of((start + core) * cells, cells), cells)
                target[place, :] = source[at, core, part].reshape(cells, target.shape[1]).astype(FULL)

    odd = lax.rem(me, 2) == 1
    pl.when(odd)(lambda: place(sources[0]))
    pl.when(jnp.logical_not(odd))(lambda: place(sources[1]))


def block_tools(size):
    block = ROW_BLOCK * size

    def rows_of(at):
        return pl.ds(pl.multiple_of(at * block, block), block)

    def columns_of(ref, at):
        return jnp.concatenate(
            [ref[pl.ds(at * ROW_BLOCK + a, size, stride=size), :] for a in range(ROW_BLOCK)], axis=0
        )

    return rows_of, columns_of


def outer_sum(size, at, row_ref, row_stride, block_stride, block_ref):
    sums = [jnp.zeros((size, block_ref.shape[1]), FULL)] * ROW_BLOCK
    for k in range(size):
        whole = block_ref[k * size : (k + 1) * size, :]
        for a in range(ROW_BLOCK):
            row = (at * ROW_BLOCK + a) * block_stride + k * row_stride
            sums[a] = sums[a] + row_ref[pl.ds(row, 1), :] * whole
    return jnp.concatenate(sums, axis=0)


def same_cell_of(size):
    row = lax.broadcasted_iota(jnp.int32, (size, HEADS * size), 0)
    lane = lax.broadcasted_iota(jnp.int32, (size, HEADS * size), 1)
    same = lane == row
    for h in range(1, HEADS):
        same = same | (lane == row + h * size)
    return jnp.where(same, 1.0, 0.0)


def real_lanes(size, real):
    lane = lax.broadcasted_iota(jnp.int32, (1, HEADS * size), 1)
    inside = lane < real
    for h in range(1, HEADS):
        inside = inside | ((lane >= h * size) & (lane < h * size + real))
    return jnp.where(inside, 1.0, 0.0)


def spread_bias_weight(target, bias_w_ref, size):
    bias_rows = bias_w_ref[...].astype(FULL)
    for h in range(HEADS):
        target[h * size : (h + 1) * size, :] = jnp.broadcast_to(
            bias_rows[h : h + 1], (size, bias_rows.shape[1])
        ).astype(HALF)


def multiply_kernel(
    size,
    masks,
    sources,
    lengths_ref,
    gains_ref,
    edge_w_ref,
    gate_w_ref,
    out_w_ref,
    left_ref,
    right_ref,
    left_a_ref,
    left_b_ref,
    right_a_ref,
    right_b_ref,
    gate_ref,
    hat_mid_ref,
    scale_mid_ref,
    edge_out_ref,
    hat_y_ref,
    scale_y_ref,
    y_ref,
    x_half_ref,
    update_ref,
    pair_ref,
    right_t_ref,
):
    channels = gains_ref.shape[1]
    block = ROW_BLOCK * size
    blocks = size // ROW_BLOCK
    rows_of, columns_of = block_tools(size)
    real = lengths_ref[0]
    gain_x = gains_ref[0:1, :]
    gain_mid = gains_ref[1:2, :]
    gain_y = gains_ref[2:3, :]
    place_rows(pair_ref, 0, sources, masks)

    def project(at, carry):
        rows = rows_of(at)
        hat, _ = kernel_norm(pair_ref[rows, :])
        normed = (hat * gain_x).astype(HALF)
        x_half_ref[rows, :] = normed
        projected = dot_nn(normed, edge_w_ref[...])
        gate_ref[rows, :] = sigmoid(dot_nn(normed, gate_w_ref[...]))
        shape = (ROW_BLOCK, size, channels)
        row = lax.broadcasted_iota(jnp.int32, shape, 0) + at * ROW_BLOCK
        col = lax.broadcasted_iota(jnp.int32, shape, 1)
        mask = jnp.where((row < real) & (col < real), 1.0, 0.0).reshape(block, channels)
        for side, (edge, first, second) in enumerate(
            ((left_ref, left_a_ref, left_b_ref), (right_ref, right_a_ref, right_b_ref))
        ):
            base = 2 * side * channels
            sig = sigmoid(projected[:, base : base + channels])
            value = projected[:, base + channels : base + 2 * channels]
            masked = mask * sig
            product = masked * value
            edge[rows, :] = product.astype(HALF).astype(FULL)
            first[rows, :] = product * (1.0 - sig)
            second[rows, :] = masked
        return carry

    lax.fori_loop(0, blocks, project, 0, unroll=4)

    def turn(at, carry):
        right_t_ref[rows_of(at), :] = columns_of(right_ref, at)
        return carry

    lax.fori_loop(0, blocks, turn, 0, unroll=4)

    def multiply(at, carry):
        rows = rows_of(at)
        product = outer_sum(size, at, left_ref, 1, size, right_t_ref)
        hat, scale = kernel_norm(product)
        hat_mid_ref[rows, :] = hat
        scale_mid_ref[rows, :] = jnp.broadcast_to(scale, hat.shape)
        update = (hat * gain_mid).astype(HALF)
        update_ref[rows, :] = update
        edge_out = dot_nn(update, out_w_ref[...])
        edge_out_ref[rows, :] = edge_out
        middle = pair_ref[rows, :] + gate_ref[rows, :] * edge_out
        hat, scale = kernel_norm(middle)
        hat_y_ref[rows, :] = hat
        scale_y_ref[rows, :] = jnp.broadcast_to(scale, hat.shape)
        y_ref[rows, :] = hat * gain_y
        return carry

    lax.fori_loop(0, blocks, multiply, 0, unroll=4)


def project_kernel(
    size,
    y_ref,
    att_w_ref,
    bias_w_ref,
    att_gate_ref,
    bias_ref,
    y_t_ref,
    query_ref,
    key_ref,
    value_ref,
    bias_rep_ref,
):
    channels = y_ref.shape[1]
    lanes = HEADS * size
    head_scale = 1.0 / math.sqrt(HEAD_DIM)
    rows_of, columns_of = block_tools(size)
    same_cell = same_cell_of(size)
    spread_bias_weight(bias_rep_ref, bias_w_ref, size)

    def prepare(at, carry):
        rows = rows_of(at)
        y = columns_of(y_ref, at).astype(HALF)
        y_t_ref[rows, :] = y
        packed = dot_nn(y, att_w_ref[...])
        query_ref[rows, :] = (packed[:, :channels] * head_scale).astype(HALF)
        key_ref[rows, :] = packed[:, channels : 2 * channels].astype(HALF)
        value_ref[rows, :] = packed[:, 2 * channels : 3 * channels].astype(HALF)
        att_gate_ref[rows, :] = sigmoid(packed[:, 3 * channels :])
        spread = dot_nt(y, bias_rep_ref[...]).astype(HALF).astype(FULL)
        spread = spread.reshape(ROW_BLOCK, size, lanes) * same_cell[None]
        bias_ref[pl.ds(at * ROW_BLOCK, ROW_BLOCK), :] = jnp.sum(spread, axis=1)
        return carry

    lax.fori_loop(0, size // ROW_BLOCK, prepare, 0, unroll=4)


def attend_kernel(
    size,
    masks,
    sources,
    lengths_ref,
    att_w_ref,
    att_out_w_ref,
    att_gate_ref,
    bias_ref,
    y_t_ref,
    query_ref,
    key_ref,
    value_ref,
    bias_rep_ref,
    cot_ref,
    grad_y_ref,
    grad_att_w_ref,
    grad_bias_ref,
    grad_att_out_ref,
    gain_part_ref,
    cot_t_ref,
    gated_ref,
    grad_packed_ref,
    bias_grad_ref,
):
    channels = cot_ref.shape[1]
    block = ROW_BLOCK * size
    blocks = size // ROW_BLOCK
    lanes = HEADS * size
    head_scale = 1.0 / math.sqrt(HEAD_DIM)
    rows_of, columns_of = block_tools(size)
    same_cell = same_cell_of(size)
    valid = real_lanes(size, lengths_ref[0])
    place_rows(cot_ref, 1, sources, masks)

    head_mask = head_blocks(size, HEAD_DIM, HALF)
    head_mask_full = head_blocks(size, HEAD_DIM, FULL)
    no_mask = jnp.zeros((lanes, channels), HALF)
    no_rows = jnp.zeros((size, channels), HALF)
    key_ones = head_blocks(size, size, HALF)
    dim_ones = head_blocks(HEAD_DIM, size, HALF)

    def attend(at, score_sum):
        rows = rows_of(at)
        parts = [slice(a * size, (a + 1) * size) for a in range(ROW_BLOCK)]
        query, key, value = (ref[rows, :] for ref in (query_ref, key_ref, value_ref))
        gate = att_gate_ref[rows, :]
        cot = columns_of(cot_ref, at).astype(HALF)
        cot_t_ref[rows, :] = cot
        grad_gated = dot_nt(cot, att_out_w_ref[...])
        grad_att = (grad_gated * gate).astype(HALF)
        keys = [jnp.concatenate([key[p]] * HEADS, axis=0) * head_mask for p in parts]
        values = [jnp.concatenate([value[p]] * HEADS, axis=0) * head_mask for p in parts]
        bias = bias_ref[...]

        def products(p, a):
            both = jnp.concatenate(
                [
                    jnp.concatenate([keys[a], no_mask], axis=1),
                    jnp.concatenate([no_mask, values[a]], axis=1),
                ],
                axis=0,
            )
            return dot_nt(jnp.concatenate([query[p], grad_att[p]], axis=1), both)

        pairs = [products(p, a) for a, p in enumerate(parts)]
        scores = jnp.concatenate([pair[:, :lanes] + bias for pair in pairs], axis=0)
        grad_attention = jnp.concatenate([pair[:, lanes:] for pair in pairs], axis=0)
        exp_scores = valid * jnp.exp(scores)
        attention = exp_scores / dot_wide(exp_scores, key_ones)
        attention_half = attention.astype(HALF)
        attended = jnp.concatenate(
            [dot_nn(attention_half[p], values[a]) for a, p in enumerate(parts)], axis=0
        )
        row_dots = dot_wide(grad_att.astype(FULL) * attended, dim_ones)
        grad_scores = attention * (grad_attention - row_dots)
        scores_half = grad_scores.astype(HALF)
        for p in parts:
            score_sum = score_sum + grad_scores[p]
        grad_query = jnp.concatenate(
            [dot_nn(scores_half[p], keys[a]) for a, p in enumerate(parts)], axis=0
        )

        def key_sums(p):
            weights = jnp.concatenate([scores_half[p], attention_half[p]], axis=0)
            vectors = jnp.concatenate(
                [
                    jnp.concatenate([query[p], no_rows], axis=1),
                    jnp.concatenate([no_rows, grad_att[p]], axis=1),
                ],
                axis=0,
            )
            whole = dot_tn(weights, vectors)
            masked = [whole[:, :channels] * head_mask_full, whole[:, channels:] * head_mask_full]
            return [sum(part[h * size : (h + 1) * size] for h in range(HEADS)) for part in masked]

        per_key = [key_sums(p) for p in parts]
        grad_key = jnp.concatenate([pair[0] for pair in per_key], axis=0)
        grad_value = jnp.concatenate([pair[1] for pair in per_key], axis=0)
        gated = gate * attended
        gated_ref[rows, :] = gated.astype(HALF)
        grad_gate_pre = grad_gated * gated * (1.0 - gate)
        grad_packed = jnp.concatenate(
            [
                (grad_query * head_scale).astype(HALF),
                grad_key.astype(HALF),
                grad_value.astype(HALF),
                grad_gate_pre.astype(HALF),
            ],
            axis=1,
        )
        grad_packed_ref[rows, : 4 * channels] = grad_packed
        grad_y_ref[rows, :] = dot_nt(grad_packed, att_w_ref[...])
        return score_sum

    score_sum = lax.fori_loop(0, blocks, attend, jnp.zeros((size, lanes), FULL), unroll=4)
    bias_grad_ref[...] = score_sum.astype(HALF).astype(FULL)

    def spread_bias(at, carry):
        rows = rows_of(at)
        part = bias_grad_ref[pl.ds(at * ROW_BLOCK, ROW_BLOCK), :]
        spread = (part[:, None, :] * same_cell[None]).reshape(block, lanes).astype(HALF)
        grad_packed_ref[rows, 4 * channels :] = spread
        grad_y_ref[rows, :] += dot_nn(spread, bias_rep_ref[...])
        return carry

    lax.fori_loop(0, blocks, spread_bias, 0, unroll=4)

    inverse = 1.0 / size
    y_sum = dot_tn(y_t_ref[...], grad_packed_ref[...]) * inverse
    att_sum, bias_sum = y_sum[:, : 4 * channels], jnp.transpose(y_sum[:, 4 * channels :])
    grad_att_w_ref[...] = att_sum
    grad_att_out_ref[...] = dot_tn(gated_ref[...], cot_t_ref[...]) * inverse
    for h in range(HEADS):
        grad_bias_ref[h : h + 1, :] = jnp.sum(
            bias_sum[h * size : (h + 1) * size], axis=0, keepdims=True
        )
    bias_part = jnp.sum(bias_rep_ref[...].astype(FULL) * bias_sum, axis=0, keepdims=True)
    gain_part_ref[...] = gain_sum(((att_w_ref[...], att_sum),)) + bias_part


def gain_sum(pairs):
    total = sum(jnp.sum(weight.astype(FULL) * grad, axis=1, keepdims=True) for weight, grad in pairs)
    channels = total.shape[0]
    return jnp.transpose(jnp.broadcast_to(total, (channels, channels)))[0:1, :]


def edges_kernel(
    size,
    devices,
    pair_ref,
    gains_ref,
    edge_w_ref,
    gate_w_ref,
    out_w_ref,
    left_ref,
    right_ref,
    left_a_ref,
    left_b_ref,
    right_a_ref,
    right_b_ref,
    gate_ref,
    hat_mid_ref,
    scale_mid_ref,
    edge_out_ref,
    hat_y_ref,
    scale_y_ref,
    x_half_ref,
    update_ref,
    cot_ref,
    grad_y_ref,
    gain_part_ref,
    grad_pair_ref,
    grad_gains_ref,
    grad_edge_ref,
    grad_gate_w_ref,
    grad_out_w_ref,
    grad_middle_ref,
    grad_product_ref,
    grad_proj_ref,
    x_sum_ref,
    out_sum_ref,
):
    channels = gains_ref.shape[1]
    blocks = size // ROW_BLOCK
    rows_of, columns_of = block_tools(size)
    gain_x = gains_ref[0:1, :]
    gain_mid = gains_ref[1:2, :]
    gain_y = gains_ref[2:3, :]

    x_sum_ref[...] = jnp.zeros(x_sum_ref.shape, FULL)
    out_sum_ref[...] = jnp.zeros(out_sum_ref.shape, FULL)

    def middle_back(at, carry):
        rows = rows_of(at)
        grad_y = columns_of(grad_y_ref, at)
        grad_middle = cot_ref[rows, :] + kernel_norm_back(
            grad_y, hat_y_ref[rows, :], scale_y_ref[rows, :], gain_y
        )
        grad_middle_ref[rows, :] = grad_middle
        gate = gate_ref[rows, :]
        gated = grad_middle * gate
        grad_edge_out = gated.astype(HALF)
        grad_gate = (gated * edge_out_ref[rows, :] * (1.0 - gate)).astype(HALF)
        grad_proj_ref[rows, 4 * channels :] = grad_gate
        x_sum_ref[:, 4 * channels :] += dot_tn(x_half_ref[rows, :], grad_gate)
        out_sum_ref[...] += dot_tn(update_ref[rows, :], grad_edge_out)
        grad_update = dot_nt(grad_edge_out, out_w_ref[...])
        grad_product = kernel_norm_back(grad_update, hat_mid_ref[rows, :], scale_mid_ref[rows, :], gain_mid)
        grad_product_ref[rows, :] = grad_product.astype(HALF).astype(FULL)
        return carry

    lax.fori_loop(0, blocks, middle_back, 0, unroll=4)

    def edges_back(at, carry):
        rows = rows_of(at)
        x_half = x_half_ref[rows, :]
        for side, (first_ref, second_ref, strides, other_ref) in enumerate(
            (
                (left_a_ref, left_b_ref, (1, size), right_ref),
                (right_a_ref, right_b_ref, (size, 1), left_ref),
            )
        ):
            grad = outer_sum(size, at, grad_product_ref, *strides, other_ref)
            both = jnp.concatenate(
                [(grad * first_ref[rows, :]).astype(HALF), (grad * second_ref[rows, :]).astype(HALF)], axis=1
            )
            place = slice(2 * side * channels, 2 * (side + 1) * channels)
            grad_proj_ref[rows, place] = both
            x_sum_ref[:, place] += dot_tn(x_half, both)
        return carry

    lax.fori_loop(0, blocks, edges_back, 0, unroll=4)

    inverse = 1.0 / size
    x_sum = x_sum_ref[...] * inverse
    edge_sum, gate_sum = x_sum[:, : 4 * channels], x_sum[:, 4 * channels :]
    grad_edge_ref[...] = edge_sum
    grad_gate_w_ref[...] = gate_sum
    out_sum = out_sum_ref[...] * inverse
    grad_out_w_ref[...] = out_sum
    grad_gains_ref[0:1, :] = gain_sum(((edge_w_ref[...], edge_sum), (gate_w_ref[...], gate_sum))) / gain_x
    grad_gains_ref[1:2, :] = gain_sum(((out_w_ref[...], out_sum),)) / gain_mid
    grad_gains_ref[2:3, :] = gain_part_ref[...] / gain_y

    own_cells = size * size // devices
    own = pl.ds(pl.multiple_of(lax.axis_index("dap") * own_cells, own_cells), own_cells)
    hat, scale = kernel_norm(pair_ref[...].reshape(own_cells, channels).astype(FULL))
    grad_x = dot_nt(grad_proj_ref[own, : 4 * channels], edge_w_ref[...])
    grad_x = grad_x + dot_nt(grad_proj_ref[own, 4 * channels :], gate_w_ref[...])
    grad_pair = grad_middle_ref[own, :] + kernel_norm_back(grad_x, hat, scale, gain_x)
    grad_pair_ref[...] = grad_pair.astype(grad_pair_ref.dtype)


def kernel_norm(values):
    center = values - lane_mean(values)
    scale = lax.rsqrt(lane_mean(center * center) + epsilon)
    return center * scale, scale


def kernel_norm_back(grad_out, hat, scale, gain):
    scaled = grad_out * gain
    return scale * (scaled - lane_mean(scaled) - hat * lane_mean(scaled * hat))


def bytes_of(arrays):
    return sum(math.prod(shape) * jnp.dtype(dtype).itemsize for shape, dtype in arrays)


def kernel_scratch(size, channels):
    cells, lanes = size * size, HEADS * size
    full, half = ((cells, channels), FULL), ((cells, channels), HALF)
    square, wide = ((channels, channels), FULL), ((channels, 4 * channels), FULL)
    return {
        "kept": [full] * 12,
        "y": [full],
        "halves": [half] * 2,
        "multiply": [full] * 2,
        "projections": [full, ((size, lanes), FULL)] + [half] * 4 + [((lanes, channels), HALF)],
        "shared": [full] * 2,
        "sums": [wide, square, ((1, channels), FULL)],
        "attend": [half] * 2 + [((cells, 4 * channels + lanes), HALF), ((size, lanes), FULL)],
        "edges": [full] * 2 + [((cells, 5 * channels), HALF), ((channels, 5 * channels), FULL), square],
    }


def whole_kernel(
    size,
    masks,
    pair_own_ref,
    gathered_ref,
    received_ref,
    lengths_ref,
    gains_ref,
    edge_w_ref,
    gate_w_ref,
    out_w_ref,
    att_w_ref,
    bias_w_ref,
    att_out_w_ref,
    grad_pair_ref,
    grad_gains_ref,
    grad_edge_ref,
    grad_gate_w_ref,
    grad_out_w_ref,
    grad_att_w_ref,
    grad_bias_ref,
    grad_att_out_ref,
    *scratch,
):
    part, at = {}, 0
    for name, arrays in kernel_scratch(size, 1).items():
        part[name] = scratch[at : at + len(arrays)]
        at += len(arrays)
    sent = scratch[at]
    weights = (edge_w_ref, gate_w_ref, out_w_ref)
    sources = (gathered_ref, received_ref)
    multiply_kernel(
        size, masks, sources, lengths_ref, gains_ref, *weights, *part["kept"], *part["y"], *part["halves"], *part["multiply"]
    )
    project_kernel(size, *part["y"], att_w_ref, bias_w_ref, *part["projections"])
    att_sum_ref, att_out_sum_ref, gain_part_ref = part["sums"]
    attend_kernel(
        size,
        masks,
        sources,
        lengths_ref,
        att_w_ref,
        att_out_w_ref,
        *part["projections"],
        *part["shared"],
        att_sum_ref,
        grad_bias_ref,
        att_out_sum_ref,
        gain_part_ref,
        *part["attend"],
    )
    copies = [
        pltpu.make_async_copy(source, target, sent.at[slot])
        for slot, (source, target) in enumerate(((att_sum_ref, grad_att_w_ref), (att_out_sum_ref, grad_att_out_ref)))
    ]
    for copy in copies:
        copy.start()
    edges_kernel(
        size,
        2 * len(masks),
        pair_own_ref,
        gains_ref,
        *weights,
        *part["kept"],
        *part["halves"],
        *part["shared"],
        gain_part_ref,
        grad_pair_ref,
        grad_gains_ref,
        grad_edge_ref,
        grad_gate_w_ref,
        grad_out_w_ref,
        *part["edges"],
    )
    for copy in copies:
        copy.wait()


def replicated_plan(
    axis_size,
    pair_map,
    cotangent,
    lengths,
    norm_gains,
    edge_weight,
    mult_gate_weight,
    mult_out_weight,
    attention_weight,
    bias_weight,
    attention_out_weight,
):
    _, size, channels = pair_map.shape
    cells = size * size
    bits = axis_size.bit_length() - 1
    far_step = 1 << (bits - 1)
    near_steps = range(2, far_step, 2)

    odd = range(1, axis_size, 2)

    def swapped(held, mask):
        return lax.ppermute(held, "dap", [(d, d ^ mask) for d in odd])

    own = jnp.stack([pair_map, cotangent])
    held = jnp.stack([lax.ppermute(own, "dap", [(d - 1, d) for d in odd]), own])[None]
    held = jnp.concatenate([held, swapped(held, far_step)], axis=0)
    masks = [0, far_step]
    gathered = jnp.concatenate([held] + [swapped(held, step) for step in near_steps], axis=0)
    masks = masks + [mask ^ step for step in near_steps for mask in masks]
    received = lax.ppermute(gathered, "dap", [(d, d - 1) for d in odd])

    square, wide = ((channels, channels), FULL), ((channels, 4 * channels), FULL)
    outs = [((cells // axis_size, channels), HALF), ((3, channels), FULL), wide, square, square]
    outs += [wide, ((HEADS, channels), FULL), square]
    scratch = sum(kernel_scratch(size, channels).values(), [])
    vmem = pl.BlockSpec(memory_space=pltpu.VMEM)
    smem = pl.BlockSpec(memory_space=pltpu.SMEM)
    anywhere = pl.BlockSpec(memory_space=pl.ANY)
    results = pl.pallas_call(
        functools.partial(whole_kernel, size, masks),
        out_shape=[jax.ShapeDtypeStruct(*out) for out in outs],
        in_specs=[vmem] * 3 + [smem] + [vmem] * 7,
        out_specs=[vmem] * 5 + [anywhere, vmem, anywhere],
        scratch_shapes=[pltpu.VMEM(*part) for part in scratch] + [pltpu.SemaphoreType.DMA((2,))],
        compiler_params=pltpu.CompilerParams(vmem_limit_bytes=bytes_of(scratch) + VMEM_SLACK),
    )(
        pair_map,
        gathered,
        received,
        lengths,
        norm_gains,
        edge_weight,
        mult_gate_weight,
        mult_out_weight,
        attention_weight,
        bias_weight.T,
        attention_out_weight,
    )
    return (results[0].reshape(pair_map.shape), *results[1:6], results[6].T, results[7])


def per_device(axis_size, pair_map, *rest):
    _, size, channels = pair_map.shape
    scratch = sum(kernel_scratch(size, channels).values(), [])
    fits = size % ROW_BLOCK == 0 and bytes_of(scratch) <= VMEM_SHARE
    if fits and axis_size >= 8 and axis_size & (axis_size - 1) == 0:
        return replicated_plan(axis_size, pair_map, *rest)
    return distributed_plan(pair_map, *rest)


def solution(mesh):
    return jax.shard_map(
        functools.partial(per_device, mesh.shape["dap"]),
        mesh=mesh,
        in_specs=(
            P(("groups", "dap"), None, None),
            P(("groups", "dap"), None, None),
            P("groups"),
            P(),
            P(),
            P(),
            P(),
            P(),
            P(),
            P(),
        ),
        out_specs=(
            P(("groups", "dap"), None, None),
            P("groups", None),
            P("groups", None),
            P("groups", None),
            P("groups", None),
            P("groups", None),
            P("groups", None),
            P("groups", None),
        ),
        check_vma=False,
    )
```

```python
import functools
import math

import jax
import jax.numpy as jnp
from jax import lax
from jax.experimental import pallas as pl
from jax.experimental.pallas import tpu as pltpu
from jax.sharding import PartitionSpec as P

HEADS = 4
HEAD_DIM = 32


epsilon = 1e-05


def norm_forward(values, gain_row):
    center = values - jnp.mean(values, axis=-1, keepdims=True)
    inv_std = lax.rsqrt(jnp.mean(center * center, axis=-1, keepdims=True) + epsilon)
    normed = center * inv_std
    return (normed * gain_row, normed, inv_std)


def norm_backward(grad_out, normed, inv_std, gain_row):
    scaled = grad_out * gain_row
    first_mean = jnp.mean(scaled, axis=-1, keepdims=True)
    second_mean = jnp.mean(scaled * normed, axis=-1, keepdims=True)
    return inv_std * (scaled - first_mean - normed * second_mean)


def distributed_plan(
    pair_map,
    cotangent,
    lengths,
    norm_gains,
    edge_weight,
    mult_gate_weight,
    mult_out_weight,
    attention_weight,
    bias_weight,
    attention_out_weight,
):
    row_count, full_size, channels = pair_map.shape
    inner_width = HEADS * HEAD_DIM
    head_scale = 1.0 / math.sqrt(HEAD_DIM)
    first_row = lax.axis_index("dap") * row_count
    real_count = lengths[0]
    valid_all = (jnp.arange(full_size) < real_count).astype(jnp.float32)
    valid_rows = (first_row + jnp.arange(row_count) < real_count).astype(jnp.float32)
    mask_pair = (valid_rows[:, None] * valid_all[None, :])[:, :, None]
    pair_f32 = pair_map.astype(jnp.float32)
    normed_full, hat_in, scale_in = norm_forward(pair_f32, norm_gains[0])
    normed_x = normed_full.astype(jnp.bfloat16)
    projected = jnp.einsum("rnc,cf->rnf", normed_x, edge_weight, preferred_element_type=jnp.float32)
    left_gate = projected[..., :channels]
    left_value = projected[..., channels : 2 * channels]
    right_gate = projected[..., 2 * channels : 3 * channels]
    right_value = projected[..., 3 * channels :]
    left_sig = jax.nn.sigmoid(left_gate)
    right_sig = jax.nn.sigmoid(right_gate)
    left_edges = (mask_pair * left_sig * left_value).astype(jnp.bfloat16)
    right_edges = (mask_pair * right_sig * right_value).astype(jnp.bfloat16)
    product = jnp.einsum(
        "ikc,jkc->ijc",
        left_edges,
        lax.all_gather(right_edges, "dap", axis=0, tiled=True),
        preferred_element_type=jnp.float32,
    )
    update_full, hat_mid, scale_mid = norm_forward(product, norm_gains[1])
    update = update_full.astype(jnp.bfloat16)
    edge_out = jnp.einsum(
        "rnc,cf->rnf", update, mult_out_weight, preferred_element_type=jnp.float32
    )
    gate_sig = jax.nn.sigmoid(
        jnp.einsum("rnc,cf->rnf", normed_x, mult_gate_weight, preferred_element_type=jnp.float32)
    )
    middle = pair_f32 + gate_sig * edge_out
    normed_mid, hat_attn, scale_attn = norm_forward(middle, norm_gains[2])
    normed_y = normed_mid.astype(jnp.bfloat16)
    bias_local = jnp.einsum(
        "kic,ch->hki", normed_y, bias_weight, preferred_element_type=jnp.float32
    ).astype(jnp.bfloat16)
    bias_whole = lax.all_gather(bias_local, "dap", axis=1, tiled=True)
    bias_query = jnp.swapaxes(bias_whole, 1, 2).astype(jnp.float32)
    column_y, column_cot = (
        lax.all_to_all(normed_y, "dap", split_axis=1, concat_axis=0, tiled=True),
        lax.all_to_all(cotangent, "dap", split_axis=1, concat_axis=0, tiled=True),
    )
    packed = jnp.einsum(
        "ijc,cf->ijf", column_y, attention_weight, preferred_element_type=jnp.float32
    )
    packed = packed.reshape(full_size, row_count, 4, HEADS, HEAD_DIM)
    query_vectors = (packed[:, :, 0] * head_scale).astype(jnp.bfloat16)
    key_vectors = packed[:, :, 1].astype(jnp.bfloat16)
    value_vectors = packed[:, :, 2].astype(jnp.bfloat16)
    att_gate = jax.nn.sigmoid(packed[:, :, 3])
    scores = (
        jnp.einsum(
            "ijhd,kjhd->jhik", query_vectors, key_vectors, preferred_element_type=jnp.float32
        )
        + bias_query[None]
    )
    exp_scores = valid_all * jnp.exp(scores)
    attention = exp_scores / jnp.sum(exp_scores, axis=-1, keepdims=True)
    attention_half = attention.astype(jnp.bfloat16)
    attended = jnp.einsum(
        "jhik,kjhd->ijhd", attention_half, value_vectors, preferred_element_type=jnp.float32
    )
    gated = (att_gate * attended).astype(jnp.bfloat16).reshape(full_size, row_count, inner_width)
    part_attn_out = jnp.einsum("ijf,ijc->fc", gated, column_cot, preferred_element_type=jnp.float32)
    grad_gated = jnp.einsum(
        "ijc,fc->ijf", column_cot, attention_out_weight, preferred_element_type=jnp.float32
    )
    grad_gated = grad_gated.reshape(full_size, row_count, HEADS, HEAD_DIM)
    grad_att = (grad_gated * att_gate).astype(jnp.bfloat16)
    grad_gate_pre = grad_gated * attended * att_gate * (1.0 - att_gate)
    grad_attention = jnp.einsum(
        "ijhd,kjhd->jhik", grad_att, value_vectors, preferred_element_type=jnp.float32
    )
    row_dots = jnp.transpose(jnp.sum(grad_att.astype(jnp.float32) * attended, axis=-1), (1, 2, 0))
    grad_scores = attention * (grad_attention - row_dots[..., None])
    scores_half = grad_scores.astype(jnp.bfloat16)
    grad_query = jnp.einsum(
        "jhik,kjhd->ijhd", scores_half, key_vectors, preferred_element_type=jnp.float32
    )
    grad_key = jnp.einsum(
        "jhik,ijhd->kjhd", scores_half, query_vectors, preferred_element_type=jnp.float32
    )
    grad_value = jnp.einsum(
        "jhik,ijhd->kjhd", attention_half, grad_att, preferred_element_type=jnp.float32
    )
    grad_packed = jnp.stack([grad_query * head_scale, grad_key, grad_value, grad_gate_pre], axis=2)
    grad_packed = grad_packed.reshape(full_size, row_count, 4 * inner_width).astype(jnp.bfloat16)
    part_attention = jnp.einsum(
        "ijc,ijf->cf", column_y, grad_packed, preferred_element_type=jnp.float32
    )
    column_grad = jnp.einsum(
        "ijf,cf->ijc", grad_packed, attention_weight, preferred_element_type=jnp.float32
    ).astype(jnp.bfloat16)
    row_grad = lax.all_to_all(column_grad, "dap", split_axis=0, concat_axis=1, tiled=True)
    score_sums = jnp.sum(grad_scores, axis=0)
    taken = score_sums
    bias_half = lax.psum_scatter(
        jnp.transpose(taken, (2, 0, 1)), "dap", scatter_dimension=0, tiled=True
    ).astype(jnp.bfloat16)
    part_bias = jnp.einsum("kic,khi->ch", normed_y, bias_half, preferred_element_type=jnp.float32)
    grad_normed_y = row_grad.astype(jnp.float32) + jnp.einsum(
        "khi,ch->kic", bias_half, bias_weight, preferred_element_type=jnp.float32
    )
    part_gain_attn = jnp.sum(grad_normed_y * hat_attn, axis=(0, 1))
    grad_middle = cotangent.astype(jnp.float32) + norm_backward(
        grad_normed_y, hat_attn, scale_attn, norm_gains[2]
    )
    grad_edge_out = (grad_middle * gate_sig).astype(jnp.bfloat16)
    grad_gate = (grad_middle * edge_out * gate_sig * (1.0 - gate_sig)).astype(jnp.bfloat16)
    part_mult_out = jnp.einsum(
        "rnc,rnf->cf", update, grad_edge_out, preferred_element_type=jnp.float32
    )
    part_mult_gate = jnp.einsum(
        "rnc,rnf->cf", normed_x, grad_gate, preferred_element_type=jnp.float32
    )
    grad_update = jnp.einsum(
        "rnf,cf->rnc", grad_edge_out, mult_out_weight, preferred_element_type=jnp.float32
    )
    part_gain_mid = jnp.sum(grad_update * hat_mid, axis=(0, 1))
    grad_product = norm_backward(grad_update, hat_mid, scale_mid, norm_gains[1]).astype(
        jnp.bfloat16
    )
    taken = grad_product
    grad_left = jnp.einsum(
        "ijc,jkc->ikc",
        taken,
        lax.all_gather(right_edges, "dap", axis=0, tiled=True),
        preferred_element_type=jnp.float32,
    )
    grad_cols = lax.all_to_all(grad_product, "dap", split_axis=1, concat_axis=0, tiled=True)
    taken = grad_cols
    grad_right = jnp.einsum(
        "ijc,ikc->jkc",
        taken,
        lax.all_gather(left_edges, "dap", axis=0, tiled=True),
        preferred_element_type=jnp.float32,
    )
    grad_proj = jnp.concatenate(
        [
            grad_left * mask_pair * left_value * left_sig * (1.0 - left_sig),
            grad_left * mask_pair * left_sig,
            grad_right * mask_pair * right_value * right_sig * (1.0 - right_sig),
            grad_right * mask_pair * right_sig,
        ],
        axis=-1,
    ).astype(jnp.bfloat16)
    part_edge = jnp.einsum("rnc,rnf->cf", normed_x, grad_proj, preferred_element_type=jnp.float32)
    grad_normed_x = jnp.einsum(
        "rnf,cf->rnc", grad_proj, edge_weight, preferred_element_type=jnp.float32
    )
    grad_normed_x = grad_normed_x + jnp.einsum(
        "rnf,cf->rnc", grad_gate, mult_gate_weight, preferred_element_type=jnp.float32
    )
    part_gain_in = jnp.sum(grad_normed_x * hat_in, axis=(0, 1))
    grad_pair = (
        grad_middle + norm_backward(grad_normed_x, hat_in, scale_in, norm_gains[0])
    ).astype(jnp.bfloat16)
    totals = lax.psum(
        (
            part_gain_in,
            part_gain_mid,
            part_edge,
            part_mult_gate,
            part_mult_out,
            part_gain_attn,
            part_attention,
            part_bias,
            part_attn_out,
        ),
        "dap",
    )
    (
        gain_in_sum,
        gain_mid_sum,
        edge_sum,
        mult_gate_sum,
        mult_out_sum,
        gain_attn_sum,
        attention_sum,
        bias_sum,
        attn_out_sum,
    ) = totals
    inverse = 1.0 / full_size
    grad_gains = jnp.stack([gain_in_sum, gain_mid_sum, gain_attn_sum]) * inverse
    return (
        grad_pair,
        grad_gains,
        edge_sum * inverse,
        mult_gate_sum * inverse,
        mult_out_sum * inverse,
        attention_sum * inverse,
        bias_sum * inverse,
        attn_out_sum * inverse,
    )


ROW_BLOCK = 8
VMEM_SLACK = 8 * 2**20
VMEM_SHARE = 32 * 2**20
HALF = jnp.bfloat16
FULL = jnp.float32


def dot_nn(left, right):
    return lax.dot_general(left, right, (((1,), (0,)), ((), ())), preferred_element_type=FULL)


def dot_nt(left, right):
    return lax.dot_general(left, right, (((1,), (1,)), ((), ())), preferred_element_type=FULL)


def dot_tn(left, right):
    return lax.dot_general(left, right, (((0,), (0,)), ((), ())), preferred_element_type=FULL)


def lane_mean(values):
    return jnp.mean(values, axis=-1, keepdims=True)


def sigmoid(values):
    return pltpu.reciprocal(1.0 + jnp.exp(-values), approx=True)


def head_blocks(row_width, col_width, dtype):
    shape = (HEADS * row_width, HEADS * col_width)
    row = lax.broadcasted_iota(jnp.int32, shape, 0)
    col = lax.broadcasted_iota(jnp.int32, shape, 1)
    same = None
    for h in range(HEADS):
        here = (row >= h * row_width) & (row < (h + 1) * row_width)
        here = here & (col >= h * col_width) & (col < (h + 1) * col_width)
        same = here if same is None else same | here
    return jnp.where(same, 1.0, 0.0).astype(dtype)


def place_rows(target, part, near_ref, far_ref, masks):
    me = lax.axis_index("dap")
    cells = target.shape[0] // (2 * len(masks))
    for other, blocks in enumerate((near_ref, far_ref)):
        for at, mask in enumerate(masks):
            place = pl.ds(pl.multiple_of((me ^ mask ^ other) * cells, cells), cells)
            target[place, :] = blocks[at, part].reshape(cells, target.shape[1]).astype(FULL)


def block_tools(size):
    block = ROW_BLOCK * size

    def rows_of(at):
        return pl.ds(pl.multiple_of(at * block, block), block)

    def columns_of(ref, at):
        return jnp.concatenate(
            [ref[pl.ds(at * ROW_BLOCK + a, size, stride=size), :] for a in range(ROW_BLOCK)], axis=0
        )

    return rows_of, columns_of


def outer_sum(size, at, row_ref, row_stride, block_stride, block_ref):
    sums = [jnp.zeros((size, block_ref.shape[1]), FULL)] * ROW_BLOCK
    for k in range(size):
        whole = block_ref[k * size : (k + 1) * size, :]
        for a in range(ROW_BLOCK):
            row = (at * ROW_BLOCK + a) * block_stride + k * row_stride
            sums[a] = sums[a] + row_ref[pl.ds(row, 1), :] * whole
    return jnp.concatenate(sums, axis=0)


def cell_of_lane(size):
    lane = lax.broadcasted_iota(jnp.int32, (1, HEADS * size), 1)
    cell = lane
    for h in range(1, HEADS):
        cell = jnp.where(lane >= h * size, lane - h * size, cell)
    return cell


def spread_bias_weight(target, bias_w_ref, size):
    bias_rows = bias_w_ref[...].astype(FULL)
    for h in range(HEADS):
        target[h * size : (h + 1) * size, :] = jnp.broadcast_to(
            bias_rows[h : h + 1], (size, bias_rows.shape[1])
        ).astype(HALF)


def multiply_kernel(
    size,
    masks,
    near_ref,
    far_ref,
    lengths_ref,
    gains_ref,
    edge_w_ref,
    gate_w_ref,
    out_w_ref,
    left_ref,
    right_ref,
    left_a_ref,
    left_b_ref,
    right_a_ref,
    right_b_ref,
    gate_ref,
    hat_mid_ref,
    scale_mid_ref,
    edge_out_ref,
    hat_y_ref,
    scale_y_ref,
    y_ref,
    x_half_ref,
    update_ref,
    pair_ref,
    right_t_ref,
):
    channels = gains_ref.shape[1]
    block = ROW_BLOCK * size
    blocks = size // ROW_BLOCK
    rows_of, columns_of = block_tools(size)
    real = lengths_ref[0]
    gain_x = gains_ref[0:1, :]
    gain_mid = gains_ref[1:2, :]
    gain_y = gains_ref[2:3, :]
    place_rows(pair_ref, 0, near_ref, far_ref, masks)

    def project(at, carry):
        rows = rows_of(at)
        hat, _ = kernel_norm(pair_ref[rows, :])
        normed = (hat * gain_x).astype(HALF)
        x_half_ref[rows, :] = normed
        projected = dot_nn(normed, edge_w_ref[...])
        gate_ref[rows, :] = sigmoid(dot_nn(normed, gate_w_ref[...]))
        shape = (ROW_BLOCK, size, channels)
        row = lax.broadcasted_iota(jnp.int32, shape, 0) + at * ROW_BLOCK
        col = lax.broadcasted_iota(jnp.int32, shape, 1)
        mask = jnp.where((row < real) & (col < real), 1.0, 0.0).reshape(block, channels)
        for side, (edge, first, second) in enumerate(
            ((left_ref, left_a_ref, left_b_ref), (right_ref, right_a_ref, right_b_ref))
        ):
            base = 2 * side * channels
            sig = sigmoid(projected[:, base : base + channels])
            value = projected[:, base + channels : base + 2 * channels]
            masked = mask * sig
            product = masked * value
            edge[rows, :] = product.astype(HALF).astype(FULL)
            first[rows, :] = product * (1.0 - sig)
            second[rows, :] = masked
        return carry

    lax.fori_loop(0, blocks, project, 0, unroll=4)

    def turn(at, carry):
        right_t_ref[rows_of(at), :] = columns_of(right_ref, at)
        return carry

    lax.fori_loop(0, blocks, turn, 0, unroll=4)

    def multiply(at, carry):
        rows = rows_of(at)
        product = outer_sum(size, at, left_ref, 1, size, right_t_ref)
        hat, scale = kernel_norm(product)
        hat_mid_ref[rows, :] = hat
        scale_mid_ref[rows, :] = jnp.broadcast_to(scale, hat.shape)
        update = (hat * gain_mid).astype(HALF)
        update_ref[rows, :] = update
        edge_out = dot_nn(update, out_w_ref[...])
        edge_out_ref[rows, :] = edge_out
        middle = pair_ref[rows, :] + gate_ref[rows, :] * edge_out
        hat, scale = kernel_norm(middle)
        hat_y_ref[rows, :] = hat
        scale_y_ref[rows, :] = jnp.broadcast_to(scale, hat.shape)
        y_ref[rows, :] = hat * gain_y
        return carry

    lax.fori_loop(0, blocks, multiply, 0, unroll=4)


def project_kernel(
    size,
    y_ref,
    att_w_ref,
    bias_w_ref,
    att_gate_ref,
    bias_ref,
    y_t_ref,
    query_ref,
    key_ref,
    value_ref,
    bias_rep_ref,
):
    channels = y_ref.shape[1]
    lanes = HEADS * size
    head_scale = 1.0 / math.sqrt(HEAD_DIM)
    rows_of, columns_of = block_tools(size)
    cell = cell_of_lane(size)
    spread_bias_weight(bias_rep_ref, bias_w_ref, size)

    def prepare(at, carry):
        rows = rows_of(at)
        y = columns_of(y_ref, at).astype(HALF)
        y_t_ref[rows, :] = y
        packed = dot_nn(y, att_w_ref[...])
        query_ref[rows, :] = (packed[:, :channels] * head_scale).astype(HALF)
        key_ref[rows, :] = packed[:, channels : 2 * channels].astype(HALF)
        value_ref[rows, :] = packed[:, 2 * channels : 3 * channels].astype(HALF)
        att_gate_ref[rows, :] = sigmoid(packed[:, 3 * channels :])
        spread = dot_nt(y, bias_rep_ref[...]).astype(HALF).astype(FULL)
        for a in range(ROW_BLOCK):
            carry = carry + jnp.where(cell == at * ROW_BLOCK + a, spread[a * size : (a + 1) * size], 0.0)
        return carry

    bias_ref[...] = lax.fori_loop(
        0, size // ROW_BLOCK, prepare, jnp.zeros((size, lanes), FULL), unroll=4
    )


def attend_kernel(
    size,
    masks,
    near_ref,
    far_ref,
    lengths_ref,
    att_w_ref,
    att_out_w_ref,
    att_gate_ref,
    bias_ref,
    y_t_ref,
    query_ref,
    key_ref,
    value_ref,
    bias_rep_ref,
    cot_ref,
    grad_y_ref,
    cot_t_ref,
    gated_ref,
    grad_packed_ref,
):
    channels = cot_ref.shape[1]
    block = ROW_BLOCK * size
    blocks = size // ROW_BLOCK
    lanes = HEADS * size
    head_scale = 1.0 / math.sqrt(HEAD_DIM)
    rows_of, columns_of = block_tools(size)
    cell = cell_of_lane(size)
    key_row = lax.broadcasted_iota(jnp.int32, (size, lanes), 0)
    valid = jnp.where(key_row < lengths_ref[0], 1.0, 0.0)
    place_rows(cot_ref, 1, near_ref, far_ref, masks)

    head_mask = head_blocks(size, HEAD_DIM, HALF)
    head_mask_full = head_blocks(size, HEAD_DIM, FULL)
    no_rows = jnp.zeros((size, channels), HALF)

    def attend(at, score_sum):
        rows = rows_of(at)
        parts = [slice(a * size, (a + 1) * size) for a in range(ROW_BLOCK)]
        query, key, value = (ref[rows, :] for ref in (query_ref, key_ref, value_ref))
        gate = att_gate_ref[rows, :]
        cot = columns_of(cot_ref, at).astype(HALF)
        cot_t_ref[rows, :] = cot
        grad_gated = dot_nt(cot, att_out_w_ref[...])
        grad_att = (grad_gated * gate).astype(HALF)
        queries = [jnp.concatenate([query[p]] * HEADS, axis=0) * head_mask for p in parts]
        grads = [jnp.concatenate([grad_att[p]] * HEADS, axis=0) * head_mask for p in parts]
        bias = bias_ref[...]

        def stacked(columns):
            return jnp.stack(columns, axis=0)

        scores = stacked([dot_nt(key[p], queries[a]) + bias for a, p in enumerate(parts)])
        grad_attention = stacked([dot_nt(value[p], grads[a]) for a, p in enumerate(parts)])
        exp_scores = valid[None] * jnp.exp(scores)
        total = jnp.sum(exp_scores, axis=1)
        scale = jnp.where(total > 2.0**100, 2.0**-60, 1.0)
        inverse_total = pltpu.reciprocal(total * scale, approx=True)
        attention = (exp_scores * scale[:, None, :]) * inverse_total[:, None, :]
        row_dots = jnp.sum(attention * grad_attention, axis=1)
        grad_scores = attention * (grad_attention - row_dots[:, None, :])
        score_sum = score_sum + jnp.sum(grad_scores, axis=0)
        attention_half = attention.astype(HALF)
        scores_half = grad_scores.astype(HALF)
        grad_key = jnp.concatenate([dot_nn(scores_half[a], queries[a]) for a in range(ROW_BLOCK)], axis=0)
        grad_value = jnp.concatenate([dot_nn(attention_half[a], grads[a]) for a in range(ROW_BLOCK)], axis=0)

        def query_sums(a, p):
            weights = jnp.concatenate([attention_half[a], scores_half[a]], axis=0)
            vectors = jnp.concatenate(
                [
                    jnp.concatenate([value[p], no_rows], axis=1),
                    jnp.concatenate([no_rows, key[p]], axis=1),
                ],
                axis=0,
            )
            whole = dot_tn(weights, vectors)
            masked = [whole[:, :channels] * head_mask_full, whole[:, channels:] * head_mask_full]
            return [sum(part[h * size : (h + 1) * size] for h in range(HEADS)) for part in masked]

        per_query = [query_sums(a, p) for a, p in enumerate(parts)]
        attended = jnp.concatenate([pair[0] for pair in per_query], axis=0)
        grad_query = jnp.concatenate([pair[1] for pair in per_query], axis=0)
        gated = gate * attended
        gated_ref[rows, :] = gated.astype(HALF)
        grad_gate_pre = grad_gated * gated * (1.0 - gate)
        grad_packed = jnp.concatenate(
            [
                (grad_query * head_scale).astype(HALF),
                grad_key.astype(HALF),
                grad_value.astype(HALF),
                grad_gate_pre.astype(HALF),
            ],
            axis=1,
        )
        grad_packed_ref[rows, : 4 * channels] = grad_packed
        grad_y_ref[rows, :] = dot_nt(grad_packed, att_w_ref[...])
        return score_sum

    score_sum = lax.fori_loop(0, blocks, attend, jnp.zeros((size, lanes), FULL), unroll=4)
    bias_grad = score_sum.astype(HALF).astype(FULL)

    def spread_bias(at, carry):
        rows = rows_of(at)
        spread = jnp.concatenate(
            [jnp.where(cell == at * ROW_BLOCK + a, bias_grad, 0.0) for a in range(ROW_BLOCK)], axis=0
        ).astype(HALF)
        grad_packed_ref[rows, 4 * channels :] = spread
        grad_y_ref[rows, :] += dot_nn(spread, bias_rep_ref[...])
        return carry

    lax.fori_loop(0, blocks, spread_bias, 0, unroll=4)


def gain_sum(pairs):
    total = sum(jnp.sum(weight.astype(FULL) * grad, axis=1, keepdims=True) for weight, grad in pairs)
    channels = total.shape[0]
    return jnp.transpose(jnp.broadcast_to(total, (channels, channels)))[0:1, :]


def edges_kernel(
    size,
    devices,
    pair_ref,
    gains_ref,
    edge_w_ref,
    gate_w_ref,
    out_w_ref,
    left_ref,
    right_ref,
    left_a_ref,
    left_b_ref,
    right_a_ref,
    right_b_ref,
    gate_ref,
    hat_mid_ref,
    scale_mid_ref,
    edge_out_ref,
    hat_y_ref,
    scale_y_ref,
    x_half_ref,
    update_ref,
    cot_ref,
    grad_y_ref,
    attention_side,
    grad_pair_ref,
    grad_gains_ref,
    grad_bias_ref,
    stage_refs,
    send,
    grad_middle_ref,
    grad_product_ref,
    grad_proj_ref,
    x_sum_ref,
    y_sum_ref,
):
    channels = gains_ref.shape[1]
    blocks = size // ROW_BLOCK
    rows_of, columns_of = block_tools(size)
    gain_x = gains_ref[0:1, :]
    gain_mid = gains_ref[1:2, :]
    gain_y = gains_ref[2:3, :]

    inverse = 1.0 / size
    y_t_ref, cot_t_ref, gated_ref, grad_packed_ref, att_w_ref, bias_rep_ref = attention_side
    edge_sum_ref, gate_sum_ref, out_sum_ref, att_sum_ref, att_out_sum_ref = stage_refs
    for sum_ref in (x_sum_ref, y_sum_ref, out_sum_ref, att_out_sum_ref):
        sum_ref[...] = jnp.zeros(sum_ref.shape, FULL)

    def attention_sums(at):
        rows = rows_of(at)
        y_sum_ref[...] += dot_tn(y_t_ref[rows, :], grad_packed_ref[rows, :])
        att_out_sum_ref[...] += dot_tn(gated_ref[rows, :], cot_t_ref[rows, :])

    def attention_results():
        att_sum = y_sum_ref[:, : 4 * channels] * inverse
        bias_sum = jnp.transpose(y_sum_ref[:, 4 * channels :] * inverse)
        att_sum_ref[...] = att_sum
        att_out_sum_ref[...] *= inverse
        send(3, 4)
        for h in range(HEADS):
            grad_bias_ref[h : h + 1, :] = jnp.sum(
                bias_sum[h * size : (h + 1) * size], axis=0, keepdims=True
            )
        bias_part = jnp.sum(bias_rep_ref[...].astype(FULL) * bias_sum, axis=0, keepdims=True)
        grad_gains_ref[2:3, :] = (gain_sum(((att_w_ref[...], att_sum),)) + bias_part) / gain_y

    def middle_back(at, carry):
        rows = rows_of(at)
        grad_y = columns_of(grad_y_ref, at)
        grad_middle = cot_ref[rows, :] + kernel_norm_back(
            grad_y, hat_y_ref[rows, :], scale_y_ref[rows, :], gain_y
        )
        grad_middle_ref[rows, :] = grad_middle
        gate = gate_ref[rows, :]
        gated = grad_middle * gate
        grad_edge_out = gated.astype(HALF)
        grad_gate = (gated * edge_out_ref[rows, :] * (1.0 - gate)).astype(HALF)
        grad_proj_ref[rows, 4 * channels :] = grad_gate
        x_sum_ref[:, 4 * channels :] += dot_tn(x_half_ref[rows, :], grad_gate)
        out_sum_ref[...] += dot_tn(update_ref[rows, :], grad_edge_out)
        grad_update = dot_nt(grad_edge_out, out_w_ref[...])
        grad_product = kernel_norm_back(grad_update, hat_mid_ref[rows, :], scale_mid_ref[rows, :], gain_mid)
        grad_product_ref[rows, :] = grad_product.astype(HALF).astype(FULL)
        return carry

    lax.fori_loop(0, blocks, middle_back, 0, unroll=4)

    def edges_back(at):
        rows = rows_of(at)
        x_half = x_half_ref[rows, :]
        for side, (first_ref, second_ref, strides, other_ref) in enumerate(
            (
                (left_a_ref, left_b_ref, (1, size), right_ref),
                (right_a_ref, right_b_ref, (size, 1), left_ref),
            )
        ):
            grad = outer_sum(size, at, grad_product_ref, *strides, other_ref)
            both = jnp.concatenate(
                [(grad * first_ref[rows, :]).astype(HALF), (grad * second_ref[rows, :]).astype(HALF)], axis=1
            )
            place = slice(2 * side * channels, 2 * (side + 1) * channels)
            grad_proj_ref[rows, place] = both
            x_sum_ref[:, place] += dot_tn(x_half, both)

    for at in range(blocks):
        for part in range(2 * at, min(2 * at + 2, blocks)):
            attention_sums(part)
        edges_back(at)
        if 2 * at < blocks <= 2 * at + 2:
            attention_results()

    edge_sum, gate_sum = x_sum_ref[:, : 4 * channels] * inverse, x_sum_ref[:, 4 * channels :] * inverse
    edge_sum_ref[...] = edge_sum
    gate_sum_ref[...] = gate_sum
    out_sum = out_sum_ref[...] * inverse
    out_sum_ref[...] = out_sum
    send(0, 1, 2)
    grad_gains_ref[0:1, :] = gain_sum(((edge_w_ref[...], edge_sum), (gate_w_ref[...], gate_sum))) / gain_x
    grad_gains_ref[1:2, :] = gain_sum(((out_w_ref[...], out_sum),)) / gain_mid

    own_cells = size * size // devices
    own = pl.ds(pl.multiple_of(lax.axis_index("dap") * own_cells, own_cells), own_cells)
    hat, scale = kernel_norm(pair_ref[...].reshape(own_cells, channels).astype(FULL))
    grad_x = dot_nt(grad_proj_ref[own, : 4 * channels], edge_w_ref[...])
    grad_x = grad_x + dot_nt(grad_proj_ref[own, 4 * channels :], gate_w_ref[...])
    grad_pair = grad_middle_ref[own, :] + kernel_norm_back(grad_x, hat, scale, gain_x)
    grad_pair_ref[...] = grad_pair.astype(grad_pair_ref.dtype)


def kernel_norm(values):
    center = values - lane_mean(values)
    scale = lax.rsqrt(lane_mean(center * center) + epsilon)
    return center * scale, scale


def kernel_norm_back(grad_out, hat, scale, gain):
    scaled = grad_out * gain
    return scale * (scaled - lane_mean(scaled) - hat * lane_mean(scaled * hat))


def bytes_of(arrays):
    return sum(math.prod(shape) * jnp.dtype(dtype).itemsize for shape, dtype in arrays)


def kernel_scratch(size, channels):
    cells, lanes = size * size, HEADS * size
    full, half = ((cells, channels), FULL), ((cells, channels), HALF)
    square, wide = ((channels, channels), FULL), ((channels, 4 * channels), FULL)
    return {
        "kept": [full] * 12,
        "y": [full],
        "halves": [half] * 2,
        "multiply": [full] * 2,
        "projections": [full, ((size, lanes), FULL)] + [half] * 4 + [((lanes, channels), HALF)],
        "shared": [full] * 2,
        "attend": [half] * 2 + [((cells, 4 * channels + lanes), HALF)],
        "stage": [wide, square, square, wide, square],
        "edges": [full] * 2
        + [((cells, 5 * channels), HALF), ((channels, 5 * channels), FULL), ((channels, 4 * channels + lanes), FULL)],
    }


def whole_kernel(
    size,
    masks,
    near_ref,
    far_ref,
    lengths_ref,
    gains_ref,
    edge_w_ref,
    gate_w_ref,
    out_w_ref,
    att_w_ref,
    bias_w_ref,
    att_out_w_ref,
    grad_pair_ref,
    grad_gains_ref,
    grad_edge_ref,
    grad_gate_w_ref,
    grad_out_w_ref,
    grad_att_w_ref,
    grad_bias_ref,
    grad_att_out_ref,
    *scratch,
):
    part, at = {}, 0
    for name, arrays in kernel_scratch(size, 1).items():
        part[name] = scratch[at : at + len(arrays)]
        at += len(arrays)
    sent = scratch[at]
    weights = (edge_w_ref, gate_w_ref, out_w_ref)
    multiply_kernel(
        size, masks, near_ref, far_ref, lengths_ref, gains_ref, *weights, *part["kept"], *part["y"], *part["halves"], *part["multiply"]
    )
    project_kernel(size, *part["y"], att_w_ref, bias_w_ref, *part["projections"])
    attend_kernel(
        size,
        masks,
        near_ref,
        far_ref,
        lengths_ref,
        att_w_ref,
        att_out_w_ref,
        *part["projections"],
        *part["shared"],
        *part["attend"],
    )
    targets = (grad_edge_ref, grad_gate_w_ref, grad_out_w_ref, grad_att_w_ref, grad_att_out_ref)
    copies = [
        pltpu.make_async_copy(source, target, sent.at[slot])
        for slot, (source, target) in enumerate(zip(part["stage"], targets))
    ]

    def send(*slots):
        for slot in slots:
            copies[slot].start()

    _, _, y_t_ref, _, _, _, bias_rep_ref = part["projections"]
    cot_t_ref, gated_ref, grad_packed_ref = part["attend"]
    edges_kernel(
        size,
        2 * len(masks),
        near_ref.at[0, 0],
        gains_ref,
        *weights,
        *part["kept"],
        *part["halves"],
        *part["shared"],
        (y_t_ref, cot_t_ref, gated_ref, grad_packed_ref, att_w_ref, bias_rep_ref),
        grad_pair_ref,
        grad_gains_ref,
        grad_bias_ref,
        part["stage"],
        send,
        *part["edges"],
    )
    for copy in copies:
        copy.wait()


def replicated_plan(
    axis_size,
    pair_map,
    cotangent,
    lengths,
    norm_gains,
    edge_weight,
    mult_gate_weight,
    mult_out_weight,
    attention_weight,
    bias_weight,
    attention_out_weight,
):
    _, size, channels = pair_map.shape
    cells = size * size
    bits = axis_size.bit_length() - 1
    far_step = 1 << (bits - 1)
    near_steps = range(2, far_step, 2)

    def swapped(held, mask):
        return lax.ppermute(held, "dap", [(d, d ^ mask) for d in range(axis_size)])

    own = jnp.stack([pair_map, cotangent])
    held = jnp.stack([own, swapped(own, far_step)])
    masks = [0, far_step]
    near = jnp.concatenate([held] + [swapped(held, step) for step in near_steps], axis=0)
    masks = masks + [mask ^ step for step in near_steps for mask in masks]
    far = swapped(near, 1)

    square, wide = ((channels, channels), FULL), ((channels, 4 * channels), FULL)
    outs = [((cells // axis_size, channels), HALF), ((3, channels), FULL), wide, square, square]
    outs += [wide, ((HEADS, channels), FULL), square]
    scratch = sum(kernel_scratch(size, channels).values(), [])
    vmem = pl.BlockSpec(memory_space=pltpu.VMEM)
    smem = pl.BlockSpec(memory_space=pltpu.SMEM)
    anywhere = pl.BlockSpec(memory_space=pl.ANY)
    results = pl.pallas_call(
        functools.partial(whole_kernel, size, masks),
        out_shape=[jax.ShapeDtypeStruct(*out) for out in outs],
        in_specs=[vmem, vmem, smem] + [vmem] * 7,
        out_specs=[vmem] * 2 + [anywhere] * 4 + [vmem, anywhere],
        scratch_shapes=[pltpu.VMEM(*part) for part in scratch] + [pltpu.SemaphoreType.DMA((5,))],
        compiler_params=pltpu.CompilerParams(vmem_limit_bytes=bytes_of(scratch) + VMEM_SLACK),
    )(
        near,
        far,
        lengths,
        norm_gains,
        edge_weight,
        mult_gate_weight,
        mult_out_weight,
        attention_weight,
        bias_weight.T,
        attention_out_weight,
    )
    return (results[0].reshape(pair_map.shape), *results[1:6], results[6].T, results[7])


def per_device(axis_size, pair_map, *rest):
    _, size, channels = pair_map.shape
    scratch = sum(kernel_scratch(size, channels).values(), [])
    fits = size % ROW_BLOCK == 0 and bytes_of(scratch) <= VMEM_SHARE
    if fits and axis_size >= 8 and axis_size & (axis_size - 1) == 0:
        return replicated_plan(axis_size, pair_map, *rest)
    return distributed_plan(pair_map, *rest)


def solution(mesh):
    return jax.shard_map(
        functools.partial(per_device, mesh.shape["dap"]),
        mesh=mesh,
        in_specs=(
            P(("groups", "dap"), None, None),
            P(("groups", "dap"), None, None),
            P("groups"),
            P(),
            P(),
            P(),
            P(),
            P(),
            P(),
            P(),
        ),
        out_specs=(
            P(("groups", "dap"), None, None),
            P("groups", None),
            P("groups", None),
            P("groups", None),
            P("groups", None),
            P("groups", None),
            P("groups", None),
            P("groups", None),
        ),
        check_vma=False,
    )
```

```python
import functools
import math

import jax
import jax.numpy as jnp
from jax import lax
from jax.experimental import pallas as pl
from jax.experimental.pallas import tpu as pltpu
from jax.sharding import PartitionSpec as P

HEADS = 4
HEAD_DIM = 32


epsilon = 1e-05


def norm_forward(values, gain_row):
    center = values - jnp.mean(values, axis=-1, keepdims=True)
    inv_std = lax.rsqrt(jnp.mean(center * center, axis=-1, keepdims=True) + epsilon)
    normed = center * inv_std
    return (normed * gain_row, normed, inv_std)


def norm_backward(grad_out, normed, inv_std, gain_row):
    scaled = grad_out * gain_row
    first_mean = jnp.mean(scaled, axis=-1, keepdims=True)
    second_mean = jnp.mean(scaled * normed, axis=-1, keepdims=True)
    return inv_std * (scaled - first_mean - normed * second_mean)


def distributed_plan(
    pair_map,
    cotangent,
    lengths,
    norm_gains,
    edge_weight,
    mult_gate_weight,
    mult_out_weight,
    attention_weight,
    bias_weight,
    attention_out_weight,
):
    row_count, full_size, channels = pair_map.shape
    inner_width = HEADS * HEAD_DIM
    head_scale = 1.0 / math.sqrt(HEAD_DIM)
    first_row = lax.axis_index("dap") * row_count
    real_count = lengths[0]
    valid_all = (jnp.arange(full_size) < real_count).astype(jnp.float32)
    valid_rows = (first_row + jnp.arange(row_count) < real_count).astype(jnp.float32)
    mask_pair = (valid_rows[:, None] * valid_all[None, :])[:, :, None]
    pair_f32 = pair_map.astype(jnp.float32)
    normed_full, hat_in, scale_in = norm_forward(pair_f32, norm_gains[0])
    normed_x = normed_full.astype(jnp.bfloat16)
    projected = jnp.einsum("rnc,cf->rnf", normed_x, edge_weight, preferred_element_type=jnp.float32)
    left_gate = projected[..., :channels]
    left_value = projected[..., channels : 2 * channels]
    right_gate = projected[..., 2 * channels : 3 * channels]
    right_value = projected[..., 3 * channels :]
    left_sig = jax.nn.sigmoid(left_gate)
    right_sig = jax.nn.sigmoid(right_gate)
    left_edges = (mask_pair * left_sig * left_value).astype(jnp.bfloat16)
    right_edges = (mask_pair * right_sig * right_value).astype(jnp.bfloat16)
    product = jnp.einsum(
        "ikc,jkc->ijc",
        left_edges,
        lax.all_gather(right_edges, "dap", axis=0, tiled=True),
        preferred_element_type=jnp.float32,
    )
    update_full, hat_mid, scale_mid = norm_forward(product, norm_gains[1])
    update = update_full.astype(jnp.bfloat16)
    edge_out = jnp.einsum(
        "rnc,cf->rnf", update, mult_out_weight, preferred_element_type=jnp.float32
    )
    gate_sig = jax.nn.sigmoid(
        jnp.einsum("rnc,cf->rnf", normed_x, mult_gate_weight, preferred_element_type=jnp.float32)
    )
    middle = pair_f32 + gate_sig * edge_out
    normed_mid, hat_attn, scale_attn = norm_forward(middle, norm_gains[2])
    normed_y = normed_mid.astype(jnp.bfloat16)
    bias_local = jnp.einsum(
        "kic,ch->hki", normed_y, bias_weight, preferred_element_type=jnp.float32
    ).astype(jnp.bfloat16)
    bias_whole = lax.all_gather(bias_local, "dap", axis=1, tiled=True)
    bias_query = jnp.swapaxes(bias_whole, 1, 2).astype(jnp.float32)
    column_y, column_cot = (
        lax.all_to_all(normed_y, "dap", split_axis=1, concat_axis=0, tiled=True),
        lax.all_to_all(cotangent, "dap", split_axis=1, concat_axis=0, tiled=True),
    )
    packed = jnp.einsum(
        "ijc,cf->ijf", column_y, attention_weight, preferred_element_type=jnp.float32
    )
    packed = packed.reshape(full_size, row_count, 4, HEADS, HEAD_DIM)
    query_vectors = (packed[:, :, 0] * head_scale).astype(jnp.bfloat16)
    key_vectors = packed[:, :, 1].astype(jnp.bfloat16)
    value_vectors = packed[:, :, 2].astype(jnp.bfloat16)
    att_gate = jax.nn.sigmoid(packed[:, :, 3])
    scores = (
        jnp.einsum(
            "ijhd,kjhd->jhik", query_vectors, key_vectors, preferred_element_type=jnp.float32
        )
        + bias_query[None]
    )
    exp_scores = valid_all * jnp.exp(scores)
    attention = exp_scores / jnp.sum(exp_scores, axis=-1, keepdims=True)
    attention_half = attention.astype(jnp.bfloat16)
    attended = jnp.einsum(
        "jhik,kjhd->ijhd", attention_half, value_vectors, preferred_element_type=jnp.float32
    )
    gated = (att_gate * attended).astype(jnp.bfloat16).reshape(full_size, row_count, inner_width)
    part_attn_out = jnp.einsum("ijf,ijc->fc", gated, column_cot, preferred_element_type=jnp.float32)
    grad_gated = jnp.einsum(
        "ijc,fc->ijf", column_cot, attention_out_weight, preferred_element_type=jnp.float32
    )
    grad_gated = grad_gated.reshape(full_size, row_count, HEADS, HEAD_DIM)
    grad_att = (grad_gated * att_gate).astype(jnp.bfloat16)
    grad_gate_pre = grad_gated * attended * att_gate * (1.0 - att_gate)
    grad_attention = jnp.einsum(
        "ijhd,kjhd->jhik", grad_att, value_vectors, preferred_element_type=jnp.float32
    )
    row_dots = jnp.transpose(jnp.sum(grad_att.astype(jnp.float32) * attended, axis=-1), (1, 2, 0))
    grad_scores = attention * (grad_attention - row_dots[..., None])
    scores_half = grad_scores.astype(jnp.bfloat16)
    grad_query = jnp.einsum(
        "jhik,kjhd->ijhd", scores_half, key_vectors, preferred_element_type=jnp.float32
    )
    grad_key = jnp.einsum(
        "jhik,ijhd->kjhd", scores_half, query_vectors, preferred_element_type=jnp.float32
    )
    grad_value = jnp.einsum(
        "jhik,ijhd->kjhd", attention_half, grad_att, preferred_element_type=jnp.float32
    )
    grad_packed = jnp.stack([grad_query * head_scale, grad_key, grad_value, grad_gate_pre], axis=2)
    grad_packed = grad_packed.reshape(full_size, row_count, 4 * inner_width).astype(jnp.bfloat16)
    part_attention = jnp.einsum(
        "ijc,ijf->cf", column_y, grad_packed, preferred_element_type=jnp.float32
    )
    column_grad = jnp.einsum(
        "ijf,cf->ijc", grad_packed, attention_weight, preferred_element_type=jnp.float32
    ).astype(jnp.bfloat16)
    row_grad = lax.all_to_all(column_grad, "dap", split_axis=0, concat_axis=1, tiled=True)
    score_sums = jnp.sum(grad_scores, axis=0)
    taken = score_sums
    bias_half = lax.psum_scatter(
        jnp.transpose(taken, (2, 0, 1)), "dap", scatter_dimension=0, tiled=True
    ).astype(jnp.bfloat16)
    part_bias = jnp.einsum("kic,khi->ch", normed_y, bias_half, preferred_element_type=jnp.float32)
    grad_normed_y = row_grad.astype(jnp.float32) + jnp.einsum(
        "khi,ch->kic", bias_half, bias_weight, preferred_element_type=jnp.float32
    )
    part_gain_attn = jnp.sum(grad_normed_y * hat_attn, axis=(0, 1))
    grad_middle = cotangent.astype(jnp.float32) + norm_backward(
        grad_normed_y, hat_attn, scale_attn, norm_gains[2]
    )
    grad_edge_out = (grad_middle * gate_sig).astype(jnp.bfloat16)
    grad_gate = (grad_middle * edge_out * gate_sig * (1.0 - gate_sig)).astype(jnp.bfloat16)
    part_mult_out = jnp.einsum(
        "rnc,rnf->cf", update, grad_edge_out, preferred_element_type=jnp.float32
    )
    part_mult_gate = jnp.einsum(
        "rnc,rnf->cf", normed_x, grad_gate, preferred_element_type=jnp.float32
    )
    grad_update = jnp.einsum(
        "rnf,cf->rnc", grad_edge_out, mult_out_weight, preferred_element_type=jnp.float32
    )
    part_gain_mid = jnp.sum(grad_update * hat_mid, axis=(0, 1))
    grad_product = norm_backward(grad_update, hat_mid, scale_mid, norm_gains[1]).astype(
        jnp.bfloat16
    )
    taken = grad_product
    grad_left = jnp.einsum(
        "ijc,jkc->ikc",
        taken,
        lax.all_gather(right_edges, "dap", axis=0, tiled=True),
        preferred_element_type=jnp.float32,
    )
    grad_cols = lax.all_to_all(grad_product, "dap", split_axis=1, concat_axis=0, tiled=True)
    taken = grad_cols
    grad_right = jnp.einsum(
        "ijc,ikc->jkc",
        taken,
        lax.all_gather(left_edges, "dap", axis=0, tiled=True),
        preferred_element_type=jnp.float32,
    )
    grad_proj = jnp.concatenate(
        [
            grad_left * mask_pair * left_value * left_sig * (1.0 - left_sig),
            grad_left * mask_pair * left_sig,
            grad_right * mask_pair * right_value * right_sig * (1.0 - right_sig),
            grad_right * mask_pair * right_sig,
        ],
        axis=-1,
    ).astype(jnp.bfloat16)
    part_edge = jnp.einsum("rnc,rnf->cf", normed_x, grad_proj, preferred_element_type=jnp.float32)
    grad_normed_x = jnp.einsum(
        "rnf,cf->rnc", grad_proj, edge_weight, preferred_element_type=jnp.float32
    )
    grad_normed_x = grad_normed_x + jnp.einsum(
        "rnf,cf->rnc", grad_gate, mult_gate_weight, preferred_element_type=jnp.float32
    )
    part_gain_in = jnp.sum(grad_normed_x * hat_in, axis=(0, 1))
    grad_pair = (
        grad_middle + norm_backward(grad_normed_x, hat_in, scale_in, norm_gains[0])
    ).astype(jnp.bfloat16)
    totals = lax.psum(
        (
            part_gain_in,
            part_gain_mid,
            part_edge,
            part_mult_gate,
            part_mult_out,
            part_gain_attn,
            part_attention,
            part_bias,
            part_attn_out,
        ),
        "dap",
    )
    (
        gain_in_sum,
        gain_mid_sum,
        edge_sum,
        mult_gate_sum,
        mult_out_sum,
        gain_attn_sum,
        attention_sum,
        bias_sum,
        attn_out_sum,
    ) = totals
    inverse = 1.0 / full_size
    grad_gains = jnp.stack([gain_in_sum, gain_mid_sum, gain_attn_sum]) * inverse
    return (
        grad_pair,
        grad_gains,
        edge_sum * inverse,
        mult_gate_sum * inverse,
        mult_out_sum * inverse,
        attention_sum * inverse,
        bias_sum * inverse,
        attn_out_sum * inverse,
    )


ROW_BLOCK = 8
VMEM_SLACK = 8 * 2**20
VMEM_SHARE = 32 * 2**20
HALF = jnp.bfloat16
FULL = jnp.float32


def dot_nn(left, right):
    return lax.dot_general(left, right, (((1,), (0,)), ((), ())), preferred_element_type=FULL)


def dot_nt(left, right):
    return lax.dot_general(left, right, (((1,), (1,)), ((), ())), preferred_element_type=FULL)


def dot_tn(left, right):
    return lax.dot_general(left, right, (((0,), (0,)), ((), ())), preferred_element_type=FULL)


def lane_mean(values):
    return jnp.mean(values, axis=-1, keepdims=True)


def sigmoid(values):
    return pltpu.reciprocal(1.0 + jnp.exp(-values), approx=True)


def head_blocks(row_width, col_width, dtype):
    shape = (HEADS * row_width, HEADS * col_width)
    row = lax.broadcasted_iota(jnp.int32, shape, 0)
    col = lax.broadcasted_iota(jnp.int32, shape, 1)
    same = None
    for h in range(HEADS):
        here = (row >= h * row_width) & (row < (h + 1) * row_width)
        here = here & (col >= h * col_width) & (col < (h + 1) * col_width)
        same = here if same is None else same | here
    return jnp.where(same, 1.0, 0.0).astype(dtype)


def place_rows(target, part, near_ref, far_ref):
    me = lax.axis_index("dap")
    square = near_ref.shape[0]
    base = me - lax.rem(me, 2 * square) + lax.rem(me, 2)
    cells = target.shape[0] // (4 * square)
    for other, blocks in enumerate((near_ref, far_ref)):
        for e in range(square):
            for f in range(2):
                source = (base + 2 * e) ^ (2 * square * f) ^ other
                place = pl.ds(pl.multiple_of(source * cells, cells), cells)
                target[place, :] = blocks[e, f, part].reshape(cells, target.shape[1]).astype(FULL)


def block_tools(size):
    block = ROW_BLOCK * size

    def rows_of(at):
        return pl.ds(pl.multiple_of(at * block, block), block)

    def columns_of(ref, at):
        return jnp.concatenate(
            [ref[pl.ds(at * ROW_BLOCK + a, size, stride=size), :] for a in range(ROW_BLOCK)], axis=0
        )

    return rows_of, columns_of


def outer_sum(size, at, row_ref, row_stride, block_stride, block_ref):
    sums = [jnp.zeros((size, block_ref.shape[1]), FULL)] * ROW_BLOCK
    for k in range(size):
        whole = block_ref[k * size : (k + 1) * size, :]
        for a in range(ROW_BLOCK):
            row = (at * ROW_BLOCK + a) * block_stride + k * row_stride
            sums[a] = sums[a] + row_ref[pl.ds(row, 1), :] * whole
    return jnp.concatenate(sums, axis=0)


def cell_of_lane(size):
    lane = lax.broadcasted_iota(jnp.int32, (1, HEADS * size), 1)
    cell = lane
    for h in range(1, HEADS):
        cell = jnp.where(lane >= h * size, lane - h * size, cell)
    return cell


def spread_bias_weight(target, bias_w_ref, size):
    bias_rows = bias_w_ref[...].astype(FULL)
    for h in range(HEADS):
        target[h * size : (h + 1) * size, :] = jnp.broadcast_to(
            bias_rows[h : h + 1], (size, bias_rows.shape[1])
        ).astype(HALF)


def multiply_kernel(
    size,
    near_ref,
    far_ref,
    lengths_ref,
    gains_ref,
    edge_w_ref,
    gate_w_ref,
    out_w_ref,
    left_ref,
    right_ref,
    left_a_ref,
    left_b_ref,
    right_a_ref,
    right_b_ref,
    gate_ref,
    hat_mid_ref,
    scale_mid_ref,
    edge_out_ref,
    hat_y_ref,
    scale_y_ref,
    y_ref,
    x_half_ref,
    update_ref,
    pair_ref,
    right_t_ref,
):
    channels = gains_ref.shape[1]
    block = ROW_BLOCK * size
    blocks = size // ROW_BLOCK
    rows_of, columns_of = block_tools(size)
    real = lengths_ref[0]
    gain_x = gains_ref[0:1, :]
    gain_mid = gains_ref[1:2, :]
    gain_y = gains_ref[2:3, :]
    place_rows(pair_ref, 0, near_ref, far_ref)

    def project(at, carry):
        rows = rows_of(at)
        hat, _ = kernel_norm(pair_ref[rows, :])
        normed = (hat * gain_x).astype(HALF)
        x_half_ref[rows, :] = normed
        projected = dot_nn(normed, edge_w_ref[...])
        gate_ref[rows, :] = sigmoid(dot_nn(normed, gate_w_ref[...]))
        shape = (ROW_BLOCK, size, channels)
        row = lax.broadcasted_iota(jnp.int32, shape, 0) + at * ROW_BLOCK
        col = lax.broadcasted_iota(jnp.int32, shape, 1)
        mask = jnp.where((row < real) & (col < real), 1.0, 0.0).reshape(block, channels)
        for side, (edge, first, second) in enumerate(
            ((left_ref, left_a_ref, left_b_ref), (right_ref, right_a_ref, right_b_ref))
        ):
            base = 2 * side * channels
            sig = sigmoid(projected[:, base : base + channels])
            value = projected[:, base + channels : base + 2 * channels]
            masked = mask * sig
            product = masked * value
            edge[rows, :] = product.astype(HALF).astype(FULL)
            first[rows, :] = product * (1.0 - sig)
            second[rows, :] = masked
        return carry

    lax.fori_loop(0, blocks, project, 0, unroll=4)

    def turn(at, carry):
        right_t_ref[rows_of(at), :] = columns_of(right_ref, at)
        return carry

    lax.fori_loop(0, blocks, turn, 0, unroll=4)

    def multiply(at, carry):
        rows = rows_of(at)
        product = outer_sum(size, at, left_ref, 1, size, right_t_ref)
        hat, scale = kernel_norm(product)
        hat_mid_ref[rows, :] = hat
        scale_mid_ref[rows, :] = jnp.broadcast_to(scale, hat.shape)
        update = (hat * gain_mid).astype(HALF)
        update_ref[rows, :] = update
        edge_out = dot_nn(update, out_w_ref[...])
        edge_out_ref[rows, :] = edge_out
        middle = pair_ref[rows, :] + gate_ref[rows, :] * edge_out
        hat, scale = kernel_norm(middle)
        hat_y_ref[rows, :] = hat
        scale_y_ref[rows, :] = jnp.broadcast_to(scale, hat.shape)
        y_ref[rows, :] = hat * gain_y
        return carry

    lax.fori_loop(0, blocks, multiply, 0, unroll=4)


def project_kernel(
    size,
    y_ref,
    att_w_ref,
    bias_w_ref,
    att_gate_ref,
    bias_ref,
    y_t_ref,
    query_ref,
    key_ref,
    value_ref,
    bias_rep_ref,
):
    channels = y_ref.shape[1]
    lanes = HEADS * size
    head_scale = 1.0 / math.sqrt(HEAD_DIM)
    rows_of, columns_of = block_tools(size)
    cell = cell_of_lane(size)
    spread_bias_weight(bias_rep_ref, bias_w_ref, size)

    def prepare(at, carry):
        rows = rows_of(at)
        y = columns_of(y_ref, at).astype(HALF)
        y_t_ref[rows, :] = y
        packed = dot_nn(y, att_w_ref[...])
        query_ref[rows, :] = (packed[:, :channels] * head_scale).astype(HALF)
        key_ref[rows, :] = packed[:, channels : 2 * channels].astype(HALF)
        value_ref[rows, :] = packed[:, 2 * channels : 3 * channels].astype(HALF)
        att_gate_ref[rows, :] = sigmoid(packed[:, 3 * channels :])
        spread = dot_nt(y, bias_rep_ref[...]).astype(HALF).astype(FULL)
        for a in range(ROW_BLOCK):
            carry = carry + jnp.where(cell == at * ROW_BLOCK + a, spread[a * size : (a + 1) * size], 0.0)
        return carry

    bias_ref[...] = lax.fori_loop(
        0, size // ROW_BLOCK, prepare, jnp.zeros((size, lanes), FULL), unroll=4
    )


def attend_kernel(
    size,
    near_ref,
    far_ref,
    lengths_ref,
    att_w_ref,
    att_out_w_ref,
    att_gate_ref,
    bias_ref,
    y_t_ref,
    query_ref,
    key_ref,
    value_ref,
    bias_rep_ref,
    cot_ref,
    grad_y_ref,
    cot_t_ref,
    gated_ref,
    grad_packed_ref,
):
    channels = cot_ref.shape[1]
    block = ROW_BLOCK * size
    blocks = size // ROW_BLOCK
    lanes = HEADS * size
    head_scale = 1.0 / math.sqrt(HEAD_DIM)
    rows_of, columns_of = block_tools(size)
    cell = cell_of_lane(size)
    key_row = lax.broadcasted_iota(jnp.int32, (size, lanes), 0)
    valid = jnp.where(key_row < lengths_ref[0], 1.0, 0.0)
    place_rows(cot_ref, 1, near_ref, far_ref)

    head_mask = head_blocks(size, HEAD_DIM, HALF)
    head_mask_full = head_blocks(size, HEAD_DIM, FULL)
    no_rows = jnp.zeros((size, channels), HALF)

    def attend(at, score_sum):
        rows = rows_of(at)
        parts = [slice(a * size, (a + 1) * size) for a in range(ROW_BLOCK)]
        query, key, value = (ref[rows, :] for ref in (query_ref, key_ref, value_ref))
        gate = att_gate_ref[rows, :]
        cot = columns_of(cot_ref, at).astype(HALF)
        cot_t_ref[rows, :] = cot
        grad_gated = dot_nt(cot, att_out_w_ref[...])
        grad_att = (grad_gated * gate).astype(HALF)
        queries = [jnp.concatenate([query[p]] * HEADS, axis=0) * head_mask for p in parts]
        grads = [jnp.concatenate([grad_att[p]] * HEADS, axis=0) * head_mask for p in parts]
        bias = bias_ref[...]

        def stacked(columns):
            return jnp.stack(columns, axis=0)

        scores = stacked([dot_nt(key[p], queries[a]) + bias for a, p in enumerate(parts)])
        grad_attention = stacked([dot_nt(value[p], grads[a]) for a, p in enumerate(parts)])
        exp_scores = valid[None] * jnp.exp(scores)
        total = jnp.sum(exp_scores, axis=1)
        scale = jnp.where(total > 2.0**100, 2.0**-60, 1.0)
        inverse_total = pltpu.reciprocal(total * scale, approx=True)
        attention = (exp_scores * scale[:, None, :]) * inverse_total[:, None, :]
        row_dots = jnp.sum(attention * grad_attention, axis=1)
        grad_scores = attention * (grad_attention - row_dots[:, None, :])
        score_sum = score_sum + jnp.sum(grad_scores, axis=0)
        attention_half = attention.astype(HALF)
        scores_half = grad_scores.astype(HALF)
        grad_key = jnp.concatenate([dot_nn(scores_half[a], queries[a]) for a in range(ROW_BLOCK)], axis=0)
        grad_value = jnp.concatenate([dot_nn(attention_half[a], grads[a]) for a in range(ROW_BLOCK)], axis=0)

        def query_sums(a, p):
            weights = jnp.concatenate([attention_half[a], scores_half[a]], axis=0)
            vectors = jnp.concatenate(
                [
                    jnp.concatenate([value[p], no_rows], axis=1),
                    jnp.concatenate([no_rows, key[p]], axis=1),
                ],
                axis=0,
            )
            whole = dot_tn(weights, vectors)
            masked = [whole[:, :channels] * head_mask_full, whole[:, channels:] * head_mask_full]
            return [sum(part[h * size : (h + 1) * size] for h in range(HEADS)) for part in masked]

        per_query = [query_sums(a, p) for a, p in enumerate(parts)]
        attended = jnp.concatenate([pair[0] for pair in per_query], axis=0)
        grad_query = jnp.concatenate([pair[1] for pair in per_query], axis=0)
        gated = gate * attended
        gated_ref[rows, :] = gated.astype(HALF)
        grad_gate_pre = grad_gated * gated * (1.0 - gate)
        grad_packed = jnp.concatenate(
            [
                (grad_query * head_scale).astype(HALF),
                grad_key.astype(HALF),
                grad_value.astype(HALF),
                grad_gate_pre.astype(HALF),
            ],
            axis=1,
        )
        grad_packed_ref[rows, : 4 * channels] = grad_packed
        grad_y_ref[rows, :] = dot_nt(grad_packed, att_w_ref[...])
        return score_sum

    score_sum = lax.fori_loop(0, blocks, attend, jnp.zeros((size, lanes), FULL), unroll=4)
    bias_grad = score_sum.astype(HALF).astype(FULL)

    def spread_bias(at, carry):
        rows = rows_of(at)
        spread = jnp.concatenate(
            [jnp.where(cell == at * ROW_BLOCK + a, bias_grad, 0.0) for a in range(ROW_BLOCK)], axis=0
        ).astype(HALF)
        grad_packed_ref[rows, 4 * channels :] = spread
        grad_y_ref[rows, :] += dot_nn(spread, bias_rep_ref[...])
        return carry

    lax.fori_loop(0, blocks, spread_bias, 0, unroll=4)


def gain_sum(pairs):
    total = sum(jnp.sum(weight.astype(FULL) * grad, axis=1, keepdims=True) for weight, grad in pairs)
    channels = total.shape[0]
    return jnp.transpose(jnp.broadcast_to(total, (channels, channels)))[0:1, :]


def edges_kernel(
    size,
    devices,
    pair_ref,
    gains_ref,
    edge_w_ref,
    gate_w_ref,
    out_w_ref,
    left_ref,
    right_ref,
    left_a_ref,
    left_b_ref,
    right_a_ref,
    right_b_ref,
    gate_ref,
    hat_mid_ref,
    scale_mid_ref,
    edge_out_ref,
    hat_y_ref,
    scale_y_ref,
    x_half_ref,
    update_ref,
    cot_ref,
    grad_y_ref,
    attention_side,
    grad_pair_ref,
    grad_gains_ref,
    grad_bias_ref,
    stage_refs,
    send,
    grad_middle_ref,
    grad_product_ref,
    grad_proj_ref,
    x_sum_ref,
    y_sum_ref,
):
    channels = gains_ref.shape[1]
    blocks = size // ROW_BLOCK
    rows_of, columns_of = block_tools(size)
    gain_x = gains_ref[0:1, :]
    gain_mid = gains_ref[1:2, :]
    gain_y = gains_ref[2:3, :]

    inverse = 1.0 / size
    y_t_ref, cot_t_ref, gated_ref, grad_packed_ref, att_w_ref, bias_rep_ref = attention_side
    edge_sum_ref, gate_sum_ref, out_sum_ref, att_sum_ref, att_out_sum_ref = stage_refs
    for sum_ref in (x_sum_ref, y_sum_ref, out_sum_ref, att_out_sum_ref):
        sum_ref[...] = jnp.zeros(sum_ref.shape, FULL)

    def attention_sums(at):
        rows = rows_of(at)
        y_sum_ref[...] += dot_tn(y_t_ref[rows, :], grad_packed_ref[rows, :])
        att_out_sum_ref[...] += dot_tn(gated_ref[rows, :], cot_t_ref[rows, :])

    def attention_results():
        att_sum = y_sum_ref[:, : 4 * channels] * inverse
        bias_sum = jnp.transpose(y_sum_ref[:, 4 * channels :] * inverse)
        att_sum_ref[...] = att_sum
        att_out_sum_ref[...] *= inverse
        send(3, 4)
        for h in range(HEADS):
            grad_bias_ref[h : h + 1, :] = jnp.sum(
                bias_sum[h * size : (h + 1) * size], axis=0, keepdims=True
            )
        bias_part = jnp.sum(bias_rep_ref[...].astype(FULL) * bias_sum, axis=0, keepdims=True)
        grad_gains_ref[2:3, :] = (gain_sum(((att_w_ref[...], att_sum),)) + bias_part) / gain_y

    def middle_back(at, carry):
        rows = rows_of(at)
        grad_y = columns_of(grad_y_ref, at)
        grad_middle = cot_ref[rows, :] + kernel_norm_back(
            grad_y, hat_y_ref[rows, :], scale_y_ref[rows, :], gain_y
        )
        grad_middle_ref[rows, :] = grad_middle
        gate = gate_ref[rows, :]
        gated = grad_middle * gate
        grad_edge_out = gated.astype(HALF)
        grad_gate = (gated * edge_out_ref[rows, :] * (1.0 - gate)).astype(HALF)
        grad_proj_ref[rows, 4 * channels :] = grad_gate
        x_sum_ref[:, 4 * channels :] += dot_tn(x_half_ref[rows, :], grad_gate)
        out_sum_ref[...] += dot_tn(update_ref[rows, :], grad_edge_out)
        grad_update = dot_nt(grad_edge_out, out_w_ref[...])
        grad_product = kernel_norm_back(grad_update, hat_mid_ref[rows, :], scale_mid_ref[rows, :], gain_mid)
        grad_product_ref[rows, :] = grad_product.astype(HALF).astype(FULL)
        return carry

    lax.fori_loop(0, blocks, middle_back, 0, unroll=4)

    def edges_back(at):
        rows = rows_of(at)
        x_half = x_half_ref[rows, :]
        for side, (first_ref, second_ref, strides, other_ref) in enumerate(
            (
                (left_a_ref, left_b_ref, (1, size), right_ref),
                (right_a_ref, right_b_ref, (size, 1), left_ref),
            )
        ):
            grad = outer_sum(size, at, grad_product_ref, *strides, other_ref)
            both = jnp.concatenate(
                [(grad * first_ref[rows, :]).astype(HALF), (grad * second_ref[rows, :]).astype(HALF)], axis=1
            )
            place = slice(2 * side * channels, 2 * (side + 1) * channels)
            grad_proj_ref[rows, place] = both
            x_sum_ref[:, place] += dot_tn(x_half, both)

    for at in range(blocks):
        for part in range(2 * at, min(2 * at + 2, blocks)):
            attention_sums(part)
        edges_back(at)
        if 2 * at < blocks <= 2 * at + 2:
            attention_results()

    edge_sum, gate_sum = x_sum_ref[:, : 4 * channels] * inverse, x_sum_ref[:, 4 * channels :] * inverse
    edge_sum_ref[...] = edge_sum
    gate_sum_ref[...] = gate_sum
    out_sum = out_sum_ref[...] * inverse
    out_sum_ref[...] = out_sum
    send(0, 1, 2)
    grad_gains_ref[0:1, :] = gain_sum(((edge_w_ref[...], edge_sum), (gate_w_ref[...], gate_sum))) / gain_x
    grad_gains_ref[1:2, :] = gain_sum(((out_w_ref[...], out_sum),)) / gain_mid

    own_cells = size * size // devices
    own = pl.ds(pl.multiple_of(lax.axis_index("dap") * own_cells, own_cells), own_cells)
    hat, scale = kernel_norm(pair_ref[...].reshape(own_cells, channels).astype(FULL))
    grad_x = dot_nt(grad_proj_ref[own, : 4 * channels], edge_w_ref[...])
    grad_x = grad_x + dot_nt(grad_proj_ref[own, 4 * channels :], gate_w_ref[...])
    grad_pair = grad_middle_ref[own, :] + kernel_norm_back(grad_x, hat, scale, gain_x)
    grad_pair_ref[...] = grad_pair.astype(grad_pair_ref.dtype)


def kernel_norm(values):
    center = values - lane_mean(values)
    scale = lax.rsqrt(lane_mean(center * center) + epsilon)
    return center * scale, scale


def kernel_norm_back(grad_out, hat, scale, gain):
    scaled = grad_out * gain
    return scale * (scaled - lane_mean(scaled) - hat * lane_mean(scaled * hat))


def bytes_of(arrays):
    return sum(math.prod(shape) * jnp.dtype(dtype).itemsize for shape, dtype in arrays)


def kernel_scratch(size, channels):
    cells, lanes = size * size, HEADS * size
    full, half = ((cells, channels), FULL), ((cells, channels), HALF)
    square, wide = ((channels, channels), FULL), ((channels, 4 * channels), FULL)
    return {
        "kept": [full] * 12,
        "y": [full],
        "halves": [half] * 2,
        "multiply": [full] * 2,
        "projections": [full, ((size, lanes), FULL)] + [half] * 4 + [((lanes, channels), HALF)],
        "shared": [full] * 2,
        "attend": [half] * 2 + [((cells, 4 * channels + lanes), HALF)],
        "stage": [wide, square, square, wide, square],
        "edges": [full] * 2
        + [((cells, 5 * channels), HALF), ((channels, 5 * channels), FULL), ((channels, 4 * channels + lanes), FULL)],
    }


def whole_kernel(
    size,
    pair_own_ref,
    near_ref,
    far_ref,
    lengths_ref,
    gains_ref,
    edge_w_ref,
    gate_w_ref,
    out_w_ref,
    att_w_ref,
    bias_w_ref,
    att_out_w_ref,
    grad_pair_ref,
    grad_gains_ref,
    grad_edge_ref,
    grad_gate_w_ref,
    grad_out_w_ref,
    grad_att_w_ref,
    grad_bias_ref,
    grad_att_out_ref,
    *scratch,
):
    part, at = {}, 0
    for name, arrays in kernel_scratch(size, 1).items():
        part[name] = scratch[at : at + len(arrays)]
        at += len(arrays)
    sent = scratch[at]
    weights = (edge_w_ref, gate_w_ref, out_w_ref)
    multiply_kernel(
        size, near_ref, far_ref, lengths_ref, gains_ref, *weights, *part["kept"], *part["y"], *part["halves"], *part["multiply"]
    )
    project_kernel(size, *part["y"], att_w_ref, bias_w_ref, *part["projections"])
    attend_kernel(
        size,
            near_ref,
        far_ref,
        lengths_ref,
        att_w_ref,
        att_out_w_ref,
        *part["projections"],
        *part["shared"],
        *part["attend"],
    )
    targets = (grad_edge_ref, grad_gate_w_ref, grad_out_w_ref, grad_att_w_ref, grad_att_out_ref)
    copies = [
        pltpu.make_async_copy(source, target, sent.at[slot])
        for slot, (source, target) in enumerate(zip(part["stage"], targets))
    ]

    def send(*slots):
        for slot in slots:
            copies[slot].start()

    _, _, y_t_ref, _, _, _, bias_rep_ref = part["projections"]
    cot_t_ref, gated_ref, grad_packed_ref = part["attend"]
    edges_kernel(
        size,
        4 * near_ref.shape[0],
        pair_own_ref,
        gains_ref,
        *weights,
        *part["kept"],
        *part["halves"],
        *part["shared"],
        (y_t_ref, cot_t_ref, gated_ref, grad_packed_ref, att_w_ref, bias_rep_ref),
        grad_pair_ref,
        grad_gains_ref,
        grad_bias_ref,
        part["stage"],
        send,
        *part["edges"],
    )
    for copy in copies:
        copy.wait()


def replicated_plan(
    axis_size,
    pair_map,
    cotangent,
    lengths,
    norm_gains,
    edge_weight,
    mult_gate_weight,
    mult_out_weight,
    attention_weight,
    bias_weight,
    attention_out_weight,
):
    _, size, channels = pair_map.shape
    cells = size * size
    bits = axis_size.bit_length() - 1
    far_step = 1 << (bits - 1)
    chips = far_step // 2
    squares = [[base + 2 * e for e in range(chips)] for base in (0, 1, far_step, far_step + 1)]

    def swapped(held, mask):
        return lax.ppermute(held, "dap", [(d, d ^ mask) for d in range(axis_size)])

    own = jnp.stack([pair_map, cotangent])
    held = jnp.stack([own, swapped(own, far_step)])
    near = lax.all_to_all(
        jnp.broadcast_to(held[None], (chips,) + held.shape),
        "dap",
        split_axis=0,
        concat_axis=0,
        axis_index_groups=squares,
    )
    far = swapped(near, 1)

    square, wide = ((channels, channels), FULL), ((channels, 4 * channels), FULL)
    outs = [((cells // axis_size, channels), HALF), ((3, channels), FULL), wide, square, square]
    outs += [wide, ((HEADS, channels), FULL), square]
    scratch = sum(kernel_scratch(size, channels).values(), [])
    vmem = pl.BlockSpec(memory_space=pltpu.VMEM)
    smem = pl.BlockSpec(memory_space=pltpu.SMEM)
    anywhere = pl.BlockSpec(memory_space=pl.ANY)
    results = pl.pallas_call(
        functools.partial(whole_kernel, size),
        out_shape=[jax.ShapeDtypeStruct(*out) for out in outs],
        in_specs=[vmem] * 3 + [smem] + [vmem] * 7,
        out_specs=[vmem] * 2 + [anywhere] * 4 + [vmem, anywhere],
        scratch_shapes=[pltpu.VMEM(*part) for part in scratch] + [pltpu.SemaphoreType.DMA((5,))],
        compiler_params=pltpu.CompilerParams(vmem_limit_bytes=bytes_of(scratch) + VMEM_SLACK),
    )(
        pair_map,
        near,
        far,
        lengths,
        norm_gains,
        edge_weight,
        mult_gate_weight,
        mult_out_weight,
        attention_weight,
        bias_weight.T,
        attention_out_weight,
    )
    return (results[0].reshape(pair_map.shape), *results[1:6], results[6].T, results[7])


def per_device(axis_size, pair_map, *rest):
    _, size, channels = pair_map.shape
    scratch = sum(kernel_scratch(size, channels).values(), [])
    fits = size % ROW_BLOCK == 0 and bytes_of(scratch) <= VMEM_SHARE
    if fits and axis_size >= 8 and axis_size & (axis_size - 1) == 0:
        return replicated_plan(axis_size, pair_map, *rest)
    return distributed_plan(pair_map, *rest)


def solution(mesh):
    return jax.shard_map(
        functools.partial(per_device, mesh.shape["dap"]),
        mesh=mesh,
        in_specs=(
            P(("groups", "dap"), None, None),
            P(("groups", "dap"), None, None),
            P("groups"),
            P(),
            P(),
            P(),
            P(),
            P(),
            P(),
            P(),
        ),
        out_specs=(
            P(("groups", "dap"), None, None),
            P("groups", None),
            P("groups", None),
            P("groups", None),
            P("groups", None),
            P("groups", None),
            P("groups", None),
            P("groups", None),
        ),
        check_vma=False,
    )
```

```python
import functools
import math

import jax
import jax.numpy as jnp
from jax import lax
from jax.experimental import pallas as pl
from jax.experimental.pallas import tpu as pltpu
from jax.sharding import PartitionSpec as P

HEADS = 4
HEAD_DIM = 32


epsilon = 1e-05


def norm_forward(values, gain_row):
    center = values - jnp.mean(values, axis=-1, keepdims=True)
    inv_std = lax.rsqrt(jnp.mean(center * center, axis=-1, keepdims=True) + epsilon)
    normed = center * inv_std
    return (normed * gain_row, normed, inv_std)


def norm_backward(grad_out, normed, inv_std, gain_row):
    scaled = grad_out * gain_row
    first_mean = jnp.mean(scaled, axis=-1, keepdims=True)
    second_mean = jnp.mean(scaled * normed, axis=-1, keepdims=True)
    return inv_std * (scaled - first_mean - normed * second_mean)


def distributed_plan(
    pair_map,
    cotangent,
    lengths,
    norm_gains,
    edge_weight,
    mult_gate_weight,
    mult_out_weight,
    attention_weight,
    bias_weight,
    attention_out_weight,
):
    row_count, full_size, channels = pair_map.shape
    inner_width = HEADS * HEAD_DIM
    head_scale = 1.0 / math.sqrt(HEAD_DIM)
    first_row = lax.axis_index("dap") * row_count
    real_count = lengths[0]
    valid_all = (jnp.arange(full_size) < real_count).astype(jnp.float32)
    valid_rows = (first_row + jnp.arange(row_count) < real_count).astype(jnp.float32)
    mask_pair = (valid_rows[:, None] * valid_all[None, :])[:, :, None]
    pair_f32 = pair_map.astype(jnp.float32)
    normed_full, hat_in, scale_in = norm_forward(pair_f32, norm_gains[0])
    normed_x = normed_full.astype(jnp.bfloat16)
    projected = jnp.einsum("rnc,cf->rnf", normed_x, edge_weight, preferred_element_type=jnp.float32)
    left_gate = projected[..., :channels]
    left_value = projected[..., channels : 2 * channels]
    right_gate = projected[..., 2 * channels : 3 * channels]
    right_value = projected[..., 3 * channels :]
    left_sig = jax.nn.sigmoid(left_gate)
    right_sig = jax.nn.sigmoid(right_gate)
    left_edges = (mask_pair * left_sig * left_value).astype(jnp.bfloat16)
    right_edges = (mask_pair * right_sig * right_value).astype(jnp.bfloat16)
    product = jnp.einsum(
        "ikc,jkc->ijc",
        left_edges,
        lax.all_gather(right_edges, "dap", axis=0, tiled=True),
        preferred_element_type=jnp.float32,
    )
    update_full, hat_mid, scale_mid = norm_forward(product, norm_gains[1])
    update = update_full.astype(jnp.bfloat16)
    edge_out = jnp.einsum(
        "rnc,cf->rnf", update, mult_out_weight, preferred_element_type=jnp.float32
    )
    gate_sig = jax.nn.sigmoid(
        jnp.einsum("rnc,cf->rnf", normed_x, mult_gate_weight, preferred_element_type=jnp.float32)
    )
    middle = pair_f32 + gate_sig * edge_out
    normed_mid, hat_attn, scale_attn = norm_forward(middle, norm_gains[2])
    normed_y = normed_mid.astype(jnp.bfloat16)
    bias_local = jnp.einsum(
        "kic,ch->hki", normed_y, bias_weight, preferred_element_type=jnp.float32
    ).astype(jnp.bfloat16)
    bias_whole = lax.all_gather(bias_local, "dap", axis=1, tiled=True)
    bias_query = jnp.swapaxes(bias_whole, 1, 2).astype(jnp.float32)
    column_y, column_cot = (
        lax.all_to_all(normed_y, "dap", split_axis=1, concat_axis=0, tiled=True),
        lax.all_to_all(cotangent, "dap", split_axis=1, concat_axis=0, tiled=True),
    )
    packed = jnp.einsum(
        "ijc,cf->ijf", column_y, attention_weight, preferred_element_type=jnp.float32
    )
    packed = packed.reshape(full_size, row_count, 4, HEADS, HEAD_DIM)
    query_vectors = (packed[:, :, 0] * head_scale).astype(jnp.bfloat16)
    key_vectors = packed[:, :, 1].astype(jnp.bfloat16)
    value_vectors = packed[:, :, 2].astype(jnp.bfloat16)
    att_gate = jax.nn.sigmoid(packed[:, :, 3])
    scores = (
        jnp.einsum(
            "ijhd,kjhd->jhik", query_vectors, key_vectors, preferred_element_type=jnp.float32
        )
        + bias_query[None]
    )
    exp_scores = valid_all * jnp.exp(scores)
    attention = exp_scores / jnp.sum(exp_scores, axis=-1, keepdims=True)
    attention_half = attention.astype(jnp.bfloat16)
    attended = jnp.einsum(
        "jhik,kjhd->ijhd", attention_half, value_vectors, preferred_element_type=jnp.float32
    )
    gated = (att_gate * attended).astype(jnp.bfloat16).reshape(full_size, row_count, inner_width)
    part_attn_out = jnp.einsum("ijf,ijc->fc", gated, column_cot, preferred_element_type=jnp.float32)
    grad_gated = jnp.einsum(
        "ijc,fc->ijf", column_cot, attention_out_weight, preferred_element_type=jnp.float32
    )
    grad_gated = grad_gated.reshape(full_size, row_count, HEADS, HEAD_DIM)
    grad_att = (grad_gated * att_gate).astype(jnp.bfloat16)
    grad_gate_pre = grad_gated * attended * att_gate * (1.0 - att_gate)
    grad_attention = jnp.einsum(
        "ijhd,kjhd->jhik", grad_att, value_vectors, preferred_element_type=jnp.float32
    )
    row_dots = jnp.transpose(jnp.sum(grad_att.astype(jnp.float32) * attended, axis=-1), (1, 2, 0))
    grad_scores = attention * (grad_attention - row_dots[..., None])
    scores_half = grad_scores.astype(jnp.bfloat16)
    grad_query = jnp.einsum(
        "jhik,kjhd->ijhd", scores_half, key_vectors, preferred_element_type=jnp.float32
    )
    grad_key = jnp.einsum(
        "jhik,ijhd->kjhd", scores_half, query_vectors, preferred_element_type=jnp.float32
    )
    grad_value = jnp.einsum(
        "jhik,ijhd->kjhd", attention_half, grad_att, preferred_element_type=jnp.float32
    )
    grad_packed = jnp.stack([grad_query * head_scale, grad_key, grad_value, grad_gate_pre], axis=2)
    grad_packed = grad_packed.reshape(full_size, row_count, 4 * inner_width).astype(jnp.bfloat16)
    part_attention = jnp.einsum(
        "ijc,ijf->cf", column_y, grad_packed, preferred_element_type=jnp.float32
    )
    column_grad = jnp.einsum(
        "ijf,cf->ijc", grad_packed, attention_weight, preferred_element_type=jnp.float32
    ).astype(jnp.bfloat16)
    row_grad = lax.all_to_all(column_grad, "dap", split_axis=0, concat_axis=1, tiled=True)
    score_sums = jnp.sum(grad_scores, axis=0)
    taken = score_sums
    bias_half = lax.psum_scatter(
        jnp.transpose(taken, (2, 0, 1)), "dap", scatter_dimension=0, tiled=True
    ).astype(jnp.bfloat16)
    part_bias = jnp.einsum("kic,khi->ch", normed_y, bias_half, preferred_element_type=jnp.float32)
    grad_normed_y = row_grad.astype(jnp.float32) + jnp.einsum(
        "khi,ch->kic", bias_half, bias_weight, preferred_element_type=jnp.float32
    )
    part_gain_attn = jnp.sum(grad_normed_y * hat_attn, axis=(0, 1))
    grad_middle = cotangent.astype(jnp.float32) + norm_backward(
        grad_normed_y, hat_attn, scale_attn, norm_gains[2]
    )
    grad_edge_out = (grad_middle * gate_sig).astype(jnp.bfloat16)
    grad_gate = (grad_middle * edge_out * gate_sig * (1.0 - gate_sig)).astype(jnp.bfloat16)
    part_mult_out = jnp.einsum(
        "rnc,rnf->cf", update, grad_edge_out, preferred_element_type=jnp.float32
    )
    part_mult_gate = jnp.einsum(
        "rnc,rnf->cf", normed_x, grad_gate, preferred_element_type=jnp.float32
    )
    grad_update = jnp.einsum(
        "rnf,cf->rnc", grad_edge_out, mult_out_weight, preferred_element_type=jnp.float32
    )
    part_gain_mid = jnp.sum(grad_update * hat_mid, axis=(0, 1))
    grad_product = norm_backward(grad_update, hat_mid, scale_mid, norm_gains[1]).astype(
        jnp.bfloat16
    )
    taken = grad_product
    grad_left = jnp.einsum(
        "ijc,jkc->ikc",
        taken,
        lax.all_gather(right_edges, "dap", axis=0, tiled=True),
        preferred_element_type=jnp.float32,
    )
    grad_cols = lax.all_to_all(grad_product, "dap", split_axis=1, concat_axis=0, tiled=True)
    taken = grad_cols
    grad_right = jnp.einsum(
        "ijc,ikc->jkc",
        taken,
        lax.all_gather(left_edges, "dap", axis=0, tiled=True),
        preferred_element_type=jnp.float32,
    )
    grad_proj = jnp.concatenate(
        [
            grad_left * mask_pair * left_value * left_sig * (1.0 - left_sig),
            grad_left * mask_pair * left_sig,
            grad_right * mask_pair * right_value * right_sig * (1.0 - right_sig),
            grad_right * mask_pair * right_sig,
        ],
        axis=-1,
    ).astype(jnp.bfloat16)
    part_edge = jnp.einsum("rnc,rnf->cf", normed_x, grad_proj, preferred_element_type=jnp.float32)
    grad_normed_x = jnp.einsum(
        "rnf,cf->rnc", grad_proj, edge_weight, preferred_element_type=jnp.float32
    )
    grad_normed_x = grad_normed_x + jnp.einsum(
        "rnf,cf->rnc", grad_gate, mult_gate_weight, preferred_element_type=jnp.float32
    )
    part_gain_in = jnp.sum(grad_normed_x * hat_in, axis=(0, 1))
    grad_pair = (
        grad_middle + norm_backward(grad_normed_x, hat_in, scale_in, norm_gains[0])
    ).astype(jnp.bfloat16)
    totals = lax.psum(
        (
            part_gain_in,
            part_gain_mid,
            part_edge,
            part_mult_gate,
            part_mult_out,
            part_gain_attn,
            part_attention,
            part_bias,
            part_attn_out,
        ),
        "dap",
    )
    (
        gain_in_sum,
        gain_mid_sum,
        edge_sum,
        mult_gate_sum,
        mult_out_sum,
        gain_attn_sum,
        attention_sum,
        bias_sum,
        attn_out_sum,
    ) = totals
    inverse = 1.0 / full_size
    grad_gains = jnp.stack([gain_in_sum, gain_mid_sum, gain_attn_sum]) * inverse
    return (
        grad_pair,
        grad_gains,
        edge_sum * inverse,
        mult_gate_sum * inverse,
        mult_out_sum * inverse,
        attention_sum * inverse,
        bias_sum * inverse,
        attn_out_sum * inverse,
    )


ROW_BLOCK = 8
COLUMN_BLOCK = 16
VMEM_SLACK = 8 * 2**20
VMEM_SHARE = 32 * 2**20
HALF = jnp.bfloat16
FULL = jnp.float32


def dot_nn(left, right):
    return lax.dot_general(left, right, (((1,), (0,)), ((), ())), preferred_element_type=FULL)


def dot_nt(left, right):
    return lax.dot_general(left, right, (((1,), (1,)), ((), ())), preferred_element_type=FULL)


def dot_tn(left, right):
    return lax.dot_general(left, right, (((0,), (0,)), ((), ())), preferred_element_type=FULL)


def lane_mean(values):
    return jnp.mean(values, axis=-1, keepdims=True)


def sigmoid(values):
    return pltpu.reciprocal(1.0 + jnp.exp(-values), approx=True)


def head_blocks(row_width, col_width, dtype):
    shape = (HEADS * row_width, HEADS * col_width)
    row = lax.broadcasted_iota(jnp.int32, shape, 0)
    col = lax.broadcasted_iota(jnp.int32, shape, 1)
    same = None
    for h in range(HEADS):
        here = (row >= h * row_width) & (row < (h + 1) * row_width)
        here = here & (col >= h * col_width) & (col < (h + 1) * col_width)
        same = here if same is None else same | here
    return jnp.where(same, 1.0, 0.0).astype(dtype)


def place_rows(target, part, near_ref, far_ref, masks):
    me = lax.axis_index("dap")
    cells = target.shape[0] // (2 * len(masks))
    for other, blocks in enumerate((near_ref, far_ref)):
        for at, mask in enumerate(masks):
            place = pl.ds(pl.multiple_of((me ^ mask ^ other) * cells, cells), cells)
            target[place, :] = blocks[at, part].reshape(cells, target.shape[1]).astype(FULL)


def block_tools(size, count=ROW_BLOCK):
    block = count * size

    def rows_of(at):
        return pl.ds(pl.multiple_of(at * block, block), block)

    def columns_of(ref, at):
        return jnp.concatenate(
            [ref[pl.ds(at * count + a, size, stride=size), :] for a in range(count)], axis=0
        )

    return rows_of, columns_of


def outer_sum(size, at, row_ref, row_stride, block_stride, block_ref):
    sums = [jnp.zeros((size, block_ref.shape[1]), FULL)] * ROW_BLOCK
    for k in range(size):
        whole = block_ref[k * size : (k + 1) * size, :]
        for a in range(ROW_BLOCK):
            row = (at * ROW_BLOCK + a) * block_stride + k * row_stride
            sums[a] = sums[a] + row_ref[pl.ds(row, 1), :] * whole
    return jnp.concatenate(sums, axis=0)


def cell_of_lane(size):
    lane = lax.broadcasted_iota(jnp.int32, (1, HEADS * size), 1)
    cell = lane
    for h in range(1, HEADS):
        cell = jnp.where(lane >= h * size, lane - h * size, cell)
    return cell


def spread_bias_weight(target, bias_w_ref, size):
    bias_rows = bias_w_ref[...].astype(FULL)
    for h in range(HEADS):
        target[h * size : (h + 1) * size, :] = jnp.broadcast_to(
            bias_rows[h : h + 1], (size, bias_rows.shape[1])
        ).astype(HALF)


def multiply_kernel(
    size,
    masks,
    near_ref,
    far_ref,
    lengths_ref,
    gains_ref,
    edge_w_ref,
    gate_w_ref,
    out_w_ref,
    left_ref,
    right_ref,
    left_a_ref,
    left_b_ref,
    right_a_ref,
    right_b_ref,
    gate_ref,
    hat_mid_ref,
    scale_mid_ref,
    edge_out_ref,
    hat_y_ref,
    scale_y_ref,
    y_ref,
    x_half_ref,
    update_ref,
    pair_ref,
    right_t_ref,
):
    channels = gains_ref.shape[1]
    block = ROW_BLOCK * size
    blocks = size // ROW_BLOCK
    rows_of, columns_of = block_tools(size)
    real = lengths_ref[0]
    gain_x = gains_ref[0:1, :]
    gain_mid = gains_ref[1:2, :]
    gain_y = gains_ref[2:3, :]
    place_rows(pair_ref, 0, near_ref, far_ref, masks)

    def project(at, carry):
        rows = rows_of(at)
        hat, _ = kernel_norm(pair_ref[rows, :])
        normed = (hat * gain_x).astype(HALF)
        x_half_ref[rows, :] = normed
        projected = dot_nn(normed, edge_w_ref[...])
        gate_ref[rows, :] = sigmoid(dot_nn(normed, gate_w_ref[...]))
        shape = (ROW_BLOCK, size, channels)
        row = lax.broadcasted_iota(jnp.int32, shape, 0) + at * ROW_BLOCK
        col = lax.broadcasted_iota(jnp.int32, shape, 1)
        mask = jnp.where((row < real) & (col < real), 1.0, 0.0).reshape(block, channels)
        for side, (edge, first, second) in enumerate(
            ((left_ref, left_a_ref, left_b_ref), (right_ref, right_a_ref, right_b_ref))
        ):
            base = 2 * side * channels
            sig = sigmoid(projected[:, base : base + channels])
            value = projected[:, base + channels : base + 2 * channels]
            masked = mask * sig
            product = masked * value
            edge[rows, :] = product.astype(HALF).astype(FULL)
            first[rows, :] = product * (1.0 - sig)
            second[rows, :] = masked
        return carry

    lax.fori_loop(0, blocks, project, 0, unroll=4)

    def turn(at, carry):
        right_t_ref[rows_of(at), :] = columns_of(right_ref, at)
        return carry

    lax.fori_loop(0, blocks, turn, 0, unroll=4)

    def multiply(at, carry):
        rows = rows_of(at)
        product = outer_sum(size, at, left_ref, 1, size, right_t_ref)
        hat, scale = kernel_norm(product)
        hat_mid_ref[rows, :] = hat
        scale_mid_ref[rows, :] = jnp.broadcast_to(scale, hat.shape)
        update = (hat * gain_mid).astype(HALF)
        update_ref[rows, :] = update
        edge_out = dot_nn(update, out_w_ref[...])
        edge_out_ref[rows, :] = edge_out
        middle = pair_ref[rows, :] + gate_ref[rows, :] * edge_out
        hat, scale = kernel_norm(middle)
        hat_y_ref[rows, :] = hat
        scale_y_ref[rows, :] = jnp.broadcast_to(scale, hat.shape)
        y_ref[rows, :] = hat * gain_y
        return carry

    lax.fori_loop(0, blocks, multiply, 0, unroll=4)


def project_kernel(
    size,
    y_ref,
    att_w_ref,
    bias_w_ref,
    att_gate_ref,
    bias_ref,
    y_t_ref,
    query_ref,
    key_ref,
    value_ref,
    bias_rep_ref,
):
    channels = y_ref.shape[1]
    lanes = HEADS * size
    head_scale = 1.0 / math.sqrt(HEAD_DIM)
    rows_of, columns_of = block_tools(size)
    cell = cell_of_lane(size)
    spread_bias_weight(bias_rep_ref, bias_w_ref, size)

    def prepare(at, carry):
        rows = rows_of(at)
        y = columns_of(y_ref, at).astype(HALF)
        y_t_ref[rows, :] = y
        packed = dot_nn(y, att_w_ref[...])
        query_ref[rows, :] = (packed[:, :channels] * head_scale).astype(HALF)
        key_ref[rows, :] = packed[:, channels : 2 * channels].astype(HALF)
        value_ref[rows, :] = packed[:, 2 * channels : 3 * channels].astype(HALF)
        att_gate_ref[rows, :] = sigmoid(packed[:, 3 * channels :])
        spread = dot_nt(y, bias_rep_ref[...]).astype(HALF).astype(FULL)
        for a in range(ROW_BLOCK):
            carry = carry + jnp.where(cell == at * ROW_BLOCK + a, spread[a * size : (a + 1) * size], 0.0)
        return carry

    bias_ref[...] = lax.fori_loop(
        0, size // ROW_BLOCK, prepare, jnp.zeros((size, lanes), FULL), unroll=4
    )


def attend_kernel(
    size,
    masks,
    near_ref,
    far_ref,
    lengths_ref,
    att_w_ref,
    att_out_w_ref,
    att_gate_ref,
    bias_ref,
    y_t_ref,
    query_ref,
    key_ref,
    value_ref,
    bias_rep_ref,
    cot_ref,
    grad_y_ref,
    cot_t_ref,
    gated_ref,
    grad_packed_ref,
):
    channels = cot_ref.shape[1]
    block = COLUMN_BLOCK * size
    blocks = size // COLUMN_BLOCK
    lanes = HEADS * size
    head_scale = 1.0 / math.sqrt(HEAD_DIM)
    rows_of, columns_of = block_tools(size, COLUMN_BLOCK)
    cell = cell_of_lane(size)
    key_row = lax.broadcasted_iota(jnp.int32, (size, lanes), 0)
    valid = jnp.where(key_row < lengths_ref[0], 1.0, 0.0)
    place_rows(cot_ref, 1, near_ref, far_ref, masks)

    head_mask = head_blocks(size, HEAD_DIM, HALF)
    head_mask_full = head_blocks(size, HEAD_DIM, FULL)
    no_rows = jnp.zeros((size, channels), HALF)

    def attend(at, score_sum):
        rows = rows_of(at)
        parts = [slice(a * size, (a + 1) * size) for a in range(COLUMN_BLOCK)]
        query, key, value = (ref[rows, :] for ref in (query_ref, key_ref, value_ref))
        gate = att_gate_ref[rows, :]
        cot = columns_of(cot_ref, at).astype(HALF)
        cot_t_ref[rows, :] = cot
        grad_gated = dot_nt(cot, att_out_w_ref[...])
        grad_att = (grad_gated * gate).astype(HALF)
        queries = [jnp.concatenate([query[p]] * HEADS, axis=0) * head_mask for p in parts]
        grads = [jnp.concatenate([grad_att[p]] * HEADS, axis=0) * head_mask for p in parts]
        bias = bias_ref[...]

        def stacked(columns):
            return jnp.stack(columns, axis=0)

        scores = stacked([dot_nt(key[p], queries[a]) + bias for a, p in enumerate(parts)])
        grad_attention = stacked([dot_nt(value[p], grads[a]) for a, p in enumerate(parts)])
        exp_scores = valid[None] * jnp.exp(scores)
        total = jnp.sum(exp_scores, axis=1)
        scale = jnp.where(total > 2.0**100, 2.0**-60, 1.0)
        inverse_total = pltpu.reciprocal(total * scale, approx=True)
        attention = (exp_scores * scale[:, None, :]) * inverse_total[:, None, :]
        row_dots = jnp.sum(attention * grad_attention, axis=1)
        grad_scores = attention * (grad_attention - row_dots[:, None, :])
        score_sum = score_sum + jnp.sum(grad_scores, axis=0)
        attention_half = attention.astype(HALF)
        scores_half = grad_scores.astype(HALF)
        grad_key = jnp.concatenate([dot_nn(scores_half[a], queries[a]) for a in range(COLUMN_BLOCK)], axis=0)
        grad_value = jnp.concatenate([dot_nn(attention_half[a], grads[a]) for a in range(COLUMN_BLOCK)], axis=0)

        def query_sums(a, p):
            weights = jnp.concatenate([attention_half[a], scores_half[a]], axis=0)
            vectors = jnp.concatenate(
                [
                    jnp.concatenate([value[p], no_rows], axis=1),
                    jnp.concatenate([no_rows, key[p]], axis=1),
                ],
                axis=0,
            )
            whole = dot_tn(weights, vectors)
            masked = [whole[:, :channels] * head_mask_full, whole[:, channels:] * head_mask_full]
            return [sum(part[h * size : (h + 1) * size] for h in range(HEADS)) for part in masked]

        per_query = [query_sums(a, p) for a, p in enumerate(parts)]
        attended = jnp.concatenate([pair[0] for pair in per_query], axis=0)
        grad_query = jnp.concatenate([pair[1] for pair in per_query], axis=0)
        gated = gate * attended
        gated_ref[rows, :] = gated.astype(HALF)
        grad_gate_pre = grad_gated * gated * (1.0 - gate)
        grad_packed = jnp.concatenate(
            [
                (grad_query * head_scale).astype(HALF),
                grad_key.astype(HALF),
                grad_value.astype(HALF),
                grad_gate_pre.astype(HALF),
            ],
            axis=1,
        )
        grad_packed_ref[rows, : 4 * channels] = grad_packed
        grad_y_ref[rows, :] = dot_nt(grad_packed, att_w_ref[...])
        return score_sum

    score_sum = lax.fori_loop(0, blocks, attend, jnp.zeros((size, lanes), FULL), unroll=True)
    bias_grad = score_sum.astype(HALF).astype(FULL)

    def spread_bias(at, carry):
        rows = rows_of(at)
        spread = jnp.concatenate(
            [jnp.where(cell == at * COLUMN_BLOCK + a, bias_grad, 0.0) for a in range(COLUMN_BLOCK)], axis=0
        ).astype(HALF)
        grad_packed_ref[rows, 4 * channels :] = spread
        grad_y_ref[rows, :] += dot_nn(spread, bias_rep_ref[...])
        return carry

    lax.fori_loop(0, blocks, spread_bias, 0, unroll=True)


def gain_sum(pairs):
    total = sum(jnp.sum(weight.astype(FULL) * grad, axis=1, keepdims=True) for weight, grad in pairs)
    channels = total.shape[0]
    return jnp.transpose(jnp.broadcast_to(total, (channels, channels)))[0:1, :]


def edges_kernel(
    size,
    devices,
    pair_ref,
    gains_ref,
    edge_w_ref,
    gate_w_ref,
    out_w_ref,
    left_ref,
    right_ref,
    left_a_ref,
    left_b_ref,
    right_a_ref,
    right_b_ref,
    gate_ref,
    hat_mid_ref,
    scale_mid_ref,
    edge_out_ref,
    hat_y_ref,
    scale_y_ref,
    x_half_ref,
    update_ref,
    cot_ref,
    grad_y_ref,
    attention_side,
    grad_pair_ref,
    grad_gains_ref,
    grad_bias_ref,
    stage_refs,
    send,
    grad_middle_ref,
    grad_product_ref,
    grad_proj_ref,
    x_sum_ref,
    y_sum_ref,
):
    channels = gains_ref.shape[1]
    blocks = size // ROW_BLOCK
    rows_of, columns_of = block_tools(size)
    gain_x = gains_ref[0:1, :]
    gain_mid = gains_ref[1:2, :]
    gain_y = gains_ref[2:3, :]

    inverse = 1.0 / size
    y_t_ref, cot_t_ref, gated_ref, grad_packed_ref, att_w_ref, bias_rep_ref = attention_side
    edge_sum_ref, gate_sum_ref, out_sum_ref, att_sum_ref, att_out_sum_ref = stage_refs
    for sum_ref in (x_sum_ref, y_sum_ref, out_sum_ref, att_out_sum_ref):
        sum_ref[...] = jnp.zeros(sum_ref.shape, FULL)

    def attention_sums(at):
        rows = rows_of(at)
        y_sum_ref[...] += dot_tn(y_t_ref[rows, :], grad_packed_ref[rows, :])
        att_out_sum_ref[...] += dot_tn(gated_ref[rows, :], cot_t_ref[rows, :])

    def attention_results():
        att_sum = y_sum_ref[:, : 4 * channels] * inverse
        bias_sum = jnp.transpose(y_sum_ref[:, 4 * channels :] * inverse)
        att_sum_ref[...] = att_sum
        att_out_sum_ref[...] *= inverse
        send(3, 4)
        for h in range(HEADS):
            grad_bias_ref[h : h + 1, :] = jnp.sum(
                bias_sum[h * size : (h + 1) * size], axis=0, keepdims=True
            )
        bias_part = jnp.sum(bias_rep_ref[...].astype(FULL) * bias_sum, axis=0, keepdims=True)
        grad_gains_ref[2:3, :] = (gain_sum(((att_w_ref[...], att_sum),)) + bias_part) / gain_y

    def middle_back(at, carry):
        rows = rows_of(at)
        grad_y = columns_of(grad_y_ref, at)
        grad_middle = cot_ref[rows, :] + kernel_norm_back(
            grad_y, hat_y_ref[rows, :], scale_y_ref[rows, :], gain_y
        )
        grad_middle_ref[rows, :] = grad_middle
        gate = gate_ref[rows, :]
        gated = grad_middle * gate
        grad_edge_out = gated.astype(HALF)
        grad_gate = (gated * edge_out_ref[rows, :] * (1.0 - gate)).astype(HALF)
        grad_proj_ref[rows, 4 * channels :] = grad_gate
        x_sum_ref[:, 4 * channels :] += dot_tn(x_half_ref[rows, :], grad_gate)
        out_sum_ref[...] += dot_tn(update_ref[rows, :], grad_edge_out)
        grad_update = dot_nt(grad_edge_out, out_w_ref[...])
        grad_product = kernel_norm_back(grad_update, hat_mid_ref[rows, :], scale_mid_ref[rows, :], gain_mid)
        grad_product_ref[rows, :] = grad_product.astype(HALF).astype(FULL)
        return carry

    lax.fori_loop(0, blocks, middle_back, 0, unroll=4)

    def edges_back(at):
        rows = rows_of(at)
        x_half = x_half_ref[rows, :]
        for side, (first_ref, second_ref, strides, other_ref) in enumerate(
            (
                (left_a_ref, left_b_ref, (1, size), right_ref),
                (right_a_ref, right_b_ref, (size, 1), left_ref),
            )
        ):
            grad = outer_sum(size, at, grad_product_ref, *strides, other_ref)
            both = jnp.concatenate(
                [(grad * first_ref[rows, :]).astype(HALF), (grad * second_ref[rows, :]).astype(HALF)], axis=1
            )
            place = slice(2 * side * channels, 2 * (side + 1) * channels)
            grad_proj_ref[rows, place] = both
            x_sum_ref[:, place] += dot_tn(x_half, both)

    for at in range(blocks):
        for part in range(2 * at, min(2 * at + 2, blocks)):
            attention_sums(part)
        edges_back(at)
        if 2 * at < blocks <= 2 * at + 2:
            attention_results()

    edge_sum, gate_sum = x_sum_ref[:, : 4 * channels] * inverse, x_sum_ref[:, 4 * channels :] * inverse
    edge_sum_ref[...] = edge_sum
    gate_sum_ref[...] = gate_sum
    out_sum = out_sum_ref[...] * inverse
    out_sum_ref[...] = out_sum
    send(0, 1, 2)
    grad_gains_ref[0:1, :] = gain_sum(((edge_w_ref[...], edge_sum), (gate_w_ref[...], gate_sum))) / gain_x
    grad_gains_ref[1:2, :] = gain_sum(((out_w_ref[...], out_sum),)) / gain_mid

    own_cells = size * size // devices
    own = pl.ds(pl.multiple_of(lax.axis_index("dap") * own_cells, own_cells), own_cells)
    hat, scale = kernel_norm(pair_ref[...].reshape(own_cells, channels).astype(FULL))
    grad_x = dot_nt(grad_proj_ref[own, : 4 * channels], edge_w_ref[...])
    grad_x = grad_x + dot_nt(grad_proj_ref[own, 4 * channels :], gate_w_ref[...])
    grad_pair = grad_middle_ref[own, :] + kernel_norm_back(grad_x, hat, scale, gain_x)
    grad_pair_ref[...] = grad_pair.astype(grad_pair_ref.dtype)


def kernel_norm(values):
    center = values - lane_mean(values)
    scale = lax.rsqrt(lane_mean(center * center) + epsilon)
    return center * scale, scale


def kernel_norm_back(grad_out, hat, scale, gain):
    scaled = grad_out * gain
    return scale * (scaled - lane_mean(scaled) - hat * lane_mean(scaled * hat))


def bytes_of(arrays):
    return sum(math.prod(shape) * jnp.dtype(dtype).itemsize for shape, dtype in arrays)


def kernel_scratch(size, channels):
    cells, lanes = size * size, HEADS * size
    full, half = ((cells, channels), FULL), ((cells, channels), HALF)
    square, wide = ((channels, channels), FULL), ((channels, 4 * channels), FULL)
    return {
        "kept": [full] * 12,
        "y": [full],
        "halves": [half] * 2,
        "multiply": [full] * 2,
        "projections": [full, ((size, lanes), FULL)] + [half] * 4 + [((lanes, channels), HALF)],
        "shared": [full] * 2,
        "attend": [half] * 2 + [((cells, 4 * channels + lanes), HALF)],
        "stage": [wide, square, square, wide, square],
        "edges": [full] * 2
        + [((cells, 5 * channels), HALF), ((channels, 5 * channels), FULL), ((channels, 4 * channels + lanes), FULL)],
    }


def whole_kernel(
    size,
    masks,
    near_ref,
    far_ref,
    lengths_ref,
    gains_ref,
    edge_w_ref,
    gate_w_ref,
    out_w_ref,
    att_w_ref,
    bias_w_ref,
    att_out_w_ref,
    grad_pair_ref,
    grad_gains_ref,
    grad_edge_ref,
    grad_gate_w_ref,
    grad_out_w_ref,
    grad_att_w_ref,
    grad_bias_ref,
    grad_att_out_ref,
    *scratch,
):
    part, at = {}, 0
    for name, arrays in kernel_scratch(size, 1).items():
        part[name] = scratch[at : at + len(arrays)]
        at += len(arrays)
    sent = scratch[at]
    weights = (edge_w_ref, gate_w_ref, out_w_ref)
    multiply_kernel(
        size, masks, near_ref, far_ref, lengths_ref, gains_ref, *weights, *part["kept"], *part["y"], *part["halves"], *part["multiply"]
    )
    project_kernel(size, *part["y"], att_w_ref, bias_w_ref, *part["projections"])
    attend_kernel(
        size,
        masks,
        near_ref,
        far_ref,
        lengths_ref,
        att_w_ref,
        att_out_w_ref,
        *part["projections"],
        *part["shared"],
        *part["attend"],
    )
    targets = (grad_edge_ref, grad_gate_w_ref, grad_out_w_ref, grad_att_w_ref, grad_att_out_ref)
    copies = [
        pltpu.make_async_copy(source, target, sent.at[slot])
        for slot, (source, target) in enumerate(zip(part["stage"], targets))
    ]

    def send(*slots):
        for slot in slots:
            copies[slot].start()

    _, _, y_t_ref, _, _, _, bias_rep_ref = part["projections"]
    cot_t_ref, gated_ref, grad_packed_ref = part["attend"]
    edges_kernel(
        size,
        2 * len(masks),
        near_ref.at[0, 0],
        gains_ref,
        *weights,
        *part["kept"],
        *part["halves"],
        *part["shared"],
        (y_t_ref, cot_t_ref, gated_ref, grad_packed_ref, att_w_ref, bias_rep_ref),
        grad_pair_ref,
        grad_gains_ref,
        grad_bias_ref,
        part["stage"],
        send,
        *part["edges"],
    )
    for copy in copies:
        copy.wait()


def replicated_plan(
    axis_size,
    pair_map,
    cotangent,
    lengths,
    norm_gains,
    edge_weight,
    mult_gate_weight,
    mult_out_weight,
    attention_weight,
    bias_weight,
    attention_out_weight,
):
    _, size, channels = pair_map.shape
    cells = size * size
    bits = axis_size.bit_length() - 1
    far_step = 1 << (bits - 1)
    near_steps = range(2, far_step, 2)

    def swapped(held, mask):
        return lax.ppermute(held, "dap", [(d, d ^ mask) for d in range(axis_size)])

    own = jnp.stack([pair_map, cotangent])
    held = jnp.stack([own, swapped(own, far_step)])
    masks = [0, far_step]
    near = jnp.concatenate([held] + [swapped(held, step) for step in near_steps], axis=0)
    masks = masks + [mask ^ step for step in near_steps for mask in masks]
    far = swapped(near, 1)

    square, wide = ((channels, channels), FULL), ((channels, 4 * channels), FULL)
    outs = [((cells // axis_size, channels), HALF), ((3, channels), FULL), wide, square, square]
    outs += [wide, ((HEADS, channels), FULL), square]
    scratch = sum(kernel_scratch(size, channels).values(), [])
    vmem = pl.BlockSpec(memory_space=pltpu.VMEM)
    smem = pl.BlockSpec(memory_space=pltpu.SMEM)
    anywhere = pl.BlockSpec(memory_space=pl.ANY)
    results = pl.pallas_call(
        functools.partial(whole_kernel, size, masks),
        out_shape=[jax.ShapeDtypeStruct(*out) for out in outs],
        in_specs=[vmem, vmem, smem] + [vmem] * 7,
        out_specs=[vmem] * 2 + [anywhere] * 4 + [vmem, anywhere],
        scratch_shapes=[pltpu.VMEM(*part) for part in scratch] + [pltpu.SemaphoreType.DMA((5,))],
        compiler_params=pltpu.CompilerParams(vmem_limit_bytes=bytes_of(scratch) + VMEM_SLACK),
    )(
        near,
        far,
        lengths,
        norm_gains,
        edge_weight,
        mult_gate_weight,
        mult_out_weight,
        attention_weight,
        bias_weight.T,
        attention_out_weight,
    )
    return (results[0].reshape(pair_map.shape), *results[1:6], results[6].T, results[7])


def per_device(axis_size, pair_map, *rest):
    _, size, channels = pair_map.shape
    scratch = sum(kernel_scratch(size, channels).values(), [])
    fits = size % max(ROW_BLOCK, COLUMN_BLOCK) == 0 and bytes_of(scratch) <= VMEM_SHARE
    if fits and axis_size >= 8 and axis_size & (axis_size - 1) == 0:
        return replicated_plan(axis_size, pair_map, *rest)
    return distributed_plan(pair_map, *rest)


def solution(mesh):
    return jax.shard_map(
        functools.partial(per_device, mesh.shape["dap"]),
        mesh=mesh,
        in_specs=(
            P(("groups", "dap"), None, None),
            P(("groups", "dap"), None, None),
            P("groups"),
            P(),
            P(),
            P(),
            P(),
            P(),
            P(),
            P(),
        ),
        out_specs=(
            P(("groups", "dap"), None, None),
            P("groups", None),
            P("groups", None),
            P("groups", None),
            P("groups", None),
            P("groups", None),
            P("groups", None),
            P("groups", None),
        ),
        check_vma=False,
    )
```

```python
import functools
import math

import jax
import jax.numpy as jnp
from jax import lax
from jax.experimental import pallas as pl
from jax.experimental.pallas import tpu as pltpu
from jax.sharding import PartitionSpec as P

HEADS = 4
HEAD_DIM = 32


epsilon = 1e-05


def norm_forward(values, gain_row):
    center = values - jnp.mean(values, axis=-1, keepdims=True)
    inv_std = lax.rsqrt(jnp.mean(center * center, axis=-1, keepdims=True) + epsilon)
    normed = center * inv_std
    return (normed * gain_row, normed, inv_std)


def norm_backward(grad_out, normed, inv_std, gain_row):
    scaled = grad_out * gain_row
    first_mean = jnp.mean(scaled, axis=-1, keepdims=True)
    second_mean = jnp.mean(scaled * normed, axis=-1, keepdims=True)
    return inv_std * (scaled - first_mean - normed * second_mean)


def distributed_plan(
    pair_map,
    cotangent,
    lengths,
    norm_gains,
    edge_weight,
    mult_gate_weight,
    mult_out_weight,
    attention_weight,
    bias_weight,
    attention_out_weight,
):
    row_count, full_size, channels = pair_map.shape
    inner_width = HEADS * HEAD_DIM
    head_scale = 1.0 / math.sqrt(HEAD_DIM)
    first_row = lax.axis_index("dap") * row_count
    real_count = lengths[0]
    valid_all = (jnp.arange(full_size) < real_count).astype(jnp.float32)
    valid_rows = (first_row + jnp.arange(row_count) < real_count).astype(jnp.float32)
    mask_pair = (valid_rows[:, None] * valid_all[None, :])[:, :, None]
    pair_f32 = pair_map.astype(jnp.float32)
    normed_full, hat_in, scale_in = norm_forward(pair_f32, norm_gains[0])
    normed_x = normed_full.astype(jnp.bfloat16)
    projected = jnp.einsum("rnc,cf->rnf", normed_x, edge_weight, preferred_element_type=jnp.float32)
    left_gate = projected[..., :channels]
    left_value = projected[..., channels : 2 * channels]
    right_gate = projected[..., 2 * channels : 3 * channels]
    right_value = projected[..., 3 * channels :]
    left_sig = jax.nn.sigmoid(left_gate)
    right_sig = jax.nn.sigmoid(right_gate)
    left_edges = (mask_pair * left_sig * left_value).astype(jnp.bfloat16)
    right_edges = (mask_pair * right_sig * right_value).astype(jnp.bfloat16)
    product = jnp.einsum(
        "ikc,jkc->ijc",
        left_edges,
        lax.all_gather(right_edges, "dap", axis=0, tiled=True),
        preferred_element_type=jnp.float32,
    )
    update_full, hat_mid, scale_mid = norm_forward(product, norm_gains[1])
    update = update_full.astype(jnp.bfloat16)
    edge_out = jnp.einsum(
        "rnc,cf->rnf", update, mult_out_weight, preferred_element_type=jnp.float32
    )
    gate_sig = jax.nn.sigmoid(
        jnp.einsum("rnc,cf->rnf", normed_x, mult_gate_weight, preferred_element_type=jnp.float32)
    )
    middle = pair_f32 + gate_sig * edge_out
    normed_mid, hat_attn, scale_attn = norm_forward(middle, norm_gains[2])
    normed_y = normed_mid.astype(jnp.bfloat16)
    bias_local = jnp.einsum(
        "kic,ch->hki", normed_y, bias_weight, preferred_element_type=jnp.float32
    ).astype(jnp.bfloat16)
    bias_whole = lax.all_gather(bias_local, "dap", axis=1, tiled=True)
    bias_query = jnp.swapaxes(bias_whole, 1, 2).astype(jnp.float32)
    column_y, column_cot = (
        lax.all_to_all(normed_y, "dap", split_axis=1, concat_axis=0, tiled=True),
        lax.all_to_all(cotangent, "dap", split_axis=1, concat_axis=0, tiled=True),
    )
    packed = jnp.einsum(
        "ijc,cf->ijf", column_y, attention_weight, preferred_element_type=jnp.float32
    )
    packed = packed.reshape(full_size, row_count, 4, HEADS, HEAD_DIM)
    query_vectors = (packed[:, :, 0] * head_scale).astype(jnp.bfloat16)
    key_vectors = packed[:, :, 1].astype(jnp.bfloat16)
    value_vectors = packed[:, :, 2].astype(jnp.bfloat16)
    att_gate = jax.nn.sigmoid(packed[:, :, 3])
    scores = (
        jnp.einsum(
            "ijhd,kjhd->jhik", query_vectors, key_vectors, preferred_element_type=jnp.float32
        )
        + bias_query[None]
    )
    exp_scores = valid_all * jnp.exp(scores)
    attention = exp_scores / jnp.sum(exp_scores, axis=-1, keepdims=True)
    attention_half = attention.astype(jnp.bfloat16)
    attended = jnp.einsum(
        "jhik,kjhd->ijhd", attention_half, value_vectors, preferred_element_type=jnp.float32
    )
    gated = (att_gate * attended).astype(jnp.bfloat16).reshape(full_size, row_count, inner_width)
    part_attn_out = jnp.einsum("ijf,ijc->fc", gated, column_cot, preferred_element_type=jnp.float32)
    grad_gated = jnp.einsum(
        "ijc,fc->ijf", column_cot, attention_out_weight, preferred_element_type=jnp.float32
    )
    grad_gated = grad_gated.reshape(full_size, row_count, HEADS, HEAD_DIM)
    grad_att = (grad_gated * att_gate).astype(jnp.bfloat16)
    grad_gate_pre = grad_gated * attended * att_gate * (1.0 - att_gate)
    grad_attention = jnp.einsum(
        "ijhd,kjhd->jhik", grad_att, value_vectors, preferred_element_type=jnp.float32
    )
    row_dots = jnp.transpose(jnp.sum(grad_att.astype(jnp.float32) * attended, axis=-1), (1, 2, 0))
    grad_scores = attention * (grad_attention - row_dots[..., None])
    scores_half = grad_scores.astype(jnp.bfloat16)
    grad_query = jnp.einsum(
        "jhik,kjhd->ijhd", scores_half, key_vectors, preferred_element_type=jnp.float32
    )
    grad_key = jnp.einsum(
        "jhik,ijhd->kjhd", scores_half, query_vectors, preferred_element_type=jnp.float32
    )
    grad_value = jnp.einsum(
        "jhik,ijhd->kjhd", attention_half, grad_att, preferred_element_type=jnp.float32
    )
    grad_packed = jnp.stack([grad_query * head_scale, grad_key, grad_value, grad_gate_pre], axis=2)
    grad_packed = grad_packed.reshape(full_size, row_count, 4 * inner_width).astype(jnp.bfloat16)
    part_attention = jnp.einsum(
        "ijc,ijf->cf", column_y, grad_packed, preferred_element_type=jnp.float32
    )
    column_grad = jnp.einsum(
        "ijf,cf->ijc", grad_packed, attention_weight, preferred_element_type=jnp.float32
    ).astype(jnp.bfloat16)
    row_grad = lax.all_to_all(column_grad, "dap", split_axis=0, concat_axis=1, tiled=True)
    score_sums = jnp.sum(grad_scores, axis=0)
    taken = score_sums
    bias_half = lax.psum_scatter(
        jnp.transpose(taken, (2, 0, 1)), "dap", scatter_dimension=0, tiled=True
    ).astype(jnp.bfloat16)
    part_bias = jnp.einsum("kic,khi->ch", normed_y, bias_half, preferred_element_type=jnp.float32)
    grad_normed_y = row_grad.astype(jnp.float32) + jnp.einsum(
        "khi,ch->kic", bias_half, bias_weight, preferred_element_type=jnp.float32
    )
    part_gain_attn = jnp.sum(grad_normed_y * hat_attn, axis=(0, 1))
    grad_middle = cotangent.astype(jnp.float32) + norm_backward(
        grad_normed_y, hat_attn, scale_attn, norm_gains[2]
    )
    grad_edge_out = (grad_middle * gate_sig).astype(jnp.bfloat16)
    grad_gate = (grad_middle * edge_out * gate_sig * (1.0 - gate_sig)).astype(jnp.bfloat16)
    part_mult_out = jnp.einsum(
        "rnc,rnf->cf", update, grad_edge_out, preferred_element_type=jnp.float32
    )
    part_mult_gate = jnp.einsum(
        "rnc,rnf->cf", normed_x, grad_gate, preferred_element_type=jnp.float32
    )
    grad_update = jnp.einsum(
        "rnf,cf->rnc", grad_edge_out, mult_out_weight, preferred_element_type=jnp.float32
    )
    part_gain_mid = jnp.sum(grad_update * hat_mid, axis=(0, 1))
    grad_product = norm_backward(grad_update, hat_mid, scale_mid, norm_gains[1]).astype(
        jnp.bfloat16
    )
    taken = grad_product
    grad_left = jnp.einsum(
        "ijc,jkc->ikc",
        taken,
        lax.all_gather(right_edges, "dap", axis=0, tiled=True),
        preferred_element_type=jnp.float32,
    )
    grad_cols = lax.all_to_all(grad_product, "dap", split_axis=1, concat_axis=0, tiled=True)
    taken = grad_cols
    grad_right = jnp.einsum(
        "ijc,ikc->jkc",
        taken,
        lax.all_gather(left_edges, "dap", axis=0, tiled=True),
        preferred_element_type=jnp.float32,
    )
    grad_proj = jnp.concatenate(
        [
            grad_left * mask_pair * left_value * left_sig * (1.0 - left_sig),
            grad_left * mask_pair * left_sig,
            grad_right * mask_pair * right_value * right_sig * (1.0 - right_sig),
            grad_right * mask_pair * right_sig,
        ],
        axis=-1,
    ).astype(jnp.bfloat16)
    part_edge = jnp.einsum("rnc,rnf->cf", normed_x, grad_proj, preferred_element_type=jnp.float32)
    grad_normed_x = jnp.einsum(
        "rnf,cf->rnc", grad_proj, edge_weight, preferred_element_type=jnp.float32
    )
    grad_normed_x = grad_normed_x + jnp.einsum(
        "rnf,cf->rnc", grad_gate, mult_gate_weight, preferred_element_type=jnp.float32
    )
    part_gain_in = jnp.sum(grad_normed_x * hat_in, axis=(0, 1))
    grad_pair = (
        grad_middle + norm_backward(grad_normed_x, hat_in, scale_in, norm_gains[0])
    ).astype(jnp.bfloat16)
    totals = lax.psum(
        (
            part_gain_in,
            part_gain_mid,
            part_edge,
            part_mult_gate,
            part_mult_out,
            part_gain_attn,
            part_attention,
            part_bias,
            part_attn_out,
        ),
        "dap",
    )
    (
        gain_in_sum,
        gain_mid_sum,
        edge_sum,
        mult_gate_sum,
        mult_out_sum,
        gain_attn_sum,
        attention_sum,
        bias_sum,
        attn_out_sum,
    ) = totals
    inverse = 1.0 / full_size
    grad_gains = jnp.stack([gain_in_sum, gain_mid_sum, gain_attn_sum]) * inverse
    return (
        grad_pair,
        grad_gains,
        edge_sum * inverse,
        mult_gate_sum * inverse,
        mult_out_sum * inverse,
        attention_sum * inverse,
        bias_sum * inverse,
        attn_out_sum * inverse,
    )


ROW_BLOCK = 8
VMEM_SLACK = 8 * 2**20
VMEM_SHARE = 32 * 2**20
HALF = jnp.bfloat16
FULL = jnp.float32


def dot_nn(left, right):
    return lax.dot_general(left, right, (((1,), (0,)), ((), ())), preferred_element_type=FULL)


def dot_nt(left, right):
    return lax.dot_general(left, right, (((1,), (1,)), ((), ())), preferred_element_type=FULL)


def dot_tn(left, right):
    return lax.dot_general(left, right, (((0,), (0,)), ((), ())), preferred_element_type=FULL)


def lane_mean(values):
    return jnp.mean(values, axis=-1, keepdims=True)


def lane_mean_half(values):
    channels = values.shape[1]
    return dot_nn(values.astype(HALF), jnp.ones((channels, channels), HALF)) * (1.0 / channels)


def sigmoid(values):
    return pltpu.reciprocal(1.0 + jnp.exp(-values), approx=True)


def head_blocks(row_width, col_width, dtype):
    shape = (HEADS * row_width, HEADS * col_width)
    row = lax.broadcasted_iota(jnp.int32, shape, 0)
    col = lax.broadcasted_iota(jnp.int32, shape, 1)
    same = None
    for h in range(HEADS):
        here = (row >= h * row_width) & (row < (h + 1) * row_width)
        here = here & (col >= h * col_width) & (col < (h + 1) * col_width)
        same = here if same is None else same | here
    return jnp.where(same, 1.0, 0.0).astype(dtype)


def place_rows(target, part, near_ref, far_ref, masks):
    me = lax.axis_index("dap")
    cells = target.shape[0] // (2 * len(masks))
    for other, blocks in enumerate((near_ref, far_ref)):
        for at, mask in enumerate(masks):
            place = pl.ds(pl.multiple_of((me ^ mask ^ other) * cells, cells), cells)
            target[place, :] = blocks[at, part].reshape(cells, target.shape[1]).astype(FULL)


def block_tools(size):
    block = ROW_BLOCK * size

    def rows_of(at):
        return pl.ds(pl.multiple_of(at * block, block), block)

    def columns_of(ref, at):
        return jnp.concatenate(
            [ref[pl.ds(at * ROW_BLOCK + a, size, stride=size), :] for a in range(ROW_BLOCK)], axis=0
        )

    return rows_of, columns_of


def outer_sum(size, at, row_ref, row_stride, block_stride, block_ref):
    sums = [jnp.zeros((size, block_ref.shape[1]), FULL)] * ROW_BLOCK
    for k in range(size):
        whole = block_ref[k * size : (k + 1) * size, :]
        for a in range(ROW_BLOCK):
            row = (at * ROW_BLOCK + a) * block_stride + k * row_stride
            sums[a] = sums[a] + row_ref[pl.ds(row, 1), :] * whole
    return jnp.concatenate(sums, axis=0)


def cell_of_lane(size):
    lane = lax.broadcasted_iota(jnp.int32, (1, HEADS * size), 1)
    cell = lane
    for h in range(1, HEADS):
        cell = jnp.where(lane >= h * size, lane - h * size, cell)
    return cell


def spread_bias_weight(target, bias_w_ref, size):
    bias_rows = bias_w_ref[...].astype(FULL)
    for h in range(HEADS):
        target[h * size : (h + 1) * size, :] = jnp.broadcast_to(
            bias_rows[h : h + 1], (size, bias_rows.shape[1])
        ).astype(HALF)


def multiply_kernel(
    size,
    masks,
    near_ref,
    far_ref,
    lengths_ref,
    gains_ref,
    edge_w_ref,
    gate_w_ref,
    out_w_ref,
    left_ref,
    right_ref,
    left_a_ref,
    left_b_ref,
    right_a_ref,
    right_b_ref,
    gate_ref,
    hat_mid_ref,
    scale_mid_ref,
    edge_out_ref,
    hat_y_ref,
    scale_y_ref,
    y_ref,
    x_half_ref,
    update_ref,
    pair_ref,
    right_t_ref,
):
    channels = gains_ref.shape[1]
    block = ROW_BLOCK * size
    blocks = size // ROW_BLOCK
    rows_of, columns_of = block_tools(size)
    real = lengths_ref[0]
    gain_x = gains_ref[0:1, :]
    gain_mid = gains_ref[1:2, :]
    gain_y = gains_ref[2:3, :]
    place_rows(pair_ref, 0, near_ref, far_ref, masks)

    def project(at, carry):
        rows = rows_of(at)
        hat, _ = kernel_norm(pair_ref[rows, :])
        normed = (hat * gain_x).astype(HALF)
        x_half_ref[rows, :] = normed
        projected = dot_nn(normed, edge_w_ref[...])
        gate_ref[rows, :] = sigmoid(dot_nn(normed, gate_w_ref[...]))
        shape = (ROW_BLOCK, size, channels)
        row = lax.broadcasted_iota(jnp.int32, shape, 0) + at * ROW_BLOCK
        col = lax.broadcasted_iota(jnp.int32, shape, 1)
        mask = jnp.where((row < real) & (col < real), 1.0, 0.0).reshape(block, channels)
        for side, (edge, first, second) in enumerate(
            ((left_ref, left_a_ref, left_b_ref), (right_ref, right_a_ref, right_b_ref))
        ):
            base = 2 * side * channels
            sig = sigmoid(projected[:, base : base + channels])
            value = projected[:, base + channels : base + 2 * channels]
            masked = mask * sig
            product = masked * value
            edge[rows, :] = product.astype(HALF).astype(FULL)
            first[rows, :] = product * (1.0 - sig)
            second[rows, :] = masked
        return carry

    lax.fori_loop(0, blocks, project, 0, unroll=4)

    def turn(at, carry):
        right_t_ref[rows_of(at), :] = columns_of(right_ref, at)
        return carry

    lax.fori_loop(0, blocks, turn, 0, unroll=4)

    def multiply(at, carry):
        rows = rows_of(at)
        product = outer_sum(size, at, left_ref, 1, size, right_t_ref)
        hat, scale = kernel_norm(product)
        hat_mid_ref[rows, :] = hat
        scale_mid_ref[rows, :] = scale
        update = (hat * gain_mid).astype(HALF)
        update_ref[rows, :] = update
        edge_out = dot_nn(update, out_w_ref[...])
        edge_out_ref[rows, :] = edge_out
        middle = pair_ref[rows, :] + gate_ref[rows, :] * edge_out
        hat, scale = kernel_norm(middle)
        hat_y_ref[rows, :] = hat
        scale_y_ref[rows, :] = scale
        y_ref[rows, :] = hat * gain_y
        return carry

    lax.fori_loop(0, blocks, multiply, 0, unroll=4)


def project_kernel(
    size,
    y_ref,
    att_w_ref,
    bias_w_ref,
    att_gate_ref,
    bias_ref,
    y_t_ref,
    query_ref,
    key_ref,
    value_ref,
    bias_rep_ref,
):
    channels = y_ref.shape[1]
    lanes = HEADS * size
    head_scale = 1.0 / math.sqrt(HEAD_DIM)
    rows_of, columns_of = block_tools(size)
    cell = cell_of_lane(size)
    spread_bias_weight(bias_rep_ref, bias_w_ref, size)

    def prepare(at, carry):
        rows = rows_of(at)
        y = columns_of(y_ref, at).astype(HALF)
        y_t_ref[rows, :] = y
        packed = dot_nn(y, att_w_ref[...])
        query_ref[rows, :] = (packed[:, :channels] * head_scale).astype(HALF)
        key_ref[rows, :] = packed[:, channels : 2 * channels].astype(HALF)
        value_ref[rows, :] = packed[:, 2 * channels : 3 * channels].astype(HALF)
        att_gate_ref[rows, :] = sigmoid(packed[:, 3 * channels :])
        spread = dot_nt(y, bias_rep_ref[...]).astype(HALF).astype(FULL)
        for a in range(ROW_BLOCK):
            carry = carry + jnp.where(cell == at * ROW_BLOCK + a, spread[a * size : (a + 1) * size], 0.0)
        return carry

    bias_ref[...] = lax.fori_loop(
        0, size // ROW_BLOCK, prepare, jnp.zeros((size, lanes), FULL), unroll=4
    )


def attend_kernel(
    size,
    masks,
    near_ref,
    far_ref,
    lengths_ref,
    att_w_ref,
    att_out_w_ref,
    att_gate_ref,
    bias_ref,
    y_t_ref,
    query_ref,
    key_ref,
    value_ref,
    bias_rep_ref,
    cot_ref,
    grad_y_ref,
    cot_t_ref,
    gated_ref,
    grad_packed_ref,
):
    channels = cot_ref.shape[1]
    block = ROW_BLOCK * size
    blocks = size // ROW_BLOCK
    lanes = HEADS * size
    head_scale = 1.0 / math.sqrt(HEAD_DIM)
    rows_of, columns_of = block_tools(size)
    cell = cell_of_lane(size)
    key_row = lax.broadcasted_iota(jnp.int32, (size, lanes), 0)
    valid = jnp.where(key_row < lengths_ref[0], 1.0, 0.0)
    place_rows(cot_ref, 1, near_ref, far_ref, masks)

    head_mask = head_blocks(size, HEAD_DIM, HALF)
    head_mask_full = head_blocks(size, HEAD_DIM, FULL)
    no_rows = jnp.zeros((size, channels), HALF)

    def attend(at, score_sum):
        rows = rows_of(at)
        parts = [slice(a * size, (a + 1) * size) for a in range(ROW_BLOCK)]
        query, key, value = (ref[rows, :] for ref in (query_ref, key_ref, value_ref))
        gate = att_gate_ref[rows, :]
        cot = columns_of(cot_ref, at).astype(HALF)
        cot_t_ref[rows, :] = cot
        grad_gated = dot_nt(cot, att_out_w_ref[...])
        grad_att = (grad_gated * gate).astype(HALF)
        queries = [jnp.concatenate([query[p]] * HEADS, axis=0) * head_mask for p in parts]
        grads = [jnp.concatenate([grad_att[p]] * HEADS, axis=0) * head_mask for p in parts]
        bias = bias_ref[...]

        def stacked(columns):
            return jnp.stack(columns, axis=0)

        scores = stacked([dot_nt(key[p], queries[a]) + bias for a, p in enumerate(parts)])
        grad_attention = stacked([dot_nt(value[p], grads[a]) for a, p in enumerate(parts)])
        exp_scores = valid[None] * jnp.exp(scores)
        total = jnp.sum(exp_scores, axis=1)
        scale = jnp.where(total > 2.0**100, 2.0**-60, 1.0)
        inverse_total = pltpu.reciprocal(total * scale, approx=True)
        attention = (exp_scores * scale[:, None, :]) * inverse_total[:, None, :]
        row_dots = jnp.sum(attention * grad_attention, axis=1)
        grad_scores = attention * (grad_attention - row_dots[:, None, :])
        score_sum = score_sum + jnp.sum(grad_scores, axis=0)
        attention_half = attention.astype(HALF)
        scores_half = grad_scores.astype(HALF)
        grad_key = jnp.concatenate([dot_nn(scores_half[a], queries[a]) for a in range(ROW_BLOCK)], axis=0)
        grad_value = jnp.concatenate([dot_nn(attention_half[a], grads[a]) for a in range(ROW_BLOCK)], axis=0)

        def query_sums(a, p):
            weights = jnp.concatenate([attention_half[a], scores_half[a]], axis=0)
            vectors = jnp.concatenate(
                [
                    jnp.concatenate([value[p], no_rows], axis=1),
                    jnp.concatenate([no_rows, key[p]], axis=1),
                ],
                axis=0,
            )
            whole = dot_tn(weights, vectors)
            masked = [whole[:, :channels] * head_mask_full, whole[:, channels:] * head_mask_full]
            return [sum(part[h * size : (h + 1) * size] for h in range(HEADS)) for part in masked]

        per_query = [query_sums(a, p) for a, p in enumerate(parts)]
        attended = jnp.concatenate([pair[0] for pair in per_query], axis=0)
        grad_query = jnp.concatenate([pair[1] for pair in per_query], axis=0)
        gated = gate * attended
        gated_ref[rows, :] = gated.astype(HALF)
        grad_gate_pre = grad_gated * gated * (1.0 - gate)
        grad_packed = jnp.concatenate(
            [
                (grad_query * head_scale).astype(HALF),
                grad_key.astype(HALF),
                grad_value.astype(HALF),
                grad_gate_pre.astype(HALF),
            ],
            axis=1,
        )
        grad_packed_ref[rows, : 4 * channels] = grad_packed
        grad_y_ref[rows, :] = dot_nt(grad_packed, att_w_ref[...])
        return score_sum

    score_sum = lax.fori_loop(0, blocks, attend, jnp.zeros((size, lanes), FULL), unroll=4)
    bias_grad = score_sum.astype(HALF).astype(FULL)

    def spread_bias(at, carry):
        rows = rows_of(at)
        spread = jnp.concatenate(
            [jnp.where(cell == at * ROW_BLOCK + a, bias_grad, 0.0) for a in range(ROW_BLOCK)], axis=0
        ).astype(HALF)
        grad_packed_ref[rows, 4 * channels :] = spread
        grad_y_ref[rows, :] += dot_nn(spread, bias_rep_ref[...])
        return carry

    lax.fori_loop(0, blocks, spread_bias, 0, unroll=4)


def gain_sum(pairs):
    total = sum(jnp.sum(weight.astype(FULL) * grad, axis=1, keepdims=True) for weight, grad in pairs)
    channels = total.shape[0]
    return jnp.transpose(jnp.broadcast_to(total, (channels, channels)))[0:1, :]


def edges_kernel(
    size,
    devices,
    pair_ref,
    gains_ref,
    edge_w_ref,
    gate_w_ref,
    out_w_ref,
    left_ref,
    right_ref,
    left_a_ref,
    left_b_ref,
    right_a_ref,
    right_b_ref,
    gate_ref,
    hat_mid_ref,
    scale_mid_ref,
    edge_out_ref,
    hat_y_ref,
    scale_y_ref,
    x_half_ref,
    update_ref,
    cot_ref,
    grad_y_ref,
    attention_side,
    grad_pair_ref,
    grad_gains_ref,
    grad_bias_ref,
    stage_refs,
    send,
    grad_middle_ref,
    grad_product_ref,
    grad_proj_ref,
    x_sum_ref,
    y_sum_ref,
):
    channels = gains_ref.shape[1]
    blocks = size // ROW_BLOCK
    rows_of, columns_of = block_tools(size)
    gain_x = gains_ref[0:1, :]
    gain_mid = gains_ref[1:2, :]
    gain_y = gains_ref[2:3, :]

    inverse = 1.0 / size
    y_t_ref, cot_t_ref, gated_ref, grad_packed_ref, att_w_ref, bias_rep_ref = attention_side
    edge_sum_ref, gate_sum_ref, out_sum_ref, att_sum_ref, att_out_sum_ref = stage_refs
    for sum_ref in (x_sum_ref, y_sum_ref, out_sum_ref, att_out_sum_ref):
        sum_ref[...] = jnp.zeros(sum_ref.shape, FULL)

    def attention_sums(at):
        rows = rows_of(at)
        y_sum_ref[...] += dot_tn(y_t_ref[rows, :], grad_packed_ref[rows, :])
        att_out_sum_ref[...] += dot_tn(gated_ref[rows, :], cot_t_ref[rows, :])

    def attention_results():
        att_sum = y_sum_ref[:, : 4 * channels] * inverse
        bias_sum = jnp.transpose(y_sum_ref[:, 4 * channels :] * inverse)
        att_sum_ref[...] = att_sum
        att_out_sum_ref[...] *= inverse
        send(3, 4)
        for h in range(HEADS):
            grad_bias_ref[h : h + 1, :] = jnp.sum(
                bias_sum[h * size : (h + 1) * size], axis=0, keepdims=True
            )
        bias_part = jnp.sum(bias_rep_ref[...].astype(FULL) * bias_sum, axis=0, keepdims=True)
        grad_gains_ref[2:3, :] = (gain_sum(((att_w_ref[...], att_sum),)) + bias_part) / gain_y

    def middle_back(at, carry):
        rows = rows_of(at)
        grad_y = columns_of(grad_y_ref, at)
        grad_middle = cot_ref[rows, :] + kernel_norm_back(
            grad_y, hat_y_ref[rows, :], scale_y_ref[rows, :], gain_y
        )
        grad_middle_ref[rows, :] = grad_middle
        gate = gate_ref[rows, :]
        gated = grad_middle * gate
        grad_edge_out = gated.astype(HALF)
        grad_gate = (gated * edge_out_ref[rows, :] * (1.0 - gate)).astype(HALF)
        grad_proj_ref[rows, 4 * channels :] = grad_gate
        x_sum_ref[:, 4 * channels :] += dot_tn(x_half_ref[rows, :], grad_gate)
        out_sum_ref[...] += dot_tn(update_ref[rows, :], grad_edge_out)
        grad_update = dot_nt(grad_edge_out, out_w_ref[...])
        grad_product = kernel_norm_back(grad_update, hat_mid_ref[rows, :], scale_mid_ref[rows, :], gain_mid)
        grad_product_ref[rows, :] = grad_product.astype(HALF).astype(FULL)
        return carry

    lax.fori_loop(0, blocks, middle_back, 0, unroll=4)

    def edges_back(at):
        rows = rows_of(at)
        x_half = x_half_ref[rows, :]
        for side, (first_ref, second_ref, strides, other_ref) in enumerate(
            (
                (left_a_ref, left_b_ref, (1, size), right_ref),
                (right_a_ref, right_b_ref, (size, 1), left_ref),
            )
        ):
            grad = outer_sum(size, at, grad_product_ref, *strides, other_ref)
            both = jnp.concatenate(
                [(grad * first_ref[rows, :]).astype(HALF), (grad * second_ref[rows, :]).astype(HALF)], axis=1
            )
            place = slice(2 * side * channels, 2 * (side + 1) * channels)
            grad_proj_ref[rows, place] = both
            x_sum_ref[:, place] += dot_tn(x_half, both)

    for at in range(blocks):
        for part in range(2 * at, min(2 * at + 2, blocks)):
            attention_sums(part)
        edges_back(at)
        if 2 * at < blocks <= 2 * at + 2:
            attention_results()

    edge_sum, gate_sum = x_sum_ref[:, : 4 * channels] * inverse, x_sum_ref[:, 4 * channels :] * inverse
    edge_sum_ref[...] = edge_sum
    gate_sum_ref[...] = gate_sum
    out_sum = out_sum_ref[...] * inverse
    out_sum_ref[...] = out_sum
    send(0, 1, 2)
    grad_gains_ref[0:1, :] = gain_sum(((edge_w_ref[...], edge_sum), (gate_w_ref[...], gate_sum))) / gain_x
    grad_gains_ref[1:2, :] = gain_sum(((out_w_ref[...], out_sum),)) / gain_mid

    own_cells = size * size // devices
    own = pl.ds(pl.multiple_of(lax.axis_index("dap") * own_cells, own_cells), own_cells)
    hat, scale = kernel_norm(pair_ref[...].reshape(own_cells, channels).astype(FULL))
    grad_x = dot_nt(grad_proj_ref[own, : 4 * channels], edge_w_ref[...])
    grad_x = grad_x + dot_nt(grad_proj_ref[own, 4 * channels :], gate_w_ref[...])
    grad_pair = grad_middle_ref[own, :] + kernel_norm_back(grad_x, hat, scale, gain_x)
    grad_pair_ref[...] = grad_pair.astype(grad_pair_ref.dtype)


def kernel_norm(values):
    center = values - lane_mean(values)
    scale = lax.rsqrt(lane_mean_half(center * center) + epsilon)
    return center * scale, scale


def kernel_norm_back(grad_out, hat, scale, gain):
    scaled = grad_out * gain
    return scale * (scaled - lane_mean_half(scaled) - hat * lane_mean_half(scaled * hat))


def bytes_of(arrays):
    return sum(math.prod(shape) * jnp.dtype(dtype).itemsize for shape, dtype in arrays)


def kernel_scratch(size, channels):
    cells, lanes = size * size, HEADS * size
    full, half = ((cells, channels), FULL), ((cells, channels), HALF)
    square, wide = ((channels, channels), FULL), ((channels, 4 * channels), FULL)
    return {
        "kept": [full] * 12,
        "y": [full],
        "halves": [half] * 2,
        "multiply": [full] * 2,
        "projections": [full, ((size, lanes), FULL)] + [half] * 4 + [((lanes, channels), HALF)],
        "shared": [full] * 2,
        "attend": [half] * 2 + [((cells, 4 * channels + lanes), HALF)],
        "stage": [wide, square, square, wide, square],
        "edges": [full] * 2
        + [((cells, 5 * channels), HALF), ((channels, 5 * channels), FULL), ((channels, 4 * channels + lanes), FULL)],
    }


def whole_kernel(
    size,
    masks,
    near_ref,
    far_ref,
    lengths_ref,
    gains_ref,
    edge_w_ref,
    gate_w_ref,
    out_w_ref,
    att_w_ref,
    bias_w_ref,
    att_out_w_ref,
    grad_pair_ref,
    grad_gains_ref,
    grad_edge_ref,
    grad_gate_w_ref,
    grad_out_w_ref,
    grad_att_w_ref,
    grad_bias_ref,
    grad_att_out_ref,
    *scratch,
):
    part, at = {}, 0
    for name, arrays in kernel_scratch(size, 1).items():
        part[name] = scratch[at : at + len(arrays)]
        at += len(arrays)
    sent = scratch[at]
    weights = (edge_w_ref, gate_w_ref, out_w_ref)
    multiply_kernel(
        size, masks, near_ref, far_ref, lengths_ref, gains_ref, *weights, *part["kept"], *part["y"], *part["halves"], *part["multiply"]
    )
    project_kernel(size, *part["y"], att_w_ref, bias_w_ref, *part["projections"])
    attend_kernel(
        size,
        masks,
        near_ref,
        far_ref,
        lengths_ref,
        att_w_ref,
        att_out_w_ref,
        *part["projections"],
        *part["shared"],
        *part["attend"],
    )
    targets = (grad_edge_ref, grad_gate_w_ref, grad_out_w_ref, grad_att_w_ref, grad_att_out_ref)
    copies = [
        pltpu.make_async_copy(source, target, sent.at[slot])
        for slot, (source, target) in enumerate(zip(part["stage"], targets))
    ]

    def send(*slots):
        for slot in slots:
            copies[slot].start()

    _, _, y_t_ref, _, _, _, bias_rep_ref = part["projections"]
    cot_t_ref, gated_ref, grad_packed_ref = part["attend"]
    edges_kernel(
        size,
        2 * len(masks),
        near_ref.at[0, 0],
        gains_ref,
        *weights,
        *part["kept"],
        *part["halves"],
        *part["shared"],
        (y_t_ref, cot_t_ref, gated_ref, grad_packed_ref, att_w_ref, bias_rep_ref),
        grad_pair_ref,
        grad_gains_ref,
        grad_bias_ref,
        part["stage"],
        send,
        *part["edges"],
    )
    for copy in copies:
        copy.wait()


def replicated_plan(
    axis_size,
    pair_map,
    cotangent,
    lengths,
    norm_gains,
    edge_weight,
    mult_gate_weight,
    mult_out_weight,
    attention_weight,
    bias_weight,
    attention_out_weight,
):
    _, size, channels = pair_map.shape
    cells = size * size
    bits = axis_size.bit_length() - 1
    far_step = 1 << (bits - 1)
    near_steps = range(2, far_step, 2)

    def swapped(held, mask):
        return lax.ppermute(held, "dap", [(d, d ^ mask) for d in range(axis_size)])

    own = jnp.stack([pair_map, cotangent])
    held = jnp.stack([own, swapped(own, far_step)])
    masks = [0, far_step]
    near = jnp.concatenate([held] + [swapped(held, step) for step in near_steps], axis=0)
    masks = masks + [mask ^ step for step in near_steps for mask in masks]
    far = swapped(near, 1)

    square, wide = ((channels, channels), FULL), ((channels, 4 * channels), FULL)
    outs = [((cells // axis_size, channels), HALF), ((3, channels), FULL), wide, square, square]
    outs += [wide, ((HEADS, channels), FULL), square]
    scratch = sum(kernel_scratch(size, channels).values(), [])
    vmem = pl.BlockSpec(memory_space=pltpu.VMEM)
    smem = pl.BlockSpec(memory_space=pltpu.SMEM)
    anywhere = pl.BlockSpec(memory_space=pl.ANY)
    results = pl.pallas_call(
        functools.partial(whole_kernel, size, masks),
        out_shape=[jax.ShapeDtypeStruct(*out) for out in outs],
        in_specs=[vmem, vmem, smem] + [vmem] * 7,
        out_specs=[vmem] * 2 + [anywhere] * 4 + [vmem, anywhere],
        scratch_shapes=[pltpu.VMEM(*part) for part in scratch] + [pltpu.SemaphoreType.DMA((5,))],
        compiler_params=pltpu.CompilerParams(vmem_limit_bytes=bytes_of(scratch) + VMEM_SLACK),
    )(
        near,
        far,
        lengths,
        norm_gains,
        edge_weight,
        mult_gate_weight,
        mult_out_weight,
        attention_weight,
        bias_weight.T,
        attention_out_weight,
    )
    return (results[0].reshape(pair_map.shape), *results[1:6], results[6].T, results[7])


def per_device(axis_size, pair_map, *rest):
    _, size, channels = pair_map.shape
    scratch = sum(kernel_scratch(size, channels).values(), [])
    fits = size % ROW_BLOCK == 0 and bytes_of(scratch) <= VMEM_SHARE
    if fits and axis_size >= 8 and axis_size & (axis_size - 1) == 0:
        return replicated_plan(axis_size, pair_map, *rest)
    return distributed_plan(pair_map, *rest)


def solution(mesh):
    return jax.shard_map(
        functools.partial(per_device, mesh.shape["dap"]),
        mesh=mesh,
        in_specs=(
            P(("groups", "dap"), None, None),
            P(("groups", "dap"), None, None),
            P("groups"),
            P(),
            P(),
            P(),
            P(),
            P(),
            P(),
            P(),
        ),
        out_specs=(
            P(("groups", "dap"), None, None),
            P("groups", None),
            P("groups", None),
            P("groups", None),
            P("groups", None),
            P("groups", None),
            P("groups", None),
            P("groups", None),
        ),
        check_vma=False,
    )
```

```python
import functools
import math

import jax
import jax.numpy as jnp
from jax import lax
from jax.experimental import pallas as pl
from jax.experimental.pallas import tpu as pltpu
from jax.sharding import PartitionSpec as P

HEADS = 4
HEAD_DIM = 32


epsilon = 1e-05


def norm_forward(values, gain_row):
    center = values - jnp.mean(values, axis=-1, keepdims=True)
    inv_std = lax.rsqrt(jnp.mean(center * center, axis=-1, keepdims=True) + epsilon)
    normed = center * inv_std
    return (normed * gain_row, normed, inv_std)


def norm_backward(grad_out, normed, inv_std, gain_row):
    scaled = grad_out * gain_row
    first_mean = jnp.mean(scaled, axis=-1, keepdims=True)
    second_mean = jnp.mean(scaled * normed, axis=-1, keepdims=True)
    return inv_std * (scaled - first_mean - normed * second_mean)


def distributed_plan(
    pair_map,
    cotangent,
    lengths,
    norm_gains,
    edge_weight,
    mult_gate_weight,
    mult_out_weight,
    attention_weight,
    bias_weight,
    attention_out_weight,
):
    row_count, full_size, channels = pair_map.shape
    inner_width = HEADS * HEAD_DIM
    head_scale = 1.0 / math.sqrt(HEAD_DIM)
    first_row = lax.axis_index("dap") * row_count
    real_count = lengths[0]
    valid_all = (jnp.arange(full_size) < real_count).astype(jnp.float32)
    valid_rows = (first_row + jnp.arange(row_count) < real_count).astype(jnp.float32)
    mask_pair = (valid_rows[:, None] * valid_all[None, :])[:, :, None]
    pair_f32 = pair_map.astype(jnp.float32)
    normed_full, hat_in, scale_in = norm_forward(pair_f32, norm_gains[0])
    normed_x = normed_full.astype(jnp.bfloat16)
    projected = jnp.einsum("rnc,cf->rnf", normed_x, edge_weight, preferred_element_type=jnp.float32)
    left_gate = projected[..., :channels]
    left_value = projected[..., channels : 2 * channels]
    right_gate = projected[..., 2 * channels : 3 * channels]
    right_value = projected[..., 3 * channels :]
    left_sig = jax.nn.sigmoid(left_gate)
    right_sig = jax.nn.sigmoid(right_gate)
    left_edges = (mask_pair * left_sig * left_value).astype(jnp.bfloat16)
    right_edges = (mask_pair * right_sig * right_value).astype(jnp.bfloat16)
    product = jnp.einsum(
        "ikc,jkc->ijc",
        left_edges,
        lax.all_gather(right_edges, "dap", axis=0, tiled=True),
        preferred_element_type=jnp.float32,
    )
    update_full, hat_mid, scale_mid = norm_forward(product, norm_gains[1])
    update = update_full.astype(jnp.bfloat16)
    edge_out = jnp.einsum(
        "rnc,cf->rnf", update, mult_out_weight, preferred_element_type=jnp.float32
    )
    gate_sig = jax.nn.sigmoid(
        jnp.einsum("rnc,cf->rnf", normed_x, mult_gate_weight, preferred_element_type=jnp.float32)
    )
    middle = pair_f32 + gate_sig * edge_out
    normed_mid, hat_attn, scale_attn = norm_forward(middle, norm_gains[2])
    normed_y = normed_mid.astype(jnp.bfloat16)
    bias_local = jnp.einsum(
        "kic,ch->hki", normed_y, bias_weight, preferred_element_type=jnp.float32
    ).astype(jnp.bfloat16)
    bias_whole = lax.all_gather(bias_local, "dap", axis=1, tiled=True)
    bias_query = jnp.swapaxes(bias_whole, 1, 2).astype(jnp.float32)
    column_y, column_cot = (
        lax.all_to_all(normed_y, "dap", split_axis=1, concat_axis=0, tiled=True),
        lax.all_to_all(cotangent, "dap", split_axis=1, concat_axis=0, tiled=True),
    )
    packed = jnp.einsum(
        "ijc,cf->ijf", column_y, attention_weight, preferred_element_type=jnp.float32
    )
    packed = packed.reshape(full_size, row_count, 4, HEADS, HEAD_DIM)
    query_vectors = (packed[:, :, 0] * head_scale).astype(jnp.bfloat16)
    key_vectors = packed[:, :, 1].astype(jnp.bfloat16)
    value_vectors = packed[:, :, 2].astype(jnp.bfloat16)
    att_gate = jax.nn.sigmoid(packed[:, :, 3])
    scores = (
        jnp.einsum(
            "ijhd,kjhd->jhik", query_vectors, key_vectors, preferred_element_type=jnp.float32
        )
        + bias_query[None]
    )
    exp_scores = valid_all * jnp.exp(scores)
    attention = exp_scores / jnp.sum(exp_scores, axis=-1, keepdims=True)
    attention_half = attention.astype(jnp.bfloat16)
    attended = jnp.einsum(
        "jhik,kjhd->ijhd", attention_half, value_vectors, preferred_element_type=jnp.float32
    )
    gated = (att_gate * attended).astype(jnp.bfloat16).reshape(full_size, row_count, inner_width)
    part_attn_out = jnp.einsum("ijf,ijc->fc", gated, column_cot, preferred_element_type=jnp.float32)
    grad_gated = jnp.einsum(
        "ijc,fc->ijf", column_cot, attention_out_weight, preferred_element_type=jnp.float32
    )
    grad_gated = grad_gated.reshape(full_size, row_count, HEADS, HEAD_DIM)
    grad_att = (grad_gated * att_gate).astype(jnp.bfloat16)
    grad_gate_pre = grad_gated * attended * att_gate * (1.0 - att_gate)
    grad_attention = jnp.einsum(
        "ijhd,kjhd->jhik", grad_att, value_vectors, preferred_element_type=jnp.float32
    )
    row_dots = jnp.transpose(jnp.sum(grad_att.astype(jnp.float32) * attended, axis=-1), (1, 2, 0))
    grad_scores = attention * (grad_attention - row_dots[..., None])
    scores_half = grad_scores.astype(jnp.bfloat16)
    grad_query = jnp.einsum(
        "jhik,kjhd->ijhd", scores_half, key_vectors, preferred_element_type=jnp.float32
    )
    grad_key = jnp.einsum(
        "jhik,ijhd->kjhd", scores_half, query_vectors, preferred_element_type=jnp.float32
    )
    grad_value = jnp.einsum(
        "jhik,ijhd->kjhd", attention_half, grad_att, preferred_element_type=jnp.float32
    )
    grad_packed = jnp.stack([grad_query * head_scale, grad_key, grad_value, grad_gate_pre], axis=2)
    grad_packed = grad_packed.reshape(full_size, row_count, 4 * inner_width).astype(jnp.bfloat16)
    part_attention = jnp.einsum(
        "ijc,ijf->cf", column_y, grad_packed, preferred_element_type=jnp.float32
    )
    column_grad = jnp.einsum(
        "ijf,cf->ijc", grad_packed, attention_weight, preferred_element_type=jnp.float32
    ).astype(jnp.bfloat16)
    row_grad = lax.all_to_all(column_grad, "dap", split_axis=0, concat_axis=1, tiled=True)
    score_sums = jnp.sum(grad_scores, axis=0)
    taken = score_sums
    bias_half = lax.psum_scatter(
        jnp.transpose(taken, (2, 0, 1)), "dap", scatter_dimension=0, tiled=True
    ).astype(jnp.bfloat16)
    part_bias = jnp.einsum("kic,khi->ch", normed_y, bias_half, preferred_element_type=jnp.float32)
    grad_normed_y = row_grad.astype(jnp.float32) + jnp.einsum(
        "khi,ch->kic", bias_half, bias_weight, preferred_element_type=jnp.float32
    )
    part_gain_attn = jnp.sum(grad_normed_y * hat_attn, axis=(0, 1))
    grad_middle = cotangent.astype(jnp.float32) + norm_backward(
        grad_normed_y, hat_attn, scale_attn, norm_gains[2]
    )
    grad_edge_out = (grad_middle * gate_sig).astype(jnp.bfloat16)
    grad_gate = (grad_middle * edge_out * gate_sig * (1.0 - gate_sig)).astype(jnp.bfloat16)
    part_mult_out = jnp.einsum(
        "rnc,rnf->cf", update, grad_edge_out, preferred_element_type=jnp.float32
    )
    part_mult_gate = jnp.einsum(
        "rnc,rnf->cf", normed_x, grad_gate, preferred_element_type=jnp.float32
    )
    grad_update = jnp.einsum(
        "rnf,cf->rnc", grad_edge_out, mult_out_weight, preferred_element_type=jnp.float32
    )
    part_gain_mid = jnp.sum(grad_update * hat_mid, axis=(0, 1))
    grad_product = norm_backward(grad_update, hat_mid, scale_mid, norm_gains[1]).astype(
        jnp.bfloat16
    )
    taken = grad_product
    grad_left = jnp.einsum(
        "ijc,jkc->ikc",
        taken,
        lax.all_gather(right_edges, "dap", axis=0, tiled=True),
        preferred_element_type=jnp.float32,
    )
    grad_cols = lax.all_to_all(grad_product, "dap", split_axis=1, concat_axis=0, tiled=True)
    taken = grad_cols
    grad_right = jnp.einsum(
        "ijc,ikc->jkc",
        taken,
        lax.all_gather(left_edges, "dap", axis=0, tiled=True),
        preferred_element_type=jnp.float32,
    )
    grad_proj = jnp.concatenate(
        [
            grad_left * mask_pair * left_value * left_sig * (1.0 - left_sig),
            grad_left * mask_pair * left_sig,
            grad_right * mask_pair * right_value * right_sig * (1.0 - right_sig),
            grad_right * mask_pair * right_sig,
        ],
        axis=-1,
    ).astype(jnp.bfloat16)
    part_edge = jnp.einsum("rnc,rnf->cf", normed_x, grad_proj, preferred_element_type=jnp.float32)
    grad_normed_x = jnp.einsum(
        "rnf,cf->rnc", grad_proj, edge_weight, preferred_element_type=jnp.float32
    )
    grad_normed_x = grad_normed_x + jnp.einsum(
        "rnf,cf->rnc", grad_gate, mult_gate_weight, preferred_element_type=jnp.float32
    )
    part_gain_in = jnp.sum(grad_normed_x * hat_in, axis=(0, 1))
    grad_pair = (
        grad_middle + norm_backward(grad_normed_x, hat_in, scale_in, norm_gains[0])
    ).astype(jnp.bfloat16)
    totals = lax.psum(
        (
            part_gain_in,
            part_gain_mid,
            part_edge,
            part_mult_gate,
            part_mult_out,
            part_gain_attn,
            part_attention,
            part_bias,
            part_attn_out,
        ),
        "dap",
    )
    (
        gain_in_sum,
        gain_mid_sum,
        edge_sum,
        mult_gate_sum,
        mult_out_sum,
        gain_attn_sum,
        attention_sum,
        bias_sum,
        attn_out_sum,
    ) = totals
    inverse = 1.0 / full_size
    grad_gains = jnp.stack([gain_in_sum, gain_mid_sum, gain_attn_sum]) * inverse
    return (
        grad_pair,
        grad_gains,
        edge_sum * inverse,
        mult_gate_sum * inverse,
        mult_out_sum * inverse,
        attention_sum * inverse,
        bias_sum * inverse,
        attn_out_sum * inverse,
    )


ROW_BLOCK = 8
WIDE_BLOCK = 16
VMEM_SLACK = 8 * 2**20
VMEM_SHARE = 32 * 2**20
HALF = jnp.bfloat16
FULL = jnp.float32


def dot_nn(left, right):
    return lax.dot_general(left, right, (((1,), (0,)), ((), ())), preferred_element_type=FULL)


def dot_nt(left, right):
    return lax.dot_general(left, right, (((1,), (1,)), ((), ())), preferred_element_type=FULL)


def dot_tn(left, right):
    return lax.dot_general(left, right, (((0,), (0,)), ((), ())), preferred_element_type=FULL)


def lane_mean(values):
    return jnp.mean(values, axis=-1, keepdims=True)


def sigmoid(values):
    return pltpu.reciprocal(1.0 + jnp.exp(-values), approx=True)


def head_blocks(row_width, col_width, dtype):
    shape = (HEADS * row_width, HEADS * col_width)
    row = lax.broadcasted_iota(jnp.int32, shape, 0)
    col = lax.broadcasted_iota(jnp.int32, shape, 1)
    same = None
    for h in range(HEADS):
        here = (row >= h * row_width) & (row < (h + 1) * row_width)
        here = here & (col >= h * col_width) & (col < (h + 1) * col_width)
        same = here if same is None else same | here
    return jnp.where(same, 1.0, 0.0).astype(dtype)


def place_rows(target, part, near_ref, far_ref, masks):
    me = lax.axis_index("dap")
    cells = target.shape[0] // (2 * len(masks))
    for other, blocks in enumerate((near_ref, far_ref)):
        for at, mask in enumerate(masks):
            place = pl.ds(pl.multiple_of((me ^ mask ^ other) * cells, cells), cells)
            target[place, :] = blocks[at, part].reshape(cells, target.shape[1]).astype(FULL)


def block_tools(size, count=ROW_BLOCK):
    block = count * size

    def rows_of(at):
        return pl.ds(pl.multiple_of(at * block, block), block)

    def columns_of(ref, at):
        return jnp.concatenate(
            [ref[pl.ds(at * count + a, size, stride=size), :] for a in range(count)], axis=0
        )

    return rows_of, columns_of


def outer_sum(size, at, row_ref, row_stride, block_stride, block_ref):
    sums = [jnp.zeros((size, block_ref.shape[1]), FULL)] * ROW_BLOCK
    for k in range(size):
        whole = block_ref[k * size : (k + 1) * size, :]
        for a in range(ROW_BLOCK):
            row = (at * ROW_BLOCK + a) * block_stride + k * row_stride
            sums[a] = sums[a] + row_ref[pl.ds(row, 1), :] * whole
    return jnp.concatenate(sums, axis=0)


def cell_of_lane(size):
    lane = lax.broadcasted_iota(jnp.int32, (1, HEADS * size), 1)
    cell = lane
    for h in range(1, HEADS):
        cell = jnp.where(lane >= h * size, lane - h * size, cell)
    return cell


def spread_bias_weight(target, bias_w_ref, size):
    bias_rows = bias_w_ref[...].astype(FULL)
    for h in range(HEADS):
        target[h * size : (h + 1) * size, :] = jnp.broadcast_to(
            bias_rows[h : h + 1], (size, bias_rows.shape[1])
        ).astype(HALF)


def multiply_kernel(
    size,
    masks,
    near_ref,
    far_ref,
    lengths_ref,
    gains_ref,
    edge_w_ref,
    gate_w_ref,
    out_w_ref,
    left_ref,
    right_ref,
    left_a_ref,
    left_b_ref,
    right_a_ref,
    right_b_ref,
    gate_ref,
    hat_mid_ref,
    scale_mid_ref,
    edge_out_ref,
    hat_y_ref,
    scale_y_ref,
    y_ref,
    x_half_ref,
    update_ref,
    pair_ref,
    right_t_ref,
):
    channels = gains_ref.shape[1]
    block = ROW_BLOCK * size
    blocks = size // ROW_BLOCK
    rows_of, columns_of = block_tools(size)
    real = lengths_ref[0]
    gain_x = gains_ref[0:1, :]
    gain_mid = gains_ref[1:2, :]
    gain_y = gains_ref[2:3, :]
    place_rows(pair_ref, 0, near_ref, far_ref, masks)

    wide_rows_of, _ = block_tools(size, WIDE_BLOCK)

    def project(at, carry):
        rows = wide_rows_of(at)
        hat, _ = kernel_norm(pair_ref[rows, :])
        normed = (hat * gain_x).astype(HALF)
        x_half_ref[rows, :] = normed
        projected = dot_nn(normed, edge_w_ref[...])
        gate_ref[rows, :] = sigmoid(dot_nn(normed, gate_w_ref[...]))
        shape = (WIDE_BLOCK, size, channels)
        row = lax.broadcasted_iota(jnp.int32, shape, 0) + at * WIDE_BLOCK
        col = lax.broadcasted_iota(jnp.int32, shape, 1)
        mask = jnp.where((row < real) & (col < real), 1.0, 0.0).reshape(WIDE_BLOCK * size, channels)
        for side, (edge, first, second) in enumerate(
            ((left_ref, left_a_ref, left_b_ref), (right_ref, right_a_ref, right_b_ref))
        ):
            base = 2 * side * channels
            sig = sigmoid(projected[:, base : base + channels])
            value = projected[:, base + channels : base + 2 * channels]
            masked = mask * sig
            product = masked * value
            edge[rows, :] = product.astype(HALF).astype(FULL)
            first[rows, :] = product * (1.0 - sig)
            second[rows, :] = masked
        return carry

    lax.fori_loop(0, size // WIDE_BLOCK, project, 0, unroll=True)

    def turn(at, carry):
        right_t_ref[rows_of(at), :] = columns_of(right_ref, at)
        return carry

    lax.fori_loop(0, blocks, turn, 0, unroll=True)

    def multiply(at, carry):
        rows = rows_of(at)
        product = outer_sum(size, at, left_ref, 1, size, right_t_ref)
        hat, scale = kernel_norm(product)
        hat_mid_ref[rows, :] = hat
        scale_mid_ref[rows, :] = jnp.broadcast_to(scale, hat.shape)
        update = (hat * gain_mid).astype(HALF)
        update_ref[rows, :] = update
        edge_out = dot_nn(update, out_w_ref[...])
        edge_out_ref[rows, :] = edge_out
        middle = pair_ref[rows, :] + gate_ref[rows, :] * edge_out
        hat, scale = kernel_norm(middle)
        hat_y_ref[rows, :] = hat
        scale_y_ref[rows, :] = jnp.broadcast_to(scale, hat.shape)
        y_ref[rows, :] = hat * gain_y
        return carry

    lax.fori_loop(0, blocks, multiply, 0, unroll=True)


def project_kernel(
    size,
    y_ref,
    att_w_ref,
    bias_w_ref,
    att_gate_ref,
    bias_ref,
    y_t_ref,
    query_ref,
    key_ref,
    value_ref,
    bias_rep_ref,
):
    channels = y_ref.shape[1]
    lanes = HEADS * size
    head_scale = 1.0 / math.sqrt(HEAD_DIM)
    rows_of, columns_of = block_tools(size, WIDE_BLOCK)
    cell = cell_of_lane(size)
    spread_bias_weight(bias_rep_ref, bias_w_ref, size)

    def prepare(at, carry):
        rows = rows_of(at)
        y = columns_of(y_ref, at).astype(HALF)
        y_t_ref[rows, :] = y
        packed = dot_nn(y, att_w_ref[...])
        query_ref[rows, :] = (packed[:, :channels] * head_scale).astype(HALF)
        key_ref[rows, :] = packed[:, channels : 2 * channels].astype(HALF)
        value_ref[rows, :] = packed[:, 2 * channels : 3 * channels].astype(HALF)
        att_gate_ref[rows, :] = sigmoid(packed[:, 3 * channels :])
        spread = dot_nt(y, bias_rep_ref[...]).astype(HALF).astype(FULL)
        for a in range(WIDE_BLOCK):
            carry = carry + jnp.where(cell == at * WIDE_BLOCK + a, spread[a * size : (a + 1) * size], 0.0)
        return carry

    bias_ref[...] = lax.fori_loop(
        0, size // WIDE_BLOCK, prepare, jnp.zeros((size, lanes), FULL), unroll=True
    )


def attend_kernel(
    size,
    masks,
    near_ref,
    far_ref,
    lengths_ref,
    att_w_ref,
    att_out_w_ref,
    att_gate_ref,
    bias_ref,
    y_t_ref,
    query_ref,
    key_ref,
    value_ref,
    bias_rep_ref,
    cot_ref,
    grad_y_ref,
    cot_t_ref,
    gated_ref,
    grad_packed_ref,
):
    channels = cot_ref.shape[1]
    block = WIDE_BLOCK * size
    blocks = size // WIDE_BLOCK
    lanes = HEADS * size
    head_scale = 1.0 / math.sqrt(HEAD_DIM)
    rows_of, columns_of = block_tools(size, WIDE_BLOCK)
    cell = cell_of_lane(size)
    key_row = lax.broadcasted_iota(jnp.int32, (size, lanes), 0)
    valid = jnp.where(key_row < lengths_ref[0], 1.0, 0.0)
    place_rows(cot_ref, 1, near_ref, far_ref, masks)

    head_mask = head_blocks(size, HEAD_DIM, HALF)
    head_mask_full = head_blocks(size, HEAD_DIM, FULL)
    no_rows = jnp.zeros((size, channels), HALF)

    def attend(at, score_sum):
        rows = rows_of(at)
        parts = [slice(a * size, (a + 1) * size) for a in range(WIDE_BLOCK)]
        query, key, value = (ref[rows, :] for ref in (query_ref, key_ref, value_ref))
        gate = att_gate_ref[rows, :]
        cot = columns_of(cot_ref, at).astype(HALF)
        cot_t_ref[rows, :] = cot
        grad_gated = dot_nt(cot, att_out_w_ref[...])
        grad_att = (grad_gated * gate).astype(HALF)
        queries = [jnp.concatenate([query[p]] * HEADS, axis=0) * head_mask for p in parts]
        grads = [jnp.concatenate([grad_att[p]] * HEADS, axis=0) * head_mask for p in parts]
        bias = bias_ref[...]

        def stacked(columns):
            return jnp.stack(columns, axis=0)

        scores = stacked([dot_nt(key[p], queries[a]) + bias for a, p in enumerate(parts)])
        grad_attention = stacked([dot_nt(value[p], grads[a]) for a, p in enumerate(parts)])
        exp_scores = valid[None] * jnp.exp(scores)
        total = jnp.sum(exp_scores, axis=1)
        scale = jnp.where(total > 2.0**100, 2.0**-60, 1.0)
        inverse_total = pltpu.reciprocal(total * scale, approx=True)
        attention = (exp_scores * scale[:, None, :]) * inverse_total[:, None, :]
        row_dots = jnp.sum(attention * grad_attention, axis=1)
        grad_scores = attention * (grad_attention - row_dots[:, None, :])
        score_sum = score_sum + jnp.sum(grad_scores, axis=0)
        attention_half = attention.astype(HALF)
        scores_half = grad_scores.astype(HALF)
        grad_key = jnp.concatenate([dot_nn(scores_half[a], queries[a]) for a in range(WIDE_BLOCK)], axis=0)
        grad_value = jnp.concatenate([dot_nn(attention_half[a], grads[a]) for a in range(WIDE_BLOCK)], axis=0)

        def query_sums(a, p):
            weights = jnp.concatenate([attention_half[a], scores_half[a]], axis=0)
            vectors = jnp.concatenate(
                [
                    jnp.concatenate([value[p], no_rows], axis=1),
                    jnp.concatenate([no_rows, key[p]], axis=1),
                ],
                axis=0,
            )
            whole = dot_tn(weights, vectors)
            masked = [whole[:, :channels] * head_mask_full, whole[:, channels:] * head_mask_full]
            return [sum(part[h * size : (h + 1) * size] for h in range(HEADS)) for part in masked]

        per_query = [query_sums(a, p) for a, p in enumerate(parts)]
        attended = jnp.concatenate([pair[0] for pair in per_query], axis=0)
        grad_query = jnp.concatenate([pair[1] for pair in per_query], axis=0)
        gated = gate * attended
        gated_ref[rows, :] = gated.astype(HALF)
        grad_gate_pre = grad_gated * gated * (1.0 - gate)
        grad_packed = jnp.concatenate(
            [
                (grad_query * head_scale).astype(HALF),
                grad_key.astype(HALF),
                grad_value.astype(HALF),
                grad_gate_pre.astype(HALF),
            ],
            axis=1,
        )
        grad_packed_ref[rows, : 4 * channels] = grad_packed
        grad_y_ref[rows, :] = dot_nt(grad_packed, att_w_ref[...])
        return score_sum

    score_sum = lax.fori_loop(0, blocks, attend, jnp.zeros((size, lanes), FULL), unroll=True)
    bias_grad = score_sum.astype(HALF).astype(FULL)

    def spread_bias(at, carry):
        rows = rows_of(at)
        spread = jnp.concatenate(
            [jnp.where(cell == at * WIDE_BLOCK + a, bias_grad, 0.0) for a in range(WIDE_BLOCK)], axis=0
        ).astype(HALF)
        grad_packed_ref[rows, 4 * channels :] = spread
        grad_y_ref[rows, :] += dot_nn(spread, bias_rep_ref[...])
        return carry

    lax.fori_loop(0, blocks, spread_bias, 0, unroll=True)


def gain_sum(pairs):
    total = sum(jnp.sum(weight.astype(FULL) * grad, axis=1, keepdims=True) for weight, grad in pairs)
    channels = total.shape[0]
    return jnp.transpose(jnp.broadcast_to(total, (channels, channels)))[0:1, :]


def edges_kernel(
    size,
    devices,
    pair_ref,
    gains_ref,
    edge_w_ref,
    gate_w_ref,
    out_w_ref,
    left_ref,
    right_ref,
    left_a_ref,
    left_b_ref,
    right_a_ref,
    right_b_ref,
    gate_ref,
    hat_mid_ref,
    scale_mid_ref,
    edge_out_ref,
    hat_y_ref,
    scale_y_ref,
    x_half_ref,
    update_ref,
    cot_ref,
    grad_y_ref,
    attention_side,
    grad_pair_ref,
    grad_gains_ref,
    grad_bias_ref,
    stage_refs,
    send,
    grad_middle_ref,
    grad_product_ref,
    grad_proj_ref,
    x_sum_ref,
    y_sum_ref,
):
    channels = gains_ref.shape[1]
    blocks = size // ROW_BLOCK
    rows_of, columns_of = block_tools(size)
    gain_x = gains_ref[0:1, :]
    gain_mid = gains_ref[1:2, :]
    gain_y = gains_ref[2:3, :]

    inverse = 1.0 / size
    y_t_ref, cot_t_ref, gated_ref, grad_packed_ref, att_w_ref, bias_rep_ref = attention_side
    edge_sum_ref, gate_sum_ref, out_sum_ref, att_sum_ref, att_out_sum_ref = stage_refs
    for sum_ref in (x_sum_ref, y_sum_ref, out_sum_ref, att_out_sum_ref):
        sum_ref[...] = jnp.zeros(sum_ref.shape, FULL)

    def attention_sums(at):
        rows = rows_of(at)
        y_sum_ref[...] += dot_tn(y_t_ref[rows, :], grad_packed_ref[rows, :])
        att_out_sum_ref[...] += dot_tn(gated_ref[rows, :], cot_t_ref[rows, :])

    def attention_results():
        att_sum = y_sum_ref[:, : 4 * channels] * inverse
        bias_sum = jnp.transpose(y_sum_ref[:, 4 * channels :] * inverse)
        att_sum_ref[...] = att_sum
        att_out_sum_ref[...] *= inverse
        send(3, 4)
        for h in range(HEADS):
            grad_bias_ref[h : h + 1, :] = jnp.sum(
                bias_sum[h * size : (h + 1) * size], axis=0, keepdims=True
            )
        bias_part = jnp.sum(bias_rep_ref[...].astype(FULL) * bias_sum, axis=0, keepdims=True)
        grad_gains_ref[2:3, :] = (gain_sum(((att_w_ref[...], att_sum),)) + bias_part) / gain_y

    wide_rows_of, wide_columns_of = block_tools(size, WIDE_BLOCK)

    def middle_back(at, carry):
        rows = wide_rows_of(at)
        grad_y = wide_columns_of(grad_y_ref, at)
        grad_middle = cot_ref[rows, :] + kernel_norm_back(
            grad_y, hat_y_ref[rows, :], scale_y_ref[rows, :], gain_y
        )
        grad_middle_ref[rows, :] = grad_middle
        gate = gate_ref[rows, :]
        gated = grad_middle * gate
        grad_edge_out = gated.astype(HALF)
        grad_gate = (gated * edge_out_ref[rows, :] * (1.0 - gate)).astype(HALF)
        grad_proj_ref[rows, 4 * channels :] = grad_gate
        x_sum_ref[:, 4 * channels :] += dot_tn(x_half_ref[rows, :], grad_gate)
        out_sum_ref[...] += dot_tn(update_ref[rows, :], grad_edge_out)
        grad_update = dot_nt(grad_edge_out, out_w_ref[...])
        grad_product = kernel_norm_back(grad_update, hat_mid_ref[rows, :], scale_mid_ref[rows, :], gain_mid)
        grad_product_ref[rows, :] = grad_product.astype(HALF).astype(FULL)
        return carry

    lax.fori_loop(0, size // WIDE_BLOCK, middle_back, 0, unroll=True)

    def edges_back(at):
        rows = rows_of(at)
        x_half = x_half_ref[rows, :]
        for side, (first_ref, second_ref, strides, other_ref) in enumerate(
            (
                (left_a_ref, left_b_ref, (1, size), right_ref),
                (right_a_ref, right_b_ref, (size, 1), left_ref),
            )
        ):
            grad = outer_sum(size, at, grad_product_ref, *strides, other_ref)
            both = jnp.concatenate(
                [(grad * first_ref[rows, :]).astype(HALF), (grad * second_ref[rows, :]).astype(HALF)], axis=1
            )
            place = slice(2 * side * channels, 2 * (side + 1) * channels)
            grad_proj_ref[rows, place] = both
            x_sum_ref[:, place] += dot_tn(x_half, both)

    for at in range(blocks):
        for part in range(2 * at, min(2 * at + 2, blocks)):
            attention_sums(part)
        edges_back(at)
        if 2 * at < blocks <= 2 * at + 2:
            attention_results()

    edge_sum, gate_sum = x_sum_ref[:, : 4 * channels] * inverse, x_sum_ref[:, 4 * channels :] * inverse
    edge_sum_ref[...] = edge_sum
    gate_sum_ref[...] = gate_sum
    out_sum = out_sum_ref[...] * inverse
    out_sum_ref[...] = out_sum
    send(0, 1, 2)
    grad_gains_ref[0:1, :] = gain_sum(((edge_w_ref[...], edge_sum), (gate_w_ref[...], gate_sum))) / gain_x
    grad_gains_ref[1:2, :] = gain_sum(((out_w_ref[...], out_sum),)) / gain_mid

    own_cells = size * size // devices
    own = pl.ds(pl.multiple_of(lax.axis_index("dap") * own_cells, own_cells), own_cells)
    hat, scale = kernel_norm(pair_ref[...].reshape(own_cells, channels).astype(FULL))
    grad_x = dot_nt(grad_proj_ref[own, : 4 * channels], edge_w_ref[...])
    grad_x = grad_x + dot_nt(grad_proj_ref[own, 4 * channels :], gate_w_ref[...])
    grad_pair = grad_middle_ref[own, :] + kernel_norm_back(grad_x, hat, scale, gain_x)
    grad_pair_ref[...] = grad_pair.astype(grad_pair_ref.dtype)


def kernel_norm(values):
    center = values - lane_mean(values)
    scale = lax.rsqrt(lane_mean(center * center) + epsilon)
    return center * scale, scale


def kernel_norm_back(grad_out, hat, scale, gain):
    scaled = grad_out * gain
    return scale * (scaled - lane_mean(scaled) - hat * lane_mean(scaled * hat))


def bytes_of(arrays):
    return sum(math.prod(shape) * jnp.dtype(dtype).itemsize for shape, dtype in arrays)


def kernel_scratch(size, channels):
    cells, lanes = size * size, HEADS * size
    full, half = ((cells, channels), FULL), ((cells, channels), HALF)
    square, wide = ((channels, channels), FULL), ((channels, 4 * channels), FULL)
    return {
        "kept": [full] * 12,
        "y": [full],
        "halves": [half] * 2,
        "multiply": [full] * 2,
        "projections": [full, ((size, lanes), FULL)] + [half] * 4 + [((lanes, channels), HALF)],
        "shared": [full] * 2,
        "attend": [half] * 2 + [((cells, 4 * channels + lanes), HALF)],
        "stage": [wide, square, square, wide, square],
        "edges": [full] * 2
        + [((cells, 5 * channels), HALF), ((channels, 5 * channels), FULL), ((channels, 4 * channels + lanes), FULL)],
    }


def whole_kernel(
    size,
    masks,
    near_ref,
    far_ref,
    lengths_ref,
    gains_ref,
    edge_w_ref,
    gate_w_ref,
    out_w_ref,
    att_w_ref,
    bias_w_ref,
    att_out_w_ref,
    grad_pair_ref,
    grad_gains_ref,
    grad_edge_ref,
    grad_gate_w_ref,
    grad_out_w_ref,
    grad_att_w_ref,
    grad_bias_ref,
    grad_att_out_ref,
    *scratch,
):
    part, at = {}, 0
    for name, arrays in kernel_scratch(size, 1).items():
        part[name] = scratch[at : at + len(arrays)]
        at += len(arrays)
    sent = scratch[at]
    weights = (edge_w_ref, gate_w_ref, out_w_ref)
    multiply_kernel(
        size, masks, near_ref, far_ref, lengths_ref, gains_ref, *weights, *part["kept"], *part["y"], *part["halves"], *part["multiply"]
    )
    project_kernel(size, *part["y"], att_w_ref, bias_w_ref, *part["projections"])
    attend_kernel(
        size,
        masks,
        near_ref,
        far_ref,
        lengths_ref,
        att_w_ref,
        att_out_w_ref,
        *part["projections"],
        *part["shared"],
        *part["attend"],
    )
    targets = (grad_edge_ref, grad_gate_w_ref, grad_out_w_ref, grad_att_w_ref, grad_att_out_ref)
    copies = [
        pltpu.make_async_copy(source, target, sent.at[slot])
        for slot, (source, target) in enumerate(zip(part["stage"], targets))
    ]

    def send(*slots):
        for slot in slots:
            copies[slot].start()

    _, _, y_t_ref, _, _, _, bias_rep_ref = part["projections"]
    cot_t_ref, gated_ref, grad_packed_ref = part["attend"]
    edges_kernel(
        size,
        2 * len(masks),
        near_ref.at[0, 0],
        gains_ref,
        *weights,
        *part["kept"],
        *part["halves"],
        *part["shared"],
        (y_t_ref, cot_t_ref, gated_ref, grad_packed_ref, att_w_ref, bias_rep_ref),
        grad_pair_ref,
        grad_gains_ref,
        grad_bias_ref,
        part["stage"],
        send,
        *part["edges"],
    )
    for copy in copies:
        copy.wait()


def replicated_plan(
    axis_size,
    pair_map,
    cotangent,
    lengths,
    norm_gains,
    edge_weight,
    mult_gate_weight,
    mult_out_weight,
    attention_weight,
    bias_weight,
    attention_out_weight,
):
    _, size, channels = pair_map.shape
    cells = size * size
    bits = axis_size.bit_length() - 1
    far_step = 1 << (bits - 1)
    near_steps = range(2, far_step, 2)

    def swapped(held, mask):
        return lax.ppermute(held, "dap", [(d, d ^ mask) for d in range(axis_size)])

    own = jnp.stack([pair_map, cotangent])
    held = jnp.stack([own, swapped(own, far_step)])
    masks = [0, far_step]
    near = jnp.concatenate([held] + [swapped(held, step) for step in near_steps], axis=0)
    masks = masks + [mask ^ step for step in near_steps for mask in masks]
    far = swapped(near, 1)

    square, wide = ((channels, channels), FULL), ((channels, 4 * channels), FULL)
    outs = [((cells // axis_size, channels), HALF), ((3, channels), FULL), wide, square, square]
    outs += [wide, ((HEADS, channels), FULL), square]
    scratch = sum(kernel_scratch(size, channels).values(), [])
    vmem = pl.BlockSpec(memory_space=pltpu.VMEM)
    smem = pl.BlockSpec(memory_space=pltpu.SMEM)
    anywhere = pl.BlockSpec(memory_space=pl.ANY)
    results = pl.pallas_call(
        functools.partial(whole_kernel, size, masks),
        out_shape=[jax.ShapeDtypeStruct(*out) for out in outs],
        in_specs=[vmem, vmem, smem] + [vmem] * 7,
        out_specs=[vmem] * 2 + [anywhere] * 4 + [vmem, anywhere],
        scratch_shapes=[pltpu.VMEM(*part) for part in scratch] + [pltpu.SemaphoreType.DMA((5,))],
        compiler_params=pltpu.CompilerParams(vmem_limit_bytes=bytes_of(scratch) + VMEM_SLACK),
    )(
        near,
        far,
        lengths,
        norm_gains,
        edge_weight,
        mult_gate_weight,
        mult_out_weight,
        attention_weight,
        bias_weight.T,
        attention_out_weight,
    )
    return (results[0].reshape(pair_map.shape), *results[1:6], results[6].T, results[7])


def per_device(axis_size, pair_map, *rest):
    _, size, channels = pair_map.shape
    scratch = sum(kernel_scratch(size, channels).values(), [])
    fits = size % WIDE_BLOCK == 0 and bytes_of(scratch) <= VMEM_SHARE
    if fits and axis_size >= 8 and axis_size & (axis_size - 1) == 0:
        return replicated_plan(axis_size, pair_map, *rest)
    return distributed_plan(pair_map, *rest)


def solution(mesh):
    return jax.shard_map(
        functools.partial(per_device, mesh.shape["dap"]),
        mesh=mesh,
        in_specs=(
            P(("groups", "dap"), None, None),
            P(("groups", "dap"), None, None),
            P("groups"),
            P(),
            P(),
            P(),
            P(),
            P(),
            P(),
            P(),
        ),
        out_specs=(
            P(("groups", "dap"), None, None),
            P("groups", None),
            P("groups", None),
            P("groups", None),
            P("groups", None),
            P("groups", None),
            P("groups", None),
            P("groups", None),
        ),
        check_vma=False,
    )
```

```python
import functools
import math

import jax
import jax.numpy as jnp
from jax import lax
from jax.experimental import pallas as pl
from jax.experimental.pallas import tpu as pltpu
from jax.sharding import PartitionSpec as P

HEADS = 4
HEAD_DIM = 32


epsilon = 1e-05


def norm_forward(values, gain_row):
    center = values - jnp.mean(values, axis=-1, keepdims=True)
    inv_std = lax.rsqrt(jnp.mean(center * center, axis=-1, keepdims=True) + epsilon)
    normed = center * inv_std
    return (normed * gain_row, normed, inv_std)


def norm_backward(grad_out, normed, inv_std, gain_row):
    scaled = grad_out * gain_row
    first_mean = jnp.mean(scaled, axis=-1, keepdims=True)
    second_mean = jnp.mean(scaled * normed, axis=-1, keepdims=True)
    return inv_std * (scaled - first_mean - normed * second_mean)


def distributed_plan(
    pair_map,
    cotangent,
    lengths,
    norm_gains,
    edge_weight,
    mult_gate_weight,
    mult_out_weight,
    attention_weight,
    bias_weight,
    attention_out_weight,
):
    row_count, full_size, channels = pair_map.shape
    inner_width = HEADS * HEAD_DIM
    head_scale = 1.0 / math.sqrt(HEAD_DIM)
    first_row = lax.axis_index("dap") * row_count
    real_count = lengths[0]
    valid_all = (jnp.arange(full_size) < real_count).astype(jnp.float32)
    valid_rows = (first_row + jnp.arange(row_count) < real_count).astype(jnp.float32)
    mask_pair = (valid_rows[:, None] * valid_all[None, :])[:, :, None]
    pair_f32 = pair_map.astype(jnp.float32)
    normed_full, hat_in, scale_in = norm_forward(pair_f32, norm_gains[0])
    normed_x = normed_full.astype(jnp.bfloat16)
    projected = jnp.einsum("rnc,cf->rnf", normed_x, edge_weight, preferred_element_type=jnp.float32)
    left_gate = projected[..., :channels]
    left_value = projected[..., channels : 2 * channels]
    right_gate = projected[..., 2 * channels : 3 * channels]
    right_value = projected[..., 3 * channels :]
    left_sig = jax.nn.sigmoid(left_gate)
    right_sig = jax.nn.sigmoid(right_gate)
    left_edges = (mask_pair * left_sig * left_value).astype(jnp.bfloat16)
    right_edges = (mask_pair * right_sig * right_value).astype(jnp.bfloat16)
    product = jnp.einsum(
        "ikc,jkc->ijc",
        left_edges,
        lax.all_gather(right_edges, "dap", axis=0, tiled=True),
        preferred_element_type=jnp.float32,
    )
    update_full, hat_mid, scale_mid = norm_forward(product, norm_gains[1])
    update = update_full.astype(jnp.bfloat16)
    edge_out = jnp.einsum(
        "rnc,cf->rnf", update, mult_out_weight, preferred_element_type=jnp.float32
    )
    gate_sig = jax.nn.sigmoid(
        jnp.einsum("rnc,cf->rnf", normed_x, mult_gate_weight, preferred_element_type=jnp.float32)
    )
    middle = pair_f32 + gate_sig * edge_out
    normed_mid, hat_attn, scale_attn = norm_forward(middle, norm_gains[2])
    normed_y = normed_mid.astype(jnp.bfloat16)
    bias_local = jnp.einsum(
        "kic,ch->hki", normed_y, bias_weight, preferred_element_type=jnp.float32
    ).astype(jnp.bfloat16)
    bias_whole = lax.all_gather(bias_local, "dap", axis=1, tiled=True)
    bias_query = jnp.swapaxes(bias_whole, 1, 2).astype(jnp.float32)
    column_y, column_cot = (
        lax.all_to_all(normed_y, "dap", split_axis=1, concat_axis=0, tiled=True),
        lax.all_to_all(cotangent, "dap", split_axis=1, concat_axis=0, tiled=True),
    )
    packed = jnp.einsum(
        "ijc,cf->ijf", column_y, attention_weight, preferred_element_type=jnp.float32
    )
    packed = packed.reshape(full_size, row_count, 4, HEADS, HEAD_DIM)
    query_vectors = (packed[:, :, 0] * head_scale).astype(jnp.bfloat16)
    key_vectors = packed[:, :, 1].astype(jnp.bfloat16)
    value_vectors = packed[:, :, 2].astype(jnp.bfloat16)
    att_gate = jax.nn.sigmoid(packed[:, :, 3])
    scores = (
        jnp.einsum(
            "ijhd,kjhd->jhik", query_vectors, key_vectors, preferred_element_type=jnp.float32
        )
        + bias_query[None]
    )
    exp_scores = valid_all * jnp.exp(scores)
    attention = exp_scores / jnp.sum(exp_scores, axis=-1, keepdims=True)
    attention_half = attention.astype(jnp.bfloat16)
    attended = jnp.einsum(
        "jhik,kjhd->ijhd", attention_half, value_vectors, preferred_element_type=jnp.float32
    )
    gated = (att_gate * attended).astype(jnp.bfloat16).reshape(full_size, row_count, inner_width)
    part_attn_out = jnp.einsum("ijf,ijc->fc", gated, column_cot, preferred_element_type=jnp.float32)
    grad_gated = jnp.einsum(
        "ijc,fc->ijf", column_cot, attention_out_weight, preferred_element_type=jnp.float32
    )
    grad_gated = grad_gated.reshape(full_size, row_count, HEADS, HEAD_DIM)
    grad_att = (grad_gated * att_gate).astype(jnp.bfloat16)
    grad_gate_pre = grad_gated * attended * att_gate * (1.0 - att_gate)
    grad_attention = jnp.einsum(
        "ijhd,kjhd->jhik", grad_att, value_vectors, preferred_element_type=jnp.float32
    )
    row_dots = jnp.transpose(jnp.sum(grad_att.astype(jnp.float32) * attended, axis=-1), (1, 2, 0))
    grad_scores = attention * (grad_attention - row_dots[..., None])
    scores_half = grad_scores.astype(jnp.bfloat16)
    grad_query = jnp.einsum(
        "jhik,kjhd->ijhd", scores_half, key_vectors, preferred_element_type=jnp.float32
    )
    grad_key = jnp.einsum(
        "jhik,ijhd->kjhd", scores_half, query_vectors, preferred_element_type=jnp.float32
    )
    grad_value = jnp.einsum(
        "jhik,ijhd->kjhd", attention_half, grad_att, preferred_element_type=jnp.float32
    )
    grad_packed = jnp.stack([grad_query * head_scale, grad_key, grad_value, grad_gate_pre], axis=2)
    grad_packed = grad_packed.reshape(full_size, row_count, 4 * inner_width).astype(jnp.bfloat16)
    part_attention = jnp.einsum(
        "ijc,ijf->cf", column_y, grad_packed, preferred_element_type=jnp.float32
    )
    column_grad = jnp.einsum(
        "ijf,cf->ijc", grad_packed, attention_weight, preferred_element_type=jnp.float32
    ).astype(jnp.bfloat16)
    row_grad = lax.all_to_all(column_grad, "dap", split_axis=0, concat_axis=1, tiled=True)
    score_sums = jnp.sum(grad_scores, axis=0)
    taken = score_sums
    bias_half = lax.psum_scatter(
        jnp.transpose(taken, (2, 0, 1)), "dap", scatter_dimension=0, tiled=True
    ).astype(jnp.bfloat16)
    part_bias = jnp.einsum("kic,khi->ch", normed_y, bias_half, preferred_element_type=jnp.float32)
    grad_normed_y = row_grad.astype(jnp.float32) + jnp.einsum(
        "khi,ch->kic", bias_half, bias_weight, preferred_element_type=jnp.float32
    )
    part_gain_attn = jnp.sum(grad_normed_y * hat_attn, axis=(0, 1))
    grad_middle = cotangent.astype(jnp.float32) + norm_backward(
        grad_normed_y, hat_attn, scale_attn, norm_gains[2]
    )
    grad_edge_out = (grad_middle * gate_sig).astype(jnp.bfloat16)
    grad_gate = (grad_middle * edge_out * gate_sig * (1.0 - gate_sig)).astype(jnp.bfloat16)
    part_mult_out = jnp.einsum(
        "rnc,rnf->cf", update, grad_edge_out, preferred_element_type=jnp.float32
    )
    part_mult_gate = jnp.einsum(
        "rnc,rnf->cf", normed_x, grad_gate, preferred_element_type=jnp.float32
    )
    grad_update = jnp.einsum(
        "rnf,cf->rnc", grad_edge_out, mult_out_weight, preferred_element_type=jnp.float32
    )
    part_gain_mid = jnp.sum(grad_update * hat_mid, axis=(0, 1))
    grad_product = norm_backward(grad_update, hat_mid, scale_mid, norm_gains[1]).astype(
        jnp.bfloat16
    )
    taken = grad_product
    grad_left = jnp.einsum(
        "ijc,jkc->ikc",
        taken,
        lax.all_gather(right_edges, "dap", axis=0, tiled=True),
        preferred_element_type=jnp.float32,
    )
    grad_cols = lax.all_to_all(grad_product, "dap", split_axis=1, concat_axis=0, tiled=True)
    taken = grad_cols
    grad_right = jnp.einsum(
        "ijc,ikc->jkc",
        taken,
        lax.all_gather(left_edges, "dap", axis=0, tiled=True),
        preferred_element_type=jnp.float32,
    )
    grad_proj = jnp.concatenate(
        [
            grad_left * mask_pair * left_value * left_sig * (1.0 - left_sig),
            grad_left * mask_pair * left_sig,
            grad_right * mask_pair * right_value * right_sig * (1.0 - right_sig),
            grad_right * mask_pair * right_sig,
        ],
        axis=-1,
    ).astype(jnp.bfloat16)
    part_edge = jnp.einsum("rnc,rnf->cf", normed_x, grad_proj, preferred_element_type=jnp.float32)
    grad_normed_x = jnp.einsum(
        "rnf,cf->rnc", grad_proj, edge_weight, preferred_element_type=jnp.float32
    )
    grad_normed_x = grad_normed_x + jnp.einsum(
        "rnf,cf->rnc", grad_gate, mult_gate_weight, preferred_element_type=jnp.float32
    )
    part_gain_in = jnp.sum(grad_normed_x * hat_in, axis=(0, 1))
    grad_pair = (
        grad_middle + norm_backward(grad_normed_x, hat_in, scale_in, norm_gains[0])
    ).astype(jnp.bfloat16)
    totals = lax.psum(
        (
            part_gain_in,
            part_gain_mid,
            part_edge,
            part_mult_gate,
            part_mult_out,
            part_gain_attn,
            part_attention,
            part_bias,
            part_attn_out,
        ),
        "dap",
    )
    (
        gain_in_sum,
        gain_mid_sum,
        edge_sum,
        mult_gate_sum,
        mult_out_sum,
        gain_attn_sum,
        attention_sum,
        bias_sum,
        attn_out_sum,
    ) = totals
    inverse = 1.0 / full_size
    grad_gains = jnp.stack([gain_in_sum, gain_mid_sum, gain_attn_sum]) * inverse
    return (
        grad_pair,
        grad_gains,
        edge_sum * inverse,
        mult_gate_sum * inverse,
        mult_out_sum * inverse,
        attention_sum * inverse,
        bias_sum * inverse,
        attn_out_sum * inverse,
    )


ROW_BLOCK = 8
WIDE_BLOCK = 16
VMEM_SLACK = 8 * 2**20
VMEM_SHARE = 32 * 2**20
LOG2_E = 1.0 / math.log(2.0)
HALF = jnp.bfloat16
FULL = jnp.float32


def dot_nn(left, right):
    return lax.dot_general(left, right, (((1,), (0,)), ((), ())), preferred_element_type=FULL)


def dot_nt(left, right):
    return lax.dot_general(left, right, (((1,), (1,)), ((), ())), preferred_element_type=FULL)


def dot_tn(left, right):
    return lax.dot_general(left, right, (((0,), (0,)), ((), ())), preferred_element_type=FULL)


def lane_mean(values):
    return jnp.mean(values, axis=-1, keepdims=True)


def sigmoid(values):
    return pltpu.reciprocal(1.0 + jnp.exp2(values * -LOG2_E), approx=True)


def head_blocks(row_width, col_width, dtype):
    shape = (HEADS * row_width, HEADS * col_width)
    row = lax.broadcasted_iota(jnp.int32, shape, 0)
    col = lax.broadcasted_iota(jnp.int32, shape, 1)
    same = None
    for h in range(HEADS):
        here = (row >= h * row_width) & (row < (h + 1) * row_width)
        here = here & (col >= h * col_width) & (col < (h + 1) * col_width)
        same = here if same is None else same | here
    return jnp.where(same, 1.0, 0.0).astype(dtype)


def place_rows(target, part, near_ref, far_ref, masks):
    me = lax.axis_index("dap")
    cells = target.shape[0] // (2 * len(masks))
    for other, blocks in enumerate((near_ref, far_ref)):
        for at, mask in enumerate(masks):
            place = pl.ds(pl.multiple_of((me ^ mask ^ other) * cells, cells), cells)
            target[place, :] = blocks[at, part].reshape(cells, target.shape[1]).astype(FULL)


def block_tools(size, count=ROW_BLOCK):
    block = count * size

    def rows_of(at):
        return pl.ds(pl.multiple_of(at * block, block), block)

    def columns_of(ref, at):
        return jnp.concatenate(
            [ref[pl.ds(at * count + a, size, stride=size), :] for a in range(count)], axis=0
        )

    return rows_of, columns_of


def outer_sum(size, at, row_ref, row_stride, block_stride, block_ref):
    sums = [jnp.zeros((size, block_ref.shape[1]), FULL)] * ROW_BLOCK
    for k in range(size):
        whole = block_ref[k * size : (k + 1) * size, :]
        for a in range(ROW_BLOCK):
            row = (at * ROW_BLOCK + a) * block_stride + k * row_stride
            sums[a] = sums[a] + row_ref[pl.ds(row, 1), :] * whole
    return jnp.concatenate(sums, axis=0)


def cell_of_lane(size):
    lane = lax.broadcasted_iota(jnp.int32, (1, HEADS * size), 1)
    cell = lane
    for h in range(1, HEADS):
        cell = jnp.where(lane >= h * size, lane - h * size, cell)
    return cell


def spread_bias_weight(target, bias_w_ref, size):
    bias_rows = bias_w_ref[...].astype(FULL)
    for h in range(HEADS):
        target[h * size : (h + 1) * size, :] = jnp.broadcast_to(
            bias_rows[h : h + 1], (size, bias_rows.shape[1])
        ).astype(HALF)


def multiply_kernel(
    size,
    masks,
    near_ref,
    far_ref,
    lengths_ref,
    gains_ref,
    edge_w_ref,
    gate_w_ref,
    out_w_ref,
    left_ref,
    right_ref,
    left_a_ref,
    left_b_ref,
    right_a_ref,
    right_b_ref,
    gate_ref,
    hat_mid_ref,
    scale_mid_ref,
    edge_out_ref,
    hat_y_ref,
    scale_y_ref,
    y_ref,
    x_half_ref,
    update_ref,
    pair_ref,
    right_t_ref,
):
    channels = gains_ref.shape[1]
    block = ROW_BLOCK * size
    blocks = size // ROW_BLOCK
    rows_of, columns_of = block_tools(size)
    real = lengths_ref[0]
    gain_x = gains_ref[0:1, :]
    gain_mid = gains_ref[1:2, :]
    gain_y = gains_ref[2:3, :]
    place_rows(pair_ref, 0, near_ref, far_ref, masks)

    wide_rows_of, _ = block_tools(size, WIDE_BLOCK)

    col_mask = jnp.where(lax.broadcasted_iota(jnp.int32, (size, channels), 0) < real, 1.0, 0.0)

    def project(at, carry):
        rows = wide_rows_of(at)
        hat, _ = kernel_norm(pair_ref[rows, :])
        normed = (hat * gain_x).astype(HALF)
        x_half_ref[rows, :] = normed
        projected = dot_nn(normed, edge_w_ref[...])
        gate_ref[rows, :] = sigmoid(dot_nn(normed, gate_w_ref[...]))
        mask = jnp.concatenate(
            [col_mask * jnp.where(at * WIDE_BLOCK + a < real, 1.0, 0.0) for a in range(WIDE_BLOCK)], axis=0
        )
        for side, (edge, first, second) in enumerate(
            ((left_ref, left_a_ref, left_b_ref), (right_ref, right_a_ref, right_b_ref))
        ):
            base = 2 * side * channels
            sig = sigmoid(projected[:, base : base + channels])
            value = projected[:, base + channels : base + 2 * channels]
            masked = mask * sig
            product = masked * value
            edge[rows, :] = product.astype(HALF).astype(FULL)
            first[rows, :] = product * (1.0 - sig)
            second[rows, :] = masked
        return carry

    lax.fori_loop(0, size // WIDE_BLOCK, project, 0, unroll=True)

    def turn(at, carry):
        right_t_ref[rows_of(at), :] = columns_of(right_ref, at)
        return carry

    lax.fori_loop(0, blocks, turn, 0, unroll=True)

    def multiply(at, carry):
        rows = rows_of(at)
        product = outer_sum(size, at, left_ref, 1, size, right_t_ref)
        hat, scale = kernel_norm(product)
        hat_mid_ref[rows, :] = hat
        scale_mid_ref[rows, :] = jnp.broadcast_to(scale, hat.shape)
        update = (hat * gain_mid).astype(HALF)
        update_ref[rows, :] = update
        edge_out = dot_nn(update, out_w_ref[...])
        edge_out_ref[rows, :] = edge_out
        middle = pair_ref[rows, :] + gate_ref[rows, :] * edge_out
        hat, scale = kernel_norm(middle)
        hat_y_ref[rows, :] = hat
        scale_y_ref[rows, :] = jnp.broadcast_to(scale, hat.shape)
        y_ref[rows, :] = hat * gain_y
        return carry

    lax.fori_loop(0, blocks, multiply, 0, unroll=True)


def project_kernel(
    size,
    y_ref,
    att_w_ref,
    bias_w_ref,
    att_gate_ref,
    bias_ref,
    y_t_ref,
    query_ref,
    key_ref,
    value_ref,
    bias_rep_ref,
):
    channels = y_ref.shape[1]
    lanes = HEADS * size
    head_scale = 1.0 / math.sqrt(HEAD_DIM)
    rows_of, columns_of = block_tools(size, WIDE_BLOCK)
    cell = cell_of_lane(size)
    spread_bias_weight(bias_rep_ref, bias_w_ref, size)

    def prepare(at, carry):
        rows = rows_of(at)
        y = columns_of(y_ref, at).astype(HALF)
        y_t_ref[rows, :] = y
        packed = dot_nn(y, att_w_ref[...])
        query_ref[rows, :] = (packed[:, :channels] * head_scale).astype(HALF)
        key_ref[rows, :] = packed[:, channels : 2 * channels].astype(HALF)
        value_ref[rows, :] = packed[:, 2 * channels : 3 * channels].astype(HALF)
        att_gate_ref[rows, :] = sigmoid(packed[:, 3 * channels :])
        spread = dot_nt(y, bias_rep_ref[...]).astype(HALF).astype(FULL)
        for a in range(WIDE_BLOCK):
            carry = carry + jnp.where(cell == at * WIDE_BLOCK + a, spread[a * size : (a + 1) * size], 0.0)
        return carry

    bias_ref[...] = lax.fori_loop(
        0, size // WIDE_BLOCK, prepare, jnp.zeros((size, lanes), FULL), unroll=True
    )


def attend_kernel(
    size,
    masks,
    near_ref,
    far_ref,
    lengths_ref,
    att_w_ref,
    att_out_w_ref,
    att_gate_ref,
    bias_ref,
    y_t_ref,
    query_ref,
    key_ref,
    value_ref,
    bias_rep_ref,
    cot_ref,
    grad_y_ref,
    cot_t_ref,
    gated_ref,
    grad_packed_ref,
):
    channels = cot_ref.shape[1]
    block = WIDE_BLOCK * size
    blocks = size // WIDE_BLOCK
    lanes = HEADS * size
    head_scale = 1.0 / math.sqrt(HEAD_DIM)
    rows_of, columns_of = block_tools(size, WIDE_BLOCK)
    cell = cell_of_lane(size)
    key_row = lax.broadcasted_iota(jnp.int32, (size, lanes), 0)
    valid = jnp.where(key_row < lengths_ref[0], 1.0, 0.0)
    place_rows(cot_ref, 1, near_ref, far_ref, masks)

    head_mask = head_blocks(size, HEAD_DIM, HALF)
    lane = lax.broadcasted_iota(jnp.int32, (size, channels), 1)
    no_rows = jnp.zeros((size, channels), HALF)

    def own_heads(whole):
        picked = whole[(HEADS - 1) * size :]
        for h in reversed(range(HEADS - 1)):
            picked = jnp.where(lane < (h + 1) * HEAD_DIM, whole[h * size : (h + 1) * size], picked)
        return picked

    def attend(at, score_sum):
        rows = rows_of(at)
        parts = [slice(a * size, (a + 1) * size) for a in range(WIDE_BLOCK)]
        query, key, value = (ref[rows, :] for ref in (query_ref, key_ref, value_ref))
        gate = att_gate_ref[rows, :]
        cot = columns_of(cot_ref, at).astype(HALF)
        cot_t_ref[rows, :] = cot
        grad_gated = dot_nt(cot, att_out_w_ref[...])
        grad_att = (grad_gated * gate).astype(HALF)
        queries = [jnp.concatenate([query[p]] * HEADS, axis=0) * head_mask for p in parts]
        grads = [jnp.concatenate([grad_att[p]] * HEADS, axis=0) * head_mask for p in parts]
        bias = bias_ref[...]

        def stacked(columns):
            return jnp.stack(columns, axis=0)

        scores = stacked([dot_nt(key[p], queries[a]) + bias for a, p in enumerate(parts)])
        grad_attention = stacked([dot_nt(value[p], grads[a]) for a, p in enumerate(parts)])
        exp_scores = valid[None] * jnp.exp2(scores * LOG2_E)
        total = jnp.sum(exp_scores, axis=1)
        scale = jnp.where(total > 2.0**100, 2.0**-60, 1.0)
        inverse_total = pltpu.reciprocal(total * scale, approx=True)
        attention = (exp_scores * scale[:, None, :]) * inverse_total[:, None, :]
        row_dots = jnp.sum(attention * grad_attention, axis=1)
        grad_scores = attention * (grad_attention - row_dots[:, None, :])
        score_sum = score_sum + jnp.sum(grad_scores, axis=0)
        attention_half = attention.astype(HALF)
        scores_half = grad_scores.astype(HALF)
        grad_key = jnp.concatenate([dot_nn(scores_half[a], queries[a]) for a in range(WIDE_BLOCK)], axis=0)
        grad_value = jnp.concatenate([dot_nn(attention_half[a], grads[a]) for a in range(WIDE_BLOCK)], axis=0)

        def query_sums(a, p):
            weights = jnp.concatenate([attention_half[a], scores_half[a]], axis=0)
            vectors = jnp.concatenate(
                [
                    jnp.concatenate([value[p], no_rows], axis=1),
                    jnp.concatenate([no_rows, key[p]], axis=1),
                ],
                axis=0,
            )
            whole = dot_tn(weights, vectors)
            return [own_heads(whole[:, :channels]), own_heads(whole[:, channels:])]

        per_query = [query_sums(a, p) for a, p in enumerate(parts)]
        attended = jnp.concatenate([pair[0] for pair in per_query], axis=0)
        grad_query = jnp.concatenate([pair[1] for pair in per_query], axis=0)
        gated = gate * attended
        gated_ref[rows, :] = gated.astype(HALF)
        grad_gate_pre = grad_gated * gated * (1.0 - gate)
        grad_packed = jnp.concatenate(
            [
                (grad_query * head_scale).astype(HALF),
                grad_key.astype(HALF),
                grad_value.astype(HALF),
                grad_gate_pre.astype(HALF),
            ],
            axis=1,
        )
        grad_packed_ref[rows, : 4 * channels] = grad_packed
        grad_y_ref[rows, :] = dot_nt(grad_packed, att_w_ref[...])
        return score_sum

    score_sum = lax.fori_loop(0, blocks, attend, jnp.zeros((size, lanes), FULL), unroll=True)
    bias_grad = score_sum.astype(HALF).astype(FULL)

    def spread_bias(at, carry):
        rows = rows_of(at)
        spread = jnp.concatenate(
            [jnp.where(cell == at * WIDE_BLOCK + a, bias_grad, 0.0) for a in range(WIDE_BLOCK)], axis=0
        ).astype(HALF)
        grad_packed_ref[rows, 4 * channels :] = spread
        grad_y_ref[rows, :] += dot_nn(spread, bias_rep_ref[...])
        return carry

    lax.fori_loop(0, blocks, spread_bias, 0, unroll=True)


def gain_sum(pairs):
    total = sum(jnp.sum(weight.astype(FULL) * grad, axis=1, keepdims=True) for weight, grad in pairs)
    channels = total.shape[0]
    return jnp.transpose(jnp.broadcast_to(total, (channels, channels)))[0:1, :]


def edges_kernel(
    size,
    devices,
    pair_ref,
    gains_ref,
    edge_w_ref,
    gate_w_ref,
    out_w_ref,
    left_ref,
    right_ref,
    left_a_ref,
    left_b_ref,
    right_a_ref,
    right_b_ref,
    gate_ref,
    hat_mid_ref,
    scale_mid_ref,
    edge_out_ref,
    hat_y_ref,
    scale_y_ref,
    x_half_ref,
    update_ref,
    cot_ref,
    grad_y_ref,
    attention_side,
    grad_pair_ref,
    grad_gains_ref,
    grad_bias_ref,
    stage_refs,
    send,
    grad_middle_ref,
    grad_product_ref,
    grad_proj_ref,
    x_sum_ref,
    y_sum_ref,
):
    channels = gains_ref.shape[1]
    blocks = size // ROW_BLOCK
    rows_of, columns_of = block_tools(size)
    gain_x = gains_ref[0:1, :]
    gain_mid = gains_ref[1:2, :]
    gain_y = gains_ref[2:3, :]

    inverse = 1.0 / size
    y_t_ref, cot_t_ref, gated_ref, grad_packed_ref, att_w_ref, bias_rep_ref = attention_side
    edge_sum_ref, gate_sum_ref, out_sum_ref, att_sum_ref, att_out_sum_ref = stage_refs
    for sum_ref in (x_sum_ref, y_sum_ref, out_sum_ref, att_out_sum_ref):
        sum_ref[...] = jnp.zeros(sum_ref.shape, FULL)

    def attention_sums(at):
        rows = rows_of(at)
        y_sum_ref[...] += dot_tn(y_t_ref[rows, :], grad_packed_ref[rows, :])
        att_out_sum_ref[...] += dot_tn(gated_ref[rows, :], cot_t_ref[rows, :])

    def attention_results():
        att_sum = y_sum_ref[:, : 4 * channels] * inverse
        bias_sum = jnp.transpose(y_sum_ref[:, 4 * channels :] * inverse)
        att_sum_ref[...] = att_sum
        att_out_sum_ref[...] *= inverse
        send(3, 4)
        for h in range(HEADS):
            grad_bias_ref[h : h + 1, :] = jnp.sum(
                bias_sum[h * size : (h + 1) * size], axis=0, keepdims=True
            )
        bias_part = jnp.sum(bias_rep_ref[...].astype(FULL) * bias_sum, axis=0, keepdims=True)
        grad_gains_ref[2:3, :] = (gain_sum(((att_w_ref[...], att_sum),)) + bias_part) / gain_y

    wide_rows_of, wide_columns_of = block_tools(size, WIDE_BLOCK)

    def middle_back(at, carry):
        rows = wide_rows_of(at)
        grad_y = wide_columns_of(grad_y_ref, at)
        grad_middle = cot_ref[rows, :] + kernel_norm_back(
            grad_y, hat_y_ref[rows, :], scale_y_ref[rows, :], gain_y
        )
        grad_middle_ref[rows, :] = grad_middle
        gate = gate_ref[rows, :]
        gated = grad_middle * gate
        grad_edge_out = gated.astype(HALF)
        grad_gate = (gated * edge_out_ref[rows, :] * (1.0 - gate)).astype(HALF)
        grad_proj_ref[rows, 4 * channels :] = grad_gate
        x_sum_ref[:, 4 * channels :] += dot_tn(x_half_ref[rows, :], grad_gate)
        out_sum_ref[...] += dot_tn(update_ref[rows, :], grad_edge_out)
        grad_update = dot_nt(grad_edge_out, out_w_ref[...])
        grad_product = kernel_norm_back(grad_update, hat_mid_ref[rows, :], scale_mid_ref[rows, :], gain_mid)
        grad_product_ref[rows, :] = grad_product.astype(HALF).astype(FULL)
        return carry

    lax.fori_loop(0, size // WIDE_BLOCK, middle_back, 0, unroll=True)

    def edges_back(at):
        rows = rows_of(at)
        x_half = x_half_ref[rows, :]
        for side, (first_ref, second_ref, strides, other_ref) in enumerate(
            (
                (left_a_ref, left_b_ref, (1, size), right_ref),
                (right_a_ref, right_b_ref, (size, 1), left_ref),
            )
        ):
            grad = outer_sum(size, at, grad_product_ref, *strides, other_ref)
            both = jnp.concatenate(
                [(grad * first_ref[rows, :]).astype(HALF), (grad * second_ref[rows, :]).astype(HALF)], axis=1
            )
            place = slice(2 * side * channels, 2 * (side + 1) * channels)
            grad_proj_ref[rows, place] = both
            x_sum_ref[:, place] += dot_tn(x_half, both)

    for at in range(blocks):
        for part in range(2 * at, min(2 * at + 2, blocks)):
            attention_sums(part)
        edges_back(at)
        if 2 * at < blocks <= 2 * at + 2:
            attention_results()

    edge_sum, gate_sum = x_sum_ref[:, : 4 * channels] * inverse, x_sum_ref[:, 4 * channels :] * inverse
    edge_sum_ref[...] = edge_sum
    gate_sum_ref[...] = gate_sum
    out_sum = out_sum_ref[...] * inverse
    out_sum_ref[...] = out_sum
    send(0, 1, 2)
    grad_gains_ref[0:1, :] = gain_sum(((edge_w_ref[...], edge_sum), (gate_w_ref[...], gate_sum))) / gain_x
    grad_gains_ref[1:2, :] = gain_sum(((out_w_ref[...], out_sum),)) / gain_mid

    own_cells = size * size // devices
    own = pl.ds(pl.multiple_of(lax.axis_index("dap") * own_cells, own_cells), own_cells)
    hat, scale = kernel_norm(pair_ref[...].reshape(own_cells, channels).astype(FULL))
    grad_x = dot_nt(grad_proj_ref[own, : 4 * channels], edge_w_ref[...])
    grad_x = grad_x + dot_nt(grad_proj_ref[own, 4 * channels :], gate_w_ref[...])
    grad_pair = grad_middle_ref[own, :] + kernel_norm_back(grad_x, hat, scale, gain_x)
    grad_pair_ref[...] = grad_pair.astype(grad_pair_ref.dtype)


def kernel_norm(values):
    center = values - lane_mean(values)
    scale = lax.rsqrt(lane_mean(center * center) + epsilon)
    return center * scale, scale


def kernel_norm_back(grad_out, hat, scale, gain):
    scaled = grad_out * gain
    return scale * (scaled - lane_mean(scaled) - hat * lane_mean(scaled * hat))


def bytes_of(arrays):
    return sum(math.prod(shape) * jnp.dtype(dtype).itemsize for shape, dtype in arrays)


def kernel_scratch(size, channels):
    cells, lanes = size * size, HEADS * size
    full, half = ((cells, channels), FULL), ((cells, channels), HALF)
    square, wide = ((channels, channels), FULL), ((channels, 4 * channels), FULL)
    return {
        "kept": [full] * 12,
        "y": [full],
        "halves": [half] * 2,
        "multiply": [full] * 2,
        "projections": [full, ((size, lanes), FULL)] + [half] * 4 + [((lanes, channels), HALF)],
        "shared": [full] * 2,
        "attend": [half] * 2 + [((cells, 4 * channels + lanes), HALF)],
        "stage": [wide, square, square, wide, square],
        "edges": [full] * 2
        + [((cells, 5 * channels), HALF), ((channels, 5 * channels), FULL), ((channels, 4 * channels + lanes), FULL)],
    }


def whole_kernel(
    size,
    masks,
    near_ref,
    far_ref,
    lengths_ref,
    gains_ref,
    edge_w_ref,
    gate_w_ref,
    out_w_ref,
    att_w_ref,
    bias_w_ref,
    att_out_w_ref,
    grad_pair_ref,
    grad_gains_ref,
    grad_edge_ref,
    grad_gate_w_ref,
    grad_out_w_ref,
    grad_att_w_ref,
    grad_bias_ref,
    grad_att_out_ref,
    *scratch,
):
    part, at = {}, 0
    for name, arrays in kernel_scratch(size, 1).items():
        part[name] = scratch[at : at + len(arrays)]
        at += len(arrays)
    sent = scratch[at]
    weights = (edge_w_ref, gate_w_ref, out_w_ref)
    multiply_kernel(
        size, masks, near_ref, far_ref, lengths_ref, gains_ref, *weights, *part["kept"], *part["y"], *part["halves"], *part["multiply"]
    )
    project_kernel(size, *part["y"], att_w_ref, bias_w_ref, *part["projections"])
    attend_kernel(
        size,
        masks,
        near_ref,
        far_ref,
        lengths_ref,
        att_w_ref,
        att_out_w_ref,
        *part["projections"],
        *part["shared"],
        *part["attend"],
    )
    targets = (grad_edge_ref, grad_gate_w_ref, grad_out_w_ref, grad_att_w_ref, grad_att_out_ref)
    copies = [
        pltpu.make_async_copy(source, target, sent.at[slot])
        for slot, (source, target) in enumerate(zip(part["stage"], targets))
    ]

    def send(*slots):
        for slot in slots:
            copies[slot].start()

    _, _, y_t_ref, _, _, _, bias_rep_ref = part["projections"]
    cot_t_ref, gated_ref, grad_packed_ref = part["attend"]
    edges_kernel(
        size,
        2 * len(masks),
        near_ref.at[0, 0],
        gains_ref,
        *weights,
        *part["kept"],
        *part["halves"],
        *part["shared"],
        (y_t_ref, cot_t_ref, gated_ref, grad_packed_ref, att_w_ref, bias_rep_ref),
        grad_pair_ref,
        grad_gains_ref,
        grad_bias_ref,
        part["stage"],
        send,
        *part["edges"],
    )
    for copy in copies:
        copy.wait()


def replicated_plan(
    axis_size,
    pair_map,
    cotangent,
    lengths,
    norm_gains,
    edge_weight,
    mult_gate_weight,
    mult_out_weight,
    attention_weight,
    bias_weight,
    attention_out_weight,
):
    _, size, channels = pair_map.shape
    cells = size * size
    bits = axis_size.bit_length() - 1
    far_step = 1 << (bits - 1)
    near_steps = range(2, far_step, 2)

    def swapped(held, mask):
        return lax.ppermute(held, "dap", [(d, d ^ mask) for d in range(axis_size)])

    own = jnp.stack([pair_map, cotangent])
    held = jnp.stack([own, swapped(own, far_step)])
    masks = [0, far_step]
    near = jnp.concatenate([held] + [swapped(held, step) for step in near_steps], axis=0)
    masks = masks + [mask ^ step for step in near_steps for mask in masks]
    far = swapped(near, 1)

    square, wide = ((channels, channels), FULL), ((channels, 4 * channels), FULL)
    outs = [((cells // axis_size, channels), HALF), ((3, channels), FULL), wide, square, square]
    outs += [wide, ((HEADS, channels), FULL), square]
    scratch = sum(kernel_scratch(size, channels).values(), [])
    vmem = pl.BlockSpec(memory_space=pltpu.VMEM)
    smem = pl.BlockSpec(memory_space=pltpu.SMEM)
    anywhere = pl.BlockSpec(memory_space=pl.ANY)
    results = pl.pallas_call(
        functools.partial(whole_kernel, size, masks),
        out_shape=[jax.ShapeDtypeStruct(*out) for out in outs],
        in_specs=[vmem, vmem, smem] + [vmem] * 7,
        out_specs=[vmem] * 2 + [anywhere] * 4 + [vmem, anywhere],
        scratch_shapes=[pltpu.VMEM(*part) for part in scratch] + [pltpu.SemaphoreType.DMA((5,))],
        compiler_params=pltpu.CompilerParams(vmem_limit_bytes=bytes_of(scratch) + VMEM_SLACK),
    )(
        near,
        far,
        lengths,
        norm_gains,
        edge_weight,
        mult_gate_weight,
        mult_out_weight,
        attention_weight,
        bias_weight.T,
        attention_out_weight,
    )
    return (results[0].reshape(pair_map.shape), *results[1:6], results[6].T, results[7])


def per_device(axis_size, pair_map, *rest):
    _, size, channels = pair_map.shape
    scratch = sum(kernel_scratch(size, channels).values(), [])
    fits = size % WIDE_BLOCK == 0 and bytes_of(scratch) <= VMEM_SHARE
    if fits and axis_size >= 8 and axis_size & (axis_size - 1) == 0:
        return replicated_plan(axis_size, pair_map, *rest)
    return distributed_plan(pair_map, *rest)


def solution(mesh):
    return jax.shard_map(
        functools.partial(per_device, mesh.shape["dap"]),
        mesh=mesh,
        in_specs=(
            P(("groups", "dap"), None, None),
            P(("groups", "dap"), None, None),
            P("groups"),
            P(),
            P(),
            P(),
            P(),
            P(),
            P(),
            P(),
        ),
        out_specs=(
            P(("groups", "dap"), None, None),
            P("groups", None),
            P("groups", None),
            P("groups", None),
            P("groups", None),
            P("groups", None),
            P("groups", None),
            P("groups", None),
        ),
        check_vma=False,
    )
```

```python
import functools
import math

import jax
import jax.numpy as jnp
from jax import lax
from jax.experimental import pallas as pl
from jax.experimental.pallas import tpu as pltpu
from jax.sharding import PartitionSpec as P

HEADS = 4
HEAD_DIM = 32


epsilon = 1e-05


def norm_forward(values, gain_row):
    center = values - jnp.mean(values, axis=-1, keepdims=True)
    inv_std = lax.rsqrt(jnp.mean(center * center, axis=-1, keepdims=True) + epsilon)
    normed = center * inv_std
    return (normed * gain_row, normed, inv_std)


def norm_backward(grad_out, normed, inv_std, gain_row):
    scaled = grad_out * gain_row
    first_mean = jnp.mean(scaled, axis=-1, keepdims=True)
    second_mean = jnp.mean(scaled * normed, axis=-1, keepdims=True)
    return inv_std * (scaled - first_mean - normed * second_mean)


def distributed_plan(
    pair_map,
    cotangent,
    lengths,
    norm_gains,
    edge_weight,
    mult_gate_weight,
    mult_out_weight,
    attention_weight,
    bias_weight,
    attention_out_weight,
):
    row_count, full_size, channels = pair_map.shape
    inner_width = HEADS * HEAD_DIM
    head_scale = 1.0 / math.sqrt(HEAD_DIM)
    first_row = lax.axis_index("dap") * row_count
    real_count = lengths[0]
    valid_all = (jnp.arange(full_size) < real_count).astype(jnp.float32)
    valid_rows = (first_row + jnp.arange(row_count) < real_count).astype(jnp.float32)
    mask_pair = (valid_rows[:, None] * valid_all[None, :])[:, :, None]
    pair_f32 = pair_map.astype(jnp.float32)
    normed_full, hat_in, scale_in = norm_forward(pair_f32, norm_gains[0])
    normed_x = normed_full.astype(jnp.bfloat16)
    projected = jnp.einsum("rnc,cf->rnf", normed_x, edge_weight, preferred_element_type=jnp.float32)
    left_gate = projected[..., :channels]
    left_value = projected[..., channels : 2 * channels]
    right_gate = projected[..., 2 * channels : 3 * channels]
    right_value = projected[..., 3 * channels :]
    left_sig = jax.nn.sigmoid(left_gate)
    right_sig = jax.nn.sigmoid(right_gate)
    left_edges = (mask_pair * left_sig * left_value).astype(jnp.bfloat16)
    right_edges = (mask_pair * right_sig * right_value).astype(jnp.bfloat16)
    product = jnp.einsum(
        "ikc,jkc->ijc",
        left_edges,
        lax.all_gather(right_edges, "dap", axis=0, tiled=True),
        preferred_element_type=jnp.float32,
    )
    update_full, hat_mid, scale_mid = norm_forward(product, norm_gains[1])
    update = update_full.astype(jnp.bfloat16)
    edge_out = jnp.einsum(
        "rnc,cf->rnf", update, mult_out_weight, preferred_element_type=jnp.float32
    )
    gate_sig = jax.nn.sigmoid(
        jnp.einsum("rnc,cf->rnf", normed_x, mult_gate_weight, preferred_element_type=jnp.float32)
    )
    middle = pair_f32 + gate_sig * edge_out
    normed_mid, hat_attn, scale_attn = norm_forward(middle, norm_gains[2])
    normed_y = normed_mid.astype(jnp.bfloat16)
    bias_local = jnp.einsum(
        "kic,ch->hki", normed_y, bias_weight, preferred_element_type=jnp.float32
    ).astype(jnp.bfloat16)
    bias_whole = lax.all_gather(bias_local, "dap", axis=1, tiled=True)
    bias_query = jnp.swapaxes(bias_whole, 1, 2).astype(jnp.float32)
    column_y, column_cot = (
        lax.all_to_all(normed_y, "dap", split_axis=1, concat_axis=0, tiled=True),
        lax.all_to_all(cotangent, "dap", split_axis=1, concat_axis=0, tiled=True),
    )
    packed = jnp.einsum(
        "ijc,cf->ijf", column_y, attention_weight, preferred_element_type=jnp.float32
    )
    packed = packed.reshape(full_size, row_count, 4, HEADS, HEAD_DIM)
    query_vectors = (packed[:, :, 0] * head_scale).astype(jnp.bfloat16)
    key_vectors = packed[:, :, 1].astype(jnp.bfloat16)
    value_vectors = packed[:, :, 2].astype(jnp.bfloat16)
    att_gate = jax.nn.sigmoid(packed[:, :, 3])
    scores = (
        jnp.einsum(
            "ijhd,kjhd->jhik", query_vectors, key_vectors, preferred_element_type=jnp.float32
        )
        + bias_query[None]
    )
    exp_scores = valid_all * jnp.exp(scores)
    attention = exp_scores / jnp.sum(exp_scores, axis=-1, keepdims=True)
    attention_half = attention.astype(jnp.bfloat16)
    attended = jnp.einsum(
        "jhik,kjhd->ijhd", attention_half, value_vectors, preferred_element_type=jnp.float32
    )
    gated = (att_gate * attended).astype(jnp.bfloat16).reshape(full_size, row_count, inner_width)
    part_attn_out = jnp.einsum("ijf,ijc->fc", gated, column_cot, preferred_element_type=jnp.float32)
    grad_gated = jnp.einsum(
        "ijc,fc->ijf", column_cot, attention_out_weight, preferred_element_type=jnp.float32
    )
    grad_gated = grad_gated.reshape(full_size, row_count, HEADS, HEAD_DIM)
    grad_att = (grad_gated * att_gate).astype(jnp.bfloat16)
    grad_gate_pre = grad_gated * attended * att_gate * (1.0 - att_gate)
    grad_attention = jnp.einsum(
        "ijhd,kjhd->jhik", grad_att, value_vectors, preferred_element_type=jnp.float32
    )
    row_dots = jnp.transpose(jnp.sum(grad_att.astype(jnp.float32) * attended, axis=-1), (1, 2, 0))
    grad_scores = attention * (grad_attention - row_dots[..., None])
    scores_half = grad_scores.astype(jnp.bfloat16)
    grad_query = jnp.einsum(
        "jhik,kjhd->ijhd", scores_half, key_vectors, preferred_element_type=jnp.float32
    )
    grad_key = jnp.einsum(
        "jhik,ijhd->kjhd", scores_half, query_vectors, preferred_element_type=jnp.float32
    )
    grad_value = jnp.einsum(
        "jhik,ijhd->kjhd", attention_half, grad_att, preferred_element_type=jnp.float32
    )
    grad_packed = jnp.stack([grad_query * head_scale, grad_key, grad_value, grad_gate_pre], axis=2)
    grad_packed = grad_packed.reshape(full_size, row_count, 4 * inner_width).astype(jnp.bfloat16)
    part_attention = jnp.einsum(
        "ijc,ijf->cf", column_y, grad_packed, preferred_element_type=jnp.float32
    )
    column_grad = jnp.einsum(
        "ijf,cf->ijc", grad_packed, attention_weight, preferred_element_type=jnp.float32
    ).astype(jnp.bfloat16)
    row_grad = lax.all_to_all(column_grad, "dap", split_axis=0, concat_axis=1, tiled=True)
    score_sums = jnp.sum(grad_scores, axis=0)
    taken = score_sums
    bias_half = lax.psum_scatter(
        jnp.transpose(taken, (2, 0, 1)), "dap", scatter_dimension=0, tiled=True
    ).astype(jnp.bfloat16)
    part_bias = jnp.einsum("kic,khi->ch", normed_y, bias_half, preferred_element_type=jnp.float32)
    grad_normed_y = row_grad.astype(jnp.float32) + jnp.einsum(
        "khi,ch->kic", bias_half, bias_weight, preferred_element_type=jnp.float32
    )
    part_gain_attn = jnp.sum(grad_normed_y * hat_attn, axis=(0, 1))
    grad_middle = cotangent.astype(jnp.float32) + norm_backward(
        grad_normed_y, hat_attn, scale_attn, norm_gains[2]
    )
    grad_edge_out = (grad_middle * gate_sig).astype(jnp.bfloat16)
    grad_gate = (grad_middle * edge_out * gate_sig * (1.0 - gate_sig)).astype(jnp.bfloat16)
    part_mult_out = jnp.einsum(
        "rnc,rnf->cf", update, grad_edge_out, preferred_element_type=jnp.float32
    )
    part_mult_gate = jnp.einsum(
        "rnc,rnf->cf", normed_x, grad_gate, preferred_element_type=jnp.float32
    )
    grad_update = jnp.einsum(
        "rnf,cf->rnc", grad_edge_out, mult_out_weight, preferred_element_type=jnp.float32
    )
    part_gain_mid = jnp.sum(grad_update * hat_mid, axis=(0, 1))
    grad_product = norm_backward(grad_update, hat_mid, scale_mid, norm_gains[1]).astype(
        jnp.bfloat16
    )
    taken = grad_product
    grad_left = jnp.einsum(
        "ijc,jkc->ikc",
        taken,
        lax.all_gather(right_edges, "dap", axis=0, tiled=True),
        preferred_element_type=jnp.float32,
    )
    grad_cols = lax.all_to_all(grad_product, "dap", split_axis=1, concat_axis=0, tiled=True)
    taken = grad_cols
    grad_right = jnp.einsum(
        "ijc,ikc->jkc",
        taken,
        lax.all_gather(left_edges, "dap", axis=0, tiled=True),
        preferred_element_type=jnp.float32,
    )
    grad_proj = jnp.concatenate(
        [
            grad_left * mask_pair * left_value * left_sig * (1.0 - left_sig),
            grad_left * mask_pair * left_sig,
            grad_right * mask_pair * right_value * right_sig * (1.0 - right_sig),
            grad_right * mask_pair * right_sig,
        ],
        axis=-1,
    ).astype(jnp.bfloat16)
    part_edge = jnp.einsum("rnc,rnf->cf", normed_x, grad_proj, preferred_element_type=jnp.float32)
    grad_normed_x = jnp.einsum(
        "rnf,cf->rnc", grad_proj, edge_weight, preferred_element_type=jnp.float32
    )
    grad_normed_x = grad_normed_x + jnp.einsum(
        "rnf,cf->rnc", grad_gate, mult_gate_weight, preferred_element_type=jnp.float32
    )
    part_gain_in = jnp.sum(grad_normed_x * hat_in, axis=(0, 1))
    grad_pair = (
        grad_middle + norm_backward(grad_normed_x, hat_in, scale_in, norm_gains[0])
    ).astype(jnp.bfloat16)
    totals = lax.psum(
        (
            part_gain_in,
            part_gain_mid,
            part_edge,
            part_mult_gate,
            part_mult_out,
            part_gain_attn,
            part_attention,
            part_bias,
            part_attn_out,
        ),
        "dap",
    )
    (
        gain_in_sum,
        gain_mid_sum,
        edge_sum,
        mult_gate_sum,
        mult_out_sum,
        gain_attn_sum,
        attention_sum,
        bias_sum,
        attn_out_sum,
    ) = totals
    inverse = 1.0 / full_size
    grad_gains = jnp.stack([gain_in_sum, gain_mid_sum, gain_attn_sum]) * inverse
    return (
        grad_pair,
        grad_gains,
        edge_sum * inverse,
        mult_gate_sum * inverse,
        mult_out_sum * inverse,
        attention_sum * inverse,
        bias_sum * inverse,
        attn_out_sum * inverse,
    )


ROW_BLOCK = 8
WIDE_BLOCK = 16
VMEM_SLACK = 8 * 2**20
VMEM_SHARE = 32 * 2**20
LOG2_E = 1.0 / math.log(2.0)
HALF = jnp.bfloat16
FULL = jnp.float32


def dot_nn(left, right):
    return lax.dot_general(left, right, (((1,), (0,)), ((), ())), preferred_element_type=FULL)


def dot_nt(left, right):
    return lax.dot_general(left, right, (((1,), (1,)), ((), ())), preferred_element_type=FULL)


def dot_tn(left, right):
    return lax.dot_general(left, right, (((0,), (0,)), ((), ())), preferred_element_type=FULL)


def lane_mean(values):
    return jnp.mean(values, axis=-1, keepdims=True)


def sigmoid(values):
    return pltpu.reciprocal(1.0 + jnp.exp2(values * -LOG2_E), approx=True)


def head_blocks(row_width, col_width, dtype):
    shape = (HEADS * row_width, HEADS * col_width)
    row = lax.broadcasted_iota(jnp.int32, shape, 0)
    col = lax.broadcasted_iota(jnp.int32, shape, 1)
    same = None
    for h in range(HEADS):
        here = (row >= h * row_width) & (row < (h + 1) * row_width)
        here = here & (col >= h * col_width) & (col < (h + 1) * col_width)
        same = here if same is None else same | here
    return jnp.where(same, 1.0, 0.0).astype(dtype)


def project_blocks(size, masks, other, blocks_ref, real_of, gains_ref, edge_w_ref, gate_w_ref, arrays):
    (
        left_ref,
        right_ref,
        left_a_ref,
        left_b_ref,
        right_a_ref,
        right_b_ref,
        gate_ref,
        x_half_ref,
        pair_ref,
        cot_ref,
    ) = arrays
    channels = gains_ref.shape[1]
    cells = size * size // (2 * len(masks))
    count = cells // size
    me = lax.axis_index("dap")
    real = col_mask = None
    group = max(1, WIDE_BLOCK // count)
    for first in range(0, len(masks), group):
        members = range(first, min(first + group, len(masks)))
        sources = [me ^ (other ^ masks[e]) for e in members]
        places = [pl.ds(pl.multiple_of(source * cells, cells), cells) for source in sources]

        def put(ref, values):
            for at, place in enumerate(places):
                ref[place, :] = values[at * cells : (at + 1) * cells]

        def taken(part):
            return jnp.concatenate(
                [blocks_ref[e, part].reshape(cells, channels) for e in members], axis=0
            ).astype(FULL)

        pair = taken(0)
        put(pair_ref, pair)
        put(cot_ref, taken(1))
        hat, _ = kernel_norm(pair)
        normed = (hat * gains_ref[0:1, :]).astype(HALF)
        put(x_half_ref, normed)
        projected = dot_nn(normed, edge_w_ref[...])
        put(gate_ref, sigmoid(dot_nn(normed, gate_w_ref[...])))
        if first == 0:
            real = real_of()
            col_mask = jnp.where(lax.broadcasted_iota(jnp.int32, (size, channels), 0) < real, 1.0, 0.0)
        mask = jnp.concatenate(
            [
                col_mask * jnp.where(real > source * count + row, 1.0, 0.0)
                for source in sources
                for row in range(count)
            ],
            axis=0,
        )
        for side, (edge, first_ref, second_ref) in enumerate(
            ((left_ref, left_a_ref, left_b_ref), (right_ref, right_a_ref, right_b_ref))
        ):
            base = 2 * side * channels
            sig = sigmoid(projected[:, base : base + channels])
            value = projected[:, base + channels : base + 2 * channels]
            masked = mask * sig
            product = masked * value
            put(edge, product.astype(HALF).astype(FULL))
            put(first_ref, product * (1.0 - sig))
            put(second_ref, masked)


def near_kernel(
    size, masks, near_ref, lengths_ref, gains_ref, edge_w_ref, gate_w_ref, bias_w_ref, reals_ref, bias_rep_ref, *refs
):
    *arrays, real_ref, sent = refs
    copy = pltpu.make_async_copy(lengths_ref, real_ref, sent)
    copy.start()

    def real_of():
        copy.wait()
        return real_ref[0]

    spread_bias_weight(bias_rep_ref, bias_w_ref, size)
    project_blocks(size, masks, 0, near_ref, real_of, gains_ref, edge_w_ref, gate_w_ref, arrays)
    reals_ref[...] = jnp.full(reals_ref.shape, real_ref[0], jnp.int32)


def block_tools(size, count=ROW_BLOCK):
    block = count * size

    def rows_of(at):
        return pl.ds(pl.multiple_of(at * block, block), block)

    def columns_of(ref, at):
        return jnp.concatenate(
            [ref[pl.ds(at * count + a, size, stride=size), :] for a in range(count)], axis=0
        )

    return rows_of, columns_of


def outer_sum(size, at, row_ref, row_stride, block_stride, block_ref):
    sums = [jnp.zeros((size, block_ref.shape[1]), FULL)] * ROW_BLOCK
    for k in range(size):
        whole = block_ref[k * size : (k + 1) * size, :]
        for a in range(ROW_BLOCK):
            row = (at * ROW_BLOCK + a) * block_stride + k * row_stride
            sums[a] = sums[a] + row_ref[pl.ds(row, 1), :] * whole
    return jnp.concatenate(sums, axis=0)


def cell_of_lane(size):
    lane = lax.broadcasted_iota(jnp.int32, (1, HEADS * size), 1)
    cell = lane
    for h in range(1, HEADS):
        cell = jnp.where(lane >= h * size, lane - h * size, cell)
    return cell


def spread_bias_weight(target, bias_w_ref, size):
    bias_rows = bias_w_ref[...].astype(FULL)
    for h in range(HEADS):
        target[h * size : (h + 1) * size, :] = jnp.broadcast_to(
            bias_rows[h : h + 1], (size, bias_rows.shape[1])
        ).astype(HALF)


def multiply_kernel(
    size,
    masks,
    far_ref,
    lengths_ref,
    gains_ref,
    edge_w_ref,
    gate_w_ref,
    out_w_ref,
    cot_ref,
    left_ref,
    right_ref,
    left_a_ref,
    left_b_ref,
    right_a_ref,
    right_b_ref,
    gate_ref,
    hat_mid_ref,
    scale_mid_ref,
    edge_out_ref,
    hat_y_ref,
    scale_y_ref,
    y_ref,
    x_half_ref,
    update_ref,
    pair_ref,
    right_t_ref,
):
    channels = gains_ref.shape[1]
    block = ROW_BLOCK * size
    blocks = size // ROW_BLOCK
    rows_of, columns_of = block_tools(size)
    gain_mid = gains_ref[1:2, :]
    gain_y = gains_ref[2:3, :]
    arrays = (left_ref, right_ref, left_a_ref, left_b_ref, right_a_ref, right_b_ref, gate_ref, x_half_ref, pair_ref, cot_ref)
    project_blocks(size, masks, 1, far_ref, lambda: lengths_ref[0:1, :], gains_ref, edge_w_ref, gate_w_ref, arrays)

    def turn(at, carry):
        right_t_ref[rows_of(at), :] = columns_of(right_ref, at)
        return carry

    lax.fori_loop(0, blocks, turn, 0, unroll=True)

    def multiply(at, carry):
        rows = rows_of(at)
        product = outer_sum(size, at, left_ref, 1, size, right_t_ref)
        hat, scale = kernel_norm(product)
        hat_mid_ref[rows, :] = hat
        scale_mid_ref[rows, :] = jnp.broadcast_to(scale, hat.shape)
        update = (hat * gain_mid).astype(HALF)
        update_ref[rows, :] = update
        edge_out = dot_nn(update, out_w_ref[...])
        edge_out_ref[rows, :] = edge_out
        middle = pair_ref[rows, :] + gate_ref[rows, :] * edge_out
        hat, scale = kernel_norm(middle)
        hat_y_ref[rows, :] = hat
        scale_y_ref[rows, :] = jnp.broadcast_to(scale, hat.shape)
        y_ref[rows, :] = hat * gain_y
        return carry

    lax.fori_loop(0, blocks, multiply, 0, unroll=True)


def project_kernel(
    size,
    y_ref,
    att_w_ref,
    bias_rep_ref,
    att_gate_ref,
    bias_ref,
    y_t_ref,
    query_ref,
    key_ref,
    value_ref,
):
    channels = y_ref.shape[1]
    lanes = HEADS * size
    head_scale = 1.0 / math.sqrt(HEAD_DIM)
    rows_of, columns_of = block_tools(size, WIDE_BLOCK)
    cell = cell_of_lane(size)

    def prepare(at, carry):
        rows = rows_of(at)
        y = columns_of(y_ref, at).astype(HALF)
        y_t_ref[rows, :] = y
        packed = dot_nn(y, att_w_ref[...])
        query_ref[rows, :] = (packed[:, :channels] * head_scale).astype(HALF)
        key_ref[rows, :] = packed[:, channels : 2 * channels].astype(HALF)
        value_ref[rows, :] = packed[:, 2 * channels : 3 * channels].astype(HALF)
        att_gate_ref[rows, :] = sigmoid(packed[:, 3 * channels :])
        spread = dot_nt(y, bias_rep_ref[...]).astype(HALF).astype(FULL)
        for a in range(WIDE_BLOCK):
            carry = carry + jnp.where(cell == at * WIDE_BLOCK + a, spread[a * size : (a + 1) * size], 0.0)
        return carry

    bias_ref[...] = lax.fori_loop(
        0, size // WIDE_BLOCK, prepare, jnp.zeros((size, lanes), FULL), unroll=True
    )


def attend_kernel(
    size,
    lengths_ref,
    att_w_ref,
    att_out_w_ref,
    att_gate_ref,
    bias_ref,
    y_t_ref,
    query_ref,
    key_ref,
    value_ref,
    bias_rep_ref,
    cot_ref,
    grad_y_ref,
    cot_t_ref,
    gated_ref,
    grad_packed_ref,
):
    channels = cot_ref.shape[1]
    block = WIDE_BLOCK * size
    blocks = size // WIDE_BLOCK
    lanes = HEADS * size
    head_scale = 1.0 / math.sqrt(HEAD_DIM)
    rows_of, columns_of = block_tools(size, WIDE_BLOCK)
    cell = cell_of_lane(size)
    key_row = lax.broadcasted_iota(jnp.int32, (size, lanes), 0)
    valid = jnp.where(key_row < lengths_ref[0:1, 0:1], 1.0, 0.0)

    head_mask = head_blocks(size, HEAD_DIM, HALF)
    lane = lax.broadcasted_iota(jnp.int32, (size, channels), 1)
    no_rows = jnp.zeros((size, channels), HALF)

    def own_heads(whole):
        picked = whole[(HEADS - 1) * size :]
        for h in reversed(range(HEADS - 1)):
            picked = jnp.where(lane < (h + 1) * HEAD_DIM, whole[h * size : (h + 1) * size], picked)
        return picked

    def attend(at, score_sum):
        rows = rows_of(at)
        parts = [slice(a * size, (a + 1) * size) for a in range(WIDE_BLOCK)]
        query, key, value = (ref[rows, :] for ref in (query_ref, key_ref, value_ref))
        gate = att_gate_ref[rows, :]
        cot = columns_of(cot_ref, at).astype(HALF)
        cot_t_ref[rows, :] = cot
        grad_gated = dot_nt(cot, att_out_w_ref[...])
        grad_att = (grad_gated * gate).astype(HALF)
        queries = [jnp.concatenate([query[p]] * HEADS, axis=0) * head_mask for p in parts]
        grads = [jnp.concatenate([grad_att[p]] * HEADS, axis=0) * head_mask for p in parts]
        bias = bias_ref[...]

        def stacked(columns):
            return jnp.stack(columns, axis=0)

        scores = stacked([dot_nt(key[p], queries[a]) + bias for a, p in enumerate(parts)])
        grad_attention = stacked([dot_nt(value[p], grads[a]) for a, p in enumerate(parts)])
        exp_scores = valid[None] * jnp.exp2(scores * LOG2_E)
        total = jnp.sum(exp_scores, axis=1)
        scale = jnp.where(total > 2.0**100, 2.0**-60, 1.0)
        inverse_total = pltpu.reciprocal(total * scale, approx=True)
        attention = (exp_scores * scale[:, None, :]) * inverse_total[:, None, :]
        row_dots = jnp.sum(attention * grad_attention, axis=1)
        grad_scores = attention * (grad_attention - row_dots[:, None, :])
        score_sum = score_sum + jnp.sum(grad_scores, axis=0)
        attention_half = attention.astype(HALF)
        scores_half = grad_scores.astype(HALF)
        grad_key = jnp.concatenate([dot_nn(scores_half[a], queries[a]) for a in range(WIDE_BLOCK)], axis=0)
        grad_value = jnp.concatenate([dot_nn(attention_half[a], grads[a]) for a in range(WIDE_BLOCK)], axis=0)

        def query_sums(a, p):
            weights = jnp.concatenate([attention_half[a], scores_half[a]], axis=0)
            vectors = jnp.concatenate(
                [
                    jnp.concatenate([value[p], no_rows], axis=1),
                    jnp.concatenate([no_rows, key[p]], axis=1),
                ],
                axis=0,
            )
            whole = dot_tn(weights, vectors)
            return [own_heads(whole[:, :channels]), own_heads(whole[:, channels:])]

        per_query = [query_sums(a, p) for a, p in enumerate(parts)]
        attended = jnp.concatenate([pair[0] for pair in per_query], axis=0)
        grad_query = jnp.concatenate([pair[1] for pair in per_query], axis=0)
        gated = gate * attended
        gated_ref[rows, :] = gated.astype(HALF)
        grad_gate_pre = grad_gated * gated * (1.0 - gate)
        grad_packed = jnp.concatenate(
            [
                (grad_query * head_scale).astype(HALF),
                grad_key.astype(HALF),
                grad_value.astype(HALF),
                grad_gate_pre.astype(HALF),
            ],
            axis=1,
        )
        grad_packed_ref[rows, : 4 * channels] = grad_packed
        grad_y_ref[rows, :] = dot_nt(grad_packed, att_w_ref[...])
        return score_sum

    score_sum = lax.fori_loop(0, blocks, attend, jnp.zeros((size, lanes), FULL), unroll=True)
    bias_grad = score_sum.astype(HALF).astype(FULL)

    def spread_bias(at, carry):
        rows = rows_of(at)
        spread = jnp.concatenate(
            [jnp.where(cell == at * WIDE_BLOCK + a, bias_grad, 0.0) for a in range(WIDE_BLOCK)], axis=0
        ).astype(HALF)
        grad_packed_ref[rows, 4 * channels :] = spread
        grad_y_ref[rows, :] += dot_nn(spread, bias_rep_ref[...])
        return carry

    lax.fori_loop(0, blocks, spread_bias, 0, unroll=True)


def gain_sum(pairs):
    total = sum(jnp.sum(weight.astype(FULL) * grad, axis=1, keepdims=True) for weight, grad in pairs)
    channels = total.shape[0]
    return jnp.transpose(jnp.broadcast_to(total, (channels, channels)))[0:1, :]


def edges_kernel(
    size,
    devices,
    pair_ref,
    gains_ref,
    edge_w_ref,
    gate_w_ref,
    out_w_ref,
    left_ref,
    right_ref,
    left_a_ref,
    left_b_ref,
    right_a_ref,
    right_b_ref,
    gate_ref,
    hat_mid_ref,
    scale_mid_ref,
    edge_out_ref,
    hat_y_ref,
    scale_y_ref,
    x_half_ref,
    update_ref,
    cot_ref,
    grad_y_ref,
    attention_side,
    grad_pair_ref,
    grad_gains_ref,
    grad_bias_ref,
    stage_refs,
    send,
    grad_middle_ref,
    grad_product_ref,
    grad_proj_ref,
    x_sum_ref,
    y_sum_ref,
):
    channels = gains_ref.shape[1]
    blocks = size // ROW_BLOCK
    rows_of, columns_of = block_tools(size)
    gain_x = gains_ref[0:1, :]
    gain_mid = gains_ref[1:2, :]
    gain_y = gains_ref[2:3, :]

    inverse = 1.0 / size
    y_t_ref, cot_t_ref, gated_ref, grad_packed_ref, att_w_ref, bias_rep_ref = attention_side
    edge_sum_ref, gate_sum_ref, out_sum_ref, att_sum_ref, att_out_sum_ref = stage_refs
    for sum_ref in (x_sum_ref, y_sum_ref, out_sum_ref, att_out_sum_ref):
        sum_ref[...] = jnp.zeros(sum_ref.shape, FULL)

    def attention_sums(at):
        rows = rows_of(at)
        y_sum_ref[...] += dot_tn(y_t_ref[rows, :], grad_packed_ref[rows, :])
        att_out_sum_ref[...] += dot_tn(gated_ref[rows, :], cot_t_ref[rows, :])

    def attention_results():
        att_sum = y_sum_ref[:, : 4 * channels] * inverse
        bias_sum = jnp.transpose(y_sum_ref[:, 4 * channels :] * inverse)
        att_sum_ref[...] = att_sum
        att_out_sum_ref[...] *= inverse
        send(3, 4)
        for h in range(HEADS):
            grad_bias_ref[h : h + 1, :] = jnp.sum(
                bias_sum[h * size : (h + 1) * size], axis=0, keepdims=True
            )
        bias_part = jnp.sum(bias_rep_ref[...].astype(FULL) * bias_sum, axis=0, keepdims=True)
        grad_gains_ref[2:3, :] = (gain_sum(((att_w_ref[...], att_sum),)) + bias_part) / gain_y

    wide_rows_of, wide_columns_of = block_tools(size, WIDE_BLOCK)

    def middle_back(at, carry):
        rows = wide_rows_of(at)
        grad_y = wide_columns_of(grad_y_ref, at)
        grad_middle = cot_ref[rows, :] + kernel_norm_back(
            grad_y, hat_y_ref[rows, :], scale_y_ref[rows, :], gain_y
        )
        grad_middle_ref[rows, :] = grad_middle
        gate = gate_ref[rows, :]
        gated = grad_middle * gate
        grad_edge_out = gated.astype(HALF)
        grad_gate = (gated * edge_out_ref[rows, :] * (1.0 - gate)).astype(HALF)
        grad_proj_ref[rows, 4 * channels :] = grad_gate
        x_sum_ref[:, 4 * channels :] += dot_tn(x_half_ref[rows, :], grad_gate)
        out_sum_ref[...] += dot_tn(update_ref[rows, :], grad_edge_out)
        grad_update = dot_nt(grad_edge_out, out_w_ref[...])
        grad_product = kernel_norm_back(grad_update, hat_mid_ref[rows, :], scale_mid_ref[rows, :], gain_mid)
        grad_product_ref[rows, :] = grad_product.astype(HALF).astype(FULL)
        return carry

    lax.fori_loop(0, size // WIDE_BLOCK, middle_back, 0, unroll=True)

    def edges_back(at):
        rows = rows_of(at)
        x_half = x_half_ref[rows, :]
        for side, (first_ref, second_ref, strides, other_ref) in enumerate(
            (
                (left_a_ref, left_b_ref, (1, size), right_ref),
                (right_a_ref, right_b_ref, (size, 1), left_ref),
            )
        ):
            grad = outer_sum(size, at, grad_product_ref, *strides, other_ref)
            both = jnp.concatenate(
                [(grad * first_ref[rows, :]).astype(HALF), (grad * second_ref[rows, :]).astype(HALF)], axis=1
            )
            place = slice(2 * side * channels, 2 * (side + 1) * channels)
            grad_proj_ref[rows, place] = both
            x_sum_ref[:, place] += dot_tn(x_half, both)

    for at in range(blocks):
        for part in range(2 * at, min(2 * at + 2, blocks)):
            attention_sums(part)
        edges_back(at)
        if 2 * at < blocks <= 2 * at + 2:
            attention_results()

    edge_sum, gate_sum = x_sum_ref[:, : 4 * channels] * inverse, x_sum_ref[:, 4 * channels :] * inverse
    edge_sum_ref[...] = edge_sum
    gate_sum_ref[...] = gate_sum
    out_sum = out_sum_ref[...] * inverse
    out_sum_ref[...] = out_sum
    send(0, 1, 2)
    grad_gains_ref[0:1, :] = gain_sum(((edge_w_ref[...], edge_sum), (gate_w_ref[...], gate_sum))) / gain_x
    grad_gains_ref[1:2, :] = gain_sum(((out_w_ref[...], out_sum),)) / gain_mid

    own_cells = size * size // devices
    own = pl.ds(pl.multiple_of(lax.axis_index("dap") * own_cells, own_cells), own_cells)
    hat, scale = kernel_norm(pair_ref[...].reshape(own_cells, channels).astype(FULL))
    grad_x = dot_nt(grad_proj_ref[own, : 4 * channels], edge_w_ref[...])
    grad_x = grad_x + dot_nt(grad_proj_ref[own, 4 * channels :], gate_w_ref[...])
    grad_pair = grad_middle_ref[own, :] + kernel_norm_back(grad_x, hat, scale, gain_x)
    grad_pair_ref[...] = grad_pair.astype(grad_pair_ref.dtype)


def kernel_norm(values):
    center = values - lane_mean(values)
    scale = lax.rsqrt(lane_mean(center * center) + epsilon)
    return center * scale, scale


def kernel_norm_back(grad_out, hat, scale, gain):
    scaled = grad_out * gain
    return scale * (scaled - lane_mean(scaled) - hat * lane_mean(scaled * hat))


def bytes_of(arrays):
    return sum(math.prod(shape) * jnp.dtype(dtype).itemsize for shape, dtype in arrays)


def kernel_scratch(size, channels):
    cells, lanes = size * size, HEADS * size
    full, half = ((cells, channels), FULL), ((cells, channels), HALF)
    square, wide = ((channels, channels), FULL), ((channels, 4 * channels), FULL)
    return {
        "kept": [full] * 5,
        "y": [full],
        "update": [half],
        "multiply": [full],
        "projections": [full, ((size, lanes), FULL)] + [half] * 4,
        "shared": [full],
        "attend": [half] * 2 + [((cells, 4 * channels + lanes), HALF)],
        "stage": [wide, square, square, wide, square],
        "edges": [full] * 2
        + [((cells, 5 * channels), HALF), ((channels, 5 * channels), FULL), ((channels, 4 * channels + lanes), FULL)],
    }


def projected_arrays(size, channels):
    shape = (size * size, channels)
    return [(shape, FULL)] * 7 + [(shape, HALF)] + [(shape, FULL)] * 2


def whole_kernel(
    size,
    masks,
    near_ref,
    far_ref,
    lengths_ref,
    gains_ref,
    edge_w_ref,
    gate_w_ref,
    out_w_ref,
    att_w_ref,
    bias_rep_ref,
    att_out_w_ref,
    *refs,
):
    count = len(projected_arrays(size, 1))
    grad_pair_ref, grad_gains_ref, grad_edge_ref, grad_gate_w_ref, grad_out_w_ref = refs[count : count + 5]
    grad_att_w_ref, grad_bias_ref, grad_att_out_ref = refs[count + 5 : count + 8]
    arrays, scratch = refs[count + 8 : 2 * count + 8], refs[2 * count + 8 :]
    *kept, x_half_ref, pair_ref, cot_ref = arrays
    part, at = {}, 0
    for name, shapes in kernel_scratch(size, 1).items():
        part[name] = scratch[at : at + len(shapes)]
        at += len(shapes)
    sent = scratch[at]
    kept = (*kept, *part["kept"])
    halves = (x_half_ref, *part["update"])
    shared = (cot_ref, *part["shared"])
    weights = (edge_w_ref, gate_w_ref, out_w_ref)
    multiply_kernel(
        size,
        masks,
        far_ref,
        lengths_ref,
        gains_ref,
        *weights,
        cot_ref,
        *kept,
        *part["y"],
        *halves,
        pair_ref,
        *part["multiply"],
    )
    project_kernel(size, *part["y"], att_w_ref, bias_rep_ref, *part["projections"])
    attend_kernel(
        size,
        lengths_ref,
        att_w_ref,
        att_out_w_ref,
        *part["projections"],
        bias_rep_ref,
        *shared,
        *part["attend"],
    )
    targets = (grad_edge_ref, grad_gate_w_ref, grad_out_w_ref, grad_att_w_ref, grad_att_out_ref)
    copies = [
        pltpu.make_async_copy(source, target, sent.at[slot])
        for slot, (source, target) in enumerate(zip(part["stage"], targets))
    ]

    def send(*slots):
        for slot in slots:
            copies[slot].start()

    y_t_ref = part["projections"][2]
    cot_t_ref, gated_ref, grad_packed_ref = part["attend"]
    edges_kernel(
        size,
        2 * len(masks),
        near_ref.at[0, 0],
        gains_ref,
        *weights,
        *kept,
        *halves,
        *shared,
        (y_t_ref, cot_t_ref, gated_ref, grad_packed_ref, att_w_ref, bias_rep_ref),
        grad_pair_ref,
        grad_gains_ref,
        grad_bias_ref,
        part["stage"],
        send,
        *part["edges"],
    )
    for copy in copies:
        copy.wait()


def replicated_plan(
    axis_size,
    pair_map,
    cotangent,
    lengths,
    norm_gains,
    edge_weight,
    mult_gate_weight,
    mult_out_weight,
    attention_weight,
    bias_weight,
    attention_out_weight,
):
    _, size, channels = pair_map.shape
    cells = size * size
    bits = axis_size.bit_length() - 1
    far_step = 1 << (bits - 1)
    near_steps = range(2, far_step, 2)

    def swapped(held, mask):
        return lax.ppermute(held, "dap", [(d, d ^ mask) for d in range(axis_size)])

    own = jnp.stack([pair_map, cotangent])
    held = jnp.stack([own, swapped(own, far_step)])
    masks = [0, far_step]
    near = jnp.concatenate([held] + [swapped(held, step) for step in near_steps], axis=0)
    masks = masks + [mask ^ step for step in near_steps for mask in masks]
    far = swapped(near, 1)

    square, wide = ((channels, channels), FULL), ((channels, 4 * channels), FULL)
    outs = [((cells // axis_size, channels), HALF), ((3, channels), FULL), wide, square, square]
    outs += [wide, ((HEADS, channels), FULL), square]
    scratch = sum(kernel_scratch(size, channels).values(), [])
    vmem = pl.BlockSpec(memory_space=pltpu.VMEM)
    anywhere = pl.BlockSpec(memory_space=pl.ANY)
    arrays = projected_arrays(size, channels)
    reals, bias_rep, *halves = pl.pallas_call(
        functools.partial(near_kernel, size, masks),
        out_shape=[jax.ShapeDtypeStruct((8, channels), jnp.int32), jax.ShapeDtypeStruct((HEADS * size, channels), HALF)]
        + [jax.ShapeDtypeStruct(*array) for array in arrays],
        in_specs=[vmem, pl.BlockSpec(memory_space=pltpu.HBM)] + [vmem] * 4,
        out_specs=[vmem] * (2 + len(arrays)),
        scratch_shapes=[pltpu.SMEM((1,), jnp.int32), pltpu.SemaphoreType.DMA],
        compiler_params=pltpu.CompilerParams(vmem_limit_bytes=VMEM_SLACK),
        cost_estimate=pl.CostEstimate(flops=0, bytes_accessed=4 * 2**20, transcendentals=0),
    )(near, lengths, norm_gains, edge_weight, mult_gate_weight, bias_weight.T)
    results = pl.pallas_call(
        functools.partial(whole_kernel, size, masks),
        out_shape=[jax.ShapeDtypeStruct(*out) for out in outs + arrays],
        in_specs=[vmem] * (10 + len(arrays)),
        out_specs=[vmem] * 2 + [anywhere] * 4 + [vmem, anywhere] + [vmem] * len(arrays),
        scratch_shapes=[pltpu.VMEM(*part) for part in scratch] + [pltpu.SemaphoreType.DMA((5,))],
        input_output_aliases={10 + at: len(outs) + at for at in range(len(arrays))},
        compiler_params=pltpu.CompilerParams(vmem_limit_bytes=bytes_of(scratch) + VMEM_SLACK),
    )(
        near,
        far,
        reals,
        norm_gains,
        edge_weight,
        mult_gate_weight,
        mult_out_weight,
        attention_weight,
        bias_rep,
        attention_out_weight,
        *halves,
    )
    return (results[0].reshape(pair_map.shape), *results[1:6], results[6].T, results[7])


def per_device(axis_size, pair_map, *rest):
    _, size, channels = pair_map.shape
    scratch = sum(kernel_scratch(size, channels).values(), [])
    fits = size % WIDE_BLOCK == 0 and bytes_of(scratch + projected_arrays(size, channels)) <= VMEM_SHARE
    if fits and axis_size >= 8 and axis_size & (axis_size - 1) == 0:
        return replicated_plan(axis_size, pair_map, *rest)
    return distributed_plan(pair_map, *rest)


def solution(mesh):
    return jax.shard_map(
        functools.partial(per_device, mesh.shape["dap"]),
        mesh=mesh,
        in_specs=(
            P(("groups", "dap"), None, None),
            P(("groups", "dap"), None, None),
            P("groups"),
            P(),
            P(),
            P(),
            P(),
            P(),
            P(),
            P(),
        ),
        out_specs=(
            P(("groups", "dap"), None, None),
            P("groups", None),
            P("groups", None),
            P("groups", None),
            P("groups", None),
            P("groups", None),
            P("groups", None),
            P("groups", None),
        ),
        check_vma=False,
    )
```

```python
import functools
import math

import jax
import jax.numpy as jnp
from jax import lax
from jax.experimental import pallas as pl
from jax.experimental.pallas import tpu as pltpu
from jax.sharding import PartitionSpec as P

HEADS = 4
HEAD_DIM = 32


epsilon = 1e-05


def norm_forward(values, gain_row):
    center = values - jnp.mean(values, axis=-1, keepdims=True)
    inv_std = lax.rsqrt(jnp.mean(center * center, axis=-1, keepdims=True) + epsilon)
    normed = center * inv_std
    return (normed * gain_row, normed, inv_std)


def norm_backward(grad_out, normed, inv_std, gain_row):
    scaled = grad_out * gain_row
    first_mean = jnp.mean(scaled, axis=-1, keepdims=True)
    second_mean = jnp.mean(scaled * normed, axis=-1, keepdims=True)
    return inv_std * (scaled - first_mean - normed * second_mean)


def distributed_plan(
    pair_map,
    cotangent,
    lengths,
    norm_gains,
    edge_weight,
    mult_gate_weight,
    mult_out_weight,
    attention_weight,
    bias_weight,
    attention_out_weight,
):
    row_count, full_size, channels = pair_map.shape
    inner_width = HEADS * HEAD_DIM
    head_scale = 1.0 / math.sqrt(HEAD_DIM)
    first_row = lax.axis_index("dap") * row_count
    real_count = lengths[0]
    valid_all = (jnp.arange(full_size) < real_count).astype(jnp.float32)
    valid_rows = (first_row + jnp.arange(row_count) < real_count).astype(jnp.float32)
    mask_pair = (valid_rows[:, None] * valid_all[None, :])[:, :, None]
    pair_f32 = pair_map.astype(jnp.float32)
    normed_full, hat_in, scale_in = norm_forward(pair_f32, norm_gains[0])
    normed_x = normed_full.astype(jnp.bfloat16)
    projected = jnp.einsum("rnc,cf->rnf", normed_x, edge_weight, preferred_element_type=jnp.float32)
    left_gate = projected[..., :channels]
    left_value = projected[..., channels : 2 * channels]
    right_gate = projected[..., 2 * channels : 3 * channels]
    right_value = projected[..., 3 * channels :]
    left_sig = jax.nn.sigmoid(left_gate)
    right_sig = jax.nn.sigmoid(right_gate)
    left_edges = (mask_pair * left_sig * left_value).astype(jnp.bfloat16)
    right_edges = (mask_pair * right_sig * right_value).astype(jnp.bfloat16)
    product = jnp.einsum(
        "ikc,jkc->ijc",
        left_edges,
        lax.all_gather(right_edges, "dap", axis=0, tiled=True),
        preferred_element_type=jnp.float32,
    )
    update_full, hat_mid, scale_mid = norm_forward(product, norm_gains[1])
    update = update_full.astype(jnp.bfloat16)
    edge_out = jnp.einsum(
        "rnc,cf->rnf", update, mult_out_weight, preferred_element_type=jnp.float32
    )
    gate_sig = jax.nn.sigmoid(
        jnp.einsum("rnc,cf->rnf", normed_x, mult_gate_weight, preferred_element_type=jnp.float32)
    )
    middle = pair_f32 + gate_sig * edge_out
    normed_mid, hat_attn, scale_attn = norm_forward(middle, norm_gains[2])
    normed_y = normed_mid.astype(jnp.bfloat16)
    bias_local = jnp.einsum(
        "kic,ch->hki", normed_y, bias_weight, preferred_element_type=jnp.float32
    ).astype(jnp.bfloat16)
    bias_whole = lax.all_gather(bias_local, "dap", axis=1, tiled=True)
    bias_query = jnp.swapaxes(bias_whole, 1, 2).astype(jnp.float32)
    column_y, column_cot = (
        lax.all_to_all(normed_y, "dap", split_axis=1, concat_axis=0, tiled=True),
        lax.all_to_all(cotangent, "dap", split_axis=1, concat_axis=0, tiled=True),
    )
    packed = jnp.einsum(
        "ijc,cf->ijf", column_y, attention_weight, preferred_element_type=jnp.float32
    )
    packed = packed.reshape(full_size, row_count, 4, HEADS, HEAD_DIM)
    query_vectors = (packed[:, :, 0] * head_scale).astype(jnp.bfloat16)
    key_vectors = packed[:, :, 1].astype(jnp.bfloat16)
    value_vectors = packed[:, :, 2].astype(jnp.bfloat16)
    att_gate = jax.nn.sigmoid(packed[:, :, 3])
    scores = (
        jnp.einsum(
            "ijhd,kjhd->jhik", query_vectors, key_vectors, preferred_element_type=jnp.float32
        )
        + bias_query[None]
    )
    exp_scores = valid_all * jnp.exp(scores)
    attention = exp_scores / jnp.sum(exp_scores, axis=-1, keepdims=True)
    attention_half = attention.astype(jnp.bfloat16)
    attended = jnp.einsum(
        "jhik,kjhd->ijhd", attention_half, value_vectors, preferred_element_type=jnp.float32
    )
    gated = (att_gate * attended).astype(jnp.bfloat16).reshape(full_size, row_count, inner_width)
    part_attn_out = jnp.einsum("ijf,ijc->fc", gated, column_cot, preferred_element_type=jnp.float32)
    grad_gated = jnp.einsum(
        "ijc,fc->ijf", column_cot, attention_out_weight, preferred_element_type=jnp.float32
    )
    grad_gated = grad_gated.reshape(full_size, row_count, HEADS, HEAD_DIM)
    grad_att = (grad_gated * att_gate).astype(jnp.bfloat16)
    grad_gate_pre = grad_gated * attended * att_gate * (1.0 - att_gate)
    grad_attention = jnp.einsum(
        "ijhd,kjhd->jhik", grad_att, value_vectors, preferred_element_type=jnp.float32
    )
    row_dots = jnp.transpose(jnp.sum(grad_att.astype(jnp.float32) * attended, axis=-1), (1, 2, 0))
    grad_scores = attention * (grad_attention - row_dots[..., None])
    scores_half = grad_scores.astype(jnp.bfloat16)
    grad_query = jnp.einsum(
        "jhik,kjhd->ijhd", scores_half, key_vectors, preferred_element_type=jnp.float32
    )
    grad_key = jnp.einsum(
        "jhik,ijhd->kjhd", scores_half, query_vectors, preferred_element_type=jnp.float32
    )
    grad_value = jnp.einsum(
        "jhik,ijhd->kjhd", attention_half, grad_att, preferred_element_type=jnp.float32
    )
    grad_packed = jnp.stack([grad_query * head_scale, grad_key, grad_value, grad_gate_pre], axis=2)
    grad_packed = grad_packed.reshape(full_size, row_count, 4 * inner_width).astype(jnp.bfloat16)
    part_attention = jnp.einsum(
        "ijc,ijf->cf", column_y, grad_packed, preferred_element_type=jnp.float32
    )
    column_grad = jnp.einsum(
        "ijf,cf->ijc", grad_packed, attention_weight, preferred_element_type=jnp.float32
    ).astype(jnp.bfloat16)
    row_grad = lax.all_to_all(column_grad, "dap", split_axis=0, concat_axis=1, tiled=True)
    score_sums = jnp.sum(grad_scores, axis=0)
    taken = score_sums
    bias_half = lax.psum_scatter(
        jnp.transpose(taken, (2, 0, 1)), "dap", scatter_dimension=0, tiled=True
    ).astype(jnp.bfloat16)
    part_bias = jnp.einsum("kic,khi->ch", normed_y, bias_half, preferred_element_type=jnp.float32)
    grad_normed_y = row_grad.astype(jnp.float32) + jnp.einsum(
        "khi,ch->kic", bias_half, bias_weight, preferred_element_type=jnp.float32
    )
    part_gain_attn = jnp.sum(grad_normed_y * hat_attn, axis=(0, 1))
    grad_middle = cotangent.astype(jnp.float32) + norm_backward(
        grad_normed_y, hat_attn, scale_attn, norm_gains[2]
    )
    grad_edge_out = (grad_middle * gate_sig).astype(jnp.bfloat16)
    grad_gate = (grad_middle * edge_out * gate_sig * (1.0 - gate_sig)).astype(jnp.bfloat16)
    part_mult_out = jnp.einsum(
        "rnc,rnf->cf", update, grad_edge_out, preferred_element_type=jnp.float32
    )
    part_mult_gate = jnp.einsum(
        "rnc,rnf->cf", normed_x, grad_gate, preferred_element_type=jnp.float32
    )
    grad_update = jnp.einsum(
        "rnf,cf->rnc", grad_edge_out, mult_out_weight, preferred_element_type=jnp.float32
    )
    part_gain_mid = jnp.sum(grad_update * hat_mid, axis=(0, 1))
    grad_product = norm_backward(grad_update, hat_mid, scale_mid, norm_gains[1]).astype(
        jnp.bfloat16
    )
    taken = grad_product
    grad_left = jnp.einsum(
        "ijc,jkc->ikc",
        taken,
        lax.all_gather(right_edges, "dap", axis=0, tiled=True),
        preferred_element_type=jnp.float32,
    )
    grad_cols = lax.all_to_all(grad_product, "dap", split_axis=1, concat_axis=0, tiled=True)
    taken = grad_cols
    grad_right = jnp.einsum(
        "ijc,ikc->jkc",
        taken,
        lax.all_gather(left_edges, "dap", axis=0, tiled=True),
        preferred_element_type=jnp.float32,
    )
    grad_proj = jnp.concatenate(
        [
            grad_left * mask_pair * left_value * left_sig * (1.0 - left_sig),
            grad_left * mask_pair * left_sig,
            grad_right * mask_pair * right_value * right_sig * (1.0 - right_sig),
            grad_right * mask_pair * right_sig,
        ],
        axis=-1,
    ).astype(jnp.bfloat16)
    part_edge = jnp.einsum("rnc,rnf->cf", normed_x, grad_proj, preferred_element_type=jnp.float32)
    grad_normed_x = jnp.einsum(
        "rnf,cf->rnc", grad_proj, edge_weight, preferred_element_type=jnp.float32
    )
    grad_normed_x = grad_normed_x + jnp.einsum(
        "rnf,cf->rnc", grad_gate, mult_gate_weight, preferred_element_type=jnp.float32
    )
    part_gain_in = jnp.sum(grad_normed_x * hat_in, axis=(0, 1))
    grad_pair = (
        grad_middle + norm_backward(grad_normed_x, hat_in, scale_in, norm_gains[0])
    ).astype(jnp.bfloat16)
    totals = lax.psum(
        (
            part_gain_in,
            part_gain_mid,
            part_edge,
            part_mult_gate,
            part_mult_out,
            part_gain_attn,
            part_attention,
            part_bias,
            part_attn_out,
        ),
        "dap",
    )
    (
        gain_in_sum,
        gain_mid_sum,
        edge_sum,
        mult_gate_sum,
        mult_out_sum,
        gain_attn_sum,
        attention_sum,
        bias_sum,
        attn_out_sum,
    ) = totals
    inverse = 1.0 / full_size
    grad_gains = jnp.stack([gain_in_sum, gain_mid_sum, gain_attn_sum]) * inverse
    return (
        grad_pair,
        grad_gains,
        edge_sum * inverse,
        mult_gate_sum * inverse,
        mult_out_sum * inverse,
        attention_sum * inverse,
        bias_sum * inverse,
        attn_out_sum * inverse,
    )


ROW_BLOCK = 8
WIDE_BLOCK = 16
VMEM_SLACK = 8 * 2**20
VMEM_SHARE = 32 * 2**20
LOG2_E = 1.0 / math.log(2.0)
HALF = jnp.bfloat16
FULL = jnp.float32


def dot_nn(left, right):
    return lax.dot_general(left, right, (((1,), (0,)), ((), ())), preferred_element_type=FULL)


def dot_nt(left, right):
    return lax.dot_general(left, right, (((1,), (1,)), ((), ())), preferred_element_type=FULL)


def dot_tn(left, right):
    return lax.dot_general(left, right, (((0,), (0,)), ((), ())), preferred_element_type=FULL)


def lane_mean(values):
    return jnp.mean(values, axis=-1, keepdims=True)


def sigmoid(values):
    return pltpu.reciprocal(1.0 + jnp.exp2(values * -LOG2_E), approx=True)


def head_blocks(row_width, col_width, dtype):
    shape = (HEADS * row_width, HEADS * col_width)
    row = lax.broadcasted_iota(jnp.int32, shape, 0)
    col = lax.broadcasted_iota(jnp.int32, shape, 1)
    same = None
    for h in range(HEADS):
        here = (row >= h * row_width) & (row < (h + 1) * row_width)
        here = here & (col >= h * col_width) & (col < (h + 1) * col_width)
        same = here if same is None else same | here
    return jnp.where(same, 1.0, 0.0).astype(dtype)


def place_rows(target, part, near_ref, far_ref, masks):
    me = lax.axis_index("dap")
    cells = target.shape[0] // (2 * len(masks))
    for other, blocks in enumerate((near_ref, far_ref)):
        for at, mask in enumerate(masks):
            place = pl.ds(pl.multiple_of((me ^ mask ^ other) * cells, cells), cells)
            target[place, :] = blocks[at, part].reshape(cells, target.shape[1]).astype(FULL)


def block_tools(size, count=ROW_BLOCK):
    block = count * size

    def rows_of(at):
        return pl.ds(pl.multiple_of(at * block, block), block)

    def columns_of(ref, at):
        return jnp.concatenate(
            [ref[pl.ds(at * count + a, size, stride=size), :] for a in range(count)], axis=0
        )

    return rows_of, columns_of


def outer_sum(size, at, row_ref, row_stride, block_stride, block_ref):
    sums = [jnp.zeros((size, block_ref.shape[1]), FULL)] * ROW_BLOCK
    for k in range(size):
        whole = block_ref[k * size : (k + 1) * size, :]
        for a in range(ROW_BLOCK):
            row = (at * ROW_BLOCK + a) * block_stride + k * row_stride
            sums[a] = sums[a] + row_ref[pl.ds(row, 1), :] * whole
    return jnp.concatenate(sums, axis=0)


def cell_of_lane(size):
    lane = lax.broadcasted_iota(jnp.int32, (1, HEADS * size), 1)
    cell = lane
    for h in range(1, HEADS):
        cell = jnp.where(lane >= h * size, lane - h * size, cell)
    return cell


def spread_bias_weight(target, bias_w_ref, size):
    bias_rows = bias_w_ref[...].astype(FULL)
    for h in range(HEADS):
        target[h * size : (h + 1) * size, :] = jnp.broadcast_to(
            bias_rows[h : h + 1], (size, bias_rows.shape[1])
        ).astype(HALF)


def multiply_kernel(
    size,
    masks,
    near_ref,
    far_ref,
    lengths_ref,
    gains_ref,
    edge_w_ref,
    gate_w_ref,
    out_w_ref,
    left_ref,
    right_ref,
    left_a_ref,
    left_b_ref,
    right_a_ref,
    right_b_ref,
    gate_ref,
    hat_mid_ref,
    scale_mid_ref,
    edge_out_ref,
    hat_y_ref,
    scale_y_ref,
    y_ref,
    x_half_ref,
    update_ref,
    pair_ref,
    right_t_ref,
):
    channels = gains_ref.shape[1]
    block = ROW_BLOCK * size
    blocks = size // ROW_BLOCK
    rows_of, columns_of = block_tools(size)
    real = lengths_ref[0]
    gain_x = gains_ref[0:1, :]
    gain_mid = gains_ref[1:2, :]
    gain_y = gains_ref[2:3, :]
    place_rows(pair_ref, 0, near_ref, far_ref, masks)

    wide_rows_of, _ = block_tools(size, WIDE_BLOCK)

    col_mask = jnp.where(lax.broadcasted_iota(jnp.int32, (size, channels), 0) < real, 1.0, 0.0)

    def project(at, carry):
        rows = wide_rows_of(at)
        hat, _ = kernel_norm(pair_ref[rows, :])
        normed = (hat * gain_x).astype(HALF)
        x_half_ref[rows, :] = normed
        projected = dot_nn(normed, edge_w_ref[...])
        gate_ref[rows, :] = sigmoid(dot_nn(normed, gate_w_ref[...]))
        mask = jnp.concatenate(
            [col_mask * jnp.where(at * WIDE_BLOCK + a < real, 1.0, 0.0) for a in range(WIDE_BLOCK)], axis=0
        )
        for side, (edge, first, second) in enumerate(
            ((left_ref, left_a_ref, left_b_ref), (right_ref, right_a_ref, right_b_ref))
        ):
            base = 2 * side * channels
            sig = sigmoid(projected[:, base : base + channels])
            value = projected[:, base + channels : base + 2 * channels]
            masked = mask * sig
            product = masked * value
            edge[rows, :] = product.astype(HALF).astype(FULL)
            first[rows, :] = product * (1.0 - sig)
            second[rows, :] = masked
        return carry

    lax.fori_loop(0, size // WIDE_BLOCK, project, 0, unroll=True)

    def turn(at, carry):
        right_t_ref[rows_of(at), :] = columns_of(right_ref, at)
        return carry

    lax.fori_loop(0, blocks, turn, 0, unroll=True)

    def multiply(at, carry):
        rows = rows_of(at)
        product = outer_sum(size, at, left_ref, 1, size, right_t_ref)
        hat, scale = kernel_norm(product)
        hat_mid_ref[rows, :] = hat
        scale_mid_ref[rows, :] = jnp.broadcast_to(scale, hat.shape)
        update = (hat * gain_mid).astype(HALF)
        update_ref[rows, :] = update
        edge_out = dot_nn(update, out_w_ref[...])
        edge_out_ref[rows, :] = edge_out
        middle = pair_ref[rows, :] + gate_ref[rows, :] * edge_out
        hat, scale = kernel_norm(middle)
        hat_y_ref[rows, :] = hat
        scale_y_ref[rows, :] = jnp.broadcast_to(scale, hat.shape)
        y_ref[rows, :] = hat * gain_y
        return carry

    lax.fori_loop(0, blocks, multiply, 0, unroll=True)


def project_kernel(
    size,
    y_ref,
    att_w_ref,
    bias_w_ref,
    att_gate_ref,
    bias_ref,
    y_t_ref,
    query_ref,
    key_ref,
    value_ref,
    bias_rep_ref,
):
    channels = y_ref.shape[1]
    lanes = HEADS * size
    head_scale = 1.0 / math.sqrt(HEAD_DIM)
    rows_of, columns_of = block_tools(size, WIDE_BLOCK)
    cell = cell_of_lane(size)
    spread_bias_weight(bias_rep_ref, bias_w_ref, size)

    def prepare(at, carry):
        rows = rows_of(at)
        y = columns_of(y_ref, at).astype(HALF)
        y_t_ref[rows, :] = y
        packed = dot_nn(y, att_w_ref[...])
        query_ref[rows, :] = (packed[:, :channels] * head_scale).astype(HALF)
        key_ref[rows, :] = packed[:, channels : 2 * channels].astype(HALF)
        value_ref[rows, :] = packed[:, 2 * channels : 3 * channels].astype(HALF)
        att_gate_ref[rows, :] = sigmoid(packed[:, 3 * channels :])
        spread = dot_nt(y, bias_rep_ref[...]).astype(HALF).astype(FULL)
        for a in range(WIDE_BLOCK):
            carry = carry + jnp.where(cell == at * WIDE_BLOCK + a, spread[a * size : (a + 1) * size], 0.0)
        return carry

    bias_ref[...] = lax.fori_loop(
        0, size // WIDE_BLOCK, prepare, jnp.zeros((size, lanes), FULL), unroll=True
    )


def attend_kernel(
    size,
    masks,
    near_ref,
    far_ref,
    lengths_ref,
    att_w_ref,
    att_out_w_ref,
    att_gate_ref,
    bias_ref,
    y_t_ref,
    query_ref,
    key_ref,
    value_ref,
    bias_rep_ref,
    cot_ref,
    grad_y_ref,
    cot_t_ref,
    gated_ref,
    grad_packed_ref,
):
    channels = cot_ref.shape[1]
    block = WIDE_BLOCK * size
    blocks = size // WIDE_BLOCK
    lanes = HEADS * size
    head_scale = 1.0 / math.sqrt(HEAD_DIM)
    rows_of, columns_of = block_tools(size, WIDE_BLOCK)
    cell = cell_of_lane(size)
    key_row = lax.broadcasted_iota(jnp.int32, (size, lanes), 0)
    valid = jnp.where(key_row < lengths_ref[0], 1.0, 0.0)
    place_rows(cot_ref, 1, near_ref, far_ref, masks)

    head_mask = head_blocks(size, HEAD_DIM, HALF)
    lane = lax.broadcasted_iota(jnp.int32, (size, channels), 1)
    no_rows = jnp.zeros((size, channels), HALF)

    def own_heads(whole):
        picked = whole[(HEADS - 1) * size :]
        for h in reversed(range(HEADS - 1)):
            picked = jnp.where(lane < (h + 1) * HEAD_DIM, whole[h * size : (h + 1) * size], picked)
        return picked

    def attend(at, score_sum):
        rows = rows_of(at)
        parts = [slice(a * size, (a + 1) * size) for a in range(WIDE_BLOCK)]
        query, key, value = (ref[rows, :] for ref in (query_ref, key_ref, value_ref))
        gate = att_gate_ref[rows, :]
        cot = columns_of(cot_ref, at).astype(HALF)
        cot_t_ref[rows, :] = cot
        grad_gated = dot_nt(cot, att_out_w_ref[...])
        grad_att = (grad_gated * gate).astype(HALF)
        queries = [jnp.concatenate([query[p]] * HEADS, axis=0) * head_mask for p in parts]
        grads = [jnp.concatenate([grad_att[p]] * HEADS, axis=0) * head_mask for p in parts]
        bias = bias_ref[...]

        def stacked(columns):
            return jnp.stack(columns, axis=0)

        scores = stacked([dot_nt(key[p], queries[a]) + bias for a, p in enumerate(parts)])
        grad_attention = stacked([dot_nt(value[p], grads[a]) for a, p in enumerate(parts)])
        exp_scores = valid[None] * jnp.exp2(scores * LOG2_E)
        total = jnp.sum(exp_scores, axis=1)
        scale = jnp.where(total > 2.0**100, 2.0**-60, 1.0)
        inverse_total = pltpu.reciprocal(total * scale, approx=True)
        attention = (exp_scores * scale[:, None, :]) * inverse_total[:, None, :]
        row_dots = jnp.sum(attention * grad_attention, axis=1)
        grad_scores = attention * (grad_attention - row_dots[:, None, :])
        score_sum = score_sum + jnp.sum(grad_scores, axis=0)
        attention_half = attention.astype(HALF)
        scores_half = grad_scores.astype(HALF)
        grad_key = jnp.concatenate([dot_nn(scores_half[a], queries[a]) for a in range(WIDE_BLOCK)], axis=0)
        grad_value = jnp.concatenate([dot_nn(attention_half[a], grads[a]) for a in range(WIDE_BLOCK)], axis=0)

        def query_sums(a, p):
            weights = jnp.concatenate([attention_half[a], scores_half[a]], axis=0)
            vectors = jnp.concatenate(
                [
                    jnp.concatenate([value[p], no_rows], axis=1),
                    jnp.concatenate([no_rows, key[p]], axis=1),
                ],
                axis=0,
            )
            whole = dot_tn(weights, vectors)
            return [own_heads(whole[:, :channels]), own_heads(whole[:, channels:])]

        per_query = [query_sums(a, p) for a, p in enumerate(parts)]
        attended = jnp.concatenate([pair[0] for pair in per_query], axis=0)
        grad_query = jnp.concatenate([pair[1] for pair in per_query], axis=0)
        gated = gate * attended
        gated_ref[rows, :] = gated.astype(HALF)
        grad_gate_pre = grad_gated * gated * (1.0 - gate)
        grad_packed = jnp.concatenate(
            [
                (grad_query * head_scale).astype(HALF),
                grad_key.astype(HALF),
                grad_value.astype(HALF),
                grad_gate_pre.astype(HALF),
            ],
            axis=1,
        )
        grad_packed_ref[rows, : 4 * channels] = grad_packed
        grad_y_ref[rows, :] = dot_nt(grad_packed, att_w_ref[...])
        return score_sum

    score_sum = lax.fori_loop(0, blocks, attend, jnp.zeros((size, lanes), FULL), unroll=True)
    bias_grad = score_sum.astype(HALF).astype(FULL)

    def spread_bias(at, carry):
        rows = rows_of(at)
        spread = jnp.concatenate(
            [jnp.where(cell == at * WIDE_BLOCK + a, bias_grad, 0.0) for a in range(WIDE_BLOCK)], axis=0
        ).astype(HALF)
        grad_packed_ref[rows, 4 * channels :] = spread
        grad_y_ref[rows, :] += dot_nn(spread, bias_rep_ref[...])
        return carry

    lax.fori_loop(0, blocks, spread_bias, 0, unroll=True)


def gain_sum(pairs):
    total = sum(jnp.sum(weight.astype(FULL) * grad, axis=1, keepdims=True) for weight, grad in pairs)
    channels = total.shape[0]
    return jnp.transpose(jnp.broadcast_to(total, (channels, channels)))[0:1, :]


def edges_kernel(
    size,
    devices,
    pair_ref,
    gains_ref,
    edge_w_ref,
    gate_w_ref,
    out_w_ref,
    left_ref,
    right_ref,
    left_a_ref,
    left_b_ref,
    right_a_ref,
    right_b_ref,
    gate_ref,
    hat_mid_ref,
    scale_mid_ref,
    edge_out_ref,
    hat_y_ref,
    scale_y_ref,
    x_half_ref,
    update_ref,
    cot_ref,
    grad_y_ref,
    attention_side,
    grad_pair_ref,
    grad_gains_ref,
    grad_bias_ref,
    stage_refs,
    send,
    grad_middle_ref,
    grad_product_ref,
    grad_proj_ref,
    x_sum_ref,
    y_sum_ref,
):
    channels = gains_ref.shape[1]
    blocks = size // ROW_BLOCK
    rows_of, columns_of = block_tools(size)
    gain_x = gains_ref[0:1, :]
    gain_mid = gains_ref[1:2, :]
    gain_y = gains_ref[2:3, :]

    inverse = 1.0 / size
    y_t_ref, cot_t_ref, gated_ref, grad_packed_ref, att_w_ref, bias_rep_ref = attention_side
    edge_sum_ref, gate_sum_ref, out_sum_ref, att_sum_ref, att_out_sum_ref = stage_refs
    for sum_ref in (x_sum_ref, y_sum_ref, out_sum_ref, att_out_sum_ref):
        sum_ref[...] = jnp.zeros(sum_ref.shape, FULL)

    def attention_sums(at):
        rows = rows_of(at)
        y_sum_ref[...] += dot_tn(y_t_ref[rows, :], grad_packed_ref[rows, :])
        att_out_sum_ref[...] += dot_tn(gated_ref[rows, :], cot_t_ref[rows, :])

    def attention_results():
        att_sum = y_sum_ref[:, : 4 * channels] * inverse
        bias_sum = jnp.transpose(y_sum_ref[:, 4 * channels :] * inverse)
        att_sum_ref[...] = att_sum
        att_out_sum_ref[...] *= inverse
        send(3, 4)
        for h in range(HEADS):
            grad_bias_ref[h : h + 1, :] = jnp.sum(
                bias_sum[h * size : (h + 1) * size], axis=0, keepdims=True
            )
        bias_part = jnp.sum(bias_rep_ref[...].astype(FULL) * bias_sum, axis=0, keepdims=True)
        grad_gains_ref[2:3, :] = (gain_sum(((att_w_ref[...], att_sum),)) + bias_part) / gain_y

    wide_rows_of, wide_columns_of = block_tools(size, WIDE_BLOCK)

    def middle_back(at, carry):
        rows = wide_rows_of(at)
        grad_y = wide_columns_of(grad_y_ref, at)
        grad_middle = cot_ref[rows, :] + kernel_norm_back(
            grad_y, hat_y_ref[rows, :], scale_y_ref[rows, :], gain_y
        )
        grad_middle_ref[rows, :] = grad_middle
        gate = gate_ref[rows, :]
        gated = grad_middle * gate
        grad_edge_out = gated.astype(HALF)
        grad_gate = (gated * edge_out_ref[rows, :] * (1.0 - gate)).astype(HALF)
        grad_proj_ref[rows, 4 * channels :] = grad_gate
        x_sum_ref[:, 4 * channels :] += dot_tn(x_half_ref[rows, :], grad_gate)
        out_sum_ref[...] += dot_tn(update_ref[rows, :], grad_edge_out)
        grad_update = dot_nt(grad_edge_out, out_w_ref[...])
        grad_product = kernel_norm_back(grad_update, hat_mid_ref[rows, :], scale_mid_ref[rows, :], gain_mid)
        grad_product_ref[rows, :] = grad_product.astype(HALF).astype(FULL)
        return carry

    lax.fori_loop(0, size // WIDE_BLOCK, middle_back, 0, unroll=True)

    def edges_back(at):
        rows = rows_of(at)
        x_half = x_half_ref[rows, :]
        for side, (first_ref, second_ref, strides, other_ref) in enumerate(
            (
                (left_a_ref, left_b_ref, (1, size), right_ref),
                (right_a_ref, right_b_ref, (size, 1), left_ref),
            )
        ):
            grad = outer_sum(size, at, grad_product_ref, *strides, other_ref)
            both = jnp.concatenate(
                [(grad * first_ref[rows, :]).astype(HALF), (grad * second_ref[rows, :]).astype(HALF)], axis=1
            )
            place = slice(2 * side * channels, 2 * (side + 1) * channels)
            grad_proj_ref[rows, place] = both
            x_sum_ref[:, place] += dot_tn(x_half, both)

    for at in range(blocks):
        for part in range(2 * at, min(2 * at + 2, blocks)):
            attention_sums(part)
        edges_back(at)
        if 2 * at < blocks <= 2 * at + 2:
            attention_results()

    edge_sum, gate_sum = x_sum_ref[:, : 4 * channels] * inverse, x_sum_ref[:, 4 * channels :] * inverse
    edge_sum_ref[...] = edge_sum
    gate_sum_ref[...] = gate_sum
    out_sum = out_sum_ref[...] * inverse
    out_sum_ref[...] = out_sum
    send(0, 1, 2)
    grad_gains_ref[0:1, :] = gain_sum(((edge_w_ref[...], edge_sum), (gate_w_ref[...], gate_sum))) / gain_x
    grad_gains_ref[1:2, :] = gain_sum(((out_w_ref[...], out_sum),)) / gain_mid

    own_cells = size * size // devices
    own = pl.ds(pl.multiple_of(lax.axis_index("dap") * own_cells, own_cells), own_cells)
    hat, scale = kernel_norm(pair_ref[...].reshape(own_cells, channels).astype(FULL))
    grad_x = dot_nt(grad_proj_ref[own, : 4 * channels], edge_w_ref[...])
    grad_x = grad_x + dot_nt(grad_proj_ref[own, 4 * channels :], gate_w_ref[...])
    grad_pair = grad_middle_ref[own, :] + kernel_norm_back(grad_x, hat, scale, gain_x)
    grad_pair_ref[...] = grad_pair.astype(grad_pair_ref.dtype)


def kernel_norm(values):
    center = values - lane_mean(values)
    scale = lax.rsqrt(lane_mean(center * center) + epsilon)
    return center * scale, scale


def kernel_norm_back(grad_out, hat, scale, gain):
    scaled = grad_out * gain
    return scale * (scaled - lane_mean(scaled) - hat * lane_mean(scaled * hat))


def bytes_of(arrays):
    return sum(math.prod(shape) * jnp.dtype(dtype).itemsize for shape, dtype in arrays)


def kernel_scratch(size, channels):
    cells, lanes = size * size, HEADS * size
    full, half = ((cells, channels), FULL), ((cells, channels), HALF)
    square, wide = ((channels, channels), FULL), ((channels, 4 * channels), FULL)
    return {
        "kept": [full] * 12,
        "y": [full],
        "halves": [half] * 2,
        "multiply": [full] * 2,
        "projections": [full, ((size, lanes), FULL)] + [half] * 4 + [((lanes, channels), HALF)],
        "shared": [full] * 2,
        "attend": [half] * 2 + [((cells, 4 * channels + lanes), HALF)],
        "stage": [wide, square, square, wide, square],
        "edges": [full] * 2
        + [((cells, 5 * channels), HALF), ((channels, 5 * channels), FULL), ((channels, 4 * channels + lanes), FULL)],
    }


def whole_kernel(
    size,
    masks,
    near_ref,
    far_ref,
    lengths_ref,
    gains_ref,
    edge_w_ref,
    gate_w_ref,
    out_w_ref,
    att_w_ref,
    bias_w_ref,
    att_out_w_ref,
    grad_pair_ref,
    grad_gains_ref,
    grad_edge_ref,
    grad_gate_w_ref,
    grad_out_w_ref,
    grad_att_w_ref,
    grad_bias_ref,
    grad_att_out_ref,
    *scratch,
):
    part, at = {}, 0
    for name, arrays in kernel_scratch(size, 1).items():
        part[name] = scratch[at : at + len(arrays)]
        at += len(arrays)
    sent = scratch[at]
    weights = (edge_w_ref, gate_w_ref, out_w_ref)
    multiply_kernel(
        size, masks, near_ref, far_ref, lengths_ref, gains_ref, *weights, *part["kept"], *part["y"], *part["halves"], *part["multiply"]
    )
    project_kernel(size, *part["y"], att_w_ref, bias_w_ref, *part["projections"])
    attend_kernel(
        size,
        masks,
        near_ref,
        far_ref,
        lengths_ref,
        att_w_ref,
        att_out_w_ref,
        *part["projections"],
        *part["shared"],
        *part["attend"],
    )
    targets = (grad_edge_ref, grad_gate_w_ref, grad_out_w_ref, grad_att_w_ref, grad_att_out_ref)
    copies = [
        pltpu.make_async_copy(source, target, sent.at[slot])
        for slot, (source, target) in enumerate(zip(part["stage"], targets))
    ]

    def send(*slots):
        for slot in slots:
            copies[slot].start()

    _, _, y_t_ref, _, _, _, bias_rep_ref = part["projections"]
    cot_t_ref, gated_ref, grad_packed_ref = part["attend"]
    edges_kernel(
        size,
        2 * len(masks),
        near_ref.at[0, 0],
        gains_ref,
        *weights,
        *part["kept"],
        *part["halves"],
        *part["shared"],
        (y_t_ref, cot_t_ref, gated_ref, grad_packed_ref, att_w_ref, bias_rep_ref),
        grad_pair_ref,
        grad_gains_ref,
        grad_bias_ref,
        part["stage"],
        send,
        *part["edges"],
    )
    for copy in copies:
        copy.wait()


def replicated_plan(
    axis_size,
    pair_map,
    cotangent,
    lengths,
    norm_gains,
    edge_weight,
    mult_gate_weight,
    mult_out_weight,
    attention_weight,
    bias_weight,
    attention_out_weight,
):
    _, size, channels = pair_map.shape
    cells = size * size
    bits = axis_size.bit_length() - 1
    far_step = 1 << (bits - 1)
    near_steps = range(far_step - 2, 0, -2)

    def swapped(held, mask):
        return lax.ppermute(held, "dap", [(d, d ^ mask) for d in range(axis_size)])

    own = jnp.stack([pair_map, cotangent])
    held = jnp.stack([own, swapped(own, far_step)])
    masks = [0, far_step]
    near = jnp.concatenate([held] + [swapped(held, step) for step in near_steps], axis=0)
    masks = masks + [mask ^ step for step in near_steps for mask in masks]
    far = swapped(near, 1)

    square, wide = ((channels, channels), FULL), ((channels, 4 * channels), FULL)
    outs = [((cells // axis_size, channels), HALF), ((3, channels), FULL), wide, square, square]
    outs += [wide, ((HEADS, channels), FULL), square]
    scratch = sum(kernel_scratch(size, channels).values(), [])
    vmem = pl.BlockSpec(memory_space=pltpu.VMEM)
    smem = pl.BlockSpec(memory_space=pltpu.SMEM)
    anywhere = pl.BlockSpec(memory_space=pl.ANY)
    results = pl.pallas_call(
        functools.partial(whole_kernel, size, masks),
        out_shape=[jax.ShapeDtypeStruct(*out) for out in outs],
        in_specs=[vmem, vmem, smem] + [vmem] * 7,
        out_specs=[vmem] * 2 + [anywhere] * 4 + [vmem, anywhere],
        scratch_shapes=[pltpu.VMEM(*part) for part in scratch] + [pltpu.SemaphoreType.DMA((5,))],
        compiler_params=pltpu.CompilerParams(vmem_limit_bytes=bytes_of(scratch) + VMEM_SLACK),
    )(
        near,
        far,
        lengths,
        norm_gains,
        edge_weight,
        mult_gate_weight,
        mult_out_weight,
        attention_weight,
        bias_weight.T,
        attention_out_weight,
    )
    return (results[0].reshape(pair_map.shape), *results[1:6], results[6].T, results[7])


def per_device(axis_size, pair_map, *rest):
    _, size, channels = pair_map.shape
    scratch = sum(kernel_scratch(size, channels).values(), [])
    fits = size % WIDE_BLOCK == 0 and bytes_of(scratch) <= VMEM_SHARE
    if fits and axis_size >= 8 and axis_size & (axis_size - 1) == 0:
        return replicated_plan(axis_size, pair_map, *rest)
    return distributed_plan(pair_map, *rest)


def solution(mesh):
    return jax.shard_map(
        functools.partial(per_device, mesh.shape["dap"]),
        mesh=mesh,
        in_specs=(
            P(("groups", "dap"), None, None),
            P(("groups", "dap"), None, None),
            P("groups"),
            P(),
            P(),
            P(),
            P(),
            P(),
            P(),
            P(),
        ),
        out_specs=(
            P(("groups", "dap"), None, None),
            P("groups", None),
            P("groups", None),
            P("groups", None),
            P("groups", None),
            P("groups", None),
            P("groups", None),
            P("groups", None),
        ),
        check_vma=False,
    )
```

```python
import functools
import math

import jax
import jax.numpy as jnp
from jax import lax
from jax.experimental import pallas as pl
from jax.experimental.pallas import tpu as pltpu
from jax.sharding import PartitionSpec as P

HEADS = 4
HEAD_DIM = 32


epsilon = 1e-05


def norm_forward(values, gain_row):
    center = values - jnp.mean(values, axis=-1, keepdims=True)
    inv_std = lax.rsqrt(jnp.mean(center * center, axis=-1, keepdims=True) + epsilon)
    normed = center * inv_std
    return (normed * gain_row, normed, inv_std)


def norm_backward(grad_out, normed, inv_std, gain_row):
    scaled = grad_out * gain_row
    first_mean = jnp.mean(scaled, axis=-1, keepdims=True)
    second_mean = jnp.mean(scaled * normed, axis=-1, keepdims=True)
    return inv_std * (scaled - first_mean - normed * second_mean)


def distributed_plan(
    pair_map,
    cotangent,
    lengths,
    norm_gains,
    edge_weight,
    mult_gate_weight,
    mult_out_weight,
    attention_weight,
    bias_weight,
    attention_out_weight,
):
    row_count, full_size, channels = pair_map.shape
    inner_width = HEADS * HEAD_DIM
    head_scale = 1.0 / math.sqrt(HEAD_DIM)
    first_row = lax.axis_index("dap") * row_count
    real_count = lengths[0]
    valid_all = (jnp.arange(full_size) < real_count).astype(jnp.float32)
    valid_rows = (first_row + jnp.arange(row_count) < real_count).astype(jnp.float32)
    mask_pair = (valid_rows[:, None] * valid_all[None, :])[:, :, None]
    pair_f32 = pair_map.astype(jnp.float32)
    normed_full, hat_in, scale_in = norm_forward(pair_f32, norm_gains[0])
    normed_x = normed_full.astype(jnp.bfloat16)
    projected = jnp.einsum("rnc,cf->rnf", normed_x, edge_weight, preferred_element_type=jnp.float32)
    left_gate = projected[..., :channels]
    left_value = projected[..., channels : 2 * channels]
    right_gate = projected[..., 2 * channels : 3 * channels]
    right_value = projected[..., 3 * channels :]
    left_sig = jax.nn.sigmoid(left_gate)
    right_sig = jax.nn.sigmoid(right_gate)
    left_edges = (mask_pair * left_sig * left_value).astype(jnp.bfloat16)
    right_edges = (mask_pair * right_sig * right_value).astype(jnp.bfloat16)
    product = jnp.einsum(
        "ikc,jkc->ijc",
        left_edges,
        lax.all_gather(right_edges, "dap", axis=0, tiled=True),
        preferred_element_type=jnp.float32,
    )
    update_full, hat_mid, scale_mid = norm_forward(product, norm_gains[1])
    update = update_full.astype(jnp.bfloat16)
    edge_out = jnp.einsum(
        "rnc,cf->rnf", update, mult_out_weight, preferred_element_type=jnp.float32
    )
    gate_sig = jax.nn.sigmoid(
        jnp.einsum("rnc,cf->rnf", normed_x, mult_gate_weight, preferred_element_type=jnp.float32)
    )
    middle = pair_f32 + gate_sig * edge_out
    normed_mid, hat_attn, scale_attn = norm_forward(middle, norm_gains[2])
    normed_y = normed_mid.astype(jnp.bfloat16)
    bias_local = jnp.einsum(
        "kic,ch->hki", normed_y, bias_weight, preferred_element_type=jnp.float32
    ).astype(jnp.bfloat16)
    bias_whole = lax.all_gather(bias_local, "dap", axis=1, tiled=True)
    bias_query = jnp.swapaxes(bias_whole, 1, 2).astype(jnp.float32)
    column_y, column_cot = (
        lax.all_to_all(normed_y, "dap", split_axis=1, concat_axis=0, tiled=True),
        lax.all_to_all(cotangent, "dap", split_axis=1, concat_axis=0, tiled=True),
    )
    packed = jnp.einsum(
        "ijc,cf->ijf", column_y, attention_weight, preferred_element_type=jnp.float32
    )
    packed = packed.reshape(full_size, row_count, 4, HEADS, HEAD_DIM)
    query_vectors = (packed[:, :, 0] * head_scale).astype(jnp.bfloat16)
    key_vectors = packed[:, :, 1].astype(jnp.bfloat16)
    value_vectors = packed[:, :, 2].astype(jnp.bfloat16)
    att_gate = jax.nn.sigmoid(packed[:, :, 3])
    scores = (
        jnp.einsum(
            "ijhd,kjhd->jhik", query_vectors, key_vectors, preferred_element_type=jnp.float32
        )
        + bias_query[None]
    )
    exp_scores = valid_all * jnp.exp(scores)
    attention = exp_scores / jnp.sum(exp_scores, axis=-1, keepdims=True)
    attention_half = attention.astype(jnp.bfloat16)
    attended = jnp.einsum(
        "jhik,kjhd->ijhd", attention_half, value_vectors, preferred_element_type=jnp.float32
    )
    gated = (att_gate * attended).astype(jnp.bfloat16).reshape(full_size, row_count, inner_width)
    part_attn_out = jnp.einsum("ijf,ijc->fc", gated, column_cot, preferred_element_type=jnp.float32)
    grad_gated = jnp.einsum(
        "ijc,fc->ijf", column_cot, attention_out_weight, preferred_element_type=jnp.float32
    )
    grad_gated = grad_gated.reshape(full_size, row_count, HEADS, HEAD_DIM)
    grad_att = (grad_gated * att_gate).astype(jnp.bfloat16)
    grad_gate_pre = grad_gated * attended * att_gate * (1.0 - att_gate)
    grad_attention = jnp.einsum(
        "ijhd,kjhd->jhik", grad_att, value_vectors, preferred_element_type=jnp.float32
    )
    row_dots = jnp.transpose(jnp.sum(grad_att.astype(jnp.float32) * attended, axis=-1), (1, 2, 0))
    grad_scores = attention * (grad_attention - row_dots[..., None])
    scores_half = grad_scores.astype(jnp.bfloat16)
    grad_query = jnp.einsum(
        "jhik,kjhd->ijhd", scores_half, key_vectors, preferred_element_type=jnp.float32
    )
    grad_key = jnp.einsum(
        "jhik,ijhd->kjhd", scores_half, query_vectors, preferred_element_type=jnp.float32
    )
    grad_value = jnp.einsum(
        "jhik,ijhd->kjhd", attention_half, grad_att, preferred_element_type=jnp.float32
    )
    grad_packed = jnp.stack([grad_query * head_scale, grad_key, grad_value, grad_gate_pre], axis=2)
    grad_packed = grad_packed.reshape(full_size, row_count, 4 * inner_width).astype(jnp.bfloat16)
    part_attention = jnp.einsum(
        "ijc,ijf->cf", column_y, grad_packed, preferred_element_type=jnp.float32
    )
    column_grad = jnp.einsum(
        "ijf,cf->ijc", grad_packed, attention_weight, preferred_element_type=jnp.float32
    ).astype(jnp.bfloat16)
    row_grad = lax.all_to_all(column_grad, "dap", split_axis=0, concat_axis=1, tiled=True)
    score_sums = jnp.sum(grad_scores, axis=0)
    taken = score_sums
    bias_half = lax.psum_scatter(
        jnp.transpose(taken, (2, 0, 1)), "dap", scatter_dimension=0, tiled=True
    ).astype(jnp.bfloat16)
    part_bias = jnp.einsum("kic,khi->ch", normed_y, bias_half, preferred_element_type=jnp.float32)
    grad_normed_y = row_grad.astype(jnp.float32) + jnp.einsum(
        "khi,ch->kic", bias_half, bias_weight, preferred_element_type=jnp.float32
    )
    part_gain_attn = jnp.sum(grad_normed_y * hat_attn, axis=(0, 1))
    grad_middle = cotangent.astype(jnp.float32) + norm_backward(
        grad_normed_y, hat_attn, scale_attn, norm_gains[2]
    )
    grad_edge_out = (grad_middle * gate_sig).astype(jnp.bfloat16)
    grad_gate = (grad_middle * edge_out * gate_sig * (1.0 - gate_sig)).astype(jnp.bfloat16)
    part_mult_out = jnp.einsum(
        "rnc,rnf->cf", update, grad_edge_out, preferred_element_type=jnp.float32
    )
    part_mult_gate = jnp.einsum(
        "rnc,rnf->cf", normed_x, grad_gate, preferred_element_type=jnp.float32
    )
    grad_update = jnp.einsum(
        "rnf,cf->rnc", grad_edge_out, mult_out_weight, preferred_element_type=jnp.float32
    )
    part_gain_mid = jnp.sum(grad_update * hat_mid, axis=(0, 1))
    grad_product = norm_backward(grad_update, hat_mid, scale_mid, norm_gains[1]).astype(
        jnp.bfloat16
    )
    taken = grad_product
    grad_left = jnp.einsum(
        "ijc,jkc->ikc",
        taken,
        lax.all_gather(right_edges, "dap", axis=0, tiled=True),
        preferred_element_type=jnp.float32,
    )
    grad_cols = lax.all_to_all(grad_product, "dap", split_axis=1, concat_axis=0, tiled=True)
    taken = grad_cols
    grad_right = jnp.einsum(
        "ijc,ikc->jkc",
        taken,
        lax.all_gather(left_edges, "dap", axis=0, tiled=True),
        preferred_element_type=jnp.float32,
    )
    grad_proj = jnp.concatenate(
        [
            grad_left * mask_pair * left_value * left_sig * (1.0 - left_sig),
            grad_left * mask_pair * left_sig,
            grad_right * mask_pair * right_value * right_sig * (1.0 - right_sig),
            grad_right * mask_pair * right_sig,
        ],
        axis=-1,
    ).astype(jnp.bfloat16)
    part_edge = jnp.einsum("rnc,rnf->cf", normed_x, grad_proj, preferred_element_type=jnp.float32)
    grad_normed_x = jnp.einsum(
        "rnf,cf->rnc", grad_proj, edge_weight, preferred_element_type=jnp.float32
    )
    grad_normed_x = grad_normed_x + jnp.einsum(
        "rnf,cf->rnc", grad_gate, mult_gate_weight, preferred_element_type=jnp.float32
    )
    part_gain_in = jnp.sum(grad_normed_x * hat_in, axis=(0, 1))
    grad_pair = (
        grad_middle + norm_backward(grad_normed_x, hat_in, scale_in, norm_gains[0])
    ).astype(jnp.bfloat16)
    totals = lax.psum(
        (
            part_gain_in,
            part_gain_mid,
            part_edge,
            part_mult_gate,
            part_mult_out,
            part_gain_attn,
            part_attention,
            part_bias,
            part_attn_out,
        ),
        "dap",
    )
    (
        gain_in_sum,
        gain_mid_sum,
        edge_sum,
        mult_gate_sum,
        mult_out_sum,
        gain_attn_sum,
        attention_sum,
        bias_sum,
        attn_out_sum,
    ) = totals
    inverse = 1.0 / full_size
    grad_gains = jnp.stack([gain_in_sum, gain_mid_sum, gain_attn_sum]) * inverse
    return (
        grad_pair,
        grad_gains,
        edge_sum * inverse,
        mult_gate_sum * inverse,
        mult_out_sum * inverse,
        attention_sum * inverse,
        bias_sum * inverse,
        attn_out_sum * inverse,
    )


ROW_BLOCK = 8
WIDE_BLOCK = 16
VMEM_SLACK = 8 * 2**20
VMEM_SHARE = 32 * 2**20
LOG2_E = 1.0 / math.log(2.0)
HALF = jnp.bfloat16
FULL = jnp.float32


def dot_nn(left, right):
    return lax.dot_general(left, right, (((1,), (0,)), ((), ())), preferred_element_type=FULL)


def dot_nt(left, right):
    return lax.dot_general(left, right, (((1,), (1,)), ((), ())), preferred_element_type=FULL)


def dot_tn(left, right):
    return lax.dot_general(left, right, (((0,), (0,)), ((), ())), preferred_element_type=FULL)


def lane_mean(values):
    return jnp.mean(values, axis=-1, keepdims=True)


def sigmoid(values):
    return pltpu.reciprocal(1.0 + jnp.exp2(values * -LOG2_E), approx=True)


def head_blocks(row_width, col_width, dtype):
    shape = (HEADS * row_width, HEADS * col_width)
    row = lax.broadcasted_iota(jnp.int32, shape, 0)
    col = lax.broadcasted_iota(jnp.int32, shape, 1)
    same = None
    for h in range(HEADS):
        here = (row >= h * row_width) & (row < (h + 1) * row_width)
        here = here & (col >= h * col_width) & (col < (h + 1) * col_width)
        same = here if same is None else same | here
    return jnp.where(same, 1.0, 0.0).astype(dtype)


def place_rows(target, part, near_ref, far_ref, masks):
    me = lax.axis_index("dap")
    cells = target.shape[0] // (2 * len(masks))
    for other, blocks in enumerate((near_ref, far_ref)):
        for at, mask in enumerate(masks):
            place = pl.ds(pl.multiple_of((me ^ mask ^ other) * cells, cells), cells)
            target[place, :] = blocks[at, part].reshape(cells, target.shape[1]).astype(FULL)


def block_tools(size, count=ROW_BLOCK):
    block = count * size

    def rows_of(at):
        return pl.ds(pl.multiple_of(at * block, block), block)

    def columns_of(ref, at):
        return jnp.concatenate(
            [ref[pl.ds(at * count + a, size, stride=size), :] for a in range(count)], axis=0
        )

    return rows_of, columns_of


def outer_sum(size, at, row_ref, row_stride, block_stride, block_ref):
    sums = [jnp.zeros((size, block_ref.shape[1]), FULL)] * ROW_BLOCK
    for k in range(size):
        whole = block_ref[k * size : (k + 1) * size, :]
        for a in range(ROW_BLOCK):
            row = (at * ROW_BLOCK + a) * block_stride + k * row_stride
            sums[a] = sums[a] + row_ref[pl.ds(row, 1), :] * whole
    return jnp.concatenate(sums, axis=0)


def cell_of_lane(size):
    lane = lax.broadcasted_iota(jnp.int32, (1, HEADS * size), 1)
    cell = lane
    for h in range(1, HEADS):
        cell = jnp.where(lane >= h * size, lane - h * size, cell)
    return cell


def spread_bias_weight(target, bias_w_ref, size):
    bias_rows = bias_w_ref[...].astype(FULL)
    for h in range(HEADS):
        target[h * size : (h + 1) * size, :] = jnp.broadcast_to(
            bias_rows[h : h + 1], (size, bias_rows.shape[1])
        ).astype(HALF)


def multiply_kernel(
    size,
    masks,
    near_ref,
    far_ref,
    lengths_ref,
    gains_ref,
    edge_w_ref,
    gate_w_ref,
    out_w_ref,
    left_ref,
    right_ref,
    left_a_ref,
    left_b_ref,
    right_a_ref,
    right_b_ref,
    gate_ref,
    hat_mid_ref,
    scale_mid_ref,
    edge_out_ref,
    hat_y_ref,
    scale_y_ref,
    y_ref,
    x_half_ref,
    update_ref,
    pair_ref,
    right_t_ref,
):
    channels = gains_ref.shape[1]
    block = ROW_BLOCK * size
    blocks = size // ROW_BLOCK
    rows_of, columns_of = block_tools(size)
    real = lengths_ref[0]
    gain_x = gains_ref[0:1, :]
    gain_mid = gains_ref[1:2, :]
    gain_y = gains_ref[2:3, :]
    place_rows(pair_ref, 0, near_ref, far_ref, masks)

    wide_rows_of, _ = block_tools(size, WIDE_BLOCK)

    col_mask = jnp.where(lax.broadcasted_iota(jnp.int32, (size, channels), 0) < real, 1.0, 0.0)

    def project(at, carry):
        rows = wide_rows_of(at)
        hat, _ = kernel_norm(pair_ref[rows, :])
        normed = (hat * gain_x).astype(HALF)
        x_half_ref[rows, :] = normed
        projected = dot_nn(normed, edge_w_ref[...])
        gate_ref[rows, :] = sigmoid(dot_nn(normed, gate_w_ref[...]))
        mask = jnp.concatenate(
            [col_mask * jnp.where(at * WIDE_BLOCK + a < real, 1.0, 0.0) for a in range(WIDE_BLOCK)], axis=0
        )
        for side, (edge, first, second) in enumerate(
            ((left_ref, left_a_ref, left_b_ref), (right_ref, right_a_ref, right_b_ref))
        ):
            base = 2 * side * channels
            sig = sigmoid(projected[:, base : base + channels])
            value = projected[:, base + channels : base + 2 * channels]
            masked = mask * sig
            product = masked * value
            edge[rows, :] = product.astype(HALF).astype(FULL)
            first[rows, :] = product * (1.0 - sig)
            second[rows, :] = masked
        return carry

    lax.fori_loop(0, size // WIDE_BLOCK, project, 0, unroll=True)

    def turn(at, carry):
        right_t_ref[rows_of(at), :] = columns_of(right_ref, at)
        return carry

    lax.fori_loop(0, blocks, turn, 0, unroll=True)

    def multiply(at, carry):
        rows = rows_of(at)
        product = outer_sum(size, at, left_ref, 1, size, right_t_ref)
        hat, scale = kernel_norm(product)
        hat_mid_ref[rows, :] = hat
        scale_mid_ref[rows, :] = jnp.broadcast_to(scale, hat.shape)
        update = (hat * gain_mid).astype(HALF)
        update_ref[rows, :] = update
        edge_out = dot_nn(update, out_w_ref[...])
        edge_out_ref[rows, :] = edge_out
        middle = pair_ref[rows, :] + gate_ref[rows, :] * edge_out
        hat, scale = kernel_norm(middle)
        hat_y_ref[rows, :] = hat
        scale_y_ref[rows, :] = jnp.broadcast_to(scale, hat.shape)
        y_ref[rows, :] = hat * gain_y
        return carry

    lax.fori_loop(0, blocks, multiply, 0, unroll=True)


def project_kernel(
    size,
    y_ref,
    att_w_ref,
    bias_w_ref,
    att_gate_ref,
    bias_ref,
    y_t_ref,
    query_ref,
    key_ref,
    value_ref,
    bias_rep_ref,
):
    channels = y_ref.shape[1]
    lanes = HEADS * size
    head_scale = 1.0 / math.sqrt(HEAD_DIM)
    rows_of, columns_of = block_tools(size, WIDE_BLOCK)
    cell = cell_of_lane(size)
    spread_bias_weight(bias_rep_ref, bias_w_ref, size)

    def prepare(at, carry):
        rows = rows_of(at)
        y = columns_of(y_ref, at).astype(HALF)
        y_t_ref[rows, :] = y
        packed = dot_nn(y, att_w_ref[...])
        query_ref[rows, :] = (packed[:, :channels] * head_scale).astype(HALF)
        key_ref[rows, :] = packed[:, channels : 2 * channels].astype(HALF)
        value_ref[rows, :] = packed[:, 2 * channels : 3 * channels].astype(HALF)
        att_gate_ref[rows, :] = sigmoid(packed[:, 3 * channels :])
        spread = dot_nt(y, bias_rep_ref[...]).astype(HALF).astype(FULL)
        for a in range(WIDE_BLOCK):
            carry = carry + jnp.where(cell == at * WIDE_BLOCK + a, spread[a * size : (a + 1) * size], 0.0)
        return carry

    bias_ref[...] = lax.fori_loop(
        0, size // WIDE_BLOCK, prepare, jnp.zeros((size, lanes), FULL), unroll=True
    )


def attend_kernel(
    size,
    masks,
    near_ref,
    far_ref,
    lengths_ref,
    att_w_ref,
    att_out_w_ref,
    att_gate_ref,
    bias_ref,
    y_t_ref,
    query_ref,
    key_ref,
    value_ref,
    bias_rep_ref,
    cot_ref,
    grad_y_ref,
    cot_t_ref,
    gated_ref,
    grad_packed_ref,
):
    channels = cot_ref.shape[1]
    block = WIDE_BLOCK * size
    blocks = size // WIDE_BLOCK
    lanes = HEADS * size
    head_scale = 1.0 / math.sqrt(HEAD_DIM)
    rows_of, columns_of = block_tools(size, WIDE_BLOCK)
    cell = cell_of_lane(size)
    key_row = lax.broadcasted_iota(jnp.int32, (size, lanes), 0)
    valid = jnp.where(key_row < lengths_ref[0], 1.0, 0.0)
    place_rows(cot_ref, 1, near_ref, far_ref, masks)

    head_mask = head_blocks(size, HEAD_DIM, HALF)
    lane = lax.broadcasted_iota(jnp.int32, (size, channels), 1)
    no_rows = jnp.zeros((size, channels), HALF)

    def own_heads(whole):
        picked = whole[(HEADS - 1) * size :]
        for h in reversed(range(HEADS - 1)):
            picked = jnp.where(lane < (h + 1) * HEAD_DIM, whole[h * size : (h + 1) * size], picked)
        return picked

    def attend(at, score_sum):
        rows = rows_of(at)
        parts = [slice(a * size, (a + 1) * size) for a in range(WIDE_BLOCK)]
        query, key, value = (ref[rows, :] for ref in (query_ref, key_ref, value_ref))
        gate = att_gate_ref[rows, :]
        cot = columns_of(cot_ref, at).astype(HALF)
        cot_t_ref[rows, :] = cot
        grad_gated = dot_nt(cot, att_out_w_ref[...])
        grad_att = (grad_gated * gate).astype(HALF)
        queries = [jnp.concatenate([query[p]] * HEADS, axis=0) * head_mask for p in parts]
        grads = [jnp.concatenate([grad_att[p]] * HEADS, axis=0) * head_mask for p in parts]
        bias = bias_ref[...]

        def stacked(columns):
            return jnp.stack(columns, axis=0)

        scores = stacked([dot_nt(key[p], queries[a]) + bias for a, p in enumerate(parts)])
        grad_attention = stacked([dot_nt(value[p], grads[a]) for a, p in enumerate(parts)])
        exp_scores = valid[None] * jnp.exp2(scores * LOG2_E)
        total = jnp.sum(exp_scores, axis=1)
        scale = jnp.where(total > 2.0**100, 2.0**-60, 1.0)
        inverse_total = pltpu.reciprocal(total * scale, approx=True)
        attention = (exp_scores * scale[:, None, :]) * inverse_total[:, None, :]
        row_dots = jnp.sum(attention * grad_attention, axis=1)
        grad_scores = attention * (grad_attention - row_dots[:, None, :])
        score_sum = score_sum + jnp.sum(grad_scores, axis=0)
        attention_half = attention.astype(HALF)
        scores_half = grad_scores.astype(HALF)
        grad_key = jnp.concatenate([dot_nn(scores_half[a], queries[a]) for a in range(WIDE_BLOCK)], axis=0)
        grad_value = jnp.concatenate([dot_nn(attention_half[a], grads[a]) for a in range(WIDE_BLOCK)], axis=0)

        def query_sums(a, p):
            weights = jnp.concatenate([attention_half[a], scores_half[a]], axis=0)
            vectors = jnp.concatenate(
                [
                    jnp.concatenate([value[p], no_rows], axis=1),
                    jnp.concatenate([no_rows, key[p]], axis=1),
                ],
                axis=0,
            )
            whole = dot_tn(weights, vectors)
            return [own_heads(whole[:, :channels]), own_heads(whole[:, channels:])]

        per_query = [query_sums(a, p) for a, p in enumerate(parts)]
        attended = jnp.concatenate([pair[0] for pair in per_query], axis=0)
        grad_query = jnp.concatenate([pair[1] for pair in per_query], axis=0)
        gated = gate * attended
        gated_ref[rows, :] = gated.astype(HALF)
        grad_gate_pre = grad_gated * gated * (1.0 - gate)
        grad_packed = jnp.concatenate(
            [
                (grad_query * head_scale).astype(HALF),
                grad_key.astype(HALF),
                grad_value.astype(HALF),
                grad_gate_pre.astype(HALF),
            ],
            axis=1,
        )
        grad_packed_ref[rows, : 4 * channels] = grad_packed
        grad_y_ref[rows, :] = dot_nt(grad_packed, att_w_ref[...])
        return score_sum

    score_sum = lax.fori_loop(0, blocks, attend, jnp.zeros((size, lanes), FULL), unroll=True)
    bias_grad = score_sum.astype(HALF).astype(FULL)

    def spread_bias(at, carry):
        rows = rows_of(at)
        spread = jnp.concatenate(
            [jnp.where(cell == at * WIDE_BLOCK + a, bias_grad, 0.0) for a in range(WIDE_BLOCK)], axis=0
        ).astype(HALF)
        grad_packed_ref[rows, 4 * channels :] = spread
        grad_y_ref[rows, :] += dot_nn(spread, bias_rep_ref[...])
        return carry

    lax.fori_loop(0, blocks, spread_bias, 0, unroll=True)


def gain_sum(pairs):
    total = sum(jnp.sum(weight.astype(FULL) * grad, axis=1, keepdims=True) for weight, grad in pairs)
    channels = total.shape[0]
    return jnp.transpose(jnp.broadcast_to(total, (channels, channels)))[0:1, :]


def edges_kernel(
    size,
    devices,
    pair_ref,
    gains_ref,
    edge_w_ref,
    gate_w_ref,
    out_w_ref,
    left_ref,
    right_ref,
    left_a_ref,
    left_b_ref,
    right_a_ref,
    right_b_ref,
    gate_ref,
    hat_mid_ref,
    scale_mid_ref,
    edge_out_ref,
    hat_y_ref,
    scale_y_ref,
    x_half_ref,
    update_ref,
    cot_ref,
    grad_y_ref,
    attention_side,
    grad_pair_ref,
    grad_gains_ref,
    grad_bias_ref,
    stage_refs,
    send,
    grad_middle_ref,
    grad_product_ref,
    grad_proj_ref,
    x_sum_ref,
    y_sum_ref,
):
    channels = gains_ref.shape[1]
    blocks = size // ROW_BLOCK
    rows_of, columns_of = block_tools(size)
    gain_x = gains_ref[0:1, :]
    gain_mid = gains_ref[1:2, :]
    gain_y = gains_ref[2:3, :]

    inverse = 1.0 / size
    y_t_ref, cot_t_ref, gated_ref, grad_packed_ref, att_w_ref, bias_rep_ref = attention_side
    edge_sum_ref, gate_sum_ref, out_sum_ref, att_sum_ref, att_out_sum_ref = stage_refs
    for sum_ref in (x_sum_ref, y_sum_ref, out_sum_ref, att_out_sum_ref):
        sum_ref[...] = jnp.zeros(sum_ref.shape, FULL)

    def attention_sums(at):
        rows = rows_of(at)
        y_sum_ref[...] += dot_tn(y_t_ref[rows, :], grad_packed_ref[rows, :])
        att_out_sum_ref[...] += dot_tn(gated_ref[rows, :], cot_t_ref[rows, :])

    def attention_results():
        att_sum = y_sum_ref[:, : 4 * channels] * inverse
        bias_sum = jnp.transpose(y_sum_ref[:, 4 * channels :] * inverse)
        att_sum_ref[...] = att_sum
        att_out_sum_ref[...] *= inverse
        send(3, 4)
        for h in range(HEADS):
            grad_bias_ref[h : h + 1, :] = jnp.sum(
                bias_sum[h * size : (h + 1) * size], axis=0, keepdims=True
            )
        bias_part = jnp.sum(bias_rep_ref[...].astype(FULL) * bias_sum, axis=0, keepdims=True)
        grad_gains_ref[2:3, :] = (gain_sum(((att_w_ref[...], att_sum),)) + bias_part) / gain_y

    wide_rows_of, wide_columns_of = block_tools(size, WIDE_BLOCK)

    def middle_back(at, carry):
        rows = wide_rows_of(at)
        grad_y = wide_columns_of(grad_y_ref, at)
        grad_middle = cot_ref[rows, :] + kernel_norm_back(
            grad_y, hat_y_ref[rows, :], scale_y_ref[rows, :], gain_y
        )
        grad_middle_ref[rows, :] = grad_middle
        gate = gate_ref[rows, :]
        gated = grad_middle * gate
        grad_edge_out = gated.astype(HALF)
        grad_gate = (gated * edge_out_ref[rows, :] * (1.0 - gate)).astype(HALF)
        grad_proj_ref[rows, 4 * channels :] = grad_gate
        x_sum_ref[:, 4 * channels :] += dot_tn(x_half_ref[rows, :], grad_gate)
        out_sum_ref[...] += dot_tn(update_ref[rows, :], grad_edge_out)
        grad_update = dot_nt(grad_edge_out, out_w_ref[...])
        grad_product = kernel_norm_back(grad_update, hat_mid_ref[rows, :], scale_mid_ref[rows, :], gain_mid)
        grad_product_ref[rows, :] = grad_product.astype(HALF).astype(FULL)
        return carry

    lax.fori_loop(0, size // WIDE_BLOCK, middle_back, 0, unroll=True)

    def edges_back(at):
        rows = rows_of(at)
        x_half = x_half_ref[rows, :]
        for side, (first_ref, second_ref, strides, other_ref) in enumerate(
            (
                (left_a_ref, left_b_ref, (1, size), right_ref),
                (right_a_ref, right_b_ref, (size, 1), left_ref),
            )
        ):
            grad = outer_sum(size, at, grad_product_ref, *strides, other_ref)
            both = jnp.concatenate(
                [(grad * first_ref[rows, :]).astype(HALF), (grad * second_ref[rows, :]).astype(HALF)], axis=1
            )
            place = slice(2 * side * channels, 2 * (side + 1) * channels)
            grad_proj_ref[rows, place] = both
            x_sum_ref[:, place] += dot_tn(x_half, both)

    for at in range(blocks):
        for part in range(2 * at, min(2 * at + 2, blocks)):
            attention_sums(part)
        edges_back(at)
        if 2 * at < blocks <= 2 * at + 2:
            attention_results()

    edge_sum, gate_sum = x_sum_ref[:, : 4 * channels] * inverse, x_sum_ref[:, 4 * channels :] * inverse
    edge_sum_ref[...] = edge_sum
    gate_sum_ref[...] = gate_sum
    out_sum = out_sum_ref[...] * inverse
    out_sum_ref[...] = out_sum
    send(0, 1, 2)
    grad_gains_ref[0:1, :] = gain_sum(((edge_w_ref[...], edge_sum), (gate_w_ref[...], gate_sum))) / gain_x
    grad_gains_ref[1:2, :] = gain_sum(((out_w_ref[...], out_sum),)) / gain_mid

    own_cells = size * size // devices
    own = pl.ds(pl.multiple_of(lax.axis_index("dap") * own_cells, own_cells), own_cells)
    hat, scale = kernel_norm(pair_ref[...].reshape(own_cells, channels).astype(FULL))
    grad_x = dot_nt(grad_proj_ref[own, : 4 * channels], edge_w_ref[...])
    grad_x = grad_x + dot_nt(grad_proj_ref[own, 4 * channels :], gate_w_ref[...])
    grad_pair = grad_middle_ref[own, :] + kernel_norm_back(grad_x, hat, scale, gain_x)
    grad_pair_ref[...] = grad_pair.astype(grad_pair_ref.dtype)


def kernel_norm(values):
    center = values - lane_mean(values)
    scale = lax.rsqrt(lane_mean(center * center) + epsilon)
    return center * scale, scale


def kernel_norm_back(grad_out, hat, scale, gain):
    scaled = grad_out * gain
    return scale * (scaled - lane_mean(scaled) - hat * lane_mean(scaled * hat))


def bytes_of(arrays):
    return sum(math.prod(shape) * jnp.dtype(dtype).itemsize for shape, dtype in arrays)


def kernel_scratch(size, channels):
    cells, lanes = size * size, HEADS * size
    full, half = ((cells, channels), FULL), ((cells, channels), HALF)
    square, wide = ((channels, channels), FULL), ((channels, 4 * channels), FULL)
    return {
        "kept": [full] * 12,
        "y": [full],
        "halves": [half] * 2,
        "multiply": [full] * 2,
        "projections": [full, ((size, lanes), FULL)] + [half] * 4 + [((lanes, channels), HALF)],
        "shared": [full] * 2,
        "attend": [half] * 2 + [((cells, 4 * channels + lanes), HALF)],
        "stage": [wide, square, square, wide, square],
        "edges": [full] * 2
        + [((cells, 5 * channels), HALF), ((channels, 5 * channels), FULL), ((channels, 4 * channels + lanes), FULL)],
    }


def whole_kernel(
    size,
    masks,
    near_ref,
    far_ref,
    lengths_ref,
    gains_ref,
    edge_w_ref,
    gate_w_ref,
    out_w_ref,
    att_w_ref,
    bias_w_ref,
    att_out_w_ref,
    grad_pair_ref,
    grad_gains_ref,
    grad_edge_ref,
    grad_gate_w_ref,
    grad_out_w_ref,
    grad_att_w_ref,
    grad_bias_ref,
    grad_att_out_ref,
    *scratch,
):
    part, at = {}, 0
    for name, arrays in kernel_scratch(size, 1).items():
        part[name] = scratch[at : at + len(arrays)]
        at += len(arrays)
    sent = scratch[at]
    weights = (edge_w_ref, gate_w_ref, out_w_ref)
    multiply_kernel(
        size, masks, near_ref, far_ref, lengths_ref, gains_ref, *weights, *part["kept"], *part["y"], *part["halves"], *part["multiply"]
    )
    project_kernel(size, *part["y"], att_w_ref, bias_w_ref, *part["projections"])
    attend_kernel(
        size,
        masks,
        near_ref,
        far_ref,
        lengths_ref,
        att_w_ref,
        att_out_w_ref,
        *part["projections"],
        *part["shared"],
        *part["attend"],
    )
    targets = (grad_edge_ref, grad_gate_w_ref, grad_out_w_ref, grad_att_w_ref, grad_att_out_ref)
    copies = [
        pltpu.make_async_copy(source, target, sent.at[slot])
        for slot, (source, target) in enumerate(zip(part["stage"], targets))
    ]

    def send(*slots):
        for slot in slots:
            copies[slot].start()

    _, _, y_t_ref, _, _, _, bias_rep_ref = part["projections"]
    cot_t_ref, gated_ref, grad_packed_ref = part["attend"]
    edges_kernel(
        size,
        2 * len(masks),
        near_ref.at[0, 0],
        gains_ref,
        *weights,
        *part["kept"],
        *part["halves"],
        *part["shared"],
        (y_t_ref, cot_t_ref, gated_ref, grad_packed_ref, att_w_ref, bias_rep_ref),
        grad_pair_ref,
        grad_gains_ref,
        grad_bias_ref,
        part["stage"],
        send,
        *part["edges"],
    )
    for copy in copies:
        copy.wait()


def replicated_plan(
    axis_size,
    pair_map,
    cotangent,
    lengths,
    norm_gains,
    edge_weight,
    mult_gate_weight,
    mult_out_weight,
    attention_weight,
    bias_weight,
    attention_out_weight,
):
    _, size, channels = pair_map.shape
    cells = size * size

    def swapped(held, mask):
        return lax.ppermute(held, "dap", [(d, d ^ mask) for d in range(axis_size)])

    own = jnp.stack([pair_map, cotangent])
    masks = list(range(0, axis_size, 2))
    near = jnp.stack([own] + [swapped(own, mask) for mask in masks[1:]])
    far = swapped(near, 1)

    square, wide = ((channels, channels), FULL), ((channels, 4 * channels), FULL)
    outs = [((cells // axis_size, channels), HALF), ((3, channels), FULL), wide, square, square]
    outs += [wide, ((HEADS, channels), FULL), square]
    scratch = sum(kernel_scratch(size, channels).values(), [])
    vmem = pl.BlockSpec(memory_space=pltpu.VMEM)
    smem = pl.BlockSpec(memory_space=pltpu.SMEM)
    anywhere = pl.BlockSpec(memory_space=pl.ANY)
    results = pl.pallas_call(
        functools.partial(whole_kernel, size, masks),
        out_shape=[jax.ShapeDtypeStruct(*out) for out in outs],
        in_specs=[vmem, vmem, smem] + [vmem] * 7,
        out_specs=[vmem] * 2 + [anywhere] * 4 + [vmem, anywhere],
        scratch_shapes=[pltpu.VMEM(*part) for part in scratch] + [pltpu.SemaphoreType.DMA((5,))],
        compiler_params=pltpu.CompilerParams(vmem_limit_bytes=bytes_of(scratch) + VMEM_SLACK),
    )(
        near,
        far,
        lengths,
        norm_gains,
        edge_weight,
        mult_gate_weight,
        mult_out_weight,
        attention_weight,
        bias_weight.T,
        attention_out_weight,
    )
    return (results[0].reshape(pair_map.shape), *results[1:6], results[6].T, results[7])


def per_device(axis_size, pair_map, *rest):
    _, size, channels = pair_map.shape
    scratch = sum(kernel_scratch(size, channels).values(), [])
    fits = size % WIDE_BLOCK == 0 and bytes_of(scratch) <= VMEM_SHARE
    if fits and axis_size >= 8 and axis_size & (axis_size - 1) == 0:
        return replicated_plan(axis_size, pair_map, *rest)
    return distributed_plan(pair_map, *rest)


def solution(mesh):
    return jax.shard_map(
        functools.partial(per_device, mesh.shape["dap"]),
        mesh=mesh,
        in_specs=(
            P(("groups", "dap"), None, None),
            P(("groups", "dap"), None, None),
            P("groups"),
            P(),
            P(),
            P(),
            P(),
            P(),
            P(),
            P(),
        ),
        out_specs=(
            P(("groups", "dap"), None, None),
            P("groups", None),
            P("groups", None),
            P("groups", None),
            P("groups", None),
            P("groups", None),
            P("groups", None),
            P("groups", None),
        ),
        check_vma=False,
    )
```

```python
import functools
import math

import jax
import jax.numpy as jnp
from jax import lax
from jax.experimental import pallas as pl
from jax.experimental.pallas import tpu as pltpu
from jax.sharding import PartitionSpec as P

HEADS = 4
HEAD_DIM = 32


epsilon = 1e-05


def norm_forward(values, gain_row):
    center = values - jnp.mean(values, axis=-1, keepdims=True)
    inv_std = lax.rsqrt(jnp.mean(center * center, axis=-1, keepdims=True) + epsilon)
    normed = center * inv_std
    return (normed * gain_row, normed, inv_std)


def norm_backward(grad_out, normed, inv_std, gain_row):
    scaled = grad_out * gain_row
    first_mean = jnp.mean(scaled, axis=-1, keepdims=True)
    second_mean = jnp.mean(scaled * normed, axis=-1, keepdims=True)
    return inv_std * (scaled - first_mean - normed * second_mean)


def distributed_plan(
    pair_map,
    cotangent,
    lengths,
    norm_gains,
    edge_weight,
    mult_gate_weight,
    mult_out_weight,
    attention_weight,
    bias_weight,
    attention_out_weight,
):
    row_count, full_size, channels = pair_map.shape
    inner_width = HEADS * HEAD_DIM
    head_scale = 1.0 / math.sqrt(HEAD_DIM)
    first_row = lax.axis_index("dap") * row_count
    real_count = lengths[0]
    valid_all = (jnp.arange(full_size) < real_count).astype(jnp.float32)
    valid_rows = (first_row + jnp.arange(row_count) < real_count).astype(jnp.float32)
    mask_pair = (valid_rows[:, None] * valid_all[None, :])[:, :, None]
    pair_f32 = pair_map.astype(jnp.float32)
    normed_full, hat_in, scale_in = norm_forward(pair_f32, norm_gains[0])
    normed_x = normed_full.astype(jnp.bfloat16)
    projected = jnp.einsum("rnc,cf->rnf", normed_x, edge_weight, preferred_element_type=jnp.float32)
    left_gate = projected[..., :channels]
    left_value = projected[..., channels : 2 * channels]
    right_gate = projected[..., 2 * channels : 3 * channels]
    right_value = projected[..., 3 * channels :]
    left_sig = jax.nn.sigmoid(left_gate)
    right_sig = jax.nn.sigmoid(right_gate)
    left_edges = (mask_pair * left_sig * left_value).astype(jnp.bfloat16)
    right_edges = (mask_pair * right_sig * right_value).astype(jnp.bfloat16)
    product = jnp.einsum(
        "ikc,jkc->ijc",
        left_edges,
        lax.all_gather(right_edges, "dap", axis=0, tiled=True),
        preferred_element_type=jnp.float32,
    )
    update_full, hat_mid, scale_mid = norm_forward(product, norm_gains[1])
    update = update_full.astype(jnp.bfloat16)
    edge_out = jnp.einsum(
        "rnc,cf->rnf", update, mult_out_weight, preferred_element_type=jnp.float32
    )
    gate_sig = jax.nn.sigmoid(
        jnp.einsum("rnc,cf->rnf", normed_x, mult_gate_weight, preferred_element_type=jnp.float32)
    )
    middle = pair_f32 + gate_sig * edge_out
    normed_mid, hat_attn, scale_attn = norm_forward(middle, norm_gains[2])
    normed_y = normed_mid.astype(jnp.bfloat16)
    bias_local = jnp.einsum(
        "kic,ch->hki", normed_y, bias_weight, preferred_element_type=jnp.float32
    ).astype(jnp.bfloat16)
    bias_whole = lax.all_gather(bias_local, "dap", axis=1, tiled=True)
    bias_query = jnp.swapaxes(bias_whole, 1, 2).astype(jnp.float32)
    column_y, column_cot = (
        lax.all_to_all(normed_y, "dap", split_axis=1, concat_axis=0, tiled=True),
        lax.all_to_all(cotangent, "dap", split_axis=1, concat_axis=0, tiled=True),
    )
    packed = jnp.einsum(
        "ijc,cf->ijf", column_y, attention_weight, preferred_element_type=jnp.float32
    )
    packed = packed.reshape(full_size, row_count, 4, HEADS, HEAD_DIM)
    query_vectors = (packed[:, :, 0] * head_scale).astype(jnp.bfloat16)
    key_vectors = packed[:, :, 1].astype(jnp.bfloat16)
    value_vectors = packed[:, :, 2].astype(jnp.bfloat16)
    att_gate = jax.nn.sigmoid(packed[:, :, 3])
    scores = (
        jnp.einsum(
            "ijhd,kjhd->jhik", query_vectors, key_vectors, preferred_element_type=jnp.float32
        )
        + bias_query[None]
    )
    exp_scores = valid_all * jnp.exp(scores)
    attention = exp_scores / jnp.sum(exp_scores, axis=-1, keepdims=True)
    attention_half = attention.astype(jnp.bfloat16)
    attended = jnp.einsum(
        "jhik,kjhd->ijhd", attention_half, value_vectors, preferred_element_type=jnp.float32
    )
    gated = (att_gate * attended).astype(jnp.bfloat16).reshape(full_size, row_count, inner_width)
    part_attn_out = jnp.einsum("ijf,ijc->fc", gated, column_cot, preferred_element_type=jnp.float32)
    grad_gated = jnp.einsum(
        "ijc,fc->ijf", column_cot, attention_out_weight, preferred_element_type=jnp.float32
    )
    grad_gated = grad_gated.reshape(full_size, row_count, HEADS, HEAD_DIM)
    grad_att = (grad_gated * att_gate).astype(jnp.bfloat16)
    grad_gate_pre = grad_gated * attended * att_gate * (1.0 - att_gate)
    grad_attention = jnp.einsum(
        "ijhd,kjhd->jhik", grad_att, value_vectors, preferred_element_type=jnp.float32
    )
    row_dots = jnp.transpose(jnp.sum(grad_att.astype(jnp.float32) * attended, axis=-1), (1, 2, 0))
    grad_scores = attention * (grad_attention - row_dots[..., None])
    scores_half = grad_scores.astype(jnp.bfloat16)
    grad_query = jnp.einsum(
        "jhik,kjhd->ijhd", scores_half, key_vectors, preferred_element_type=jnp.float32
    )
    grad_key = jnp.einsum(
        "jhik,ijhd->kjhd", scores_half, query_vectors, preferred_element_type=jnp.float32
    )
    grad_value = jnp.einsum(
        "jhik,ijhd->kjhd", attention_half, grad_att, preferred_element_type=jnp.float32
    )
    grad_packed = jnp.stack([grad_query * head_scale, grad_key, grad_value, grad_gate_pre], axis=2)
    grad_packed = grad_packed.reshape(full_size, row_count, 4 * inner_width).astype(jnp.bfloat16)
    part_attention = jnp.einsum(
        "ijc,ijf->cf", column_y, grad_packed, preferred_element_type=jnp.float32
    )
    column_grad = jnp.einsum(
        "ijf,cf->ijc", grad_packed, attention_weight, preferred_element_type=jnp.float32
    ).astype(jnp.bfloat16)
    row_grad = lax.all_to_all(column_grad, "dap", split_axis=0, concat_axis=1, tiled=True)
    score_sums = jnp.sum(grad_scores, axis=0)
    taken = score_sums
    bias_half = lax.psum_scatter(
        jnp.transpose(taken, (2, 0, 1)), "dap", scatter_dimension=0, tiled=True
    ).astype(jnp.bfloat16)
    part_bias = jnp.einsum("kic,khi->ch", normed_y, bias_half, preferred_element_type=jnp.float32)
    grad_normed_y = row_grad.astype(jnp.float32) + jnp.einsum(
        "khi,ch->kic", bias_half, bias_weight, preferred_element_type=jnp.float32
    )
    part_gain_attn = jnp.sum(grad_normed_y * hat_attn, axis=(0, 1))
    grad_middle = cotangent.astype(jnp.float32) + norm_backward(
        grad_normed_y, hat_attn, scale_attn, norm_gains[2]
    )
    grad_edge_out = (grad_middle * gate_sig).astype(jnp.bfloat16)
    grad_gate = (grad_middle * edge_out * gate_sig * (1.0 - gate_sig)).astype(jnp.bfloat16)
    part_mult_out = jnp.einsum(
        "rnc,rnf->cf", update, grad_edge_out, preferred_element_type=jnp.float32
    )
    part_mult_gate = jnp.einsum(
        "rnc,rnf->cf", normed_x, grad_gate, preferred_element_type=jnp.float32
    )
    grad_update = jnp.einsum(
        "rnf,cf->rnc", grad_edge_out, mult_out_weight, preferred_element_type=jnp.float32
    )
    part_gain_mid = jnp.sum(grad_update * hat_mid, axis=(0, 1))
    grad_product = norm_backward(grad_update, hat_mid, scale_mid, norm_gains[1]).astype(
        jnp.bfloat16
    )
    taken = grad_product
    grad_left = jnp.einsum(
        "ijc,jkc->ikc",
        taken,
        lax.all_gather(right_edges, "dap", axis=0, tiled=True),
        preferred_element_type=jnp.float32,
    )
    grad_cols = lax.all_to_all(grad_product, "dap", split_axis=1, concat_axis=0, tiled=True)
    taken = grad_cols
    grad_right = jnp.einsum(
        "ijc,ikc->jkc",
        taken,
        lax.all_gather(left_edges, "dap", axis=0, tiled=True),
        preferred_element_type=jnp.float32,
    )
    grad_proj = jnp.concatenate(
        [
            grad_left * mask_pair * left_value * left_sig * (1.0 - left_sig),
            grad_left * mask_pair * left_sig,
            grad_right * mask_pair * right_value * right_sig * (1.0 - right_sig),
            grad_right * mask_pair * right_sig,
        ],
        axis=-1,
    ).astype(jnp.bfloat16)
    part_edge = jnp.einsum("rnc,rnf->cf", normed_x, grad_proj, preferred_element_type=jnp.float32)
    grad_normed_x = jnp.einsum(
        "rnf,cf->rnc", grad_proj, edge_weight, preferred_element_type=jnp.float32
    )
    grad_normed_x = grad_normed_x + jnp.einsum(
        "rnf,cf->rnc", grad_gate, mult_gate_weight, preferred_element_type=jnp.float32
    )
    part_gain_in = jnp.sum(grad_normed_x * hat_in, axis=(0, 1))
    grad_pair = (
        grad_middle + norm_backward(grad_normed_x, hat_in, scale_in, norm_gains[0])
    ).astype(jnp.bfloat16)
    totals = lax.psum(
        (
            part_gain_in,
            part_gain_mid,
            part_edge,
            part_mult_gate,
            part_mult_out,
            part_gain_attn,
            part_attention,
            part_bias,
            part_attn_out,
        ),
        "dap",
    )
    (
        gain_in_sum,
        gain_mid_sum,
        edge_sum,
        mult_gate_sum,
        mult_out_sum,
        gain_attn_sum,
        attention_sum,
        bias_sum,
        attn_out_sum,
    ) = totals
    inverse = 1.0 / full_size
    grad_gains = jnp.stack([gain_in_sum, gain_mid_sum, gain_attn_sum]) * inverse
    return (
        grad_pair,
        grad_gains,
        edge_sum * inverse,
        mult_gate_sum * inverse,
        mult_out_sum * inverse,
        attention_sum * inverse,
        bias_sum * inverse,
        attn_out_sum * inverse,
    )


ROW_BLOCK = 8
WIDE_BLOCK = 16
VMEM_SLACK = 8 * 2**20
VMEM_SHARE = 32 * 2**20
LOG2_E = 1.0 / math.log(2.0)
HALF = jnp.bfloat16
FULL = jnp.float32


def dot_nn(left, right):
    return lax.dot_general(left, right, (((1,), (0,)), ((), ())), preferred_element_type=FULL)


def dot_nt(left, right):
    return lax.dot_general(left, right, (((1,), (1,)), ((), ())), preferred_element_type=FULL)


def dot_tn(left, right):
    return lax.dot_general(left, right, (((0,), (0,)), ((), ())), preferred_element_type=FULL)


def lane_mean(values):
    return jnp.mean(values, axis=-1, keepdims=True)


def sigmoid(values):
    return pltpu.reciprocal(1.0 + jnp.exp2(values * -LOG2_E), approx=True)


def head_blocks(row_width, col_width, dtype):
    shape = (HEADS * row_width, HEADS * col_width)
    row = lax.broadcasted_iota(jnp.int32, shape, 0)
    col = lax.broadcasted_iota(jnp.int32, shape, 1)
    same = None
    for h in range(HEADS):
        here = (row >= h * row_width) & (row < (h + 1) * row_width)
        here = here & (col >= h * col_width) & (col < (h + 1) * col_width)
        same = here if same is None else same | here
    return jnp.where(same, 1.0, 0.0).astype(dtype)


def place_rows(target, part, near_ref, far_ref, masks):
    me = lax.axis_index("dap")
    cells = target.shape[0] // (2 * len(masks))
    for other, blocks in enumerate((near_ref, far_ref)):
        for at, mask in enumerate(masks):
            place = pl.ds(pl.multiple_of((me ^ mask ^ other) * cells, cells), cells)
            target[place, :] = blocks[at, part].reshape(cells, target.shape[1]).astype(FULL)


def block_tools(size, count=ROW_BLOCK):
    block = count * size

    def rows_of(at):
        return pl.ds(pl.multiple_of(at * block, block), block)

    def columns_of(ref, at):
        return jnp.concatenate(
            [ref[pl.ds(at * count + a, size, stride=size), :] for a in range(count)], axis=0
        )

    return rows_of, columns_of


def outer_sum(size, at, row_ref, row_stride, block_stride, block_ref):
    sums = [jnp.zeros((size, block_ref.shape[1]), FULL)] * ROW_BLOCK
    for k in range(size):
        whole = block_ref[k * size : (k + 1) * size, :]
        for a in range(ROW_BLOCK):
            row = (at * ROW_BLOCK + a) * block_stride + k * row_stride
            sums[a] = sums[a] + row_ref[pl.ds(row, 1), :] * whole
    return jnp.concatenate(sums, axis=0)


def cell_of_lane(size):
    lane = lax.broadcasted_iota(jnp.int32, (1, HEADS * size), 1)
    cell = lane
    for h in range(1, HEADS):
        cell = jnp.where(lane >= h * size, lane - h * size, cell)
    return cell


def spread_bias_weight(target, bias_w_ref, size):
    bias_rows = bias_w_ref[...].astype(FULL)
    for h in range(HEADS):
        target[h * size : (h + 1) * size, :] = jnp.broadcast_to(
            bias_rows[h : h + 1], (size, bias_rows.shape[1])
        ).astype(HALF)


def multiply_kernel(
    size,
    masks,
    near_ref,
    far_ref,
    lengths_ref,
    gains_ref,
    edge_w_ref,
    gate_w_ref,
    out_w_ref,
    left_ref,
    right_ref,
    left_a_ref,
    left_b_ref,
    right_a_ref,
    right_b_ref,
    gate_ref,
    hat_mid_ref,
    scale_mid_ref,
    edge_out_ref,
    hat_y_ref,
    scale_y_ref,
    y_ref,
    x_half_ref,
    update_ref,
    pair_ref,
    right_t_ref,
):
    channels = gains_ref.shape[1]
    block = ROW_BLOCK * size
    blocks = size // ROW_BLOCK
    rows_of, columns_of = block_tools(size)
    real = lengths_ref[0]
    gain_x = gains_ref[0:1, :]
    gain_mid = gains_ref[1:2, :]
    gain_y = gains_ref[2:3, :]
    place_rows(pair_ref, 0, near_ref, far_ref, masks)

    wide_rows_of, _ = block_tools(size, WIDE_BLOCK)

    col_mask = jnp.where(lax.broadcasted_iota(jnp.int32, (size, channels), 0) < real, 1.0, 0.0)

    def project(at, carry):
        rows = wide_rows_of(at)
        hat, _ = kernel_norm(pair_ref[rows, :])
        normed = (hat * gain_x).astype(HALF)
        x_half_ref[rows, :] = normed
        projected = dot_nn(normed, edge_w_ref[...])
        gate_ref[rows, :] = sigmoid(dot_nn(normed, gate_w_ref[...]))
        mask = jnp.concatenate(
            [col_mask * jnp.where(at * WIDE_BLOCK + a < real, 1.0, 0.0) for a in range(WIDE_BLOCK)], axis=0
        )
        for side, (edge, first, second) in enumerate(
            ((left_ref, left_a_ref, left_b_ref), (right_ref, right_a_ref, right_b_ref))
        ):
            base = 2 * side * channels
            sig = sigmoid(projected[:, base : base + channels])
            value = projected[:, base + channels : base + 2 * channels]
            masked = mask * sig
            product = masked * value
            edge[rows, :] = product.astype(HALF).astype(FULL)
            first[rows, :] = product * (1.0 - sig)
            second[rows, :] = masked
        return carry

    lax.fori_loop(0, size // WIDE_BLOCK, project, 0, unroll=True)

    def turn(at, carry):
        right_t_ref[rows_of(at), :] = columns_of(right_ref, at)
        return carry

    lax.fori_loop(0, blocks, turn, 0, unroll=True)

    def multiply(at, carry):
        rows = rows_of(at)
        product = outer_sum(size, at, left_ref, 1, size, right_t_ref)
        hat, scale = kernel_norm(product)
        hat_mid_ref[rows, :] = hat
        scale_mid_ref[rows, :] = jnp.broadcast_to(scale, hat.shape)
        update = (hat * gain_mid).astype(HALF)
        update_ref[rows, :] = update
        edge_out = dot_nn(update, out_w_ref[...])
        edge_out_ref[rows, :] = edge_out
        middle = pair_ref[rows, :] + gate_ref[rows, :] * edge_out
        hat, scale = kernel_norm(middle)
        hat_y_ref[rows, :] = hat
        scale_y_ref[rows, :] = jnp.broadcast_to(scale, hat.shape)
        y_ref[rows, :] = hat * gain_y
        return carry

    lax.fori_loop(0, blocks, multiply, 0, unroll=True)


def project_kernel(
    size,
    y_ref,
    att_w_ref,
    bias_w_ref,
    att_gate_ref,
    bias_ref,
    y_t_ref,
    query_ref,
    key_ref,
    value_ref,
    bias_rep_ref,
):
    channels = y_ref.shape[1]
    lanes = HEADS * size
    head_scale = 1.0 / math.sqrt(HEAD_DIM)
    rows_of, columns_of = block_tools(size, WIDE_BLOCK)
    cell = cell_of_lane(size)
    spread_bias_weight(bias_rep_ref, bias_w_ref, size)

    def prepare(at, carry):
        rows = rows_of(at)
        y = columns_of(y_ref, at).astype(HALF)
        y_t_ref[rows, :] = y
        packed = dot_nn(y, att_w_ref[...])
        query_ref[rows, :] = (packed[:, :channels] * head_scale).astype(HALF)
        key_ref[rows, :] = packed[:, channels : 2 * channels].astype(HALF)
        value_ref[rows, :] = packed[:, 2 * channels : 3 * channels].astype(HALF)
        att_gate_ref[rows, :] = sigmoid(packed[:, 3 * channels :])
        spread = dot_nt(y, bias_rep_ref[...]).astype(HALF).astype(FULL)
        for a in range(WIDE_BLOCK):
            carry = carry + jnp.where(cell == at * WIDE_BLOCK + a, spread[a * size : (a + 1) * size], 0.0)
        return carry

    bias_ref[...] = lax.fori_loop(
        0, size // WIDE_BLOCK, prepare, jnp.zeros((size, lanes), FULL), unroll=True
    )


def attend_kernel(
    size,
    lengths_ref,
    att_w_ref,
    att_out_w_ref,
    att_gate_ref,
    bias_ref,
    y_t_ref,
    query_ref,
    key_ref,
    value_ref,
    bias_rep_ref,
    cot_ref,
    grad_y_ref,
    cot_t_ref,
    gated_ref,
    grad_packed_ref,
):
    channels = cot_ref.shape[1]
    block = WIDE_BLOCK * size
    blocks = size // WIDE_BLOCK
    lanes = HEADS * size
    head_scale = 1.0 / math.sqrt(HEAD_DIM)
    rows_of, columns_of = block_tools(size, WIDE_BLOCK)
    cell = cell_of_lane(size)
    key_row = lax.broadcasted_iota(jnp.int32, (size, lanes), 0)
    valid = jnp.where(key_row < lengths_ref[0], 1.0, 0.0)

    head_mask = head_blocks(size, HEAD_DIM, HALF)
    lane = lax.broadcasted_iota(jnp.int32, (size, channels), 1)
    no_rows = jnp.zeros((size, channels), HALF)

    def own_heads(whole):
        picked = whole[(HEADS - 1) * size :]
        for h in reversed(range(HEADS - 1)):
            picked = jnp.where(lane < (h + 1) * HEAD_DIM, whole[h * size : (h + 1) * size], picked)
        return picked

    def attend(at, score_sum):
        rows = rows_of(at)
        parts = [slice(a * size, (a + 1) * size) for a in range(WIDE_BLOCK)]
        query, key, value = (ref[rows, :] for ref in (query_ref, key_ref, value_ref))
        gate = att_gate_ref[rows, :]
        cot = columns_of(cot_ref, at).astype(HALF)
        cot_t_ref[rows, :] = cot
        grad_gated = dot_nt(cot, att_out_w_ref[...])
        grad_att = (grad_gated * gate).astype(HALF)
        queries = [jnp.concatenate([query[p]] * HEADS, axis=0) * head_mask for p in parts]
        grads = [jnp.concatenate([grad_att[p]] * HEADS, axis=0) * head_mask for p in parts]
        bias = bias_ref[...]

        def stacked(columns):
            return jnp.stack(columns, axis=0)

        scores = stacked([dot_nt(key[p], queries[a]) + bias for a, p in enumerate(parts)])
        grad_attention = stacked([dot_nt(value[p], grads[a]) for a, p in enumerate(parts)])
        exp_scores = valid[None] * jnp.exp2(scores * LOG2_E)
        total = jnp.sum(exp_scores, axis=1)
        scale = jnp.where(total > 2.0**100, 2.0**-60, 1.0)
        inverse_total = pltpu.reciprocal(total * scale, approx=True)
        attention = (exp_scores * scale[:, None, :]) * inverse_total[:, None, :]
        row_dots = jnp.sum(attention * grad_attention, axis=1)
        grad_scores = attention * (grad_attention - row_dots[:, None, :])
        score_sum = score_sum + jnp.sum(grad_scores, axis=0)
        attention_half = attention.astype(HALF)
        scores_half = grad_scores.astype(HALF)
        grad_key = jnp.concatenate([dot_nn(scores_half[a], queries[a]) for a in range(WIDE_BLOCK)], axis=0)
        grad_value = jnp.concatenate([dot_nn(attention_half[a], grads[a]) for a in range(WIDE_BLOCK)], axis=0)

        def query_sums(a, p):
            weights = jnp.concatenate([attention_half[a], scores_half[a]], axis=0)
            vectors = jnp.concatenate(
                [
                    jnp.concatenate([value[p], no_rows], axis=1),
                    jnp.concatenate([no_rows, key[p]], axis=1),
                ],
                axis=0,
            )
            whole = dot_tn(weights, vectors)
            return [own_heads(whole[:, :channels]), own_heads(whole[:, channels:])]

        per_query = [query_sums(a, p) for a, p in enumerate(parts)]
        attended = jnp.concatenate([pair[0] for pair in per_query], axis=0)
        grad_query = jnp.concatenate([pair[1] for pair in per_query], axis=0)
        gated = gate * attended
        gated_ref[rows, :] = gated.astype(HALF)
        grad_gate_pre = grad_gated * gated * (1.0 - gate)
        grad_packed = jnp.concatenate(
            [
                (grad_query * head_scale).astype(HALF),
                grad_key.astype(HALF),
                grad_value.astype(HALF),
                grad_gate_pre.astype(HALF),
            ],
            axis=1,
        )
        grad_packed_ref[rows, : 4 * channels] = grad_packed
        grad_y_ref[rows, :] = dot_nt(grad_packed, att_w_ref[...])
        return score_sum

    score_sum = lax.fori_loop(0, blocks, attend, jnp.zeros((size, lanes), FULL), unroll=True)
    bias_grad = score_sum.astype(HALF).astype(FULL)

    def spread_bias(at, carry):
        rows = rows_of(at)
        spread = jnp.concatenate(
            [jnp.where(cell == at * WIDE_BLOCK + a, bias_grad, 0.0) for a in range(WIDE_BLOCK)], axis=0
        ).astype(HALF)
        grad_packed_ref[rows, 4 * channels :] = spread
        grad_y_ref[rows, :] += dot_nn(spread, bias_rep_ref[...])
        return carry

    lax.fori_loop(0, blocks, spread_bias, 0, unroll=True)


def gain_sum(pairs):
    total = sum(jnp.sum(weight.astype(FULL) * grad, axis=1, keepdims=True) for weight, grad in pairs)
    channels = total.shape[0]
    return jnp.transpose(jnp.broadcast_to(total, (channels, channels)))[0:1, :]


def edges_kernel(
    size,
    devices,
    pair_ref,
    gains_ref,
    edge_w_ref,
    gate_w_ref,
    out_w_ref,
    left_ref,
    right_ref,
    left_a_ref,
    left_b_ref,
    right_a_ref,
    right_b_ref,
    gate_ref,
    hat_mid_ref,
    scale_mid_ref,
    edge_out_ref,
    hat_y_ref,
    scale_y_ref,
    x_half_ref,
    update_ref,
    cot_ref,
    grad_y_ref,
    attention_side,
    grad_pair_ref,
    grad_gains_ref,
    grad_bias_ref,
    stage_refs,
    send,
    grad_middle_ref,
    grad_product_ref,
    grad_proj_ref,
    x_sum_ref,
    y_sum_ref,
):
    channels = gains_ref.shape[1]
    blocks = size // ROW_BLOCK
    rows_of, columns_of = block_tools(size)
    gain_x = gains_ref[0:1, :]
    gain_mid = gains_ref[1:2, :]
    gain_y = gains_ref[2:3, :]

    inverse = 1.0 / size
    y_t_ref, cot_t_ref, gated_ref, grad_packed_ref, att_w_ref, bias_rep_ref = attention_side
    edge_sum_ref, gate_sum_ref, out_sum_ref, att_sum_ref, att_out_sum_ref = stage_refs
    for sum_ref in (x_sum_ref, y_sum_ref, out_sum_ref, att_out_sum_ref):
        sum_ref[...] = jnp.zeros(sum_ref.shape, FULL)

    def attention_sums(at):
        rows = rows_of(at)
        y_sum_ref[...] += dot_tn(y_t_ref[rows, :], grad_packed_ref[rows, :])
        att_out_sum_ref[...] += dot_tn(gated_ref[rows, :], cot_t_ref[rows, :])

    def attention_results():
        att_sum = y_sum_ref[:, : 4 * channels] * inverse
        bias_sum = jnp.transpose(y_sum_ref[:, 4 * channels :] * inverse)
        att_sum_ref[...] = att_sum
        att_out_sum_ref[...] *= inverse
        send(3, 4)
        for h in range(HEADS):
            grad_bias_ref[h : h + 1, :] = jnp.sum(
                bias_sum[h * size : (h + 1) * size], axis=0, keepdims=True
            )
        bias_part = jnp.sum(bias_rep_ref[...].astype(FULL) * bias_sum, axis=0, keepdims=True)
        grad_gains_ref[2:3, :] = (gain_sum(((att_w_ref[...], att_sum),)) + bias_part) / gain_y

    wide_rows_of, wide_columns_of = block_tools(size, WIDE_BLOCK)

    def middle_back(at, carry):
        rows = wide_rows_of(at)
        grad_y = wide_columns_of(grad_y_ref, at)
        grad_middle = cot_ref[rows, :] + kernel_norm_back(
            grad_y, hat_y_ref[rows, :], scale_y_ref[rows, :], gain_y
        )
        grad_middle_ref[rows, :] = grad_middle
        gate = gate_ref[rows, :]
        gated = grad_middle * gate
        grad_edge_out = gated.astype(HALF)
        grad_gate = (gated * edge_out_ref[rows, :] * (1.0 - gate)).astype(HALF)
        grad_proj_ref[rows, 4 * channels :] = grad_gate
        x_sum_ref[:, 4 * channels :] += dot_tn(x_half_ref[rows, :], grad_gate)
        out_sum_ref[...] += dot_tn(update_ref[rows, :], grad_edge_out)
        grad_update = dot_nt(grad_edge_out, out_w_ref[...])
        grad_product = kernel_norm_back(grad_update, hat_mid_ref[rows, :], scale_mid_ref[rows, :], gain_mid)
        grad_product_ref[rows, :] = grad_product.astype(HALF).astype(FULL)
        return carry

    lax.fori_loop(0, size // WIDE_BLOCK, middle_back, 0, unroll=True)

    def edges_back(at):
        rows = rows_of(at)
        x_half = x_half_ref[rows, :]
        for side, (first_ref, second_ref, strides, other_ref) in enumerate(
            (
                (left_a_ref, left_b_ref, (1, size), right_ref),
                (right_a_ref, right_b_ref, (size, 1), left_ref),
            )
        ):
            grad = outer_sum(size, at, grad_product_ref, *strides, other_ref)
            both = jnp.concatenate(
                [(grad * first_ref[rows, :]).astype(HALF), (grad * second_ref[rows, :]).astype(HALF)], axis=1
            )
            place = slice(2 * side * channels, 2 * (side + 1) * channels)
            grad_proj_ref[rows, place] = both
            x_sum_ref[:, place] += dot_tn(x_half, both)

    for at in range(blocks):
        for part in range(2 * at, min(2 * at + 2, blocks)):
            attention_sums(part)
        edges_back(at)
        if 2 * at < blocks <= 2 * at + 2:
            attention_results()

    edge_sum, gate_sum = x_sum_ref[:, : 4 * channels] * inverse, x_sum_ref[:, 4 * channels :] * inverse
    edge_sum_ref[...] = edge_sum
    gate_sum_ref[...] = gate_sum
    out_sum = out_sum_ref[...] * inverse
    out_sum_ref[...] = out_sum
    send(0, 1, 2)
    grad_gains_ref[0:1, :] = gain_sum(((edge_w_ref[...], edge_sum), (gate_w_ref[...], gate_sum))) / gain_x
    grad_gains_ref[1:2, :] = gain_sum(((out_w_ref[...], out_sum),)) / gain_mid

    own_cells = size * size // devices
    own = pl.ds(pl.multiple_of(lax.axis_index("dap") * own_cells, own_cells), own_cells)
    hat, scale = kernel_norm(pair_ref[...].reshape(own_cells, channels).astype(FULL))
    grad_x = dot_nt(grad_proj_ref[own, : 4 * channels], edge_w_ref[...])
    grad_x = grad_x + dot_nt(grad_proj_ref[own, 4 * channels :], gate_w_ref[...])
    grad_pair = grad_middle_ref[own, :] + kernel_norm_back(grad_x, hat, scale, gain_x)
    grad_pair_ref[...] = grad_pair.astype(grad_pair_ref.dtype)


def kernel_norm(values):
    center = values - lane_mean(values)
    scale = lax.rsqrt(lane_mean(center * center) + epsilon)
    return center * scale, scale


def kernel_norm_back(grad_out, hat, scale, gain):
    scaled = grad_out * gain
    return scale * (scaled - lane_mean(scaled) - hat * lane_mean(scaled * hat))


def bytes_of(arrays):
    return sum(math.prod(shape) * jnp.dtype(dtype).itemsize for shape, dtype in arrays)


def kernel_scratch(size, channels):
    cells, lanes = size * size, HEADS * size
    full, half = ((cells, channels), FULL), ((cells, channels), HALF)
    square, wide = ((channels, channels), FULL), ((channels, 4 * channels), FULL)
    return {
        "kept": [full] * 12,
        "y": [full],
        "halves": [half] * 2,
        "multiply": [full] * 2,
        "projections": [full, ((size, lanes), FULL)] + [half] * 4 + [((lanes, channels), HALF)],
        "shared": [full] * 2,
        "attend": [half] * 2 + [((cells, 4 * channels + lanes), HALF)],
        "stage": [wide, square, square, wide, square],
        "edges": [full] * 2
        + [((cells, 5 * channels), HALF), ((channels, 5 * channels), FULL), ((channels, 4 * channels + lanes), FULL)],
    }


def whole_kernel(
    size,
    masks,
    near_ref,
    far_ref,
    lengths_ref,
    gains_ref,
    edge_w_ref,
    gate_w_ref,
    out_w_ref,
    att_w_ref,
    bias_w_ref,
    att_out_w_ref,
    grad_pair_ref,
    grad_gains_ref,
    grad_edge_ref,
    grad_gate_w_ref,
    grad_out_w_ref,
    grad_att_w_ref,
    grad_bias_ref,
    grad_att_out_ref,
    *scratch,
):
    part, at = {}, 0
    for name, arrays in kernel_scratch(size, 1).items():
        part[name] = scratch[at : at + len(arrays)]
        at += len(arrays)
    sent = scratch[at]
    weights = (edge_w_ref, gate_w_ref, out_w_ref)
    place_rows(part["shared"][0], 1, near_ref, far_ref, masks)
    multiply_kernel(
        size, masks, near_ref, far_ref, lengths_ref, gains_ref, *weights, *part["kept"], *part["y"], *part["halves"], *part["multiply"]
    )
    project_kernel(size, *part["y"], att_w_ref, bias_w_ref, *part["projections"])
    attend_kernel(
        size,
        lengths_ref,
        att_w_ref,
        att_out_w_ref,
        *part["projections"],
        *part["shared"],
        *part["attend"],
    )
    targets = (grad_edge_ref, grad_gate_w_ref, grad_out_w_ref, grad_att_w_ref, grad_att_out_ref)
    copies = [
        pltpu.make_async_copy(source, target, sent.at[slot])
        for slot, (source, target) in enumerate(zip(part["stage"], targets))
    ]

    def send(*slots):
        for slot in slots:
            copies[slot].start()

    _, _, y_t_ref, _, _, _, bias_rep_ref = part["projections"]
    cot_t_ref, gated_ref, grad_packed_ref = part["attend"]
    edges_kernel(
        size,
        2 * len(masks),
        near_ref.at[0, 0],
        gains_ref,
        *weights,
        *part["kept"],
        *part["halves"],
        *part["shared"],
        (y_t_ref, cot_t_ref, gated_ref, grad_packed_ref, att_w_ref, bias_rep_ref),
        grad_pair_ref,
        grad_gains_ref,
        grad_bias_ref,
        part["stage"],
        send,
        *part["edges"],
    )
    for copy in copies:
        copy.wait()


def replicated_plan(
    axis_size,
    pair_map,
    cotangent,
    lengths,
    norm_gains,
    edge_weight,
    mult_gate_weight,
    mult_out_weight,
    attention_weight,
    bias_weight,
    attention_out_weight,
):
    _, size, channels = pair_map.shape
    cells = size * size
    bits = axis_size.bit_length() - 1
    far_step = 1 << (bits - 1)
    near_steps = range(2, far_step, 2)

    def swapped(held, mask):
        return lax.ppermute(held, "dap", [(d, d ^ mask) for d in range(axis_size)])

    own = jnp.stack([pair_map, cotangent])
    held = jnp.stack([own, swapped(own, far_step)])
    masks = [0, far_step]
    near = jnp.concatenate([held] + [swapped(held, step) for step in near_steps], axis=0)
    masks = masks + [mask ^ step for step in near_steps for mask in masks]
    far = swapped(near, 1)

    square, wide = ((channels, channels), FULL), ((channels, 4 * channels), FULL)
    outs = [((cells // axis_size, channels), HALF), ((3, channels), FULL), wide, square, square]
    outs += [wide, ((HEADS, channels), FULL), square]
    scratch = sum(kernel_scratch(size, channels).values(), [])
    vmem = pl.BlockSpec(memory_space=pltpu.VMEM)
    smem = pl.BlockSpec(memory_space=pltpu.SMEM)
    anywhere = pl.BlockSpec(memory_space=pl.ANY)
    results = pl.pallas_call(
        functools.partial(whole_kernel, size, masks),
        out_shape=[jax.ShapeDtypeStruct(*out) for out in outs],
        in_specs=[vmem, vmem, smem] + [vmem] * 7,
        out_specs=[vmem] * 2 + [anywhere] * 4 + [vmem, anywhere],
        scratch_shapes=[pltpu.VMEM(*part) for part in scratch] + [pltpu.SemaphoreType.DMA((5,))],
        compiler_params=pltpu.CompilerParams(vmem_limit_bytes=bytes_of(scratch) + VMEM_SLACK),
    )(
        near,
        far,
        lengths,
        norm_gains,
        edge_weight,
        mult_gate_weight,
        mult_out_weight,
        attention_weight,
        bias_weight.T,
        attention_out_weight,
    )
    return (results[0].reshape(pair_map.shape), *results[1:6], results[6].T, results[7])


def per_device(axis_size, pair_map, *rest):
    _, size, channels = pair_map.shape
    scratch = sum(kernel_scratch(size, channels).values(), [])
    fits = size % WIDE_BLOCK == 0 and bytes_of(scratch) <= VMEM_SHARE
    if fits and axis_size >= 8 and axis_size & (axis_size - 1) == 0:
        return replicated_plan(axis_size, pair_map, *rest)
    return distributed_plan(pair_map, *rest)


def solution(mesh):
    return jax.shard_map(
        functools.partial(per_device, mesh.shape["dap"]),
        mesh=mesh,
        in_specs=(
            P(("groups", "dap"), None, None),
            P(("groups", "dap"), None, None),
            P("groups"),
            P(),
            P(),
            P(),
            P(),
            P(),
            P(),
            P(),
        ),
        out_specs=(
            P(("groups", "dap"), None, None),
            P("groups", None),
            P("groups", None),
            P("groups", None),
            P("groups", None),
            P("groups", None),
            P("groups", None),
            P("groups", None),
        ),
        check_vma=False,
    )
```
